32 devices in a mesh: req: 8 (over z, y), head: 4 (over x, core).
Axes of the slice: x: 2, y: 2, z: 4, core: 2. Of those that a mesh axis runs over, the one named last changes fastest.
Arguments:
- tokens: bfloat16 [32, 64, 2048], P(('req', 'head')), may hold values from -3 to 3
- live: int32 [32, 64], P(('req', 'head')), may hold values from 0 to 1, as said below
- parents: int32 [32, 64], P('req'), may hold values from -1 to 62, as said below
- lengths: int32 [32], P('req'), may hold values from 1 to 2048, as said below
- accepted: int32 [32, 8], P('req'), may hold values from 0 to 31, as said below
- routes: int32 [32, 64, 6], P(('req', 'head')), may hold values from 0 to 15, all different within a row; in each aligned block of 64 rows (0 to 63, 64 to 127, ..., all dimensions but the last counted through in order) at most 32 rows name the same one
- cache: bfloat16 [32, 4, 2048, 256], P('req', 'head'), may hold values from -160 to 160, as said below
- attn_gain: float32 [2048], replicated, may hold values from 0.1 to 1.9
- w_qkv: bfloat16 [2048, 3072], P(None, 'head'), may hold values from -0.125 to 0.125
- w_out: bfloat16 [2048, 2048], P('head'), may hold values from -0.125 to 0.125
- ffn_gain: float32 [2048], replicated, may hold values from 0.1 to 1.9
- shared_gate: bfloat16 [2048, 1408], P(None, 'head'), may hold values from -0.125 to 0.125
- shared_up: bfloat16 [2048, 1408], P(None, 'head'), may hold values from -0.125 to 0.125
- shared_down: bfloat16 [1408, 2048], P('head'), may hold values from -0.15625 to 0.15625
- router: bfloat16 [2048, 16], replicated, may hold values from -0.125 to 0.125
- expert_in: bfloat16 [32, 2048, 1408], P(('req', 'head')), may hold values from -0.125 to 0.125
- expert_out: bfloat16 [32, 704, 2048], P(('req', 'head')), may hold values from -0.21875 to 0.21875
Outputs:
- hidden_out: bfloat16 [32, 64, 2048], P(('req', 'head'))
- accepted_kv: bfloat16 [32, 4, 8, 256], P('req', 'head')
The draws below stay inside these ranges and needn't reach their ends.
Inputs may be any that keep to these rules, and one draw needn't show every extreme that they name: lengths run from 1 to 2048; every draw has a request with all 2048 slots filled. Each request's live entries are its first ones; at least 32 are live and some request has all 64 live. parents[r, 0] = -1 and parents[r, i] < i for i > 0. `accepted`: each request's entries are distinct, ascending, begin with 0 and name live nodes; some request names node 31. `routes`: within the 64 nodes of one request no expert is named more than 32 times, and in some request one expert is named exactly 32 times; the 6 experts of a node differ. `cache`: entries are finite.
All inputs are finite; a program needn't handle non-finite values.
Results may differ from the reference program's by a relative error of at most 0.012.
The reference program's roundings to bfloat16 on the way count: a program that leaves them out, or rounds other values in their place, can miss the bound.
Values may be sent and summed in bfloat16 or wider, within the bound.
No kernel may reach another device: no remote copies, remote signals or barrier semaphores. Data moves between devices by JAX's collectives and lax.ppermute only.
A program may use at most 128 MiB of HBM per device.

```python
import math
import jax
import jax.numpy as jnp
import numpy as np
from jax import lax

D = 2048
HEADS = 16
KVH = 4
HD = 128
EXP_FF = 1408
TOP = 6
SHARED_FF = 1408
CACHE = 2048
TREE = 64
ACCEPT = 8
REQS = 32
EXPERTS = 16
CAP = 32


def draw_live(key, part):
    key_count, key_full = jax.random.split(key, 2)
    counts = jax.random.randint(key_count, (REQS,), TREE // 2, TREE + 1)
    full_one = jax.random.randint(key_full, (), 0, REQS)
    counts = jnp.where(jnp.arange(REQS) == full_one, TREE, counts)
    return (jnp.arange(TREE)[None, :] < counts[:, None]).astype(jnp.int32)


def draw_parents(key, part):
    nodes = jnp.arange(TREE, dtype=jnp.int32)
    lower = jnp.maximum(nodes - 6, 0)
    upper = jnp.maximum(nodes, 1)
    picked = jax.random.randint(key, (REQS, TREE), lower[None, :], upper[None, :])
    return jnp.where(nodes[None, :] == 0, -1, picked).astype(jnp.int32)


def draw_lengths(key, part):
    key_shift, key_len, key_full = jax.random.split(key, 3)
    shrink = jax.random.randint(key_shift, (REQS,), 0, 6)
    base = CACHE // jnp.power(2, shrink)
    picked = jax.random.randint(key_len, (REQS,), base // 2 + 1, base + 1)
    full_one = jax.random.randint(key_full, (), 0, REQS)
    return jnp.where(jnp.arange(REQS) == full_one, CACHE, picked).astype(jnp.int32)


def draw_accepted(key, part):
    key_rows, key_full = jax.random.split(key, 2)
    row_keys = jax.random.split(key_rows, REQS)

    def one_row(row_key):
        order = jax.random.permutation(row_key, TREE // 2 - 1) + 1
        return jnp.sort(order[:ACCEPT - 1])
    rest = jax.vmap(one_row)(row_keys)
    full_one = jax.random.randint(key_full, (), 0, REQS)
    rest = rest.at[full_one, ACCEPT - 2].set(TREE // 2 - 1)
    return jnp.concatenate([jnp.zeros((REQS, 1), jnp.int32), rest.astype(jnp.int32)], axis=1)


def draw_cache(key, part):
    key_keys, key_values = jax.random.split(key, 2)
    shape = (REQS, KVH, CACHE, HD)
    keys = jnp.clip(jax.random.normal(key_keys, shape, jnp.float32), -6.0, 6.0)
    values = jnp.clip(6.0 * jax.random.normal(key_values, shape, jnp.float32), -36.0, 36.0)
    return jnp.concatenate([keys, values], axis=-1).astype(jnp.bfloat16)


def levels(rng, shape, cuts, least, largest):
    loudness, own = 1.0, jax.random.fold_in(rng, 6)
    for dim, blocks in cuts:
        draws = jnp.exp(jax.random.uniform(jax.random.fold_in(own, dim), (blocks,), jnp.float32, least / len(cuts), largest / len(cuts)))
        loudness = loudness * jnp.repeat(draws, shape[dim] // blocks).reshape([-1 if axis == dim else 1 for axis in range(len(shape))])
    return loudness


def assign_block(rng, own, number, rows, number_of, top, most, slope):
    ranking = jax.random.permutation(rng, number_of)
    packed, usual = shares(number_of, rows * top, most, slope, True), shares(number_of, rows * top, most, slope, False)
    places = jnp.arange(number_of)

    def named(sizes, rotation):
        used = int((sizes > 0).sum())
        fixed = max(1, used // 4)
        moved = fixed + (places - fixed + rotation * (used - fixed)) % max(1, number_of - fixed)
        return jnp.zeros((number_of,), jnp.int32).at[ranking[jnp.where(places < fixed, places, moved)]].set(jnp.asarray(sizes, jnp.int32))

    sizes = jnp.where(number % 4 == 0, named(packed, number // 4), named(usual, number - number // 4 - 1))
    mixed = jax.random.permutation(jax.random.fold_in(own, 3), number_of)
    donor, sink = mixed[0:number_of // 2 * 2:2], mixed[1:number_of // 2 * 2:2]
    slack = jnp.minimum(sizes[donor] - 1, most - sizes[sink]) // 2
    slack = jnp.where((donor == ranking[0]) | (sink == ranking[0]) | (sizes[sink] == 0), 0, jnp.maximum(slack, 0))
    moved = jax.random.randint(jax.random.fold_in(own, 4), (number_of // 2,), 0, 1 << 20) % (slack + 1)
    sizes = sizes.at[donor].add(-moved).at[sink].add(moved)
    items = jnp.searchsorted(jnp.cumsum(sizes), jnp.arange(rows * top), side="right").astype(jnp.int32)
    listing = items.reshape(top, rows).T
    listing = listing[jax.random.permutation(jax.random.fold_in(own, 1), rows)]
    rotation = jax.random.randint(jax.random.fold_in(own, 2), (rows, 1), 0, top)
    return jnp.take_along_axis(listing, (jnp.arange(top)[None, :] + rotation) % top, axis=1)


def shares(count, total, bound, skew, full):
    loads = [(1 << 20) // math.isqrt(standing ** skew) + 1 for standing in range(1, count + 1)]
    largest = bound if full else min(bound, max(-(-total // count), total * loads[0] // sum(loads)))
    least = 1 if total - largest >= count - 1 else 0
    given, surplus = [largest] + [least] * (count - 1), total - largest - least * (count - 1)
    while surplus > 0:
        movable = [i for i in range(1, count) if given[i] < largest] or [i for i in range(1, count) if given[i] < bound]
        mass, left = sum([loads[i] for i in movable]), surplus
        for i in movable:
            addition = min(bound - given[i], max(1, left * loads[i] // mass), surplus)
            given[i] = given[i] + addition
            surplus = surplus - addition
    return np.array(given)


def centred(stream_key, extent, scale, bound, cuts=(), kind=jnp.bfloat16):
    factor_of = levels(stream_key, extent, cuts, -0.22, 0.18) if cuts else 1.0
    drawn = jax.random.normal(stream_key, extent, jnp.float32) * scale * factor_of
    return jnp.minimum(jnp.maximum(drawn, -bound), bound).astype(kind)


def setup_inputs(seed: int = 0) -> dict:
    key_list = jax.random.split(jax.random.key(seed), 18)
    tokens = centred(key_list[0], (REQS, TREE, D), 0.5, 3.0, ((0, 32),))
    live = draw_live(jax.random.fold_in(key_list[17], 71), 0)
    parents = draw_parents(jax.random.fold_in(key_list[17], 71), 0)
    lengths = draw_lengths(jax.random.fold_in(key_list[17], 71), 0)
    accepted = draw_accepted(jax.random.fold_in(key_list[17], 71), 0)
    routes_keys = jax.random.split(jax.random.fold_in(key_list[5], 1), REQS * TREE // TREE)
    routes_turns = jax.random.permutation(jax.random.fold_in(key_list[5], 3), REQS * TREE // TREE)
    routes = jax.vmap(lambda own, number: assign_block(jax.random.fold_in(key_list[5], 2), own, number, TREE, EXPERTS, TOP, CAP, 2))(routes_keys, routes_turns).reshape((REQS, TREE, TOP))
    cache = draw_cache(jax.random.fold_in(key_list[17], 71), 0)
    attn_gain = jnp.clip(1.0 + 0.18 * jax.random.normal(key_list[7], (D,), jnp.float32), 0.1, 1.9)
    w_qkv = centred(key_list[8], (D, KVH * (HEADS // KVH + 2) * HD), D ** -0.5, 0.125, ((1, 4),))
    w_out = centred(key_list[9], (HEADS * HD, D), (HEADS * HD) ** -0.5, 0.125, ((0, 4),))
    ffn_gain = jnp.clip(1.0 + 0.18 * jax.random.normal(key_list[10], (D,), jnp.float32), 0.1, 1.9)
    shared_gate = centred(key_list[11], (D, SHARED_FF), D ** -0.5, 0.125, ((1, 4),))
    shared_up = centred(key_list[12], (D, SHARED_FF), D ** -0.5, 0.125, ((1, 4),))
    shared_down = centred(key_list[13], (SHARED_FF, D), SHARED_FF ** -0.5, 0.15625, ((0, 4),))
    router = centred(key_list[14], (D, EXPERTS), D ** -0.5, 0.125)
    expert_in = centred(key_list[15], (2 * EXPERTS, D, EXP_FF), D ** -0.5, 0.125, ((0, 32),))
    expert_out = centred(key_list[16], (2 * EXPERTS, EXP_FF // 2, D), (EXP_FF // 2) ** -0.5, 0.21875, ((0, 32),))
    return {"tokens": tokens, "live": live, "parents": parents, "lengths": lengths, "accepted": accepted, "routes": routes, "cache": cache, "attn_gain": attn_gain, "w_qkv": w_qkv, "w_out": w_out, "ffn_gain": ffn_gain, "shared_gate": shared_gate, "shared_up": shared_up, "shared_down": shared_down, "router": router, "expert_in": expert_in, "expert_out": expert_out}


EPSILON = 1e-06
ROPE_BASE = 10000.0

def rms_norm(values, gain):
    wide = values.astype(jnp.float32)
    power = lax.optimization_barrier(jnp.mean(wide * wide, axis=-1, keepdims=True))
    return (wide * lax.rsqrt(power + EPSILON) * gain).astype(jnp.bfloat16)

def rotate(values, position):
    half = values.shape[-1] // 2
    frequency = ROPE_BASE ** (-jnp.arange(half, dtype=jnp.float32) / half)
    angle = position[..., None] * frequency
    cosine = jnp.cos(angle)
    sine = jnp.sin(angle)
    first = values[..., :half]
    second = values[..., half:]
    return jnp.concatenate([first * cosine - second * sine, second * cosine + first * sine], axis=-1)

def ancestry(parents):
    nodes_count = parents.shape[-1]
    nodes = jnp.arange(nodes_count, dtype=jnp.int32)
    reach = (parents[..., :, None] == nodes).astype(jnp.float32) + jnp.eye(nodes_count, dtype=jnp.float32)
    for turn in range(nodes_count.bit_length()):
        reach = jnp.minimum(jnp.einsum('rij,rjk->rik', reach, reach, precision=lax.Precision.HIGHEST), 1.0)
    depth = lax.optimization_barrier(jnp.sum(reach, axis=-1)) - 1.0
    return (reach, depth)

def head_group(projected, position, length, reach, cache_rows):
    group = projected.shape[0] - 2
    tree = projected.shape[1]
    head_dim = projected.shape[2]
    query = rotate(projected[:group], position).astype(jnp.bfloat16).reshape(group * tree, head_dim)
    key_new = rotate(projected[group], position).astype(jnp.bfloat16)
    value_new = projected[group + 1].astype(jnp.bfloat16)
    scale = 1.0 / math.sqrt(head_dim)
    cache_keys = cache_rows[:, :head_dim]
    cache_values = cache_rows[:, head_dim:]
    old_scores = jnp.einsum('qd,kd->qk', query, cache_keys, preferred_element_type=jnp.float32) * scale
    new_scores = jnp.einsum('qd,kd->qk', query, key_new, preferred_element_type=jnp.float32) * scale
    visible = jnp.arange(cache_rows.shape[0], dtype=jnp.int32) < length
    old_scores = jnp.where(visible[None, :], old_scores, -1e+30)
    new_scores = jnp.where(jnp.tile(reach, (group, 1)) > 0.5, new_scores, -1e+30)
    peak = jnp.maximum(lax.optimization_barrier(jnp.max(old_scores, axis=-1, keepdims=True)), lax.optimization_barrier(jnp.max(new_scores, axis=-1, keepdims=True)))
    old_weights = jnp.exp(old_scores - peak)
    new_weights = jnp.exp(new_scores - peak)
    denominator = lax.optimization_barrier(jnp.sum(old_weights, axis=-1, keepdims=True)) + lax.optimization_barrier(jnp.sum(new_weights, axis=-1, keepdims=True))
    old_probs = (old_weights / denominator).astype(jnp.bfloat16)
    new_probs = (new_weights / denominator).astype(jnp.bfloat16)
    mixed = jnp.dot(old_probs, cache_values, preferred_element_type=jnp.float32) + jnp.dot(new_probs, value_new, preferred_element_type=jnp.float32)
    mixed = mixed.astype(jnp.bfloat16).reshape(group, tree, head_dim).transpose(1, 0, 2).reshape(tree, group * head_dim)
    return (mixed, jnp.concatenate([key_new, value_new], axis=-1))

def expert_half(rows, inner, outer):
    both = jnp.dot(rows, inner, preferred_element_type=jnp.float32)
    half = inner.shape[1] // 2
    hidden = (jax.nn.silu(both[:, :half]) * both[:, half:]).astype(jnp.bfloat16)
    return jnp.dot(hidden, outer, preferred_element_type=jnp.float32).astype(jnp.bfloat16)

def reference(tokens, live, parents, lengths, accepted, routes, cache, attn_gain, w_qkv, w_out, ffn_gain, shared_gate, shared_up, shared_down, router, expert_in, expert_out):
    request_count, tree, width = tokens.shape
    kv_heads = cache.shape[1]
    head_dim = cache.shape[3] // 2
    group = w_qkv.shape[1] // (kv_heads * head_dim) - 2
    top_count = routes.shape[2]
    expert_count = router.shape[1]
    capacity = 4 * tree * top_count // (3 * expert_count)
    normed = rms_norm(tokens, attn_gain)
    reach, depth = ancestry(parents)
    positions = lengths[:, None].astype(jnp.float32) + depth

    def one_request(inputs):
        rows, raw_rows, reach_one, position, length, chosen, cache_one = inputs
        projected = jnp.dot(rows, w_qkv, preferred_element_type=jnp.float32)
        projected = projected.reshape(tree, kv_heads, group + 2, head_dim).transpose(1, 2, 0, 3)
        mixed, fresh = jax.vmap(head_group, in_axes=(0, None, None, None, 0))(projected, position, length, reach_one, cache_one)
        mixed = mixed.transpose(1, 0, 2).reshape(tree, kv_heads * group * head_dim)
        attn = jnp.dot(mixed, w_out, preferred_element_type=jnp.float32)
        resid_one = (raw_rows.astype(jnp.float32) + attn).astype(jnp.bfloat16)
        return (resid_one, fresh[:, chosen])
    resid, accepted_kv = lax.map(one_request, (normed, tokens, reach, positions, lengths, accepted, cache))
    normed2 = rms_norm(resid, ffn_gain)
    flat = normed2.reshape(request_count * tree, width)
    shared_hidden = (jax.nn.silu(jnp.dot(flat, shared_gate, preferred_element_type=jnp.float32)) * jnp.dot(flat, shared_up, preferred_element_type=jnp.float32)).astype(jnp.bfloat16)
    shared = jnp.dot(shared_hidden, shared_down, preferred_element_type=jnp.float32)
    logits = jnp.dot(flat, router, preferred_element_type=jnp.float32)
    route_flat = routes.reshape(request_count * tree, top_count)
    picked = jax.nn.sigmoid(jnp.take_along_axis(logits, route_flat, axis=1))
    gates = picked / lax.optimization_barrier(jnp.sum(picked, axis=-1, keepdims=True))
    assign = routes.reshape(request_count, tree * top_count)
    onehot = (assign[..., None] == jnp.arange(expert_count, dtype=jnp.int32)).astype(jnp.int32)
    earlier = jnp.cumsum(onehot, axis=1) - onehot
    slots = lax.optimization_barrier(jnp.sum(earlier * onehot, axis=-1)).astype(jnp.int32)
    request_rows = jnp.broadcast_to(jnp.arange(request_count, dtype=jnp.int32)[:, None], assign.shape)
    token_ids = (jnp.arange(request_count * tree * top_count, dtype=jnp.int32) // top_count).reshape(request_count, tree * top_count)
    table = jnp.zeros((expert_count, request_count, capacity), jnp.int32).at[assign, request_rows, slots].set(token_ids)
    gate_table = jnp.zeros((expert_count, request_count, capacity), jnp.float32).at[assign, request_rows, slots].set(gates.reshape(request_count, tree * top_count))
    inner_all = expert_in.reshape(expert_count, 2, width, expert_in.shape[2])
    outer_all = expert_out.reshape(expert_count, 2, expert_out.shape[1], width)

    def one_expert(total, inputs):
        rows_index, rows_gate, inner, outer = inputs
        index_flat = rows_index.reshape(-1)
        chosen_rows = flat[index_flat]
        first = expert_half(chosen_rows, inner[0], outer[0]).astype(jnp.float32)
        second = expert_half(chosen_rows, inner[1], outer[1]).astype(jnp.float32)
        total = total.at[index_flat].add(rows_gate.reshape(-1, 1) * (first + second))
        return (total, None)
    routed, unused = lax.scan(one_expert, jnp.zeros((request_count * tree, width), jnp.float32), (table, gate_table, inner_all, outer_all))
    total_out = resid.reshape(request_count * tree, width).astype(jnp.float32) + shared + routed
    keep = live.reshape(request_count * tree, 1) == 1
    hidden_out = jnp.where(keep, total_out, 0.0).astype(jnp.bfloat16).reshape(request_count, tree, width)
    return (hidden_out, accepted_kv)
```

```python
import math

import jax
import jax.numpy as jnp
from jax import lax
from jax.sharding import Mesh
from jax.sharding import PartitionSpec as P

EPSILON = 1e-06
ROPE_BASE = 10000.0
PARTS = 2
ALL = ("z", "y", "x", "c")
PLANE = ("y", "x")
HEAD = ("x", "c")


def partner(value, axes, offset):
    if offset == 0:
        return value
    size = lax.axis_size(axes)
    return lax.ppermute(value, axes, [(i, i ^ offset) for i in range(size)])


def rms_norm(values, gain):
    wide = values.astype(jnp.float32)
    power = jnp.mean(wide * wide, axis=-1, keepdims=True)
    return (wide * lax.rsqrt(power + EPSILON) * gain).astype(jnp.bfloat16)


def dot(left, right):
    return jnp.dot(left, right, preferred_element_type=jnp.float32)


def rotate(values, position):
    half = values.shape[-1] // 2
    frequency = ROPE_BASE ** (-jnp.arange(half, dtype=jnp.float32) / half)
    angle = position[..., None] * frequency
    cosine = jnp.cos(angle)
    sine = jnp.sin(angle)
    first = values[..., :half]
    second = values[..., half:]
    return jnp.concatenate(
        [first * cosine - second * sine, second * cosine + first * sine], axis=-1
    )


def ancestry(parents):
    nodes_count = parents.shape[-1]
    nodes = jnp.arange(nodes_count, dtype=jnp.int32)
    reach = (parents[..., :, None] == nodes).astype(jnp.float32) + jnp.eye(
        nodes_count, dtype=jnp.float32
    )
    for turn in range((nodes_count - 1).bit_length()):
        near = reach.astype(jnp.bfloat16)
        reach = jnp.minimum(
            jnp.einsum("rij,rjk->rik", near, near, preferred_element_type=jnp.float32), 1.0
        )
    depth = jnp.sum(reach, axis=-1) - 1.0
    return (reach, depth)


def head_group(projected, position, length, reach, cache_rows):
    group = projected.shape[0] - 2
    tree = projected.shape[1]
    head_dim = projected.shape[2]
    query = rotate(projected[:group], position).astype(jnp.bfloat16).reshape(group * tree, head_dim)
    key_new = rotate(projected[group], position).astype(jnp.bfloat16)
    value_new = projected[group + 1].astype(jnp.bfloat16)
    scale = 1.0 / math.sqrt(head_dim)
    cache_keys = cache_rows[:, :head_dim]
    cache_values = cache_rows[:, head_dim:]
    old_scores = (
        jnp.einsum("qd,kd->qk", query, cache_keys, preferred_element_type=jnp.float32) * scale
    )
    new_scores = jnp.einsum("qd,kd->qk", query, key_new, preferred_element_type=jnp.float32) * scale
    visible = jnp.arange(cache_rows.shape[0], dtype=jnp.int32) < length
    old_scores = jnp.where(visible[None, :], old_scores, -1e30)
    new_scores = jnp.where(jnp.tile(reach, (group, 1)) > 0.5, new_scores, -1e30)
    peak = jnp.maximum(
        jnp.max(old_scores, axis=-1, keepdims=True), jnp.max(new_scores, axis=-1, keepdims=True)
    )
    old_weights = jnp.exp(old_scores - peak)
    new_weights = jnp.exp(new_scores - peak)
    denominator = jnp.sum(old_weights, axis=-1, keepdims=True) + jnp.sum(
        new_weights, axis=-1, keepdims=True
    )
    old_probs = (old_weights / denominator).astype(jnp.bfloat16)
    new_probs = (new_weights / denominator).astype(jnp.bfloat16)
    mixed = dot(old_probs, cache_values) + dot(new_probs, value_new)
    mixed = (
        mixed.astype(jnp.bfloat16)
        .reshape(group, tree, head_dim)
        .transpose(1, 0, 2)
        .reshape(tree, group * head_dim)
    )
    return (mixed, jnp.concatenate([key_new, value_new], axis=-1))


def body(
    tokens,
    live,
    parents,
    lengths,
    accepted,
    routes,
    cache,
    attn_gain,
    w_qkv,
    w_out,
    ffn_gain,
    shared_gate,
    shared_up,
    shared_down,
    router,
    expert_in,
    expert_out,
):
    tree = tokens.shape[1]
    width = tokens.shape[2]
    own_rows = tokens[0]
    group_count = lax.axis_size(HEAD)
    local_heads = cache.shape[1]
    head_dim = cache.shape[3] // 2
    group = w_qkv.shape[1] // (local_heads * head_dim) - 2
    me = lax.axis_index(HEAD)

    core_rows = partner(own_rows, "c", 1)
    side = lax.axis_size("x")
    near = [own_rows] + [partner(own_rows, "x", o) for o in range(1, side)]
    rows_by = []
    for o in range(side):
        rows_by += [near[o], core_rows if o == 0 else partner(near[o], "c", 1)]

    line = lax.axis_size("z")
    chosen = [partner(routes[0], "z", k) for k in range(line)]
    inner = [expert_in[0], partner(expert_in[0], "c", 1)]
    outer = [expert_out[0], partner(expert_out[0], "c", 1)]
    out_pair = [w_out, partner(w_out, "c", 1)]
    gate_pair = [shared_gate, partner(shared_gate, "c", 1)]
    up_pair = [shared_up, partner(shared_up, "c", 1)]
    down_pair = [shared_down, partner(shared_down, "c", 1)]

    order = me ^ jnp.arange(group_count, dtype=jnp.int32)
    rows = jnp.stack(rows_by)[order].reshape(group_count * tree, width)
    projected = dot(rms_norm(rows, attn_gain), w_qkv)
    projected = projected.reshape(group_count, tree, local_heads, group + 2, head_dim).transpose(
        0, 2, 3, 1, 4
    )
    reach, depth = ancestry(parents)
    positions = lengths[:, None].astype(jnp.float32) + depth
    inner_map = jax.vmap(head_group, in_axes=(0, None, None, None, 0))
    mixed, fresh = jax.vmap(inner_map)(projected, positions, lengths, reach, cache)
    mixed = mixed.transpose(0, 2, 1, 3).reshape(group_count, tree, local_heads * group * head_dim)
    accepted_kv = jnp.take_along_axis(fresh, accepted[:, None, :, None], axis=2)

    mixed = mixed[order].reshape(side, 2, tree, -1)
    mine = mixed[:, 0].reshape(side * tree, -1)
    other = partner(mixed[:, 1].reshape(side * tree, -1), "c", 1)
    terms = (dot(mine, out_pair[0]) + dot(other, out_pair[1])).reshape(side, tree, width)
    attn = terms[0]
    for o in range(1, side):
        attn = attn + partner(terms[o].astype(jnp.bfloat16), "x", o).astype(jnp.float32)
    resid = (own_rows.astype(jnp.float32) + attn).astype(jnp.bfloat16)
    normed = rms_norm(resid, ffn_gain)

    expert_count = router.shape[1]
    top_count = routes.shape[2]
    capacity = 4 * tree * top_count // (3 * expert_count)
    plane = lax.axis_size(PLANE)
    spot = lax.axis_index(PLANE)
    first = lax.axis_index("z") * plane
    choose = jnp.stack(chosen)
    member = jnp.any(
        choose[..., None] == jnp.arange(expert_count, dtype=jnp.int32), axis=2
    )
    before = jnp.tril(jnp.ones((tree, tree), jnp.bfloat16), -1)
    ranks = jnp.einsum(
        "nm,kme->kne", before, member.astype(jnp.bfloat16), preferred_element_type=jnp.float32
    ).astype(jnp.int32)
    near_experts = first + (spot ^ jnp.arange(plane, dtype=jnp.int32))
    is_near = near_experts[:, None] == jnp.arange(expert_count, dtype=jnp.int32)
    slot = jnp.where(member, ranks, -1)
    slot_near = jnp.sum(
        jnp.where(is_near[:, None, None, :], slot[None] + 1, 0), axis=-1
    ) - 1
    places = jnp.arange(capacity, dtype=jnp.int32)
    pick = slot_near[:, :, None, :] == places[:, None]
    pick_bf = pick.astype(jnp.bfloat16)

    cols = width // PARTS
    line_rows = []
    received = []
    for p in range(PARTS):
        piece = normed[:, p * cols : (p + 1) * cols]
        line_piece = [partner(piece, "z", k) for k in range(line)]
        line_rows.append(line_piece)
        stack = jnp.stack(line_piece)
        got = []
        for o in range(plane):
            out = jnp.einsum(
                "ksn,knd->ksd", pick_bf[o], stack, preferred_element_type=jnp.float32
            ).astype(jnp.bfloat16)
            got.append(partner(out.reshape(line * capacity, cols), PLANE, o))
        received.append(jnp.concatenate(got, axis=0))

    near_normed = [normed] + [partner(normed, "x", o) for o in range(1, side)]
    block = jnp.concatenate(near_normed, axis=0)
    shared_terms = 0.0
    for i in range(2):
        hidden = (jax.nn.silu(dot(block, gate_pair[i])) * dot(block, up_pair[i])).astype(
            jnp.bfloat16
        )
        shared_terms = shared_terms + dot(hidden, down_pair[i])
    shared_terms = shared_terms.reshape(side, tree, width)
    shared = shared_terms[0]
    for o in range(1, side):
        shared = shared + partner(shared_terms[o].astype(jnp.bfloat16), "x", o).astype(jnp.float32)

    logits = sum(
        dot(jnp.concatenate(line_rows[p], axis=0), router[p * cols : (p + 1) * cols])
        for p in range(PARTS)
    ).reshape(line, tree, expert_count)
    picked = jnp.where(member, jax.nn.sigmoid(logits), 0.0)
    gates = picked / jnp.sum(picked, axis=-1, keepdims=True)
    gates_near = jnp.sum(jnp.where(is_near[:, None, None, :], gates[None], 0.0), axis=-1)
    spread = jnp.where(pick, gates_near[:, :, None, :], 0.0)
    spread = spread.astype(jnp.bfloat16)

    hidden = []
    for i in range(2):
        both = sum(dot(received[p], inner[i][p * cols : (p + 1) * cols]) for p in range(PARTS))
        half = both.shape[1] // 2
        hidden.append((jax.nn.silu(both[:, :half]) * both[:, half:]).astype(jnp.bfloat16))

    routed = []
    for p in range(PARTS):
        result = sum(
            dot(hidden[i], outer[i][:, p * cols : (p + 1) * cols])
            .astype(jnp.bfloat16)
            .astype(jnp.float32)
            for i in range(2)
        ).astype(jnp.bfloat16)
        result = result.reshape(plane, line, capacity, cols)
        back = jnp.stack([partner(result[o], PLANE, o) for o in range(plane)])
        partial = jnp.einsum(
            "oksn,oksd->knd", spread, back, preferred_element_type=jnp.float32
        )
        total = partial[0]
        for k in range(1, line):
            total = total + partner(partial[k].astype(jnp.bfloat16), "z", k).astype(jnp.float32)
        routed.append(total)
    routed = jnp.concatenate(routed, axis=1)

    total_out = resid.astype(jnp.float32) + shared + routed
    hidden_out = jnp.where(live[0][:, None] == 1, total_out, 0.0).astype(jnp.bfloat16)
    return (hidden_out[None], accepted_kv)


def solution(mesh):
    line = 4
    shape = (line, mesh.shape["req"] // line, mesh.shape["head"] // 2, 2)
    grid = Mesh(mesh.devices.reshape(shape), ALL)
    req = ("z", "y")
    in_specs = (
        P(ALL, None, None),
        P(ALL, None),
        P(req, None),
        P(req),
        P(req, None),
        P(ALL, None, None),
        P(req, HEAD, None, None),
        P(),
        P(None, HEAD),
        P(HEAD, None),
        P(),
        P(None, HEAD),
        P(None, HEAD),
        P(HEAD, None),
        P(),
        P(ALL, None, None),
        P(ALL, None, None),
    )
    out_specs = (P(ALL, None, None), P(req, HEAD, None, None))
    return jax.shard_map(body, mesh=grid, in_specs=in_specs, out_specs=out_specs, check_vma=False)
```

```python
import math

import jax
import jax.numpy as jnp
from jax import lax
from jax.experimental import pallas as pl
from jax.experimental.pallas import tpu as pltpu
from jax.sharding import Mesh
from jax.sharding import PartitionSpec as P

EPSILON = 1e-06
ROPE_BASE = 10000.0
GROUPS = ((0, 1), (3,), (2,))
CHUNK = 512
ALL = ("z", "y", "x", "c")
PLANE = ("y", "x")
HEAD = ("x", "c")


def partner(value, axes, offset):
    if offset == 0:
        return value
    size = lax.axis_size(axes)
    return lax.ppermute(value, axes, [(i, i ^ offset) for i in range(size)])


def rms_norm(values, gain):
    wide = values.astype(jnp.float32)
    power = jnp.mean(wide * wide, axis=-1, keepdims=True)
    return (wide * lax.rsqrt(power + EPSILON) * gain).astype(jnp.bfloat16)


def dot(left, right):
    return jnp.dot(left, right, preferred_element_type=jnp.float32)


def ancestry(parents):
    nodes_count = parents.shape[-1]
    nodes = jnp.arange(nodes_count, dtype=jnp.int32)
    reach = (parents[..., :, None] == nodes).astype(jnp.float32) + jnp.eye(
        nodes_count, dtype=jnp.float32
    )
    for turn in range((nodes_count - 1).bit_length()):
        near = reach.astype(jnp.bfloat16)
        reach = jnp.minimum(
            jnp.einsum("rij,rjk->rik", near, near, preferred_element_type=jnp.float32), 1.0
        )
    depth = jnp.sum(reach, axis=-1) - 1.0
    return (reach, depth)


def attend_kernel(
    ids, lengths, first, second, gain, weight, cosine, sine, reach, cache, mixed, fresh, projected
):
    step = pl.program_id(0)
    tree = first.shape[0]
    head_dim = cosine.shape[2]
    group = weight.shape[1] // head_dim - 2

    @pl.when(step == 0)
    def _():
        wide = jnp.concatenate([first[...], second[...]], axis=0).astype(jnp.float32)
        power = jnp.mean(wide * wide, axis=-1, keepdims=True)
        normed = (wide * lax.rsqrt(power + EPSILON) * gain[...]).astype(jnp.bfloat16)
        projected[...] = dot(normed, weight[...])

    rows = pl.ds(pl.multiple_of(step * tree, tree), tree)
    length = lengths[ids[step]]

    def rope(values):
        return values * cosine[0] + pltpu.roll(values, head_dim // 2, 1) * sine[0]

    def column(i):
        return projected[rows, i * head_dim : (i + 1) * head_dim]

    query = jnp.concatenate([rope(column(h)).astype(jnp.bfloat16) for h in range(group)], axis=0)
    key_new = rope(column(group)).astype(jnp.bfloat16)
    value_new = column(group + 1).astype(jnp.bfloat16)
    fresh[0, :, :head_dim] = key_new
    fresh[0, :, head_dim:] = value_new
    scale = 1.0 / math.sqrt(head_dim)

    def against(keys):
        return (
            lax.dot_general(
                query, keys, (((1,), (1,)), ((), ())), preferred_element_type=jnp.float32
            )
            * scale
        )

    allowed = jnp.concatenate([reach[0]] * group, axis=0) > 0.5
    scores = jnp.where(allowed, against(key_new), -1e30)
    peak = jnp.max(scores, axis=-1, keepdims=True)
    weights = jnp.exp(scores - peak)
    total = jnp.sum(weights, axis=-1, keepdims=True)
    summed = dot(weights.astype(jnp.bfloat16), value_new)

    def chunk(j, carry):
        peak, total, summed = carry
        block = pl.ds(pl.multiple_of(j * CHUNK, CHUNK), CHUNK)
        scores = against(cache[0, block, :head_dim])
        place = j * CHUNK + lax.broadcasted_iota(jnp.int32, scores.shape, 1)
        scores = jnp.where(place < length, scores, -1e30)
        higher = jnp.maximum(peak, jnp.max(scores, axis=-1, keepdims=True))
        fade = jnp.exp(peak - higher)
        weights = jnp.exp(scores - higher)
        total = total * fade + jnp.sum(weights, axis=-1, keepdims=True)
        summed = summed * fade + dot(weights.astype(jnp.bfloat16), cache[0, block, head_dim:])
        return (higher, total, summed)

    peak, total, summed = lax.fori_loop(
        0, lax.div(length + CHUNK - 1, CHUNK), chunk, (peak, total, summed)
    )
    result = (summed / total).astype(jnp.bfloat16)
    for h in range(group):
        mixed[0, :, h * head_dim : (h + 1) * head_dim] = result[h * tree : (h + 1) * tree]


def attend(ids, lengths, first, second, gain, weight, cosine, sine, reach, cache):
    tree, width = first.shape
    slots, pair = cache.shape[1:]
    head_dim = pair // 2
    columns = weight.shape[1]
    whole = lambda i, ids, lengths: (0, 0)
    by_request = lambda i, ids, lengths: (ids[i], 0, 0)
    by_step = lambda i, ids, lengths: (i, 0, 0)
    group_columns = columns - pair
    return pl.pallas_call(
        attend_kernel,
        grid_spec=pltpu.PrefetchScalarGridSpec(
            num_scalar_prefetch=2,
            grid=(2,),
            in_specs=[
                pl.BlockSpec((tree, width), whole),
                pl.BlockSpec((tree, width), whole),
                pl.BlockSpec((1, width), whole),
                pl.BlockSpec((width, columns), whole),
                pl.BlockSpec((1, tree, head_dim), by_request),
                pl.BlockSpec((1, tree, head_dim), by_request),
                pl.BlockSpec((1, tree, tree), by_request),
                pl.BlockSpec((1, slots, pair), by_request),
            ],
            out_specs=[
                pl.BlockSpec((1, tree, group_columns), by_step),
                pl.BlockSpec((1, tree, pair), by_step),
            ],
            scratch_shapes=[pltpu.VMEM((2 * tree, columns), jnp.float32)],
        ),
        out_shape=[
            jax.ShapeDtypeStruct((2, tree, group_columns), jnp.bfloat16),
            jax.ShapeDtypeStruct((2, tree, pair), jnp.bfloat16),
        ],
        compiler_params=pltpu.CompilerParams(vmem_limit_bytes=24 * 2**20),
        cost_estimate=pl.CostEstimate(
            flops=4 * tree * (width * columns + group_columns * slots * 2),
            bytes_accessed=2 * (width * columns + 2 * slots * pair),
            transcendentals=2 * tree * slots * group_columns // head_dim,
        ),
    )(ids, lengths, first, second, gain, weight, cosine, sine, reach, cache)


def body(
    tokens,
    live,
    parents,
    lengths,
    accepted,
    routes,
    cache,
    attn_gain,
    w_qkv,
    w_out,
    ffn_gain,
    shared_gate,
    shared_up,
    shared_down,
    router,
    expert_in,
    expert_out,
):
    tree = tokens.shape[1]
    width = tokens.shape[2]
    own_rows = tokens[0]
    group_count = lax.axis_size(HEAD)
    head_dim = cache.shape[3] // 2
    me = lax.axis_index(HEAD)

    side = lax.axis_size("x")
    near = [own_rows] + [partner(own_rows, "x", o) for o in range(1, side)]
    near_core = [partner(rows, "c", 1) for rows in near]

    reach, depth = ancestry(parents)
    positions = lengths[:, None].astype(jnp.float32) + depth
    frequency = ROPE_BASE ** (-jnp.arange(head_dim // 2, dtype=jnp.float32) / (head_dim // 2))
    angle = positions[..., None] * frequency
    cosine = jnp.cos(angle)
    sine = jnp.sin(angle)
    cosine = jnp.concatenate([cosine, cosine], axis=-1)
    sine = jnp.concatenate([-sine, sine], axis=-1)

    line = lax.axis_size("z")
    own_routes, _ = lax.optimization_barrier((routes[0], sine))
    chosen = [partner(own_routes, "z", k) for k in range(line)]
    early, _ = lax.optimization_barrier(((w_out, shared_gate), near_core[0]))
    late, _ = lax.optimization_barrier(
        ((expert_in[0], expert_out[0], shared_up, shared_down), near_core[side - 1])
    )
    early = [partner(weight, "c", 1) for weight in early]
    late = [partner(weight, "c", 1) for weight in late]
    out_pair = [w_out, early[0]]

    terms = [None] * side
    fresh = [None] * side
    follow = None
    for o in reversed(range(side)):
        if follow is not None:
            near_core[o], _ = lax.optimization_barrier((near_core[o], follow))
        ids = me ^ jnp.arange(2 * o, 2 * o + 2, dtype=jnp.int32)
        mixed, fresh[o] = attend(
            ids,
            lengths,
            near[o],
            near_core[o],
            attn_gain[None],
            w_qkv,
            cosine,
            sine,
            reach,
            cache[:, 0],
        )
        follow = mixed
        other = partner(mixed[1], "c", 1)
        terms[o] = dot(mixed[0], out_pair[0]) + dot(other, out_pair[1])
    attn = terms[0]
    for o in range(1, side):
        attn = attn + partner(terms[o].astype(jnp.bfloat16), "x", o).astype(jnp.float32)
    resid = (own_rows.astype(jnp.float32) + attn).astype(jnp.bfloat16)
    normed = rms_norm(resid, ffn_gain)
    normed, gate_core, late = lax.optimization_barrier((normed, early[1], late))
    inner = [expert_in[0], late[0]]
    outer = [expert_out[0], late[1]]
    gate_pair = [shared_gate, gate_core]
    up_pair = [shared_up, late[2]]
    down_pair = [shared_down, late[3]]
    order = me ^ jnp.arange(group_count, dtype=jnp.int32)
    kept = accepted[order][:, :, None] == jnp.arange(tree, dtype=jnp.int32)
    accepted_kv = jnp.einsum(
        "ran,rnd->rad",
        kept.astype(jnp.bfloat16),
        jnp.concatenate(fresh, axis=0),
        preferred_element_type=jnp.float32,
    ).astype(jnp.bfloat16)[order][:, None]

    expert_count = router.shape[1]
    top_count = routes.shape[2]
    capacity = 4 * tree * top_count // (3 * expert_count)
    plane = lax.axis_size(PLANE)
    spot = lax.axis_index(PLANE)
    first = lax.axis_index("z") * plane
    choose = jnp.stack(chosen)
    member = jnp.any(
        choose[..., None] == jnp.arange(expert_count, dtype=jnp.int32), axis=2
    )
    before = jnp.tril(jnp.ones((tree, tree), jnp.bfloat16), -1)
    ranks = jnp.einsum(
        "nm,kme->kne", before, member.astype(jnp.bfloat16), preferred_element_type=jnp.float32
    ).astype(jnp.int32)
    near_experts = first + (spot ^ jnp.arange(plane, dtype=jnp.int32))
    is_near = near_experts[:, None] == jnp.arange(expert_count, dtype=jnp.int32)
    slot = jnp.where(member, ranks, -1)
    slot_near = jnp.sum(
        jnp.where(is_near[:, None, None, :], slot[None] + 1, 0), axis=-1
    ) - 1
    places = jnp.arange(capacity, dtype=jnp.int32)
    pick = slot_near[:, :, None, :] == places[:, None]
    pick_bf = pick.astype(jnp.bfloat16)

    line_rows = [partner(normed, "z", k) for k in range(line)]
    calm, _ = lax.optimization_barrier((normed, line_rows[1]))
    near_normed = [normed] + [partner(calm, "x", o) for o in range(1, side)]

    def dispatch(ks):
        out = [
            dot(pick_bf[:, k].reshape(plane * capacity, tree), line_rows[k])
            .astype(jnp.bfloat16)
            .reshape(plane, capacity, width)
            for k in ks
        ]
        return [
            partner(jnp.concatenate([piece[o] for piece in out], axis=0), PLANE, o)
            for o in range(plane)
        ]

    def experts(got):
        rows = jnp.concatenate(got, axis=0)
        result = 0.0
        for i in range(2):
            both = dot(rows, inner[i])
            half = both.shape[1] // 2
            hidden = (jax.nn.silu(both[:, :half]) * both[:, half:]).astype(jnp.bfloat16)
            result = result + dot(hidden, outer[i]).astype(jnp.bfloat16).astype(jnp.float32)
        return result.astype(jnp.bfloat16).reshape(plane, -1, capacity, width)

    results = {}
    for ks in GROUPS:
        made = experts(dispatch(ks))
        for i, k in enumerate(ks):
            results[k] = made[:, i]

    block = jnp.concatenate(near_normed, axis=0)
    shared_terms = 0.0
    for i in range(2):
        hidden = (jax.nn.silu(dot(block, gate_pair[i])) * dot(block, up_pair[i])).astype(
            jnp.bfloat16
        )
        shared_terms = shared_terms + dot(hidden, down_pair[i])
    shared_terms = shared_terms.reshape(side, tree, width)
    shared = shared_terms[0]
    for o in range(1, side):
        shared = shared + partner(shared_terms[o].astype(jnp.bfloat16), "x", o).astype(jnp.float32)

    logits = jnp.stack([dot(rows, router) for rows in line_rows])
    picked = jnp.where(member, jax.nn.sigmoid(logits), 0.0)
    gates = picked / jnp.sum(picked, axis=-1, keepdims=True)
    gates_near = jnp.sum(jnp.where(is_near[:, None, None, :], gates[None], 0.0), axis=-1)
    spread = jnp.where(pick, gates_near[:, :, None, :], 0.0)
    spread = spread.astype(jnp.bfloat16)

    routed = 0.0
    for k in reversed(range(line)):
        back = jnp.concatenate([partner(results[k][o], PLANE, o) for o in range(plane)], axis=0)
        weights = spread[:, k].reshape(plane * capacity, tree)
        partial = jnp.einsum("sn,sd->nd", weights, back, preferred_element_type=jnp.float32)
        if k:
            partial = partner(partial.astype(jnp.bfloat16), "z", k).astype(jnp.float32)
        routed = routed + partial

    total_out = resid.astype(jnp.float32) + shared + routed
    hidden_out = jnp.where(live[0][:, None] == 1, total_out, 0.0).astype(jnp.bfloat16)
    return (hidden_out[None], accepted_kv)


def solution(mesh):
    line = 4
    shape = (line, mesh.shape["req"] // line, mesh.shape["head"] // 2, 2)
    grid = Mesh(mesh.devices.reshape(shape), ALL)
    req = ("z", "y")
    in_specs = (
        P(ALL, None, None),
        P(ALL, None),
        P(req, None),
        P(req),
        P(req, None),
        P(ALL, None, None),
        P(req, HEAD, None, None),
        P(),
        P(None, HEAD),
        P(HEAD, None),
        P(),
        P(None, HEAD),
        P(None, HEAD),
        P(HEAD, None),
        P(),
        P(ALL, None, None),
        P(ALL, None, None),
    )
    out_specs = (P(ALL, None, None), P(req, HEAD, None, None))
    return jax.shard_map(body, mesh=grid, in_specs=in_specs, out_specs=out_specs, check_vma=False)
```

```python
import functools
import math

import jax
import jax.numpy as jnp
from jax import lax
from jax.experimental import pallas as pl
from jax.experimental.pallas import tpu as pltpu
from jax.sharding import Mesh
from jax.sharding import PartitionSpec as P

EPSILON = 1e-06
ROPE_BASE = 10000.0
GROUPS = ((0, 1), (3,), (2,))
CHUNK = 512
ALL = ("z", "y", "x", "c")
PLANE = ("y", "x")
HEAD = ("x", "c")


def partner(value, axes, offset):
    if offset == 0:
        return value
    size = lax.axis_size(axes)
    return lax.ppermute(value, axes, [(i, i ^ offset) for i in range(size)])


def rms_norm(values, gain):
    wide = values.astype(jnp.float32)
    power = jnp.mean(wide * wide, axis=-1, keepdims=True)
    return (wide * lax.rsqrt(power + EPSILON) * gain).astype(jnp.bfloat16)


def dot(left, right):
    return jnp.dot(left, right, preferred_element_type=jnp.float32)


def ancestry(parents):
    nodes_count = parents.shape[-1]
    nodes = jnp.arange(nodes_count, dtype=jnp.int32)
    reach = (parents[..., :, None] == nodes).astype(jnp.float32) + jnp.eye(
        nodes_count, dtype=jnp.float32
    )
    for turn in range((nodes_count - 1).bit_length()):
        near = reach.astype(jnp.bfloat16)
        reach = jnp.minimum(
            jnp.einsum("rij,rjk->rik", near, near, preferred_element_type=jnp.float32), 1.0
        )
    depth = jnp.sum(reach, axis=-1) - 1.0
    return (reach, depth)


def arrive(copies):
    for copy in copies:
        copy.wait()


def attend_kernel(
    info, first, second, gain, weight, cosine, sine, reach, cache, *outs_and_scratch
):
    mixed = outs_and_scratch[0:2]
    fresh = outs_and_scratch[2:4]
    weight_here, cache_here, gain_here, sems = outs_and_scratch[4:]
    tree = first.shape[0]
    width, columns = weight.shape
    head_dim = cosine.shape[2]
    group = columns // head_dim - 2
    deep = width // 2

    gain_copy = pltpu.make_async_copy(gain, gain_here, sems.at[0])
    weight_copies = [
        pltpu.make_async_copy(
            weight.at[pl.ds(i * deep, deep)], weight_here.at[pl.ds(i * deep, deep)], sems.at[1 + i]
        )
        for i in range(2)
    ]
    cache_copies = [
        pltpu.make_async_copy(cache.at[info[i]], cache_here.at[i], sems.at[3 + i])
        for i in range(2)
    ]
    for copy in [gain_copy, *weight_copies, *cache_copies]:
        copy.start()

    wide = jnp.concatenate([first[...], second[...]], axis=0).astype(jnp.float32)
    power = jnp.mean(wide * wide, axis=-1, keepdims=True)
    gain_copy.wait()
    normed = (wide * lax.rsqrt(power + EPSILON) * gain_here[...]).astype(jnp.bfloat16)
    weight_copies[0].wait()
    projected = dot(normed[:, :deep], weight_here[:deep])
    weight_copies[1].wait()
    projected = projected + dot(normed[:, deep:], weight_here[deep:])
    scale = 1.0 / math.sqrt(head_dim)

    for i in range(2):
        own = projected[i * tree : (i + 1) * tree]
        request = info[i]
        length = info[2 + i]

        def rope(values):
            return values * cosine[request] + pltpu.roll(values, head_dim // 2, 1) * sine[request]

        def column(c):
            return own[:, c * head_dim : (c + 1) * head_dim]

        query = jnp.concatenate(
            [rope(column(h)).astype(jnp.bfloat16) for h in range(group)], axis=0
        )
        key_new = rope(column(group)).astype(jnp.bfloat16)
        value_new = column(group + 1).astype(jnp.bfloat16)
        fresh[i][:, :head_dim] = key_new
        fresh[i][:, head_dim:] = value_new

        def against(keys):
            return (
                lax.dot_general(
                    query, keys, (((1,), (1,)), ((), ())), preferred_element_type=jnp.float32
                )
                * scale
            )

        allowed = jnp.concatenate([reach[request]] * group, axis=0) > 0.5
        scores = jnp.where(allowed, against(key_new), -1e30)
        peak = jnp.max(scores, axis=-1, keepdims=True)
        weights = jnp.exp(scores - peak)
        total = jnp.sum(weights, axis=-1, keepdims=True)
        summed = dot(weights.astype(jnp.bfloat16), value_new)
        cache_copies[i].wait()

        def chunk(j, carry):
            peak, total, summed = carry
            block = pl.ds(pl.multiple_of(j * CHUNK, CHUNK), CHUNK)
            scores = against(cache_here[i, block, :head_dim])
            place = j * CHUNK + lax.broadcasted_iota(jnp.int32, scores.shape, 1)
            scores = jnp.where(place < length, scores, -1e30)
            higher = jnp.maximum(peak, jnp.max(scores, axis=-1, keepdims=True))
            fade = jnp.exp(peak - higher)
            weights = jnp.exp(scores - higher)
            total = total * fade + jnp.sum(weights, axis=-1, keepdims=True)
            values = cache_here[i, block, head_dim:]
            summed = summed * fade + dot(weights.astype(jnp.bfloat16), values)
            return (higher, total, summed)

        peak, total, summed = lax.fori_loop(
            0, lax.div(length + CHUNK - 1, CHUNK), chunk, (peak, total, summed)
        )
        result = (summed / total).astype(jnp.bfloat16)
        for h in range(group):
            mixed[i][:, h * head_dim : (h + 1) * head_dim] = result[h * tree : (h + 1) * tree]


def in_vmem():
    return pl.BlockSpec(memory_space=pltpu.VMEM)


def in_hbm():
    return pl.BlockSpec(memory_space=pltpu.HBM)


def attend(info, first, second, gain, weight, cosine, sine, reach, cache):
    tree, width = first.shape
    slots, pair = cache.shape[1:]
    head_dim = pair // 2
    columns = weight.shape[1]
    group_columns = columns - pair
    return pl.pallas_call(
        attend_kernel,
        in_specs=[
            pl.BlockSpec(memory_space=pltpu.SMEM),
            in_vmem(),
            in_vmem(),
            in_hbm(),
            in_hbm(),
            in_vmem(),
            in_vmem(),
            in_vmem(),
            in_hbm(),
        ],
        out_specs=[in_vmem()] * 4,
        out_shape=[jax.ShapeDtypeStruct((tree, group_columns), jnp.bfloat16)] * 2
        + [jax.ShapeDtypeStruct((tree, pair), jnp.bfloat16)] * 2,
        scratch_shapes=[
            pltpu.VMEM((width, columns), jnp.bfloat16),
            pltpu.VMEM((2, slots, pair), jnp.bfloat16),
            pltpu.VMEM((1, width), jnp.float32),
            pltpu.SemaphoreType.DMA((5,)),
        ],
        compiler_params=pltpu.CompilerParams(vmem_limit_bytes=24 * 2**20),
        name="attend",
    )(info, first, second, gain, weight, cosine, sine, reach, cache)


def silu(values):
    return values / (1.0 + jnp.exp(-values))


def expert_kernel(*refs, plane, deep):
    pieces = refs[:plane]
    weights = refs[plane : plane + 4]
    outs = refs[plane + 4 : 2 * plane + 4]
    rows, inner_a, outer_a, inner_b, outer_b, sems = refs[2 * plane + 4 :]
    each = pieces[0].shape[0]
    width = rows.shape[1]
    parts = width // deep
    copies = []
    for n, (inner, outer, inner_here, outer_here) in enumerate(
        ((weights[0], weights[1], inner_a, outer_a), (weights[2], weights[3], inner_b, outer_b))
    ):
        base = n * (parts + 1)
        for p in range(parts):
            block = pl.ds(p * deep, deep)
            copies.append(
                pltpu.make_async_copy(inner.at[block], inner_here.at[block], sems.at[base + p])
            )
        copies.append(pltpu.make_async_copy(outer, outer_here, sems.at[base + parts]))
    for copy in copies:
        copy.start()
    for i in range(plane):
        rows[i * each : (i + 1) * each] = pieces[i][...]
    result = None
    for n, (inner_here, outer_here) in enumerate(((inner_a, outer_a), (inner_b, outer_b))):
        base = n * (parts + 1)
        both = None
        for p in range(parts):
            copies[base + p].wait()
            term = dot(rows[:, p * deep : (p + 1) * deep], inner_here[p * deep : (p + 1) * deep])
            both = term if both is None else both + term
        half = both.shape[1] // 2
        hidden = (silu(both[:, :half]) * both[:, half:]).astype(jnp.bfloat16)
        copies[base + parts].wait()
        term = dot(hidden, outer_here[...]).astype(jnp.bfloat16).astype(jnp.float32)
        result = term if result is None else result + term
    for i in range(plane):
        outs[i][...] = result[i * each : (i + 1) * each].astype(jnp.bfloat16)


def experts(pieces, inner, outer):
    plane = len(pieces)
    each, width = pieces[0].shape
    hidden = inner[0].shape[1]
    deep = width // 2
    kernel = functools.partial(expert_kernel, plane=plane, deep=deep)
    weight_scratch = [
        pltpu.VMEM((width, hidden), jnp.bfloat16),
        pltpu.VMEM((hidden // 2, width), jnp.bfloat16),
    ]
    return pl.pallas_call(
        kernel,
        in_specs=[in_vmem()] * plane + [in_hbm()] * 4,
        out_specs=[in_vmem()] * plane,
        out_shape=[jax.ShapeDtypeStruct((each, width), jnp.bfloat16)] * plane,
        scratch_shapes=[pltpu.VMEM((plane * each, width), jnp.bfloat16)]
        + weight_scratch * 2
        + [pltpu.SemaphoreType.DMA((2 * (width // deep + 1),))],
        compiler_params=pltpu.CompilerParams(vmem_limit_bytes=40 * 2**20),
        name="expert",
    )(*pieces, inner[0], outer[0], inner[1], outer[1])


def shared_kernel(*refs, side):
    blocks = refs[:side]
    weights = refs[side : side + 6]
    outs = refs[side + 6 : 2 * side + 6]
    here, sems = refs[2 * side + 6 :]
    copies = [pltpu.make_async_copy(weights[i], here.at[i], sems.at[i]) for i in range(6)]
    for copy in copies:
        copy.start()
    tree = blocks[0].shape[0]
    rows = jnp.concatenate([block[...] for block in blocks], axis=0)

    def turned(i):
        copies[i].wait()
        return lax.dot_general(
            rows, here[i], (((1,), (1,)), ((), ())), preferred_element_type=jnp.float32
        )

    result = None
    for n in range(2):
        hidden = silu(turned(3 * n))
        hidden = (hidden * turned(3 * n + 1)).astype(jnp.bfloat16)
        copies[3 * n + 2].wait()
        term = dot(hidden, here[3 * n + 2])
        result = term if result is None else result + term
    for i in range(side):
        outs[i][...] = result[i * tree : (i + 1) * tree].astype(outs[i].dtype)


def shared_terms(own, beside, weights):
    tree, width = own.shape
    units = weights[0].shape[0]
    side = 1 + len(beside)
    outs = pl.pallas_call(
        functools.partial(shared_kernel, side=side),
        in_specs=[in_vmem()] * side + [in_hbm()] * 6,
        out_specs=[in_vmem()] * side,
        out_shape=[jax.ShapeDtypeStruct((tree, width), jnp.float32)]
        + [jax.ShapeDtypeStruct((tree, width), jnp.bfloat16)] * (side - 1),
        scratch_shapes=[
            pltpu.VMEM((6, units, width), jnp.bfloat16),
            pltpu.SemaphoreType.DMA((6,)),
        ],
        compiler_params=pltpu.CompilerParams(vmem_limit_bytes=24 * 2**20),
        name="shared",
    )(own, *beside, *weights)
    return outs[0], list(outs[1:])


def combine_kernel(spread, *refs, start):
    out = refs[-1]
    slots = spread.shape[0] // (len(refs) - 1)
    total = None
    for i, piece in enumerate(refs[:-1]):
        term = lax.dot_general(
            spread[i * slots : (i + 1) * slots],
            piece[start : start + slots],
            (((0,), (0,)), ((), ())),
            preferred_element_type=jnp.float32,
        )
        total = term if total is None else total + term
    out[...] = total.astype(out.dtype)


def combine(spread, pieces, start, dtype):
    tree = spread.shape[1]
    width = pieces[0].shape[1]
    return pl.pallas_call(
        functools.partial(combine_kernel, start=start),
        in_specs=[in_vmem()] * (1 + len(pieces)),
        out_specs=in_vmem(),
        out_shape=jax.ShapeDtypeStruct((tree, width), dtype),
        compiler_params=pltpu.CompilerParams(vmem_limit_bytes=16 * 2**20),
        name="combine",
    )(spread, *pieces)


def body(
    tokens,
    live,
    parents,
    lengths,
    accepted,
    routes,
    cache,
    attn_gain,
    w_qkv,
    w_out,
    ffn_gain,
    shared_gate,
    shared_up,
    shared_down,
    router,
    expert_in,
    expert_out,
):
    tree = tokens.shape[1]
    width = tokens.shape[2]
    own_rows = tokens[0]
    group_count = lax.axis_size(HEAD)
    head_dim = cache.shape[3] // 2
    me = lax.axis_index(HEAD)

    side = lax.axis_size("x")
    near = [own_rows] + [partner(own_rows, "x", o) for o in range(1, side)]
    near_core = [partner(own_rows, "c", 1)]

    reach, depth = ancestry(parents)
    positions = lengths[:, None].astype(jnp.float32) + depth
    frequency = ROPE_BASE ** (-jnp.arange(head_dim // 2, dtype=jnp.float32) / (head_dim // 2))
    angle = positions[..., None] * frequency
    cosine = jnp.cos(angle)
    sine = jnp.sin(angle)
    cosine = jnp.concatenate([cosine, cosine], axis=-1)
    sine = jnp.concatenate([-sine, sine], axis=-1)
    for o in range(1, side):
        near[o], cosine, sine, reach = lax.optimization_barrier((near[o], cosine, sine, reach))
        near_core.append(partner(near[o], "c", 1))

    gate_turned, up_turned = shared_gate.T, shared_up.T
    early, _ = lax.optimization_barrier(((w_out, gate_turned), near_core[0]))
    early = [partner(weight, "c", 1) for weight in early]
    late, _ = lax.optimization_barrier(
        ((up_turned, shared_down, expert_in[0], expert_out[0]), near_core[side - 1])
    )
    late = [partner(weight, "c", 1) for weight in late]

    terms = [None] * side
    fresh = [None] * side
    follow = None
    for o in reversed(range(side)):
        if follow is not None:
            near_core[o], _ = lax.optimization_barrier((near_core[o], follow))
        ids = me ^ jnp.arange(2 * o, 2 * o + 2, dtype=jnp.int32)
        here = ids[:, None] == jnp.arange(group_count, dtype=jnp.int32)
        info = jnp.concatenate([ids, jnp.sum(jnp.where(here, lengths, 0), axis=1)])
        mixed_own, mixed_other, fresh_own, fresh_other = attend(
            info,
            near[o],
            near_core[o],
            attn_gain[None],
            w_qkv,
            cosine,
            sine,
            reach,
            cache[:, 0],
        )
        follow = mixed_own
        fresh[o] = jnp.stack([fresh_own, fresh_other])
        other = partner(mixed_other, "c", 1)
        terms[o] = dot(mixed_own, w_out) + dot(other, early[0])
        if o:
            terms[o] = terms[o].astype(jnp.bfloat16)
            terms[o], early, late[0], late[1] = lax.optimization_barrier(
                (terms[o], early, late[0], late[1])
            )
    own_routes, _ = lax.optimization_barrier((routes[0], terms[side - 1]))
    attn = terms[0]
    for o in range(1, side):
        attn = attn + partner(terms[o], "x", o).astype(jnp.float32)
    resid = (own_rows.astype(jnp.float32) + attn).astype(jnp.bfloat16)
    normed = rms_norm(resid, ffn_gain)
    line = lax.axis_size("z")
    chosen = [partner(own_routes, "z", k) for k in range(line)]
    normed, chosen, late = lax.optimization_barrier((normed, chosen, late))
    inner = [expert_in[0], late[2]]
    outer = [expert_out[0], late[3]]
    shared_weights = [gate_turned, up_turned, shared_down, early[1], late[0], late[1]]
    order = me ^ jnp.arange(group_count, dtype=jnp.int32)
    kept = accepted[order][:, :, None] == jnp.arange(tree, dtype=jnp.int32)
    accepted_kv = jnp.einsum(
        "ran,rnd->rad",
        kept.astype(jnp.bfloat16),
        jnp.concatenate(fresh, axis=0),
        preferred_element_type=jnp.float32,
    ).astype(jnp.bfloat16)[order][:, None]

    expert_count = router.shape[1]
    top_count = routes.shape[2]
    capacity = 4 * tree * top_count // (3 * expert_count)
    plane = lax.axis_size(PLANE)
    spot = lax.axis_index(PLANE)
    first = lax.axis_index("z") * plane
    choose = jnp.stack(chosen)
    member = jnp.any(
        choose[..., None] == jnp.arange(expert_count, dtype=jnp.int32), axis=2
    )
    before = jnp.tril(jnp.ones((tree, tree), jnp.bfloat16), -1)
    ranks = jnp.einsum(
        "nm,kme->kne", before, member.astype(jnp.bfloat16), preferred_element_type=jnp.float32
    ).astype(jnp.int32)
    near_experts = first + (spot ^ jnp.arange(plane, dtype=jnp.int32))
    is_near = near_experts[:, None] == jnp.arange(expert_count, dtype=jnp.int32)
    slot = jnp.where(member, ranks, -1)
    slot_near = jnp.sum(
        jnp.where(is_near[:, None, None, :], slot[None] + 1, 0), axis=-1
    ) - 1
    places = jnp.arange(capacity, dtype=jnp.int32)
    pick = slot_near[:, :, None, :] == places[:, None]
    pick_bf = pick.astype(jnp.bfloat16)

    line_rows = [normed] + [partner(normed, "z", k) for k in range(1, line)]
    beside = [partner(normed, "x", o) for o in range(1, side)]

    own_part, beside_part = shared_terms(normed, beside, shared_weights)

    line_rows[1], beside_part = lax.optimization_barrier((line_rows[1], beside_part))

    logits = jnp.stack([dot(rows, router) for rows in line_rows])
    picked = jnp.where(member, jax.nn.sigmoid(logits), 0.0)
    gates = picked / jnp.sum(picked, axis=-1, keepdims=True)
    gates_near = jnp.sum(jnp.where(is_near[:, None, None, :], gates[None], 0.0), axis=-1)
    spread = jnp.where(pick, gates_near[:, :, None, :], 0.0)
    spread = spread.astype(jnp.bfloat16)

    def dispatch(ks):
        out = [
            dot(pick_bf[:, k].reshape(plane * capacity, tree), line_rows[k])
            .astype(jnp.bfloat16)
            .reshape(plane, capacity, width)
            for k in ks
        ]
        return [
            partner(jnp.concatenate([piece[o] for piece in out], axis=0), PLANE, o)
            for o in range(plane)
        ]

    sent = [dispatch(ks) for ks in GROUPS]
    made = []
    for pieces in sent:
        if made:
            pieces, made[-1] = lax.optimization_barrier((pieces, made[-1]))
        made.append(experts(pieces, inner, outer))

    shared = own_part
    for o in range(1, side):
        shared = shared + partner(beside_part[o - 1], "x", o).astype(jnp.float32)
    routed = 0.0
    for ks, pieces in reversed(list(zip(GROUPS, made))):
        back = [partner(pieces[o], PLANE, o) for o in range(plane)]
        for i, k in enumerate(ks):
            weights = spread[:, k].reshape(plane * capacity, tree)
            partial = combine(
                weights, back, i * capacity, jnp.bfloat16 if k else jnp.float32
            )
            routed = routed + partner(partial, "z", k).astype(jnp.float32)

    total_out = resid.astype(jnp.float32) + shared + routed
    hidden_out = jnp.where(live[0][:, None] == 1, total_out, 0.0).astype(jnp.bfloat16)
    return (hidden_out[None], accepted_kv)


def solution(mesh):
    line = 4
    shape = (line, mesh.shape["req"] // line, mesh.shape["head"] // 2, 2)
    grid = Mesh(mesh.devices.reshape(shape), ALL)
    req = ("z", "y")
    in_specs = (
        P(ALL, None, None),
        P(ALL, None),
        P(req, None),
        P(req),
        P(req, None),
        P(ALL, None, None),
        P(req, HEAD, None, None),
        P(),
        P(None, HEAD),
        P(HEAD, None),
        P(),
        P(None, HEAD),
        P(None, HEAD),
        P(HEAD, None),
        P(),
        P(ALL, None, None),
        P(ALL, None, None),
    )
    out_specs = (P(ALL, None, None), P(req, HEAD, None, None))
    return jax.shard_map(body, mesh=grid, in_specs=in_specs, out_specs=out_specs, check_vma=False)
```

```python
import functools
import math

import jax
import jax.numpy as jnp
from jax import lax
from jax.experimental import pallas as pl
from jax.experimental.pallas import tpu as pltpu
from jax.sharding import Mesh
from jax.sharding import PartitionSpec as P

EPSILON = 1e-06
ROPE_BASE = 10000.0
GROUPS = ((0, 1), (3,), (2,))
CHUNK = 512
EXTRA = 128
ALL = ("z", "y", "x", "c")
PLANE = ("y", "x")
HEAD = ("x", "c")


def partner(value, axes, offset):
    if offset == 0:
        return value
    size = lax.axis_size(axes)
    return lax.ppermute(value, axes, [(i, i ^ offset) for i in range(size)])


def dot(left, right):
    return jnp.dot(left, right, preferred_element_type=jnp.float32)


def ancestry(parents):
    nodes_count = parents.shape[-1]
    nodes = jnp.arange(nodes_count, dtype=jnp.int32)
    reach = (parents[..., :, None] == nodes).astype(jnp.float32) + jnp.eye(
        nodes_count, dtype=jnp.float32
    )
    for turn in range((nodes_count - 1).bit_length()):
        near = reach.astype(jnp.bfloat16)
        reach = jnp.minimum(
            jnp.einsum("rij,rjk->rik", near, near, preferred_element_type=jnp.float32), 1.0
        )
    depth = jnp.sum(reach, axis=-1) - 1.0
    return (reach, depth)


def arrive(copies):
    for copy in copies:
        copy.wait()


def attend_kernel(
    info, first, second, gain, weight, cosine, sine, reach, cache, *outs_and_scratch
):
    mixed = outs_and_scratch[0:2]
    fresh = outs_and_scratch[2:4]
    weight_here, cache_here, gain_here, sems = outs_and_scratch[4:]
    tree = first.shape[0]
    width, columns = weight.shape
    head_dim = cosine.shape[2]
    group = columns // head_dim - 2
    deep = width // 2

    gain_copy = pltpu.make_async_copy(gain, gain_here, sems.at[0])
    weight_copies = [
        pltpu.make_async_copy(
            weight.at[pl.ds(i * deep, deep)], weight_here.at[pl.ds(i * deep, deep)], sems.at[1 + i]
        )
        for i in range(2)
    ]
    cache_copies = [
        pltpu.make_async_copy(cache.at[info[i]], cache_here.at[i], sems.at[3 + i])
        for i in range(2)
    ]
    for copy in [gain_copy, *weight_copies, *cache_copies]:
        copy.start()

    wide = jnp.concatenate([first[...], second[...]], axis=0).astype(jnp.float32)
    power = jnp.mean(wide * wide, axis=-1, keepdims=True)
    gain_copy.wait()
    normed = (wide * lax.rsqrt(power + EPSILON) * gain_here[...]).astype(jnp.bfloat16)
    weight_copies[0].wait()
    projected = dot(normed[:, :deep], weight_here[:deep])
    weight_copies[1].wait()
    projected = projected + dot(normed[:, deep:], weight_here[deep:])
    scale = 1.0 / math.sqrt(head_dim)

    for i in range(2):
        own = projected[i * tree : (i + 1) * tree]
        request = info[i]
        length = info[2 + i]

        def rope(values):
            return values * cosine[request] + pltpu.roll(values, head_dim // 2, 1) * sine[request]

        def column(c):
            return own[:, c * head_dim : (c + 1) * head_dim]

        query = jnp.concatenate(
            [rope(column(h)).astype(jnp.bfloat16) for h in range(group)], axis=0
        )
        key_new = rope(column(group)).astype(jnp.bfloat16)
        value_new = column(group + 1).astype(jnp.bfloat16)
        fresh[i][:, :head_dim] = key_new
        fresh[i][:, head_dim:] = value_new

        def against(keys):
            return (
                lax.dot_general(
                    query, keys, (((1,), (1,)), ((), ())), preferred_element_type=jnp.float32
                )
                * scale
            )

        allowed = jnp.concatenate([reach[request]] * group, axis=0) > 0.5
        scores = jnp.where(allowed, against(key_new), -1e30)
        peak = jnp.max(scores, axis=-1, keepdims=True)
        weights = jnp.exp(scores - peak)
        total = jnp.sum(weights, axis=-1, keepdims=True)
        summed = dot(weights.astype(jnp.bfloat16), value_new)
        cache_copies[i].wait()

        def chunk(j, carry):
            peak, total, summed = carry
            block = pl.ds(pl.multiple_of(j * CHUNK, CHUNK), CHUNK)
            scores = against(cache_here[i, block, :head_dim])
            place = j * CHUNK + lax.broadcasted_iota(jnp.int32, scores.shape, 1)
            scores = jnp.where(place < length, scores, -1e30)
            higher = jnp.maximum(peak, jnp.max(scores, axis=-1, keepdims=True))
            fade = jnp.exp(peak - higher)
            weights = jnp.exp(scores - higher)
            total = total * fade + jnp.sum(weights, axis=-1, keepdims=True)
            values = cache_here[i, block, head_dim:]
            summed = summed * fade + dot(weights.astype(jnp.bfloat16), values)
            return (higher, total, summed)

        peak, total, summed = lax.fori_loop(
            0, lax.div(length + CHUNK - 1, CHUNK), chunk, (peak, total, summed)
        )
        result = (summed / total).astype(jnp.bfloat16)
        for h in range(group):
            mixed[i][:, h * head_dim : (h + 1) * head_dim] = result[h * tree : (h + 1) * tree]


def in_vmem():
    return pl.BlockSpec(memory_space=pltpu.VMEM)


def in_hbm():
    return pl.BlockSpec(memory_space=pltpu.HBM)


def attend(info, first, second, gain, weight, cosine, sine, reach, cache):
    tree, width = first.shape
    slots, pair = cache.shape[1:]
    head_dim = pair // 2
    columns = weight.shape[1]
    group_columns = columns - pair
    return pl.pallas_call(
        attend_kernel,
        in_specs=[
            pl.BlockSpec(memory_space=pltpu.SMEM),
            in_vmem(),
            in_vmem(),
            in_hbm(),
            in_hbm(),
            in_vmem(),
            in_vmem(),
            in_vmem(),
            in_hbm(),
        ],
        out_specs=[in_vmem()] * 4,
        out_shape=[jax.ShapeDtypeStruct((tree, group_columns), jnp.bfloat16)] * 2
        + [jax.ShapeDtypeStruct((tree, pair), jnp.bfloat16)] * 2,
        scratch_shapes=[
            pltpu.VMEM((width, columns), jnp.bfloat16),
            pltpu.VMEM((2, slots, pair), jnp.bfloat16),
            pltpu.VMEM((1, width), jnp.float32),
            pltpu.SemaphoreType.DMA((5,)),
        ],
        compiler_params=pltpu.CompilerParams(vmem_limit_bytes=60 * 2**20),
        name="attend",
    )(info, first, second, gain, weight, cosine, sine, reach, cache)


def silu(values):
    return values / (1.0 + jnp.exp(-values))


def expert_kernel(*refs, plane, deep):
    pieces = refs[:plane]
    weights = refs[plane : plane + 4]
    outs = refs[plane + 4 : 2 * plane + 4]
    rows, inner_a, outer_a, inner_b, outer_b, sems = refs[2 * plane + 4 :]
    each = pieces[0].shape[0]
    width = rows.shape[1]
    parts = width // deep
    copies = []
    for n, (inner, outer, inner_here, outer_here) in enumerate(
        ((weights[0], weights[1], inner_a, outer_a), (weights[2], weights[3], inner_b, outer_b))
    ):
        base = n * (parts + 1)
        for p in range(parts):
            block = pl.ds(p * deep, deep)
            copies.append(
                pltpu.make_async_copy(inner.at[block], inner_here.at[block], sems.at[base + p])
            )
        copies.append(pltpu.make_async_copy(outer, outer_here, sems.at[base + parts]))
    for copy in copies:
        copy.start()
    for i in range(plane):
        rows[i * each : (i + 1) * each] = pieces[i][...]
    result = None
    for n, (inner_here, outer_here) in enumerate(((inner_a, outer_a), (inner_b, outer_b))):
        base = n * (parts + 1)
        both = None
        for p in range(parts):
            copies[base + p].wait()
            term = dot(rows[:, p * deep : (p + 1) * deep], inner_here[p * deep : (p + 1) * deep])
            both = term if both is None else both + term
        half = both.shape[1] // 2
        hidden = (silu(both[:, :half]) * both[:, half:]).astype(jnp.bfloat16)
        copies[base + parts].wait()
        term = dot(hidden, outer_here[...]).astype(jnp.bfloat16).astype(jnp.float32)
        result = term if result is None else result + term
    for i in range(plane):
        outs[i][...] = result[i * each : (i + 1) * each].astype(jnp.bfloat16)


def experts(pieces, inner, outer):
    plane = len(pieces)
    each, width = pieces[0].shape
    hidden = inner[0].shape[1]
    deep = width // 2
    kernel = functools.partial(expert_kernel, plane=plane, deep=deep)
    weight_scratch = [
        pltpu.VMEM((width, hidden), jnp.bfloat16),
        pltpu.VMEM((hidden // 2, width), jnp.bfloat16),
    ]
    return pl.pallas_call(
        kernel,
        in_specs=[in_vmem()] * plane + [in_hbm()] * 4,
        out_specs=[in_vmem()] * plane,
        out_shape=[jax.ShapeDtypeStruct((each, width), jnp.bfloat16)] * plane,
        scratch_shapes=[pltpu.VMEM((plane * each, width), jnp.bfloat16)]
        + weight_scratch * 2
        + [pltpu.SemaphoreType.DMA((2 * (width // deep + 1),))],
        compiler_params=pltpu.CompilerParams(vmem_limit_bytes=40 * 2**20),
        name="expert",
    )(*pieces, inner[0], outer[0], inner[1], outer[1])


def shared_kernel(*refs, side):
    blocks = refs[:side]
    weights = refs[side : side + 6]
    outs = refs[side + 6 : 2 * side + 6]
    here, sems = refs[2 * side + 6 :]
    copies = [pltpu.make_async_copy(weights[i], here.at[i], sems.at[i]) for i in range(6)]
    for copy in copies:
        copy.start()
    tree = blocks[0].shape[0]
    rows = jnp.concatenate([block[...] for block in blocks], axis=0)

    def turned(i):
        copies[i].wait()
        return lax.dot_general(
            rows, here[i], (((1,), (1,)), ((), ())), preferred_element_type=jnp.float32
        )

    result = None
    for n in range(2):
        hidden = silu(turned(3 * n))
        hidden = (hidden * turned(3 * n + 1)).astype(jnp.bfloat16)
        copies[3 * n + 2].wait()
        term = dot(hidden, here[3 * n + 2])
        result = term if result is None else result + term
    for i in range(side):
        outs[i][...] = result[i * tree : (i + 1) * tree].astype(outs[i].dtype)


def shared_terms(own, beside, weights):
    tree, width = own.shape
    units = weights[0].shape[0]
    side = 1 + len(beside)
    outs = pl.pallas_call(
        functools.partial(shared_kernel, side=side),
        in_specs=[in_vmem()] * side + [in_hbm()] * 6,
        out_specs=[in_vmem()] * side,
        out_shape=[jax.ShapeDtypeStruct((tree, width), jnp.float32)]
        + [jax.ShapeDtypeStruct((tree, width), jnp.bfloat16)] * (side - 1),
        scratch_shapes=[
            pltpu.VMEM((6, units, width), jnp.bfloat16),
            pltpu.SemaphoreType.DMA((6,)),
        ],
        compiler_params=pltpu.CompilerParams(vmem_limit_bytes=24 * 2**20),
        name="shared",
    )(own, *beside, *weights)
    return outs[0], list(outs[1:])


def finish_kernel(tokens, term, gain, routes, *refs):
    others = refs[:-3]
    resid, normed, payload = refs[-3:]
    width = tokens.shape[1]
    attn = term[...]
    for other in others:
        attn = attn + other[...].astype(jnp.float32)
    rounded = (tokens[...].astype(jnp.float32) + attn).astype(jnp.bfloat16)
    resid[...] = rounded
    wide = rounded.astype(jnp.float32)
    power = jnp.mean(wide * wide, axis=-1, keepdims=True)
    rows = (wide * lax.rsqrt(power + EPSILON) * gain[...]).astype(jnp.bfloat16)
    normed[...] = rows
    payload[:, :width] = rows
    extra = payload.shape[1] - width
    lane = lax.broadcasted_iota(jnp.int32, (tokens.shape[0], extra), 1)
    numbers = jnp.zeros(lane.shape, jnp.float32)
    for t in range(routes.shape[1]):
        numbers = jnp.where(lane == t, routes[:, t : t + 1].astype(jnp.float32), numbers)
    payload[:, width:] = numbers.astype(jnp.bfloat16)


def finish(tokens, term, others, gain, routes):
    tree, width = tokens.shape
    return pl.pallas_call(
        finish_kernel,
        in_specs=[in_vmem()] * (4 + len(others)),
        out_specs=[in_vmem()] * 3,
        out_shape=[
            jax.ShapeDtypeStruct((tree, width), jnp.bfloat16),
            jax.ShapeDtypeStruct((tree, width), jnp.bfloat16),
            jax.ShapeDtypeStruct((tree, width + EXTRA), jnp.bfloat16),
        ],
        compiler_params=pltpu.CompilerParams(vmem_limit_bytes=16 * 2**20),
        name="finish",
    )(tokens, term, gain, routes, *others)


def select_kernel(*refs, count, plane, capacity, top_count):
    near = refs[0]
    router = refs[1]
    sources = refs[2 : 2 + count]
    outs = refs[2 + count : 2 + count + plane]
    spreads = refs[2 + count + plane :]
    width, expert_count = router.shape
    tree = sources[0].shape[0]
    lane = lax.broadcasted_iota(jnp.int32, (tree, plane * capacity), 1)
    place = lax.rem(lane, capacity).astype(jnp.float32)
    owner = lax.div(lane, capacity)
    expert = lax.broadcasted_iota(jnp.int32, (tree, expert_count), 1)
    row = lax.broadcasted_iota(jnp.int32, (tree, tree), 0)
    column = lax.broadcasted_iota(jnp.int32, (tree, tree), 1)
    before = jnp.where(column < row, 1.0, 0.0).astype(jnp.bfloat16)
    for i in range(count):
        rows = sources[i][:, :width]
        routes = sources[i][:, width:].astype(jnp.float32)
        member = jnp.zeros((tree, expert_count), jnp.float32)
        for t in range(top_count):
            named = routes[:, t : t + 1] == expert.astype(jnp.float32)
            member = jnp.where(named, 1.0, member)
        ranks = dot(before, member.astype(jnp.bfloat16))
        slots = jnp.where(member > 0.5, ranks, -1.0)
        logits = dot(rows, router[...])
        picked = member / (1.0 + jnp.exp(-logits))
        gates = picked / jnp.sum(picked, axis=-1, keepdims=True)
        slot = jnp.zeros(lane.shape, jnp.float32)
        gate = jnp.zeros(lane.shape, jnp.float32)
        for o in range(plane):
            mine = expert == near[o]
            slot_o = jnp.sum(jnp.where(mine, slots, 0.0), axis=-1, keepdims=True)
            gate_o = jnp.sum(jnp.where(mine, gates, 0.0), axis=-1, keepdims=True)
            slot = jnp.where(owner == o, slot_o, slot)
            gate = jnp.where(owner == o, gate_o, gate)
        pick = slot == place
        spreads[i][...] = jnp.where(pick, gate, 0.0).astype(jnp.bfloat16)
        chosen = lax.dot_general(
            jnp.where(pick, 1.0, 0.0).astype(jnp.bfloat16),
            rows,
            (((0,), (0,)), ((), ())),
            preferred_element_type=jnp.float32,
        ).astype(jnp.bfloat16)
        for o in range(plane):
            outs[o][i * capacity : (i + 1) * capacity] = chosen[o * capacity : (o + 1) * capacity]


def select(near, router, sources, plane, capacity, top_count):
    tree = sources[0].shape[0]
    width = router.shape[0]
    count = len(sources)
    made = pl.pallas_call(
        functools.partial(
            select_kernel, count=count, plane=plane, capacity=capacity, top_count=top_count
        ),
        in_specs=[pl.BlockSpec(memory_space=pltpu.SMEM)] + [in_vmem()] * (1 + count),
        out_specs=[in_vmem()] * (plane + count),
        out_shape=[jax.ShapeDtypeStruct((count * capacity, width), jnp.bfloat16)] * plane
        + [jax.ShapeDtypeStruct((tree, plane * capacity), jnp.bfloat16)] * count,
        compiler_params=pltpu.CompilerParams(vmem_limit_bytes=16 * 2**20),
        name="select",
    )(near, router, *sources)
    return list(made[:plane]), list(made[plane:])


def combine_kernel(spread, *refs, start):
    out = refs[-1]
    slots = spread.shape[1] // (len(refs) - 1)
    back = jnp.concatenate([piece[start : start + slots] for piece in refs[:-1]], axis=0)
    out[...] = dot(spread[...], back).astype(out.dtype)


def combine(spread, pieces, start, dtype):
    tree = spread.shape[0]
    width = pieces[0].shape[1]
    return pl.pallas_call(
        functools.partial(combine_kernel, start=start),
        in_specs=[in_vmem()] * (1 + len(pieces)),
        out_specs=in_vmem(),
        out_shape=jax.ShapeDtypeStruct((tree, width), dtype),
        compiler_params=pltpu.CompilerParams(vmem_limit_bytes=16 * 2**20),
        name="combine",
    )(spread, *pieces)


def final_kernel(live, resid, shared, routed, *refs):
    total = resid[...].astype(jnp.float32) + shared[...] + routed[...]
    for part in refs[:-1]:
        total = total + part[...].astype(jnp.float32)
    refs[-1][...] = jnp.where(live[...] == 1, total, 0.0).astype(jnp.bfloat16)


def final(live, resid, shared, routed, parts):
    return pl.pallas_call(
        final_kernel,
        in_specs=[in_vmem()] * (4 + len(parts)),
        out_specs=in_vmem(),
        out_shape=jax.ShapeDtypeStruct(resid.shape, jnp.bfloat16),
        compiler_params=pltpu.CompilerParams(vmem_limit_bytes=16 * 2**20),
        name="final",
    )(live, resid, shared, routed, *parts)


def body(
    tokens,
    live,
    parents,
    lengths,
    accepted,
    routes,
    cache,
    attn_gain,
    w_qkv,
    w_out,
    ffn_gain,
    shared_gate,
    shared_up,
    shared_down,
    router,
    expert_in,
    expert_out,
):
    tree = tokens.shape[1]
    width = tokens.shape[2]
    own_rows = tokens[0]
    group_count = lax.axis_size(HEAD)
    head_dim = cache.shape[3] // 2
    me = lax.axis_index(HEAD)

    side = lax.axis_size("x")
    near = [own_rows] + [partner(own_rows, "x", o) for o in range(1, side)]
    near_core = [partner(own_rows, "c", 1)]

    reach, depth = ancestry(parents)
    positions = lengths[:, None].astype(jnp.float32) + depth
    frequency = ROPE_BASE ** (-jnp.arange(head_dim // 2, dtype=jnp.float32) / (head_dim // 2))
    angle = positions[..., None] * frequency
    cosine = jnp.cos(angle)
    sine = jnp.sin(angle)
    cosine = jnp.concatenate([cosine, cosine], axis=-1)
    sine = jnp.concatenate([-sine, sine], axis=-1)
    for o in range(1, side):
        near[o], cosine, sine, reach = lax.optimization_barrier((near[o], cosine, sine, reach))
        near_core.append(partner(near[o], "c", 1))

    gate_turned, up_turned = shared_gate.T, shared_up.T
    early, _ = lax.optimization_barrier(((w_out, gate_turned), near_core[0]))
    early = [partner(weight, "c", 1) for weight in early]
    late, near_core = lax.optimization_barrier(
        ((up_turned, shared_down, expert_in[0], expert_out[0]), near_core)
    )
    late = [partner(weight, "c", 1) for weight in late]

    terms = [None] * side
    fresh = [None] * side
    follow = None
    for o in reversed(range(side)):
        if follow is not None:
            near_core[o], _ = lax.optimization_barrier((near_core[o], follow))
        ids = me ^ jnp.arange(2 * o, 2 * o + 2, dtype=jnp.int32)
        here = ids[:, None] == jnp.arange(group_count, dtype=jnp.int32)
        info = jnp.concatenate([ids, jnp.sum(jnp.where(here, lengths, 0), axis=1)])
        mixed_own, mixed_other, fresh_own, fresh_other = attend(
            info,
            near[o],
            near_core[o],
            attn_gain[None],
            w_qkv,
            cosine,
            sine,
            reach,
            cache[:, 0],
        )
        fresh[o] = jnp.stack([fresh_own, fresh_other])
        other = partner(mixed_other, "c", 1)
        terms[o] = dot(mixed_own, w_out) + dot(other, early[0])
        if o:
            terms[o] = terms[o].astype(jnp.bfloat16)
        follow = terms[o]
    others = [partner(terms[o], "x", o) for o in range(1, side)]
    own_term, late, early = lax.optimization_barrier((terms[0], late, early))
    resid, normed, payload = finish(own_rows, own_term, others, ffn_gain[None], routes[0])
    inner = [expert_in[0], late[2]]
    outer = [expert_out[0], late[3]]
    shared_weights = [gate_turned, up_turned, shared_down, early[1], late[0], late[1]]
    order = me ^ jnp.arange(group_count, dtype=jnp.int32)
    kept = accepted[order][:, :, None] == jnp.arange(tree, dtype=jnp.int32)
    accepted_kv = jnp.einsum(
        "ran,rnd->rad",
        kept.astype(jnp.bfloat16),
        jnp.concatenate(fresh, axis=0),
        preferred_element_type=jnp.float32,
    ).astype(jnp.bfloat16)[order][:, None]

    expert_count = router.shape[1]
    top_count = routes.shape[2]
    capacity = 4 * tree * top_count // (3 * expert_count)
    plane = lax.axis_size(PLANE)
    line = lax.axis_size("z")
    near_experts = lax.axis_index("z") * plane + (
        lax.axis_index(PLANE) ^ jnp.arange(plane, dtype=jnp.int32)
    )
    line_rows = [payload] + [partner(payload, "z", k) for k in range(1, line)]
    beside = [partner(normed, "x", o) for o in range(1, side)]

    shared, beside = shared_terms(normed, beside, shared_weights)
    line_rows[1], beside = lax.optimization_barrier((line_rows[1], beside))

    sent = []
    spread = {}
    for ks in GROUPS:
        pieces, spreads = select(
            near_experts, router, [line_rows[k] for k in ks], plane, capacity, top_count
        )
        spread.update(zip(ks, spreads))
        sent.append([partner(pieces[o], PLANE, o) for o in range(plane)])
    made = []
    for pieces in sent:
        if made:
            pieces, made[-1] = lax.optimization_barrier((pieces, made[-1]))
        made.append(experts(pieces, inner, outer))

    parts = [partner(beside[o - 1], "x", o) for o in range(1, side)]
    routed = None
    follow = None
    for ks, pieces in reversed(list(zip(GROUPS, made))):
        if len(ks) > 1:
            pieces, follow = lax.optimization_barrier((pieces, follow))
        back = [partner(pieces[o], PLANE, o) for o in range(plane)]
        for i, k in reversed(list(enumerate(ks))):
            if k:
                follow = combine(spread[k], back, i * capacity, jnp.bfloat16)
                parts.append(partner(follow, "z", k))
            else:
                routed = combine(spread[k], back, i * capacity, jnp.float32)
    hidden_out = final(live[0][:, None], resid, shared, routed, parts)
    return (hidden_out[None], accepted_kv)


def solution(mesh):
    line = 4
    shape = (line, mesh.shape["req"] // line, mesh.shape["head"] // 2, 2)
    grid = Mesh(mesh.devices.reshape(shape), ALL)
    req = ("z", "y")
    in_specs = (
        P(ALL, None, None),
        P(ALL, None),
        P(req, None),
        P(req),
        P(req, None),
        P(ALL, None, None),
        P(req, HEAD, None, None),
        P(),
        P(None, HEAD),
        P(HEAD, None),
        P(),
        P(None, HEAD),
        P(None, HEAD),
        P(HEAD, None),
        P(),
        P(ALL, None, None),
        P(ALL, None, None),
    )
    out_specs = (P(ALL, None, None), P(req, HEAD, None, None))
    return jax.shard_map(body, mesh=grid, in_specs=in_specs, out_specs=out_specs, check_vma=False)
```

```python
import functools
import math

import jax
import jax.numpy as jnp
from jax import lax
from jax.experimental import pallas as pl
from jax.experimental.pallas import tpu as pltpu
from jax.sharding import Mesh
from jax.sharding import PartitionSpec as P

EPSILON = 1e-06
ROPE_BASE = 10000.0
GROUPS = ((0, 1), (3, 2))
BACK = ((1, None), (3, None), (2, 3), (0, 2))
CHUNK = 512
EXTRA = 128
SMALL = pl.CostEstimate(flops=1024, bytes_accessed=1024, transcendentals=0)
ALL = ("z", "y", "x", "c")
PLANE = ("y", "x")
HEAD = ("x", "c")


def partner(value, axes, offset):
    if offset == 0:
        return value
    size = lax.axis_size(axes)
    return lax.ppermute(value, axes, [(i, i ^ offset) for i in range(size)])


def dot(left, right):
    return jnp.dot(left, right, preferred_element_type=jnp.float32)


def ancestry(parents):
    nodes_count = parents.shape[-1]
    nodes = jnp.arange(nodes_count, dtype=jnp.int32)
    reach = (parents[..., :, None] == nodes).astype(jnp.float32) + jnp.eye(
        nodes_count, dtype=jnp.float32
    )
    for turn in range((nodes_count - 1).bit_length()):
        near = reach.astype(jnp.bfloat16)
        reach = jnp.minimum(
            jnp.einsum("rij,rjk->rik", near, near, preferred_element_type=jnp.float32), 1.0
        )
    depth = jnp.sum(reach, axis=-1) - 1.0
    return (reach, depth)


def arrive(copies):
    for copy in copies:
        copy.wait()


def attend_kernel(
    info, first, second, gain, weight, cosine, sine, reach, cache, outward, *outs_and_scratch
):
    term, mixed = outs_and_scratch[0:2]
    fresh = outs_and_scratch[2:4]
    weight_here, cache_here, gain_here, outward_here, sems = outs_and_scratch[4:]
    tree = first.shape[0]
    width, columns = weight.shape
    head_dim = cosine.shape[2]
    group = columns // head_dim - 2
    deep = width // 2

    gain_copy = pltpu.make_async_copy(gain, gain_here, sems.at[0])
    weight_copies = [
        pltpu.make_async_copy(
            weight.at[pl.ds(i * deep, deep)], weight_here.at[pl.ds(i * deep, deep)], sems.at[1 + i]
        )
        for i in range(2)
    ]
    cache_copies = [
        pltpu.make_async_copy(cache.at[info[i]], cache_here.at[i], sems.at[3 + i])
        for i in range(2)
    ]
    outward_copy = pltpu.make_async_copy(outward, outward_here, sems.at[5])
    for copy in [gain_copy, *weight_copies, *cache_copies, outward_copy]:
        copy.start()

    wide = jnp.concatenate([first[...], second[...]], axis=0).astype(jnp.float32)
    power = jnp.mean(wide * wide, axis=-1, keepdims=True)
    gain_copy.wait()
    normed = (wide * lax.rsqrt(power + EPSILON) * gain_here[...]).astype(jnp.bfloat16)
    weight_copies[0].wait()
    projected = dot(normed[:, :deep], weight_here[:deep])
    weight_copies[1].wait()
    projected = projected + dot(normed[:, deep:], weight_here[deep:])
    scale = 1.0 / math.sqrt(head_dim)

    for i in range(2):
        own = projected[i * tree : (i + 1) * tree]
        request = info[i]
        length = info[2 + i]

        def rope(values):
            return values * cosine[request] + pltpu.roll(values, head_dim // 2, 1) * sine[request]

        def column(c):
            return own[:, c * head_dim : (c + 1) * head_dim]

        query = jnp.concatenate(
            [rope(column(h)).astype(jnp.bfloat16) for h in range(group)], axis=0
        )
        key_new = rope(column(group)).astype(jnp.bfloat16)
        value_new = column(group + 1).astype(jnp.bfloat16)
        fresh[i][:, :head_dim] = key_new
        fresh[i][:, head_dim:] = value_new

        def against(keys):
            return (
                lax.dot_general(
                    query, keys, (((1,), (1,)), ((), ())), preferred_element_type=jnp.float32
                )
                * scale
            )

        allowed = jnp.concatenate([reach[request]] * group, axis=0) > 0.5
        scores = jnp.where(allowed, against(key_new), -1e30)
        peak = jnp.max(scores, axis=-1, keepdims=True)
        weights = jnp.exp(scores - peak)
        total = jnp.sum(weights, axis=-1, keepdims=True)
        summed = dot(weights.astype(jnp.bfloat16), value_new)
        cache_copies[i].wait()

        def chunk(j, carry):
            peak, total, summed = carry
            block = pl.ds(pl.multiple_of(j * CHUNK, CHUNK), CHUNK)
            scores = against(cache_here[i, block, :head_dim])
            place = j * CHUNK + lax.broadcasted_iota(jnp.int32, scores.shape, 1)
            scores = jnp.where(place < length, scores, -1e30)
            higher = jnp.maximum(peak, jnp.max(scores, axis=-1, keepdims=True))
            fade = jnp.exp(peak - higher)
            weights = jnp.exp(scores - higher)
            total = total * fade + jnp.sum(weights, axis=-1, keepdims=True)
            values = cache_here[i, block, head_dim:]
            summed = summed * fade + dot(weights.astype(jnp.bfloat16), values)
            return (higher, total, summed)

        peak, total, summed = lax.fori_loop(
            0, lax.div(length + CHUNK - 1, CHUNK), chunk, (peak, total, summed)
        )
        result = (summed / total).astype(jnp.bfloat16)
        result = jnp.concatenate(
            [result[h * tree : (h + 1) * tree] for h in range(group)], axis=1
        )
        if i:
            mixed[...] = result
        else:
            kept = result
    outward_copy.wait()
    term[...] = dot(kept, outward_here[...])


def in_vmem():
    return pl.BlockSpec(memory_space=pltpu.VMEM)


def in_hbm():
    return pl.BlockSpec(memory_space=pltpu.HBM)


def attend(info, first, second, gain, weight, cosine, sine, reach, cache, outward):
    tree, width = first.shape
    slots, pair = cache.shape[1:]
    head_dim = pair // 2
    columns = weight.shape[1]
    group_columns = columns - pair
    return pl.pallas_call(
        attend_kernel,
        in_specs=[
            pl.BlockSpec(memory_space=pltpu.SMEM),
            in_vmem(),
            in_vmem(),
            in_hbm(),
            in_hbm(),
            in_vmem(),
            in_vmem(),
            in_vmem(),
            in_hbm(),
            in_hbm(),
        ],
        out_specs=[in_vmem()] * 4,
        out_shape=[
            jax.ShapeDtypeStruct((tree, width), jnp.float32),
            jax.ShapeDtypeStruct((tree, group_columns), jnp.bfloat16),
        ]
        + [jax.ShapeDtypeStruct((tree, pair), jnp.bfloat16)] * 2,
        scratch_shapes=[
            pltpu.VMEM((width, columns), jnp.bfloat16),
            pltpu.VMEM((2, slots, pair), jnp.bfloat16),
            pltpu.VMEM((1, width), jnp.float32),
            pltpu.VMEM((group_columns, width), jnp.bfloat16),
            pltpu.SemaphoreType.DMA((6,)),
        ],
        compiler_params=pltpu.CompilerParams(vmem_limit_bytes=60 * 2**20),
        cost_estimate=SMALL,
        name="attend",
    )(info, first, second, gain, weight, cosine, sine, reach, cache, outward)


def project_kernel(term, mixed, outward, out, here, sems):
    half = here.shape[0] // 2
    copies = [
        pltpu.make_async_copy(
            outward.at[pl.ds(i * half, half)], here.at[pl.ds(i * half, half)], sems.at[i]
        )
        for i in range(2)
    ]
    for copy in copies:
        copy.start()
    total = term[...]
    for i, copy in enumerate(copies):
        copy.wait()
        block = slice(i * half, (i + 1) * half)
        total = total + dot(mixed[:, block], here[block])
    out[...] = total.astype(out.dtype)


def project(term, mixed, outward, dtype):
    return pl.pallas_call(
        project_kernel,
        in_specs=[in_vmem(), in_vmem(), in_hbm()],
        out_specs=in_vmem(),
        out_shape=jax.ShapeDtypeStruct(term.shape, dtype),
        scratch_shapes=[pltpu.VMEM(outward.shape, jnp.bfloat16), pltpu.SemaphoreType.DMA((2,))],
        compiler_params=pltpu.CompilerParams(vmem_limit_bytes=60 * 2**20),
        cost_estimate=SMALL,
        name="project",
    )(term, mixed, outward)


def silu(values):
    return values / (1.0 + jnp.exp(-values))


def expert_kernel(*refs, plane, count, deep):
    pieces = refs[:plane]
    weights = refs[plane : plane + 4]
    outs = refs[plane + 4 : plane + 4 + count * plane]
    rows, inner_a, outer_a, inner_b, outer_b, sems = refs[plane + 4 + count * plane :]
    each = pieces[0].shape[0]
    width = rows.shape[1]
    parts = width // deep
    copies = []
    for n, (inner, outer, inner_here, outer_here) in enumerate(
        ((weights[0], weights[1], inner_a, outer_a), (weights[2], weights[3], inner_b, outer_b))
    ):
        base = n * (parts + 1)
        for p in range(parts):
            block = pl.ds(p * deep, deep)
            copies.append(
                pltpu.make_async_copy(inner.at[block], inner_here.at[block], sems.at[base + p])
            )
        copies.append(pltpu.make_async_copy(outer, outer_here, sems.at[base + parts]))
    for copy in copies:
        copy.start()
    for i in range(plane):
        rows[i * each : (i + 1) * each] = pieces[i][...]
    result = None
    for n, (inner_here, outer_here) in enumerate(((inner_a, outer_a), (inner_b, outer_b))):
        base = n * (parts + 1)
        both = None
        for p in range(parts):
            copies[base + p].wait()
            term = dot(rows[:, p * deep : (p + 1) * deep], inner_here[p * deep : (p + 1) * deep])
            both = term if both is None else both + term
        half = both.shape[1] // 2
        hidden = (silu(both[:, :half]) * both[:, half:]).astype(jnp.bfloat16)
        copies[base + parts].wait()
        term = dot(hidden, outer_here[...]).astype(jnp.bfloat16).astype(jnp.float32)
        result = term if result is None else result + term
    step = each // count
    for n in range(count * plane):
        base = (n % plane) * each + (n // plane) * step
        outs[n][...] = result[base : base + step].astype(jnp.bfloat16)


def experts(pieces, count, inner, outer):
    plane = len(pieces)
    each, width = pieces[0].shape
    hidden = inner[0].shape[1]
    deep = width // 2
    kernel = functools.partial(expert_kernel, plane=plane, count=count, deep=deep)
    weight_scratch = [
        pltpu.VMEM((width, hidden), jnp.bfloat16),
        pltpu.VMEM((hidden // 2, width), jnp.bfloat16),
    ]
    made = pl.pallas_call(
        kernel,
        in_specs=[in_vmem()] * plane + [in_hbm()] * 4,
        out_specs=[in_vmem()] * (count * plane),
        out_shape=[jax.ShapeDtypeStruct((each // count, width), jnp.bfloat16)] * (count * plane),
        scratch_shapes=[pltpu.VMEM((plane * each, width), jnp.bfloat16)]
        + weight_scratch * 2
        + [pltpu.SemaphoreType.DMA((2 * (width // deep + 1),))],
        compiler_params=pltpu.CompilerParams(vmem_limit_bytes=60 * 2**20),
        cost_estimate=SMALL,
        name="expert",
    )(*pieces, inner[0], outer[0], inner[1], outer[1])
    return [list(made[i * plane : (i + 1) * plane]) for i in range(count)]


def shared_kernel(*refs, side):
    blocks = refs[:side]
    weights = refs[side : side + 6]
    outs = refs[side + 6 : 2 * side + 6]
    here, sems = refs[2 * side + 6 :]
    copies = [pltpu.make_async_copy(weights[i], here.at[i], sems.at[i]) for i in range(6)]
    for copy in copies:
        copy.start()
    tree = blocks[0].shape[0]
    rows = jnp.concatenate([block[...] for block in blocks], axis=0)

    def turned(i):
        copies[i].wait()
        return lax.dot_general(
            rows, here[i], (((1,), (1,)), ((), ())), preferred_element_type=jnp.float32
        )

    result = None
    for n in range(2):
        hidden = silu(turned(3 * n))
        hidden = (hidden * turned(3 * n + 1)).astype(jnp.bfloat16)
        copies[3 * n + 2].wait()
        term = dot(hidden, here[3 * n + 2])
        result = term if result is None else result + term
    for i in range(side):
        outs[i][...] = result[i * tree : (i + 1) * tree].astype(outs[i].dtype)


def shared_terms(own, beside, weights):
    tree, width = own.shape
    units = weights[0].shape[0]
    side = 1 + len(beside)
    outs = pl.pallas_call(
        functools.partial(shared_kernel, side=side),
        in_specs=[in_vmem()] * side + [in_hbm()] * 6,
        out_specs=[in_vmem()] * side,
        out_shape=[jax.ShapeDtypeStruct((tree, width), jnp.float32)]
        + [jax.ShapeDtypeStruct((tree, width), jnp.bfloat16)] * (side - 1),
        scratch_shapes=[
            pltpu.VMEM((6, units, width), jnp.bfloat16),
            pltpu.SemaphoreType.DMA((6,)),
        ],
        compiler_params=pltpu.CompilerParams(vmem_limit_bytes=60 * 2**20),
        cost_estimate=SMALL,
        name="shared",
    )(own, *beside, *weights)
    return outs[0], list(outs[1:])


def finish_kernel(tokens, term, gain, routes, *refs):
    others = refs[:-3]
    resid, normed, payload = refs[-3:]
    width = tokens.shape[1]
    attn = term[...]
    for other in others:
        attn = attn + other[...].astype(jnp.float32)
    rounded = (tokens[...].astype(jnp.float32) + attn).astype(jnp.bfloat16)
    resid[...] = rounded
    wide = rounded.astype(jnp.float32)
    power = jnp.mean(wide * wide, axis=-1, keepdims=True)
    rows = (wide * lax.rsqrt(power + EPSILON) * gain[...]).astype(jnp.bfloat16)
    normed[...] = rows
    payload[:, :width] = rows
    extra = payload.shape[1] - width
    lane = lax.broadcasted_iota(jnp.int32, (tokens.shape[0], extra), 1)
    numbers = jnp.zeros(lane.shape, jnp.float32)
    for t in range(routes.shape[1]):
        numbers = jnp.where(lane == t, routes[:, t : t + 1].astype(jnp.float32), numbers)
    payload[:, width:] = numbers.astype(jnp.bfloat16)


def finish(tokens, term, others, gain, routes):
    tree, width = tokens.shape
    return pl.pallas_call(
        finish_kernel,
        in_specs=[in_vmem()] * (4 + len(others)),
        out_specs=[in_vmem()] * 3,
        out_shape=[
            jax.ShapeDtypeStruct((tree, width), jnp.bfloat16),
            jax.ShapeDtypeStruct((tree, width), jnp.bfloat16),
            jax.ShapeDtypeStruct((tree, width + EXTRA), jnp.bfloat16),
        ],
        compiler_params=pltpu.CompilerParams(vmem_limit_bytes=16 * 2**20),
        cost_estimate=SMALL,
        name="finish",
    )(tokens, term, gain, routes, *others)


def select_kernel(*refs, count, plane, capacity, top_count):
    near = refs[0]
    router = refs[1]
    sources = refs[2 : 2 + count]
    outs = refs[2 + count : 2 + count + plane]
    spreads = refs[2 + count + plane :]
    width, expert_count = router.shape
    tree = sources[0].shape[0]
    lane = lax.broadcasted_iota(jnp.int32, (tree, plane * capacity), 1)
    place = lax.rem(lane, capacity).astype(jnp.float32)
    owner = lax.div(lane, capacity)
    expert = lax.broadcasted_iota(jnp.int32, (tree, expert_count), 1)
    row = lax.broadcasted_iota(jnp.int32, (tree, tree), 0)
    column = lax.broadcasted_iota(jnp.int32, (tree, tree), 1)
    before = jnp.where(column < row, 1.0, 0.0).astype(jnp.bfloat16)
    for i in range(count):
        rows = sources[i][:, :width]
        routes = sources[i][:, width:].astype(jnp.float32)
        member = jnp.zeros((tree, expert_count), jnp.float32)
        for t in range(top_count):
            named = routes[:, t : t + 1] == expert.astype(jnp.float32)
            member = jnp.where(named, 1.0, member)
        ranks = dot(before, member.astype(jnp.bfloat16))
        slots = jnp.where(member > 0.5, ranks, -1.0)
        logits = dot(rows, router[...])
        picked = member / (1.0 + jnp.exp(-logits))
        gates = picked / jnp.sum(picked, axis=-1, keepdims=True)
        slot = jnp.zeros(lane.shape, jnp.float32)
        gate = jnp.zeros(lane.shape, jnp.float32)
        for o in range(plane):
            mine = expert == near[o]
            slot_o = jnp.sum(jnp.where(mine, slots, 0.0), axis=-1, keepdims=True)
            gate_o = jnp.sum(jnp.where(mine, gates, 0.0), axis=-1, keepdims=True)
            slot = jnp.where(owner == o, slot_o, slot)
            gate = jnp.where(owner == o, gate_o, gate)
        pick = slot == place
        spreads[i][...] = jnp.where(pick, gate, 0.0).astype(jnp.bfloat16)
        chosen = lax.dot_general(
            jnp.where(pick, 1.0, 0.0).astype(jnp.bfloat16),
            rows,
            (((0,), (0,)), ((), ())),
            preferred_element_type=jnp.float32,
        ).astype(jnp.bfloat16)
        for o in range(plane):
            outs[o][i * capacity : (i + 1) * capacity] = chosen[o * capacity : (o + 1) * capacity]


def select(near, router, sources, plane, capacity, top_count):
    tree = sources[0].shape[0]
    width = router.shape[0]
    count = len(sources)
    made = pl.pallas_call(
        functools.partial(
            select_kernel, count=count, plane=plane, capacity=capacity, top_count=top_count
        ),
        in_specs=[pl.BlockSpec(memory_space=pltpu.SMEM)] + [in_vmem()] * (1 + count),
        out_specs=[in_vmem()] * (plane + count),
        out_shape=[jax.ShapeDtypeStruct((count * capacity, width), jnp.bfloat16)] * plane
        + [jax.ShapeDtypeStruct((tree, plane * capacity), jnp.bfloat16)] * count,
        compiler_params=pltpu.CompilerParams(vmem_limit_bytes=16 * 2**20),
        cost_estimate=SMALL,
        name="select",
    )(near, router, *sources)
    return list(made[:plane]), list(made[plane:])


def combine_kernel(spread, *refs):
    out = refs[-1]
    back = jnp.concatenate([piece[...] for piece in refs[:-1]], axis=0)
    out[...] = dot(spread[...], back).astype(out.dtype)


def combine(spread, pieces, dtype):
    tree = spread.shape[0]
    width = pieces[0].shape[1]
    return pl.pallas_call(
        combine_kernel,
        in_specs=[in_vmem()] * (1 + len(pieces)),
        out_specs=in_vmem(),
        out_shape=jax.ShapeDtypeStruct((tree, width), dtype),
        compiler_params=pltpu.CompilerParams(vmem_limit_bytes=16 * 2**20),
        cost_estimate=SMALL,
        name="combine",
    )(spread, *pieces)


def final_kernel(live, resid, shared, routed, *refs):
    total = resid[...].astype(jnp.float32) + shared[...] + routed[...]
    for part in refs[:-1]:
        total = total + part[...].astype(jnp.float32)
    refs[-1][...] = jnp.where(live[...] == 1, total, 0.0).astype(jnp.bfloat16)


def final(live, resid, shared, routed, parts):
    return pl.pallas_call(
        final_kernel,
        in_specs=[in_vmem()] * (4 + len(parts)),
        out_specs=in_vmem(),
        out_shape=jax.ShapeDtypeStruct(resid.shape, jnp.bfloat16),
        compiler_params=pltpu.CompilerParams(vmem_limit_bytes=16 * 2**20),
        cost_estimate=SMALL,
        name="final",
    )(live, resid, shared, routed, *parts)


def body(
    tokens,
    live,
    parents,
    lengths,
    accepted,
    routes,
    cache,
    attn_gain,
    w_qkv,
    w_out,
    ffn_gain,
    shared_gate,
    shared_up,
    shared_down,
    router,
    expert_in,
    expert_out,
):
    tree = tokens.shape[1]
    width = tokens.shape[2]
    own_rows = tokens[0]
    group_count = lax.axis_size(HEAD)
    head_dim = cache.shape[3] // 2
    me = lax.axis_index(HEAD)

    side = lax.axis_size("x")
    near = [own_rows] + [partner(own_rows, "x", o) for o in range(1, side)]
    near_core = [partner(own_rows, "c", 1)]

    reach, depth = ancestry(parents)
    positions = lengths[:, None].astype(jnp.float32) + depth
    frequency = ROPE_BASE ** (-jnp.arange(head_dim // 2, dtype=jnp.float32) / (head_dim // 2))
    angle = positions[..., None] * frequency
    cosine = jnp.cos(angle)
    sine = jnp.sin(angle)
    cosine = jnp.concatenate([cosine, cosine], axis=-1)
    sine = jnp.concatenate([-sine, sine], axis=-1)
    info = []
    for o in range(side):
        ids = me ^ jnp.arange(2 * o, 2 * o + 2, dtype=jnp.int32)
        here = ids[:, None] == jnp.arange(group_count, dtype=jnp.int32)
        info.append(jnp.concatenate([ids, jnp.sum(jnp.where(here, lengths, 0), axis=1)]))
    for o in range(1, side):
        near[o], cosine, sine, reach, info = lax.optimization_barrier(
            (near[o], cosine, sine, reach, info)
        )
        near_core.append(partner(near[o], "c", 1))

    gate_turned, up_turned = shared_gate.T, shared_up.T
    early, near_core[0] = lax.optimization_barrier(((w_out, expert_out[0]), near_core[0]))
    early = [partner(weight, "c", 1) for weight in early]
    middle, near_core = lax.optimization_barrier(
        ((gate_turned, up_turned, shared_down), near_core)
    )
    middle = [partner(weight, "c", 1) for weight in middle]
    near_core, early = lax.optimization_barrier((near_core, early))

    terms = [None] * side
    fresh = [None] * side
    follow = None
    late = expert_in[0]
    for o in reversed(range(side)):
        if follow is not None:
            near_core[o], follow = lax.optimization_barrier((near_core[o], follow))
        own_part, mixed, fresh_own, fresh_other = attend(
            info[o],
            near[o],
            near_core[o],
            attn_gain[None],
            w_qkv,
            cosine,
            sine,
            reach,
            cache[:, 0],
            w_out,
        )
        fresh[o] = jnp.stack([fresh_own, fresh_other])
        other = partner(mixed, "c", 1)
        if o == side - 1:
            other, middle, late = lax.optimization_barrier((other, middle, late))
            late = partner(late, "c", 1)
        terms[o] = project(own_part, other, early[0], jnp.bfloat16 if o else jnp.float32)
        follow = terms[o]
    others = [partner(terms[o], "x", o) for o in range(1, side)]
    own_term, late = lax.optimization_barrier((terms[0], late))
    resid, normed, payload = finish(own_rows, own_term, others, ffn_gain[None], routes[0])
    inner = [expert_in[0], late]
    outer = [expert_out[0], early[1]]
    shared_weights = [gate_turned, up_turned, shared_down, *middle]
    order = me ^ jnp.arange(group_count, dtype=jnp.int32)
    kept = accepted[order][:, :, None] == jnp.arange(tree, dtype=jnp.int32)
    accepted_kv = jnp.einsum(
        "ran,rnd->rad",
        kept.astype(jnp.bfloat16),
        jnp.concatenate(fresh, axis=0),
        preferred_element_type=jnp.float32,
    ).astype(jnp.bfloat16)[order][:, None]

    expert_count = router.shape[1]
    top_count = routes.shape[2]
    capacity = 4 * tree * top_count // (3 * expert_count)
    plane = lax.axis_size(PLANE)
    line = lax.axis_size("z")
    near_experts = lax.axis_index("z") * plane + (
        lax.axis_index(PLANE) ^ jnp.arange(plane, dtype=jnp.int32)
    )
    line_rows = [payload] + [partner(payload, "z", k) for k in range(1, line)]
    beside = [partner(normed, "x", o) for o in range(1, side)]

    shared, beside = shared_terms(normed, beside, shared_weights)
    line_rows[1], beside = lax.optimization_barrier((line_rows[1], beside))

    sent = []
    spread = {}
    for ks in GROUPS:
        pieces, spreads = select(
            near_experts, router, [line_rows[k] for k in ks], plane, capacity, top_count
        )
        spread.update(zip(ks, spreads))
        sent.append([partner(pieces[o], PLANE, o) for o in range(plane)])
    parts = [partner(beside[o - 1], "x", o) for o in range(1, side)]
    made = None
    results = {}
    for ks, pieces in zip(GROUPS, sent):
        if made is not None:
            pieces, made = lax.optimization_barrier((pieces, made))
        made = experts(pieces, len(ks), inner, outer)
        results.update(zip(ks, made))
    totals = {}
    for k, after in BACK:
        pieces = results[k]
        if after is not None:
            pieces, totals[after] = lax.optimization_barrier((pieces, totals[after]))
        back = [partner(pieces[o], PLANE, o) for o in range(plane)]
        totals[k] = combine(spread[k], back, jnp.bfloat16 if k else jnp.float32)
    parts += [partner(totals[k], "z", k) for k, after in BACK if k]
    routed = totals[0]
    hidden_out = final(live[0][:, None], resid, shared, routed, parts)
    return (hidden_out[None], accepted_kv)


def solution(mesh):
    line = 4
    shape = (line, mesh.shape["req"] // line, mesh.shape["head"] // 2, 2)
    grid = Mesh(mesh.devices.reshape(shape), ALL)
    req = ("z", "y")
    in_specs = (
        P(ALL, None, None),
        P(ALL, None),
        P(req, None),
        P(req),
        P(req, None),
        P(ALL, None, None),
        P(req, HEAD, None, None),
        P(),
        P(None, HEAD),
        P(HEAD, None),
        P(),
        P(None, HEAD),
        P(None, HEAD),
        P(HEAD, None),
        P(),
        P(ALL, None, None),
        P(ALL, None, None),
    )
    out_specs = (P(ALL, None, None), P(req, HEAD, None, None))
    return jax.shard_map(body, mesh=grid, in_specs=in_specs, out_specs=out_specs, check_vma=False)
```

```python
import functools
import math

import jax
import jax.numpy as jnp
import numpy as np
from jax import lax
from jax.experimental import pallas as pl
from jax.experimental.pallas import tpu as pltpu
from jax.sharding import Mesh
from jax.sharding import PartitionSpec as P

EPSILON = 1e-06
ROPE_BASE = 10000.0
GROUPS = ((0, 1), (3, 2))
BACK = ((1, None), (3, None), (2, 3), (0, 2))
CHUNK = 512
EXTRA = 128
SMALL = pl.CostEstimate(flops=1024, bytes_accessed=1024, transcendentals=0)
ALL = ("z", "y", "x", "c")
PLANE = ("y", "x")
HEAD = ("x", "c")


def partner(value, axes, offset):
    if offset == 0:
        return value
    size = lax.axis_size(axes)
    return lax.ppermute(value, axes, [(i, i ^ offset) for i in range(size)])


def dot(left, right):
    return jnp.dot(left, right, preferred_element_type=jnp.float32)


def in_vmem():
    return pl.BlockSpec(memory_space=pltpu.VMEM)


def in_hbm():
    return pl.BlockSpec(memory_space=pltpu.HBM)


def in_smem():
    return pl.BlockSpec(memory_space=pltpu.SMEM)


def vmem(mib):
    return pltpu.CompilerParams(vmem_limit_bytes=mib * 2**20)


def load_kernel(*refs):
    count = len(refs) // 2
    sems = refs[2 * count]
    copies = [pltpu.make_async_copy(refs[i], refs[count + i], sems.at[i]) for i in range(count)]
    for copy in copies:
        copy.start()
    for copy in copies:
        copy.wait()


def load(arrays):
    return pl.pallas_call(
        load_kernel,
        in_specs=[in_hbm()] * len(arrays),
        out_specs=[in_vmem()] * len(arrays),
        out_shape=[jax.ShapeDtypeStruct(array.shape, array.dtype) for array in arrays],
        scratch_shapes=[pltpu.SemaphoreType.DMA((len(arrays),))],
        compiler_params=vmem(20),
        cost_estimate=SMALL,
        name="load",
    )(*arrays)


def prepare_kernel(lengths, parents, frequency, *refs):
    count = (len(refs) - 4) // 2
    sources = refs[:count]
    reach, cosine, sine = refs[count : count + 3]
    targets = refs[count + 3 : 2 * count + 3]
    sems = refs[-1]
    copies = [
        pltpu.make_async_copy(sources[i], targets[i], sems.at[i]) for i in range(count)
    ]
    for copy in copies:
        copy.start()
    requests, tree = parents.shape[:2]
    row = lax.broadcasted_iota(jnp.int32, (tree, tree), 0)
    column = lax.broadcasted_iota(jnp.int32, (tree, tree), 1)
    near = [
        jnp.where((parents[r] == column) | (row == column), 1.0, 0.0) for r in range(requests)
    ]
    for turn in range((tree - 1).bit_length()):
        for r in range(requests):
            step = near[r].astype(jnp.bfloat16)
            near[r] = jnp.minimum(dot(step, step), 1.0)
    half = cosine.shape[2] // 2
    lane = lax.broadcasted_iota(jnp.int32, cosine.shape[1:], 1)
    for r in range(requests):
        reach[r] = near[r]
        depth = jnp.sum(near[r], axis=-1, keepdims=True) - 1.0
        angle = (lengths[r].astype(jnp.float32) + depth) * frequency[...]
        cosine[r] = jnp.cos(angle)
        sines = jnp.sin(angle)
        sine[r] = jnp.where(lane < half, -sines, sines)
    for copy in copies:
        copy.wait()


def prepare(lengths, parents, head_dim, arrays):
    requests, tree = parents.shape
    half = head_dim // 2
    frequency = ROPE_BASE ** (-np.arange(half, dtype=np.float64) / half)
    frequency = np.concatenate([frequency, frequency])[None].astype(np.float32)
    table = jax.ShapeDtypeStruct((requests, tree, head_dim), jnp.float32)
    made = pl.pallas_call(
        prepare_kernel,
        in_specs=[in_smem(), in_vmem(), in_vmem()] + [in_hbm()] * len(arrays),
        out_specs=[in_vmem()] * (3 + len(arrays)),
        out_shape=[jax.ShapeDtypeStruct((requests, tree, tree), jnp.float32), table, table]
        + [jax.ShapeDtypeStruct(array.shape, array.dtype) for array in arrays],
        scratch_shapes=[pltpu.SemaphoreType.DMA((len(arrays),))],
        compiler_params=vmem(20),
        cost_estimate=SMALL,
        name="prepare",
    )(lengths, parents[..., None], frequency, *arrays)
    return made[:3], made[3:]


def attend_kernel(
    place, lengths, first, second, gain, weight, cosine, sine, reach, cache, outward, *outs, offset
):
    term, mixed = outs[0:2]
    fresh = outs[2:4]
    tree = first.shape[0]
    columns = weight.shape[1]
    head_dim = cosine.shape[2]
    group = columns // head_dim - 2
    wide = jnp.concatenate([first[...], second[...]], axis=0).astype(jnp.float32)
    power = jnp.mean(wide * wide, axis=-1, keepdims=True)
    normed = (wide * lax.rsqrt(power + EPSILON) * gain[...]).astype(jnp.bfloat16)
    projected = dot(normed, weight[...])
    scale = 1.0 / math.sqrt(head_dim)

    for i in range(2):
        own = projected[i * tree : (i + 1) * tree]
        request = place[0] ^ (offset + i)
        length = lengths[request]

        def rope(values):
            return values * cosine[request] + pltpu.roll(values, head_dim // 2, 1) * sine[request]

        def column(c):
            return own[:, c * head_dim : (c + 1) * head_dim]

        query = jnp.concatenate(
            [rope(column(h)).astype(jnp.bfloat16) for h in range(group)], axis=0
        )
        key_new = rope(column(group)).astype(jnp.bfloat16)
        value_new = column(group + 1).astype(jnp.bfloat16)
        fresh[i][:, :head_dim] = key_new
        fresh[i][:, head_dim:] = value_new

        def against(keys):
            return (
                lax.dot_general(
                    query, keys, (((1,), (1,)), ((), ())), preferred_element_type=jnp.float32
                )
                * scale
            )

        allowed = jnp.concatenate([reach[request]] * group, axis=0) > 0.5
        scores = jnp.where(allowed, against(key_new), -1e30)
        peak = jnp.max(scores, axis=-1, keepdims=True)
        weights = jnp.exp(scores - peak)
        total = jnp.sum(weights, axis=-1, keepdims=True)
        summed = dot(weights.astype(jnp.bfloat16), value_new)

        def chunk(j, carry):
            peak, total, summed = carry
            block = pl.ds(pl.multiple_of(j * CHUNK, CHUNK), CHUNK)
            scores = against(cache[request, block, :head_dim])
            place = j * CHUNK + lax.broadcasted_iota(jnp.int32, scores.shape, 1)
            scores = jnp.where(place < length, scores, -1e30)
            higher = jnp.maximum(peak, jnp.max(scores, axis=-1, keepdims=True))
            fade = jnp.exp(peak - higher)
            weights = jnp.exp(scores - higher)
            total = total * fade + jnp.sum(weights, axis=-1, keepdims=True)
            values = cache[request, block, head_dim:]
            summed = summed * fade + dot(weights.astype(jnp.bfloat16), values)
            return (higher, total, summed)

        peak, total, summed = lax.fori_loop(
            0, lax.div(length + CHUNK - 1, CHUNK), chunk, (peak, total, summed)
        )
        result = (summed / total).astype(jnp.bfloat16)
        result = jnp.concatenate(
            [result[h * tree : (h + 1) * tree] for h in range(group)], axis=1
        )
        if i:
            mixed[...] = result
        else:
            kept = result
    term[...] = dot(kept, outward[...])


def attend(offset, place, lengths, first, second, gain, weight, tables, cache, outward):
    tree, width = first.shape
    slots, pair = cache.shape[1:]
    columns = weight.shape[1]
    group_columns = columns - pair
    reach, cosine, sine = tables
    return pl.pallas_call(
        functools.partial(attend_kernel, offset=offset),
        in_specs=[in_smem()] * 2 + [in_vmem()] * 9,
        out_specs=[in_vmem()] * 4,
        out_shape=[
            jax.ShapeDtypeStruct((tree, width), jnp.float32),
            jax.ShapeDtypeStruct((tree, group_columns), jnp.bfloat16),
        ]
        + [jax.ShapeDtypeStruct((tree, pair), jnp.bfloat16)] * 2,
        compiler_params=vmem(24),
        cost_estimate=SMALL,
        name="attend",
    )(place, lengths, first, second, gain, weight, cosine, sine, reach, cache, outward)


def project_kernel(term, mixed, outward, out):
    out[...] = (term[...] + dot(mixed[...], outward[...])).astype(out.dtype)


def project(term, mixed, outward, dtype):
    return pl.pallas_call(
        project_kernel,
        in_specs=[in_vmem()] * 3,
        out_specs=in_vmem(),
        out_shape=jax.ShapeDtypeStruct(term.shape, dtype),
        compiler_params=vmem(16),
        cost_estimate=SMALL,
        name="project",
    )(term, mixed, outward)


def silu(values):
    return values / (1.0 + jnp.exp(-values))


def expert_kernel(*refs, plane, count):
    pieces = refs[:plane]
    weights = refs[plane : plane + 4]
    outs = refs[plane + 4 :]
    each = pieces[0].shape[0]
    rows = jnp.concatenate([piece[...] for piece in pieces], axis=0)
    result = None
    for n in range(2):
        both = dot(rows, weights[2 * n][...])
        half = both.shape[1] // 2
        hidden = (silu(both[:, :half]) * both[:, half:]).astype(jnp.bfloat16)
        term = dot(hidden, weights[2 * n + 1][...]).astype(jnp.bfloat16).astype(jnp.float32)
        result = term if result is None else result + term
    step = each // count
    for n in range(count * plane):
        base = (n % plane) * each + (n // plane) * step
        outs[n][...] = result[base : base + step].astype(jnp.bfloat16)


def experts(pieces, count, weights):
    plane = len(pieces)
    each, width = pieces[0].shape
    made = pl.pallas_call(
        functools.partial(expert_kernel, plane=plane, count=count),
        in_specs=[in_vmem()] * (plane + 4),
        out_specs=[in_vmem()] * (count * plane),
        out_shape=[jax.ShapeDtypeStruct((each // count, width), jnp.bfloat16)] * (count * plane),
        compiler_params=vmem(36),
        cost_estimate=SMALL,
        name="expert",
    )(*pieces, *weights)
    return [list(made[i * plane : (i + 1) * plane]) for i in range(count)]


def shared_kernel(*refs, side):
    blocks = refs[:side]
    near = refs[side : side + 3]
    weights = refs[side + 3 : side + 6]
    outs = refs[side + 6 : 2 * side + 6]
    here, sems = refs[2 * side + 6 :]
    copies = [pltpu.make_async_copy(weights[i], here.at[i], sems.at[i]) for i in range(3)]
    for copy in copies:
        copy.start()
    tree = blocks[0].shape[0]
    rows = jnp.concatenate([block[...] for block in blocks], axis=0)

    def turned(weight):
        return lax.dot_general(
            rows, weight, (((1,), (1,)), ((), ())), preferred_element_type=jnp.float32
        )

    hidden = (silu(turned(near[0][...])) * turned(near[1][...])).astype(jnp.bfloat16)
    result = dot(hidden, near[2][...])
    copies[0].wait()
    gated = silu(turned(here[0]))
    copies[1].wait()
    hidden = (gated * turned(here[1])).astype(jnp.bfloat16)
    copies[2].wait()
    result = result + dot(hidden, here[2])
    for i in range(side):
        outs[i][...] = result[i * tree : (i + 1) * tree].astype(outs[i].dtype)


def shared_terms(own, beside, near, weights):
    tree, width = own.shape
    side = 1 + len(beside)
    outs = pl.pallas_call(
        functools.partial(shared_kernel, side=side),
        in_specs=[in_vmem()] * (side + 3) + [in_hbm()] * 3,
        out_specs=[in_vmem()] * side,
        out_shape=[jax.ShapeDtypeStruct((tree, width), jnp.float32)]
        + [jax.ShapeDtypeStruct((tree, width), jnp.bfloat16)] * (side - 1),
        scratch_shapes=[
            pltpu.VMEM((3, *weights[0].shape), jnp.bfloat16),
            pltpu.SemaphoreType.DMA((3,)),
        ],
        compiler_params=vmem(20),
        cost_estimate=SMALL,
        name="shared",
    )(own, *beside, *near, *weights)
    return outs[0], list(outs[1:])


def finish_kernel(tokens, term, gain, routes, *refs):
    others = refs[:-3]
    resid, normed, payload = refs[-3:]
    width = tokens.shape[1]
    attn = term[...]
    for other in others:
        attn = attn + other[...].astype(jnp.float32)
    rounded = (tokens[...].astype(jnp.float32) + attn).astype(jnp.bfloat16)
    resid[...] = rounded
    wide = rounded.astype(jnp.float32)
    power = jnp.mean(wide * wide, axis=-1, keepdims=True)
    rows = (wide * lax.rsqrt(power + EPSILON) * gain[...]).astype(jnp.bfloat16)
    normed[...] = rows
    payload[:, :width] = rows
    extra = payload.shape[1] - width
    lane = lax.broadcasted_iota(jnp.int32, (tokens.shape[0], extra), 1)
    numbers = jnp.zeros(lane.shape, jnp.float32)
    for t in range(routes.shape[1]):
        numbers = jnp.where(lane == t, routes[:, t : t + 1].astype(jnp.float32), numbers)
    payload[:, width:] = numbers.astype(jnp.bfloat16)


def finish(tokens, term, others, gain, routes):
    tree, width = tokens.shape
    return pl.pallas_call(
        finish_kernel,
        in_specs=[in_vmem()] * (4 + len(others)),
        out_specs=[in_vmem()] * 3,
        out_shape=[
            jax.ShapeDtypeStruct((tree, width), jnp.bfloat16),
            jax.ShapeDtypeStruct((tree, width), jnp.bfloat16),
            jax.ShapeDtypeStruct((tree, width + EXTRA), jnp.bfloat16),
        ],
        compiler_params=vmem(16),
        cost_estimate=SMALL,
        name="finish",
    )(tokens, term, gain, routes, *others)


def select_kernel(*refs, count, plane, capacity, top_count):
    near = refs[0]
    router = refs[1]
    sources = refs[2 : 2 + count]
    outs = refs[2 + count : 2 + count + plane]
    spreads = refs[2 + count + plane :]
    width, expert_count = router.shape
    tree = sources[0].shape[0]
    lane = lax.broadcasted_iota(jnp.int32, (tree, plane * capacity), 1)
    place = lax.rem(lane, capacity).astype(jnp.float32)
    owner = lax.div(lane, capacity)
    expert = lax.broadcasted_iota(jnp.int32, (tree, expert_count), 1)
    row = lax.broadcasted_iota(jnp.int32, (tree, tree), 0)
    column = lax.broadcasted_iota(jnp.int32, (tree, tree), 1)
    before = jnp.where(column < row, 1.0, 0.0).astype(jnp.bfloat16)
    for i in range(count):
        rows = sources[i][:, :width]
        routes = sources[i][:, width:].astype(jnp.float32)
        member = jnp.zeros((tree, expert_count), jnp.float32)
        for t in range(top_count):
            named = routes[:, t : t + 1] == expert.astype(jnp.float32)
            member = jnp.where(named, 1.0, member)
        ranks = dot(before, member.astype(jnp.bfloat16))
        slots = jnp.where(member > 0.5, ranks, -1.0)
        logits = dot(rows, router[...])
        picked = member / (1.0 + jnp.exp(-logits))
        gates = picked / jnp.sum(picked, axis=-1, keepdims=True)
        slot = jnp.zeros(lane.shape, jnp.float32)
        gate = jnp.zeros(lane.shape, jnp.float32)
        for o in range(plane):
            mine = expert == near[o]
            slot_o = jnp.sum(jnp.where(mine, slots, 0.0), axis=-1, keepdims=True)
            gate_o = jnp.sum(jnp.where(mine, gates, 0.0), axis=-1, keepdims=True)
            slot = jnp.where(owner == o, slot_o, slot)
            gate = jnp.where(owner == o, gate_o, gate)
        pick = slot == place
        spreads[i][...] = jnp.where(pick, gate, 0.0).astype(jnp.bfloat16)
        chosen = lax.dot_general(
            jnp.where(pick, 1.0, 0.0).astype(jnp.bfloat16),
            rows,
            (((0,), (0,)), ((), ())),
            preferred_element_type=jnp.float32,
        ).astype(jnp.bfloat16)
        for o in range(plane):
            outs[o][i * capacity : (i + 1) * capacity] = chosen[o * capacity : (o + 1) * capacity]


def select(near, router, sources, plane, capacity, top_count):
    tree = sources[0].shape[0]
    width = router.shape[0]
    count = len(sources)
    made = pl.pallas_call(
        functools.partial(
            select_kernel, count=count, plane=plane, capacity=capacity, top_count=top_count
        ),
        in_specs=[in_smem()] + [in_vmem()] * (1 + count),
        out_specs=[in_vmem()] * (plane + count),
        out_shape=[jax.ShapeDtypeStruct((count * capacity, width), jnp.bfloat16)] * plane
        + [jax.ShapeDtypeStruct((tree, plane * capacity), jnp.bfloat16)] * count,
        compiler_params=vmem(16),
        cost_estimate=SMALL,
        name="select",
    )(near, router, *sources)
    return list(made[:plane]), list(made[plane:])


def combine_kernel(spread, *refs):
    out = refs[-1]
    back = jnp.concatenate([piece[...] for piece in refs[:-1]], axis=0)
    out[...] = dot(spread[...], back).astype(out.dtype)


def combine(spread, pieces, dtype):
    tree = spread.shape[0]
    width = pieces[0].shape[1]
    return pl.pallas_call(
        combine_kernel,
        in_specs=[in_vmem()] * (1 + len(pieces)),
        out_specs=in_vmem(),
        out_shape=jax.ShapeDtypeStruct((tree, width), dtype),
        compiler_params=vmem(16),
        cost_estimate=SMALL,
        name="combine",
    )(spread, *pieces)


def final_kernel(live, resid, shared, routed, *refs):
    total = resid[...].astype(jnp.float32) + shared[...] + routed[...]
    for part in refs[:-1]:
        total = total + part[...].astype(jnp.float32)
    refs[-1][...] = jnp.where(live[...] == 1, total, 0.0).astype(jnp.bfloat16)


def final(live, resid, shared, routed, parts):
    return pl.pallas_call(
        final_kernel,
        in_specs=[in_vmem()] * (4 + len(parts)),
        out_specs=in_vmem(),
        out_shape=jax.ShapeDtypeStruct(resid.shape, jnp.bfloat16),
        compiler_params=vmem(16),
        cost_estimate=SMALL,
        name="final",
    )(live, resid, shared, routed, *parts)


def body(
    tokens,
    live,
    parents,
    lengths,
    accepted,
    routes,
    cache,
    attn_gain,
    w_qkv,
    w_out,
    ffn_gain,
    shared_gate,
    shared_up,
    shared_down,
    router,
    expert_in,
    expert_out,
):
    tree = tokens.shape[1]
    width = tokens.shape[2]
    own_rows = tokens[0]
    group_count = lax.axis_size(HEAD)
    head_dim = cache.shape[3] // 2
    me = lax.axis_index(HEAD)

    side = lax.axis_size("x")
    near = [own_rows] + [partner(own_rows, "x", o) for o in range(1, side)]
    near_core = [partner(own_rows, "c", 1)]

    tables, (qkv_here, cache_here, out_here) = prepare(
        lengths, parents, head_dim, [w_qkv, cache[:, 0], w_out]
    )
    place = me.astype(jnp.int32)[None]
    for o in range(1, side):
        near[o], tables, place = lax.optimization_barrier((near[o], tables, place))
        near_core.append(partner(near[o], "c", 1))

    gate_turned, up_turned = shared_gate.T, shared_up.T
    early, near_core[0] = lax.optimization_barrier(((w_out, expert_out[0]), near_core[0]))
    early = [partner(weight, "c", 1) for weight in early]
    middle, near_core = lax.optimization_barrier(
        ((gate_turned, up_turned, shared_down), near_core)
    )
    middle = [partner(weight, "c", 1) for weight in middle]
    near_core, early = lax.optimization_barrier((near_core, early))

    terms = [None] * side
    fresh = [None] * side
    follow = None
    late = expert_in[0]
    for o in reversed(range(side)):
        if follow is not None:
            near_core[o], follow = lax.optimization_barrier((near_core[o], follow))
        own_part, mixed, fresh_own, fresh_other = attend(
            2 * o,
            place,
            lengths,
            near[o],
            near_core[o],
            attn_gain[None],
            qkv_here,
            tables,
            cache_here,
            out_here,
        )
        fresh[o] = jnp.stack([fresh_own, fresh_other])
        other = partner(mixed, "c", 1)
        if o == side - 1:
            other, middle, late = lax.optimization_barrier((other, middle, late))
            late = partner(late, "c", 1)
        terms[o] = project(own_part, other, early[0], jnp.bfloat16 if o else jnp.float32)
        follow = terms[o]
    others = [partner(terms[o], "x", o) for o in range(1, side)]
    expert_in_own, expert_out_own, _ = lax.optimization_barrier(
        (expert_in[0], expert_out[0], terms[0])
    )
    inner_here, outer_here = load([expert_in_own, expert_out_own])
    own_term, late, inner_here = lax.optimization_barrier((terms[0], late, inner_here))
    resid, normed, payload = finish(own_rows, own_term, others, ffn_gain[None], routes[0])
    expert_weights = [inner_here, outer_here, late, early[1]]
    order = me ^ jnp.arange(group_count, dtype=jnp.int32)
    kept = accepted[order][:, :, None] == jnp.arange(tree, dtype=jnp.int32)
    accepted_kv = jnp.einsum(
        "ran,rnd->rad",
        kept.astype(jnp.bfloat16),
        jnp.concatenate(fresh, axis=0),
        preferred_element_type=jnp.float32,
    ).astype(jnp.bfloat16)[order][:, None]

    expert_count = router.shape[1]
    top_count = routes.shape[2]
    capacity = 4 * tree * top_count // (3 * expert_count)
    plane = lax.axis_size(PLANE)
    line = lax.axis_size("z")
    near_experts = lax.axis_index("z") * plane + (
        lax.axis_index(PLANE) ^ jnp.arange(plane, dtype=jnp.int32)
    )
    line_rows = [payload] + [partner(payload, "z", k) for k in range(1, line)]
    beside = [partner(normed, "x", o) for o in range(1, side)]

    shared, beside = shared_terms(
        normed, beside, middle, [gate_turned, up_turned, shared_down]
    )
    line_rows[1], beside = lax.optimization_barrier((line_rows[1], beside))

    sent = []
    spread = {}
    for ks in GROUPS:
        pieces, spreads = select(
            near_experts, router, [line_rows[k] for k in ks], plane, capacity, top_count
        )
        spread.update(zip(ks, spreads))
        sent.append([partner(pieces[o], PLANE, o) for o in range(plane)])
    parts = [partner(beside[o - 1], "x", o) for o in range(1, side)]
    made = None
    results = {}
    for ks, pieces in zip(GROUPS, sent):
        if made is not None:
            pieces, made = lax.optimization_barrier((pieces, made))
        made = experts(pieces, len(ks), expert_weights)
        results.update(zip(ks, made))
    totals = {}
    for k, after in BACK:
        pieces = results[k]
        if after is not None:
            pieces, totals[after] = lax.optimization_barrier((pieces, totals[after]))
        back = [partner(pieces[o], PLANE, o) for o in range(plane)]
        totals[k] = combine(spread[k], back, jnp.bfloat16 if k else jnp.float32)
    parts += [partner(totals[k], "z", k) for k, after in BACK if k]
    routed = totals[0]
    hidden_out = final(live[0][:, None], resid, shared, routed, parts)
    return (hidden_out[None], accepted_kv)


def solution(mesh):
    line = 4
    shape = (line, mesh.shape["req"] // line, mesh.shape["head"] // 2, 2)
    grid = Mesh(mesh.devices.reshape(shape), ALL)
    req = ("z", "y")
    in_specs = (
        P(ALL, None, None),
        P(ALL, None),
        P(req, None),
        P(req),
        P(req, None),
        P(ALL, None, None),
        P(req, HEAD, None, None),
        P(),
        P(None, HEAD),
        P(HEAD, None),
        P(),
        P(None, HEAD),
        P(None, HEAD),
        P(HEAD, None),
        P(),
        P(ALL, None, None),
        P(ALL, None, None),
    )
    out_specs = (P(ALL, None, None), P(req, HEAD, None, None))
    return jax.shard_map(body, mesh=grid, in_specs=in_specs, out_specs=out_specs, check_vma=False)
```

```python
import functools
import math

import jax
import jax.numpy as jnp
from jax import lax
from jax.experimental import pallas as pl
from jax.experimental.pallas import tpu as pltpu
from jax.sharding import Mesh
from jax.sharding import PartitionSpec as P

EPSILON = 1e-06
ROPE_BASE = 10000.0
GROUPS = ((0, 1), (3, 2))
BACK = ((3, None, None), (2, 3, None), (1, 3, None), (0, 2, 3))
CHUNK = 512
EXTRA = 128
SMALL = pl.CostEstimate(flops=1024, bytes_accessed=1024, transcendentals=0)
ALL = ("z", "y", "x", "c")
PLANE = ("y", "x")
HEAD = ("x", "c")


def partner(value, axes, offset):
    if offset == 0:
        return value
    size = lax.axis_size(axes)
    return lax.ppermute(value, axes, [(i, i ^ offset) for i in range(size)])


def dot(left, right):
    return jnp.dot(left, right, preferred_element_type=jnp.float32)


def ancestry(parents):
    nodes_count = parents.shape[-1]
    nodes = jnp.arange(nodes_count, dtype=jnp.int32)
    reach = (parents[..., :, None] == nodes).astype(jnp.float32) + jnp.eye(
        nodes_count, dtype=jnp.float32
    )
    for turn in range((nodes_count - 1).bit_length()):
        near = reach.astype(jnp.bfloat16)
        reach = jnp.minimum(
            jnp.einsum("rij,rjk->rik", near, near, preferred_element_type=jnp.float32), 1.0
        )
    depth = jnp.sum(reach, axis=-1) - 1.0
    return (reach, depth)


def arrive(copies):
    for copy in copies:
        copy.wait()


def attend_kernel(
    info, first, second, gain, weight, cosine, sine, reach, cache, outward, *outs_and_scratch
):
    term, term_other = outs_and_scratch[0:2]
    fresh = outs_and_scratch[2:4]
    weight_here, cache_here, gain_here, outward_here, sems = outs_and_scratch[4:]
    tree = first.shape[0]
    width, columns = weight.shape
    head_dim = cosine.shape[2]
    group = columns // head_dim - 2
    deep = width // 2

    gain_copy = pltpu.make_async_copy(gain, gain_here, sems.at[0])
    weight_copies = [
        pltpu.make_async_copy(
            weight.at[pl.ds(i * deep, deep)], weight_here.at[pl.ds(i * deep, deep)], sems.at[1 + i]
        )
        for i in range(2)
    ]
    cache_copies = [
        pltpu.make_async_copy(cache.at[info[i]], cache_here.at[i], sems.at[3 + i])
        for i in range(2)
    ]
    outward_copy = pltpu.make_async_copy(outward, outward_here, sems.at[5])
    for copy in [gain_copy, *weight_copies]:
        copy.start()

    wide = jnp.concatenate([first[...], second[...]], axis=0).astype(jnp.float32)
    power = jnp.mean(wide * wide, axis=-1, keepdims=True)
    gain_copy.wait()
    normed = (wide * lax.rsqrt(power + EPSILON) * gain_here[...]).astype(jnp.bfloat16)
    weight_copies[0].wait()
    cache_copies[0].start()
    projected = dot(normed[:, :deep], weight_here[:deep])
    weight_copies[1].wait()
    cache_copies[1].start()
    projected = projected + dot(normed[:, deep:], weight_here[deep:])
    scale = 1.0 / math.sqrt(head_dim)
    results = []

    for i in range(2):
        own = projected[i * tree : (i + 1) * tree]
        request = info[i]
        length = info[2 + i]

        def rope(values):
            return values * cosine[request] + pltpu.roll(values, head_dim // 2, 1) * sine[request]

        def column(c):
            return own[:, c * head_dim : (c + 1) * head_dim]

        query = jnp.concatenate(
            [rope(column(h)).astype(jnp.bfloat16) for h in range(group)], axis=0
        )
        key_new = rope(column(group)).astype(jnp.bfloat16)
        value_new = column(group + 1).astype(jnp.bfloat16)
        fresh[i][:, :head_dim] = key_new
        fresh[i][:, head_dim:] = value_new

        def against(keys):
            return (
                lax.dot_general(
                    query, keys, (((1,), (1,)), ((), ())), preferred_element_type=jnp.float32
                )
                * scale
            )

        allowed = jnp.concatenate([reach[request]] * group, axis=0) > 0.5
        scores = jnp.where(allowed, against(key_new), -1e30)
        peak = jnp.max(scores, axis=-1, keepdims=True)
        weights = jnp.exp(scores - peak)
        total = jnp.sum(weights, axis=-1, keepdims=True)
        summed = dot(weights.astype(jnp.bfloat16), value_new)
        cache_copies[i].wait()
        if i == 0:
            outward_copy.start()

        def chunk(j, carry):
            peak, total, summed = carry
            block = pl.ds(pl.multiple_of(j * CHUNK, CHUNK), CHUNK)
            scores = against(cache_here[i, block, :head_dim])
            place = j * CHUNK + lax.broadcasted_iota(jnp.int32, scores.shape, 1)
            scores = jnp.where(place < length, scores, -1e30)
            higher = jnp.maximum(peak, jnp.max(scores, axis=-1, keepdims=True))
            fade = jnp.exp(peak - higher)
            weights = jnp.exp(scores - higher)
            total = total * fade + jnp.sum(weights, axis=-1, keepdims=True)
            values = cache_here[i, block, head_dim:]
            summed = summed * fade + dot(weights.astype(jnp.bfloat16), values)
            return (higher, total, summed)

        peak, total, summed = lax.fori_loop(
            0, lax.div(length + CHUNK - 1, CHUNK), chunk, (peak, total, summed)
        )
        result = (summed / total).astype(jnp.bfloat16)
        result = jnp.concatenate(
            [result[h * tree : (h + 1) * tree] for h in range(group)], axis=1
        )
        results.append(result)
    outward_copy.wait()
    terms = dot(jnp.concatenate(results, axis=0), outward_here[...])
    term[...] = terms[:tree]
    term_other[...] = terms[tree:].astype(jnp.bfloat16)


def in_vmem():
    return pl.BlockSpec(memory_space=pltpu.VMEM)


def in_hbm():
    return pl.BlockSpec(memory_space=pltpu.HBM)


def attend(info, first, second, gain, weight, cosine, sine, reach, cache, outward):
    tree, width = first.shape
    slots, pair = cache.shape[1:]
    head_dim = pair // 2
    columns = weight.shape[1]
    group_columns = columns - pair
    return pl.pallas_call(
        attend_kernel,
        in_specs=[
            pl.BlockSpec(memory_space=pltpu.SMEM),
            in_vmem(),
            in_vmem(),
            in_hbm(),
            in_hbm(),
            in_vmem(),
            in_vmem(),
            in_vmem(),
            in_hbm(),
            in_hbm(),
        ],
        out_specs=[in_vmem()] * 4,
        out_shape=[
            jax.ShapeDtypeStruct((tree, width), jnp.float32),
            jax.ShapeDtypeStruct((tree, width), jnp.bfloat16),
        ]
        + [jax.ShapeDtypeStruct((tree, pair), jnp.bfloat16)] * 2,
        scratch_shapes=[
            pltpu.VMEM((width, columns), jnp.bfloat16),
            pltpu.VMEM((2, slots, pair), jnp.bfloat16),
            pltpu.VMEM((1, width), jnp.float32),
            pltpu.VMEM((group_columns, width), jnp.bfloat16),
            pltpu.SemaphoreType.DMA((6,)),
        ],
        compiler_params=pltpu.CompilerParams(vmem_limit_bytes=60 * 2**20),
        cost_estimate=SMALL,
        name="attend",
    )(info, first, second, gain, weight, cosine, sine, reach, cache, outward)


def silu(values):
    return values / (1.0 + jnp.exp(-values))


def expert_kernel(*refs, plane, count, deep):
    pieces = refs[:plane]
    weights = refs[plane : plane + 4]
    outs = refs[plane + 4 : plane + 4 + count * plane]
    rows, inner_a, outer_a, inner_b, outer_b, sems = refs[plane + 4 + count * plane :]
    each = pieces[0].shape[0]
    width = rows.shape[1]
    parts = width // deep
    copies = []
    for n, (inner, outer, inner_here, outer_here) in enumerate(
        ((weights[0], weights[1], inner_a, outer_a), (weights[2], weights[3], inner_b, outer_b))
    ):
        base = n * (parts + 1)
        for p in range(parts):
            block = pl.ds(p * deep, deep)
            copies.append(
                pltpu.make_async_copy(inner.at[block], inner_here.at[block], sems.at[base + p])
            )
        copies.append(pltpu.make_async_copy(outer, outer_here, sems.at[base + parts]))
    for copy in copies[:2]:
        copy.start()

    def take(number):
        copies[number].wait()
        if number + 2 < len(copies):
            copies[number + 2].start()

    for i in range(plane):
        rows[i * each : (i + 1) * each] = pieces[i][...]
    result = None
    for n, (inner_here, outer_here) in enumerate(((inner_a, outer_a), (inner_b, outer_b))):
        base = n * (parts + 1)
        both = None
        for p in range(parts):
            take(base + p)
            term = dot(rows[:, p * deep : (p + 1) * deep], inner_here[p * deep : (p + 1) * deep])
            both = term if both is None else both + term
        half = both.shape[1] // 2
        hidden = (silu(both[:, :half]) * both[:, half:]).astype(jnp.bfloat16)
        take(base + parts)
        term = dot(hidden, outer_here[...]).astype(jnp.bfloat16).astype(jnp.float32)
        result = term if result is None else result + term
    step = each // count
    for n in range(count * plane):
        base = (n % plane) * each + (n // plane) * step
        outs[n][...] = result[base : base + step].astype(jnp.bfloat16)


def experts(pieces, count, inner, outer):
    plane = len(pieces)
    each, width = pieces[0].shape
    hidden = inner[0].shape[1]
    deep = width // 2
    kernel = functools.partial(expert_kernel, plane=plane, count=count, deep=deep)
    weight_scratch = [
        pltpu.VMEM((width, hidden), jnp.bfloat16),
        pltpu.VMEM((hidden // 2, width), jnp.bfloat16),
    ]
    made = pl.pallas_call(
        kernel,
        in_specs=[in_vmem()] * plane + [in_hbm()] * 4,
        out_specs=[in_vmem()] * (count * plane),
        out_shape=[jax.ShapeDtypeStruct((each // count, width), jnp.bfloat16)] * (count * plane),
        scratch_shapes=[pltpu.VMEM((plane * each, width), jnp.bfloat16)]
        + weight_scratch * 2
        + [pltpu.SemaphoreType.DMA((2 * (width // deep + 1),))],
        compiler_params=pltpu.CompilerParams(vmem_limit_bytes=60 * 2**20),
        cost_estimate=SMALL,
        name="expert",
    )(*pieces, inner[0], outer[0], inner[1], outer[1])
    return [list(made[i * plane : (i + 1) * plane]) for i in range(count)]


def shared_kernel(*refs, side):
    blocks = refs[:side]
    weights = refs[side : side + 6]
    outs = refs[side + 6 : 2 * side + 6]
    here, sems = refs[2 * side + 6 :]
    copies = [pltpu.make_async_copy(weights[i], here.at[i], sems.at[i]) for i in range(6)]
    for copy in copies[:2]:
        copy.start()

    def take(number):
        copies[number].wait()
        if number + 2 < len(copies):
            copies[number + 2].start()

    tree = blocks[0].shape[0]
    rows = jnp.concatenate([block[...] for block in blocks], axis=0)

    def turned(i):
        take(i)
        return lax.dot_general(
            rows, here[i], (((1,), (1,)), ((), ())), preferred_element_type=jnp.float32
        )

    result = None
    for n in range(2):
        hidden = silu(turned(3 * n))
        hidden = (hidden * turned(3 * n + 1)).astype(jnp.bfloat16)
        take(3 * n + 2)
        term = dot(hidden, here[3 * n + 2])
        result = term if result is None else result + term
    for i in range(side):
        outs[i][...] = result[i * tree : (i + 1) * tree].astype(outs[i].dtype)


def shared_terms(own, beside, weights):
    tree, width = own.shape
    units = weights[0].shape[0]
    side = 1 + len(beside)
    outs = pl.pallas_call(
        functools.partial(shared_kernel, side=side),
        in_specs=[in_vmem()] * side + [in_hbm()] * 6,
        out_specs=[in_vmem()] * side,
        out_shape=[jax.ShapeDtypeStruct((tree, width), jnp.float32)]
        + [jax.ShapeDtypeStruct((tree, width), jnp.bfloat16)] * (side - 1),
        scratch_shapes=[
            pltpu.VMEM((6, units, width), jnp.bfloat16),
            pltpu.SemaphoreType.DMA((6,)),
        ],
        compiler_params=pltpu.CompilerParams(vmem_limit_bytes=60 * 2**20),
        cost_estimate=SMALL,
        name="shared",
    )(own, *beside, *weights)
    return outs[0], list(outs[1:])


def finish_kernel(tokens, term, gain, routes, *refs):
    others = refs[:-3]
    resid, normed, payload = refs[-3:]
    width = tokens.shape[1]
    attn = term[...]
    for other in others:
        attn = attn + other[...].astype(jnp.float32)
    rounded = (tokens[...].astype(jnp.float32) + attn).astype(jnp.bfloat16)
    resid[...] = rounded
    wide = rounded.astype(jnp.float32)
    power = jnp.mean(wide * wide, axis=-1, keepdims=True)
    rows = (wide * lax.rsqrt(power + EPSILON) * gain[...]).astype(jnp.bfloat16)
    normed[...] = rows
    payload[:, :width] = rows
    extra = payload.shape[1] - width
    lane = lax.broadcasted_iota(jnp.int32, (tokens.shape[0], extra), 1)
    numbers = jnp.zeros(lane.shape, jnp.float32)
    for t in range(routes.shape[1]):
        numbers = jnp.where(lane == t, routes[:, t : t + 1].astype(jnp.float32), numbers)
    payload[:, width:] = numbers.astype(jnp.bfloat16)


def finish(tokens, term, others, gain, routes):
    tree, width = tokens.shape
    return pl.pallas_call(
        finish_kernel,
        in_specs=[in_vmem()] * (4 + len(others)),
        out_specs=[in_vmem()] * 3,
        out_shape=[
            jax.ShapeDtypeStruct((tree, width), jnp.bfloat16),
            jax.ShapeDtypeStruct((tree, width), jnp.bfloat16),
            jax.ShapeDtypeStruct((tree, width + EXTRA), jnp.bfloat16),
        ],
        compiler_params=pltpu.CompilerParams(vmem_limit_bytes=16 * 2**20),
        cost_estimate=SMALL,
        name="finish",
    )(tokens, term, gain, routes, *others)


def select_kernel(*refs, count, plane, capacity, top_count):
    near = refs[0]
    router = refs[1]
    sources = refs[2 : 2 + count]
    outs = refs[2 + count : 2 + count + plane]
    spreads = refs[2 + count + plane :]
    width, expert_count = router.shape
    tree = sources[0].shape[0]
    lane = lax.broadcasted_iota(jnp.int32, (tree, plane * capacity), 1)
    place = lax.rem(lane, capacity).astype(jnp.float32)
    owner = lax.div(lane, capacity)
    expert = lax.broadcasted_iota(jnp.int32, (tree, expert_count), 1)
    row = lax.broadcasted_iota(jnp.int32, (tree, tree), 0)
    column = lax.broadcasted_iota(jnp.int32, (tree, tree), 1)
    before = jnp.where(column < row, 1.0, 0.0).astype(jnp.bfloat16)
    for i in range(count):
        rows = sources[i][:, :width]
        routes = sources[i][:, width:].astype(jnp.float32)
        member = jnp.zeros((tree, expert_count), jnp.float32)
        for t in range(top_count):
            named = routes[:, t : t + 1] == expert.astype(jnp.float32)
            member = jnp.where(named, 1.0, member)
        ranks = dot(before, member.astype(jnp.bfloat16))
        slots = jnp.where(member > 0.5, ranks, -1.0)
        logits = dot(rows, router[...])
        picked = member / (1.0 + jnp.exp(-logits))
        gates = picked / jnp.sum(picked, axis=-1, keepdims=True)
        slot = jnp.zeros(lane.shape, jnp.float32)
        gate = jnp.zeros(lane.shape, jnp.float32)
        for o in range(plane):
            mine = expert == near[o]
            slot_o = jnp.sum(jnp.where(mine, slots, 0.0), axis=-1, keepdims=True)
            gate_o = jnp.sum(jnp.where(mine, gates, 0.0), axis=-1, keepdims=True)
            slot = jnp.where(owner == o, slot_o, slot)
            gate = jnp.where(owner == o, gate_o, gate)
        pick = slot == place
        spreads[i][...] = jnp.where(pick, gate, 0.0).astype(jnp.bfloat16)
        chosen = lax.dot_general(
            jnp.where(pick, 1.0, 0.0).astype(jnp.bfloat16),
            rows,
            (((0,), (0,)), ((), ())),
            preferred_element_type=jnp.float32,
        ).astype(jnp.bfloat16)
        for o in range(plane):
            outs[o][i * capacity : (i + 1) * capacity] = chosen[o * capacity : (o + 1) * capacity]


def select(near, router, sources, plane, capacity, top_count):
    tree = sources[0].shape[0]
    width = router.shape[0]
    count = len(sources)
    made = pl.pallas_call(
        functools.partial(
            select_kernel, count=count, plane=plane, capacity=capacity, top_count=top_count
        ),
        in_specs=[pl.BlockSpec(memory_space=pltpu.SMEM)] + [in_vmem()] * (1 + count),
        out_specs=[in_vmem()] * (plane + count),
        out_shape=[jax.ShapeDtypeStruct((count * capacity, width), jnp.bfloat16)] * plane
        + [jax.ShapeDtypeStruct((tree, plane * capacity), jnp.bfloat16)] * count,
        compiler_params=pltpu.CompilerParams(vmem_limit_bytes=16 * 2**20),
        cost_estimate=SMALL,
        name="select",
    )(near, router, *sources)
    return list(made[:plane]), list(made[plane:])


def combine_kernel(spread, *refs):
    out = refs[-1]
    back = jnp.concatenate([piece[...] for piece in refs[:-1]], axis=0)
    out[...] = dot(spread[...], back).astype(out.dtype)


def combine(spread, pieces, dtype):
    tree = spread.shape[0]
    width = pieces[0].shape[1]
    return pl.pallas_call(
        combine_kernel,
        in_specs=[in_vmem()] * (1 + len(pieces)),
        out_specs=in_vmem(),
        out_shape=jax.ShapeDtypeStruct((tree, width), dtype),
        compiler_params=pltpu.CompilerParams(vmem_limit_bytes=16 * 2**20),
        cost_estimate=SMALL,
        name="combine",
    )(spread, *pieces)


def final_kernel(live, resid, shared, routed, *refs):
    total = resid[...].astype(jnp.float32) + shared[...] + routed[...]
    for part in refs[:-1]:
        total = total + part[...].astype(jnp.float32)
    refs[-1][...] = jnp.where(live[...] == 1, total, 0.0).astype(jnp.bfloat16)


def final(live, resid, shared, routed, parts):
    return pl.pallas_call(
        final_kernel,
        in_specs=[in_vmem()] * (4 + len(parts)),
        out_specs=in_vmem(),
        out_shape=jax.ShapeDtypeStruct(resid.shape, jnp.bfloat16),
        compiler_params=pltpu.CompilerParams(vmem_limit_bytes=16 * 2**20),
        cost_estimate=SMALL,
        name="final",
    )(live, resid, shared, routed, *parts)


def body(
    tokens,
    live,
    parents,
    lengths,
    accepted,
    routes,
    cache,
    attn_gain,
    w_qkv,
    w_out,
    ffn_gain,
    shared_gate,
    shared_up,
    shared_down,
    router,
    expert_in,
    expert_out,
):
    tree = tokens.shape[1]
    width = tokens.shape[2]
    own_rows = tokens[0]
    group_count = lax.axis_size(HEAD)
    head_dim = cache.shape[3] // 2
    me = lax.axis_index(HEAD)

    side = lax.axis_size("x")
    near = [own_rows] + [partner(own_rows, "x", o) for o in range(1, side)]
    near_core = [partner(own_rows, "c", 1)]

    reach, depth = ancestry(parents)
    positions = lengths[:, None].astype(jnp.float32) + depth
    frequency = ROPE_BASE ** (-jnp.arange(head_dim // 2, dtype=jnp.float32) / (head_dim // 2))
    angle = positions[..., None] * frequency
    cosine = jnp.cos(angle)
    sine = jnp.sin(angle)
    cosine = jnp.concatenate([cosine, cosine], axis=-1)
    sine = jnp.concatenate([-sine, sine], axis=-1)
    info = []
    for o in range(side):
        ids = me ^ jnp.arange(2 * o, 2 * o + 2, dtype=jnp.int32)
        here = ids[:, None] == jnp.arange(group_count, dtype=jnp.int32)
        info.append(jnp.concatenate([ids, jnp.sum(jnp.where(here, lengths, 0), axis=1)]))
    for o in range(1, side):
        near[o], cosine, sine, reach, info = lax.optimization_barrier(
            (near[o], cosine, sine, reach, info)
        )
        near_core.append(partner(near[o], "c", 1))

    gate_turned, up_turned = shared_gate.T, shared_up.T
    early, near_core[0] = lax.optimization_barrier(((gate_turned, expert_out[0]), near_core[0]))
    early = [partner(weight, "c", 1) for weight in early]
    middle, near_core = lax.optimization_barrier(
        ((up_turned, shared_down), near_core)
    )
    middle = [partner(weight, "c", 1) for weight in middle]
    near_core, early = lax.optimization_barrier((near_core, early))

    terms = [None] * side
    fresh = [None] * side
    follow = None
    late = expert_in[0]
    for o in reversed(range(side)):
        if follow is not None:
            near_core[o], follow = lax.optimization_barrier((near_core[o], follow))
        own_part, other_part, fresh_own, fresh_other = attend(
            info[o],
            near[o],
            near_core[o],
            attn_gain[None],
            w_qkv,
            cosine,
            sine,
            reach,
            cache[:, 0],
            w_out,
        )
        fresh[o] = jnp.stack([fresh_own, fresh_other])
        other = partner(other_part, "c", 1)
        if o == side - 1:
            other, middle, late = lax.optimization_barrier((other, middle, late))
            late = partner(late, "c", 1)
        terms[o] = own_part + other.astype(jnp.float32)
        if o:
            terms[o] = terms[o].astype(jnp.bfloat16)
        follow = terms[o]
    others = [partner(terms[o], "x", o) for o in range(1, side)]
    own_term, late = lax.optimization_barrier((terms[0], late))
    resid, normed, payload = finish(own_rows, own_term, others, ffn_gain[None], routes[0])
    inner = [expert_in[0], late]
    outer = [expert_out[0], early[1]]
    shared_weights = [gate_turned, up_turned, shared_down, early[0], *middle]
    order = me ^ jnp.arange(group_count, dtype=jnp.int32)
    kept = accepted[order][:, :, None] == jnp.arange(tree, dtype=jnp.int32)
    accepted_kv = jnp.einsum(
        "ran,rnd->rad",
        kept.astype(jnp.bfloat16),
        jnp.concatenate(fresh, axis=0),
        preferred_element_type=jnp.float32,
    ).astype(jnp.bfloat16)[order][:, None]

    expert_count = router.shape[1]
    top_count = routes.shape[2]
    capacity = 4 * tree * top_count // (3 * expert_count)
    plane = lax.axis_size(PLANE)
    line = lax.axis_size("z")
    near_experts = lax.axis_index("z") * plane + (
        lax.axis_index(PLANE) ^ jnp.arange(plane, dtype=jnp.int32)
    )
    line_rows = [payload] + [partner(payload, "z", k) for k in range(1, line)]
    beside = [partner(normed, "x", o) for o in range(1, side)]

    shared, beside = shared_terms(normed, beside, shared_weights)
    line_rows[1], beside = lax.optimization_barrier((line_rows[1], beside))

    sent = []
    spread = {}
    for ks in GROUPS:
        pieces, spreads = select(
            near_experts, router, [line_rows[k] for k in ks], plane, capacity, top_count
        )
        spread.update(zip(ks, spreads))
        sent.append([partner(pieces[o], PLANE, o) for o in range(plane)])
    parts = [partner(beside[o - 1], "x", o) for o in range(1, side)]
    made = None
    results = {}
    for ks, pieces in zip(GROUPS, sent):
        if made is not None:
            pieces, made = lax.optimization_barrier((pieces, made))
        made = experts(pieces, len(ks), inner, outer)
        results.update(zip(ks, made))
    totals = {}
    landed = {}
    for k, after, arrived in BACK:
        pieces = results[k]
        if after is not None:
            pieces, totals[after] = lax.optimization_barrier((pieces, totals[after]))
        if arrived is not None:
            pieces, landed[arrived] = lax.optimization_barrier((pieces, landed[arrived]))
        back = [partner(pieces[o], PLANE, o) for o in range(plane)]
        totals[k] = combine(spread[k], back, jnp.bfloat16 if k else jnp.float32)
        if k:
            landed[k] = partner(totals[k], "z", k)
    parts += list(landed.values())
    routed = totals[0]
    hidden_out = final(live[0][:, None], resid, shared, routed, parts)
    return (hidden_out[None], accepted_kv)


def solution(mesh):
    line = 4
    shape = (line, mesh.shape["req"] // line, mesh.shape["head"] // 2, 2)
    grid = Mesh(mesh.devices.reshape(shape), ALL)
    req = ("z", "y")
    in_specs = (
        P(ALL, None, None),
        P(ALL, None),
        P(req, None),
        P(req),
        P(req, None),
        P(ALL, None, None),
        P(req, HEAD, None, None),
        P(),
        P(None, HEAD),
        P(HEAD, None),
        P(),
        P(None, HEAD),
        P(None, HEAD),
        P(HEAD, None),
        P(),
        P(ALL, None, None),
        P(ALL, None, None),
    )
    out_specs = (P(ALL, None, None), P(req, HEAD, None, None))
    return jax.shard_map(body, mesh=grid, in_specs=in_specs, out_specs=out_specs, check_vma=False)
```

```python
import functools
import math

import jax
import jax.numpy as jnp
from jax import lax
from jax.experimental import pallas as pl
from jax.experimental.pallas import tpu as pltpu
from jax.sharding import Mesh
from jax.sharding import PartitionSpec as P

EPSILON = 1e-06
ROPE_BASE = 10000.0
GROUPS = ((0, 1), (3, 2))
BACK = ((3, None, None), (2, 3, None), (1, 3, None), (0, 2, 3))
CHUNK = 512
EXTRA = 128
SMALL = pl.CostEstimate(flops=1024, bytes_accessed=1024, transcendentals=0)
ALL = ("z", "y", "x", "c")
PLANE = ("y", "x")
HEAD = ("x", "c")


def partner(value, axes, offset):
    if offset == 0:
        return value
    size = lax.axis_size(axes)
    return lax.ppermute(value, axes, [(i, i ^ offset) for i in range(size)])


def dot(left, right):
    return jnp.dot(left, right, preferred_element_type=jnp.float32)


def ancestry(parents):
    nodes_count = parents.shape[-1]
    nodes = jnp.arange(nodes_count, dtype=jnp.int32)
    reach = (parents[..., :, None] == nodes).astype(jnp.float32) + jnp.eye(
        nodes_count, dtype=jnp.float32
    )
    for turn in range((nodes_count - 1).bit_length()):
        near = reach.astype(jnp.bfloat16)
        reach = jnp.minimum(
            jnp.einsum("rij,rjk->rik", near, near, preferred_element_type=jnp.float32), 1.0
        )
    depth = jnp.sum(reach, axis=-1) - 1.0
    return (reach, depth)


def arrive(copies):
    for copy in copies:
        copy.wait()


def attend_kernel(
    info, first, second, gain, weight, cosine, sine, reach, cache, outward, *outs_and_scratch
):
    term, term_other = outs_and_scratch[0:2]
    fresh = outs_and_scratch[2:4]
    weight_here, cache_here, gain_here, outward_here, sems = outs_and_scratch[4:]
    tree = first.shape[0]
    width, columns = weight.shape
    head_dim = cosine.shape[2]
    group = columns // head_dim - 2
    deep = width // 2

    gain_copy = pltpu.make_async_copy(gain, gain_here, sems.at[0])
    weight_copies = [
        pltpu.make_async_copy(
            weight.at[pl.ds(i * deep, deep)], weight_here.at[pl.ds(i * deep, deep)], sems.at[1 + i]
        )
        for i in range(2)
    ]
    cache_copies = [
        pltpu.make_async_copy(cache.at[info[i]], cache_here.at[i], sems.at[3 + i])
        for i in range(2)
    ]
    outward_copy = pltpu.make_async_copy(outward, outward_here, sems.at[5])
    for copy in [gain_copy, *weight_copies]:
        copy.start()

    wide = jnp.concatenate([first[...], second[...]], axis=0).astype(jnp.float32)
    power = jnp.mean(wide * wide, axis=-1, keepdims=True)
    gain_copy.wait()
    normed = (wide * lax.rsqrt(power + EPSILON) * gain_here[...]).astype(jnp.bfloat16)
    weight_copies[0].wait()
    cache_copies[0].start()
    projected = dot(normed[:, :deep], weight_here[:deep])
    weight_copies[1].wait()
    cache_copies[1].start()
    projected = projected + dot(normed[:, deep:], weight_here[deep:])
    scale = 1.0 / math.sqrt(head_dim)
    results = []

    for i in range(2):
        own = projected[i * tree : (i + 1) * tree]
        request = info[i]
        length = info[2 + i]

        def rope(values):
            return values * cosine[request] + pltpu.roll(values, head_dim // 2, 1) * sine[request]

        def column(c):
            return own[:, c * head_dim : (c + 1) * head_dim]

        query = jnp.concatenate(
            [rope(column(h)).astype(jnp.bfloat16) for h in range(group)], axis=0
        )
        key_new = rope(column(group)).astype(jnp.bfloat16)
        value_new = column(group + 1).astype(jnp.bfloat16)
        fresh[i][:, :head_dim] = key_new
        fresh[i][:, head_dim:] = value_new

        def against(keys):
            return (
                lax.dot_general(
                    query, keys, (((1,), (1,)), ((), ())), preferred_element_type=jnp.float32
                )
                * scale
            )

        allowed = jnp.concatenate([reach[request]] * group, axis=0) > 0.5
        scores = jnp.where(allowed, against(key_new), -1e30)
        peak = jnp.max(scores, axis=-1, keepdims=True)
        weights = jnp.exp(scores - peak)
        total = jnp.sum(weights, axis=-1, keepdims=True)
        summed = dot(weights.astype(jnp.bfloat16), value_new)
        cache_copies[i].wait()
        if i == 0:
            outward_copy.start()

        def chunk(j, carry):
            peak, total, summed = carry
            block = pl.ds(pl.multiple_of(j * CHUNK, CHUNK), CHUNK)
            scores = against(cache_here[i, block, :head_dim])
            place = j * CHUNK + lax.broadcasted_iota(jnp.int32, scores.shape, 1)
            scores = jnp.where(place < length, scores, -1e30)
            higher = jnp.maximum(peak, jnp.max(scores, axis=-1, keepdims=True))
            fade = jnp.exp(peak - higher)
            weights = jnp.exp(scores - higher)
            total = total * fade + jnp.sum(weights, axis=-1, keepdims=True)
            values = cache_here[i, block, head_dim:]
            summed = summed * fade + dot(weights.astype(jnp.bfloat16), values)
            return (higher, total, summed)

        peak, total, summed = lax.fori_loop(
            0, lax.div(length + CHUNK - 1, CHUNK), chunk, (peak, total, summed)
        )
        result = (summed / total).astype(jnp.bfloat16)
        result = jnp.concatenate(
            [result[h * tree : (h + 1) * tree] for h in range(group)], axis=1
        )
        results.append(result)
    outward_copy.wait()
    terms = dot(jnp.concatenate(results, axis=0), outward_here[...])
    term[...] = terms[:tree]
    term_other[...] = terms[tree:].astype(jnp.bfloat16)


def in_vmem():
    return pl.BlockSpec(memory_space=pltpu.VMEM)


def in_hbm():
    return pl.BlockSpec(memory_space=pltpu.HBM)


def attend(info, first, second, gain, weight, cosine, sine, reach, cache, outward):
    tree, width = first.shape
    slots, pair = cache.shape[1:]
    head_dim = pair // 2
    columns = weight.shape[1]
    group_columns = columns - pair
    return pl.pallas_call(
        attend_kernel,
        in_specs=[
            pl.BlockSpec(memory_space=pltpu.SMEM),
            in_vmem(),
            in_vmem(),
            in_hbm(),
            in_hbm(),
            in_vmem(),
            in_vmem(),
            in_vmem(),
            in_hbm(),
            in_hbm(),
        ],
        out_specs=[in_vmem()] * 4,
        out_shape=[
            jax.ShapeDtypeStruct((tree, width), jnp.float32),
            jax.ShapeDtypeStruct((tree, width), jnp.bfloat16),
        ]
        + [jax.ShapeDtypeStruct((tree, pair), jnp.bfloat16)] * 2,
        scratch_shapes=[
            pltpu.VMEM((width, columns), jnp.bfloat16),
            pltpu.VMEM((2, slots, pair), jnp.bfloat16),
            pltpu.VMEM((1, width), jnp.float32),
            pltpu.VMEM((group_columns, width), jnp.bfloat16),
            pltpu.SemaphoreType.DMA((6,)),
        ],
        compiler_params=pltpu.CompilerParams(vmem_limit_bytes=60 * 2**20),
        cost_estimate=SMALL,
        name="attend",
    )(info, first, second, gain, weight, cosine, sine, reach, cache, outward)


def silu(values):
    return values / (1.0 + jnp.exp(-values))


def expert_kernel(*refs, plane, count, deep):
    pieces = refs[:plane]
    weights = refs[plane : plane + 4]
    outs = refs[plane + 4 : plane + 4 + count * plane]
    rows, inner_a, outer_a, inner_b, outer_b, sems = refs[plane + 4 + count * plane :]
    each = pieces[0].shape[0]
    width = rows.shape[1]
    parts = width // deep
    copies = []
    for n, (inner, outer, inner_here, outer_here) in enumerate(
        ((weights[0], weights[1], inner_a, outer_a), (weights[2], weights[3], inner_b, outer_b))
    ):
        base = n * (parts + 1)
        for p in range(parts):
            block = pl.ds(p * deep, deep)
            copies.append(
                pltpu.make_async_copy(inner.at[block], inner_here.at[block], sems.at[base + p])
            )
        copies.append(pltpu.make_async_copy(outer, outer_here, sems.at[base + parts]))
    for copy in copies[:2]:
        copy.start()

    def take(number):
        copies[number].wait()
        if number + 2 < len(copies):
            copies[number + 2].start()

    for i in range(plane):
        rows[i * each : (i + 1) * each] = pieces[i][...]
    result = None
    for n, (inner_here, outer_here) in enumerate(((inner_a, outer_a), (inner_b, outer_b))):
        base = n * (parts + 1)
        both = None
        for p in range(parts):
            take(base + p)
            term = dot(rows[:, p * deep : (p + 1) * deep], inner_here[p * deep : (p + 1) * deep])
            both = term if both is None else both + term
        half = both.shape[1] // 2
        hidden = (silu(both[:, :half]) * both[:, half:]).astype(jnp.bfloat16)
        take(base + parts)
        term = dot(hidden, outer_here[...]).astype(jnp.bfloat16).astype(jnp.float32)
        result = term if result is None else result + term
    step = each // count
    for n in range(count * plane):
        base = (n % plane) * each + (n // plane) * step
        outs[n][...] = result[base : base + step].astype(jnp.bfloat16)


def experts(pieces, count, inner, outer):
    plane = len(pieces)
    each, width = pieces[0].shape
    hidden = inner[0].shape[1]
    deep = width // 2
    kernel = functools.partial(expert_kernel, plane=plane, count=count, deep=deep)
    weight_scratch = [
        pltpu.VMEM((width, hidden), jnp.bfloat16),
        pltpu.VMEM((hidden // 2, width), jnp.bfloat16),
    ]
    made = pl.pallas_call(
        kernel,
        in_specs=[in_vmem()] * plane + [in_hbm()] * 4,
        out_specs=[in_vmem()] * (count * plane),
        out_shape=[jax.ShapeDtypeStruct((each // count, width), jnp.bfloat16)] * (count * plane),
        scratch_shapes=[pltpu.VMEM((plane * each, width), jnp.bfloat16)]
        + weight_scratch * 2
        + [pltpu.SemaphoreType.DMA((2 * (width // deep + 1),))],
        compiler_params=pltpu.CompilerParams(vmem_limit_bytes=40 * 2**20),
        cost_estimate=SMALL,
        name="expert",
    )(*pieces, inner[0], outer[0], inner[1], outer[1])
    return [list(made[i * plane : (i + 1) * plane]) for i in range(count)]


def shared_kernel(*refs, side):
    blocks = refs[:side]
    weights = refs[side : side + 6]
    outs = refs[side + 6 : 2 * side + 6]
    here, sems = refs[2 * side + 6 :]
    copies = [pltpu.make_async_copy(weights[i], here.at[i], sems.at[i]) for i in range(6)]
    for copy in copies[:2]:
        copy.start()

    def take(number):
        copies[number].wait()
        if number + 2 < len(copies):
            copies[number + 2].start()

    tree = blocks[0].shape[0]
    rows = jnp.concatenate([block[...] for block in blocks], axis=0).T

    def turned(i):
        take(i)
        return dot(here[i], rows)

    result = None
    for n in range(2):
        hidden = silu(turned(3 * n))
        hidden = (hidden * turned(3 * n + 1)).astype(jnp.bfloat16)
        take(3 * n + 2)
        term = lax.dot_general(
            hidden, here[3 * n + 2], (((0,), (0,)), ((), ())), preferred_element_type=jnp.float32
        )
        result = term if result is None else result + term
    for i in range(side):
        outs[i][...] = result[i * tree : (i + 1) * tree].astype(outs[i].dtype)


def shared_terms(own, beside, weights):
    tree, width = own.shape
    units = weights[0].shape[0]
    side = 1 + len(beside)
    outs = pl.pallas_call(
        functools.partial(shared_kernel, side=side),
        in_specs=[in_vmem()] * side + [in_hbm()] * 6,
        out_specs=[in_vmem()] * side,
        out_shape=[jax.ShapeDtypeStruct((tree, width), jnp.float32)]
        + [jax.ShapeDtypeStruct((tree, width), jnp.bfloat16)] * (side - 1),
        scratch_shapes=[
            pltpu.VMEM((6, units, width), jnp.bfloat16),
            pltpu.SemaphoreType.DMA((6,)),
        ],
        compiler_params=pltpu.CompilerParams(vmem_limit_bytes=60 * 2**20),
        cost_estimate=SMALL,
        name="shared",
    )(own, *beside, *weights)
    return outs[0], list(outs[1:])


def finish_kernel(tokens, term, gain, routes, *refs):
    others = refs[:-3]
    resid, normed, payload = refs[-3:]
    width = tokens.shape[1]
    attn = term[...]
    for other in others:
        attn = attn + other[...].astype(jnp.float32)
    rounded = (tokens[...].astype(jnp.float32) + attn).astype(jnp.bfloat16)
    resid[...] = rounded
    wide = rounded.astype(jnp.float32)
    power = jnp.mean(wide * wide, axis=-1, keepdims=True)
    rows = (wide * lax.rsqrt(power + EPSILON) * gain[...]).astype(jnp.bfloat16)
    normed[...] = rows
    payload[:, :width] = rows
    extra = payload.shape[1] - width
    lane = lax.broadcasted_iota(jnp.int32, (tokens.shape[0], extra), 1)
    numbers = jnp.zeros(lane.shape, jnp.float32)
    for t in range(routes.shape[1]):
        numbers = jnp.where(lane == t, routes[:, t : t + 1].astype(jnp.float32), numbers)
    payload[:, width:] = numbers.astype(jnp.bfloat16)


def finish(tokens, term, others, gain, routes):
    tree, width = tokens.shape
    return pl.pallas_call(
        finish_kernel,
        in_specs=[in_vmem()] * (4 + len(others)),
        out_specs=[in_vmem()] * 3,
        out_shape=[
            jax.ShapeDtypeStruct((tree, width), jnp.bfloat16),
            jax.ShapeDtypeStruct((tree, width), jnp.bfloat16),
            jax.ShapeDtypeStruct((tree, width + EXTRA), jnp.bfloat16),
        ],
        compiler_params=pltpu.CompilerParams(vmem_limit_bytes=16 * 2**20),
        cost_estimate=SMALL,
        name="finish",
    )(tokens, term, gain, routes, *others)


def select_kernel(*refs, count, plane, capacity, top_count):
    near = refs[0]
    router = refs[1]
    sources = refs[2 : 2 + count]
    outs = refs[2 + count : 2 + count + plane]
    spreads = refs[2 + count + plane :]
    width, expert_count = router.shape
    tree = sources[0].shape[0]
    lane = lax.broadcasted_iota(jnp.int32, (tree, plane * capacity), 1)
    place = lax.rem(lane, capacity).astype(jnp.float32)
    owner = lax.div(lane, capacity)
    expert = lax.broadcasted_iota(jnp.int32, (tree, expert_count), 1)
    row = lax.broadcasted_iota(jnp.int32, (tree, tree), 0)
    column = lax.broadcasted_iota(jnp.int32, (tree, tree), 1)
    before = jnp.where(column < row, 1.0, 0.0).astype(jnp.bfloat16)
    for i in range(count):
        rows = sources[i][:, :width]
        routes = sources[i][:, width:].astype(jnp.float32)
        member = jnp.zeros((tree, expert_count), jnp.float32)
        for t in range(top_count):
            named = routes[:, t : t + 1] == expert.astype(jnp.float32)
            member = jnp.where(named, 1.0, member)
        ranks = dot(before, member.astype(jnp.bfloat16))
        slots = jnp.where(member > 0.5, ranks, -1.0)
        logits = dot(rows, router[...])
        picked = member / (1.0 + jnp.exp(-logits))
        gates = picked / jnp.sum(picked, axis=-1, keepdims=True)
        slot = jnp.zeros(lane.shape, jnp.float32)
        gate = jnp.zeros(lane.shape, jnp.float32)
        for o in range(plane):
            mine = expert == near[o]
            slot_o = jnp.sum(jnp.where(mine, slots, 0.0), axis=-1, keepdims=True)
            gate_o = jnp.sum(jnp.where(mine, gates, 0.0), axis=-1, keepdims=True)
            slot = jnp.where(owner == o, slot_o, slot)
            gate = jnp.where(owner == o, gate_o, gate)
        pick = slot == place
        spreads[i][...] = jnp.where(pick, gate, 0.0).astype(jnp.bfloat16)
        chosen = lax.dot_general(
            jnp.where(pick, 1.0, 0.0).astype(jnp.bfloat16),
            rows,
            (((0,), (0,)), ((), ())),
            preferred_element_type=jnp.float32,
        ).astype(jnp.bfloat16)
        for o in range(plane):
            outs[o][i * capacity : (i + 1) * capacity] = chosen[o * capacity : (o + 1) * capacity]


def select(near, router, sources, plane, capacity, top_count):
    tree = sources[0].shape[0]
    width = router.shape[0]
    count = len(sources)
    made = pl.pallas_call(
        functools.partial(
            select_kernel, count=count, plane=plane, capacity=capacity, top_count=top_count
        ),
        in_specs=[pl.BlockSpec(memory_space=pltpu.SMEM)] + [in_vmem()] * (1 + count),
        out_specs=[in_vmem()] * (plane + count),
        out_shape=[jax.ShapeDtypeStruct((count * capacity, width), jnp.bfloat16)] * plane
        + [jax.ShapeDtypeStruct((tree, plane * capacity), jnp.bfloat16)] * count,
        compiler_params=pltpu.CompilerParams(vmem_limit_bytes=16 * 2**20),
        cost_estimate=SMALL,
        name="select",
    )(near, router, *sources)
    return list(made[:plane]), list(made[plane:])


def combine_kernel(spread, *refs):
    out = refs[-1]
    back = jnp.concatenate([piece[...] for piece in refs[:-1]], axis=0)
    out[...] = dot(spread[...], back).astype(out.dtype)


def combine(spread, pieces, dtype):
    tree = spread.shape[0]
    width = pieces[0].shape[1]
    return pl.pallas_call(
        combine_kernel,
        in_specs=[in_vmem()] * (1 + len(pieces)),
        out_specs=in_vmem(),
        out_shape=jax.ShapeDtypeStruct((tree, width), dtype),
        compiler_params=pltpu.CompilerParams(vmem_limit_bytes=16 * 2**20),
        cost_estimate=SMALL,
        name="combine",
    )(spread, *pieces)


def final_kernel(live, resid, shared, routed, *refs):
    total = resid[...].astype(jnp.float32) + shared[...] + routed[...]
    for part in refs[:-1]:
        total = total + part[...].astype(jnp.float32)
    refs[-1][...] = jnp.where(live[...] == 1, total, 0.0).astype(jnp.bfloat16)


def final(live, resid, shared, routed, parts):
    return pl.pallas_call(
        final_kernel,
        in_specs=[in_vmem()] * (4 + len(parts)),
        out_specs=in_vmem(),
        out_shape=jax.ShapeDtypeStruct(resid.shape, jnp.bfloat16),
        compiler_params=pltpu.CompilerParams(vmem_limit_bytes=16 * 2**20),
        cost_estimate=SMALL,
        name="final",
    )(live, resid, shared, routed, *parts)


def body(
    tokens,
    live,
    parents,
    lengths,
    accepted,
    routes,
    cache,
    attn_gain,
    w_qkv,
    w_out,
    ffn_gain,
    shared_gate,
    shared_up,
    shared_down,
    router,
    expert_in,
    expert_out,
):
    tree = tokens.shape[1]
    width = tokens.shape[2]
    own_rows = tokens[0]
    group_count = lax.axis_size(HEAD)
    head_dim = cache.shape[3] // 2
    me = lax.axis_index(HEAD)

    side = lax.axis_size("x")
    near = [own_rows] + [partner(own_rows, "x", o) for o in range(1, side)]
    near_core = [partner(own_rows, "c", 1)]

    reach, depth = ancestry(parents)
    positions = lengths[:, None].astype(jnp.float32) + depth
    frequency = ROPE_BASE ** (-jnp.arange(head_dim // 2, dtype=jnp.float32) / (head_dim // 2))
    angle = positions[..., None] * frequency
    cosine = jnp.cos(angle)
    sine = jnp.sin(angle)
    cosine = jnp.concatenate([cosine, cosine], axis=-1)
    sine = jnp.concatenate([-sine, sine], axis=-1)
    info = []
    for o in range(side):
        ids = me ^ jnp.arange(2 * o, 2 * o + 2, dtype=jnp.int32)
        here = ids[:, None] == jnp.arange(group_count, dtype=jnp.int32)
        info.append(jnp.concatenate([ids, jnp.sum(jnp.where(here, lengths, 0), axis=1)]))
    for o in range(1, side):
        near[o], cosine, sine, reach, info = lax.optimization_barrier(
            (near[o], cosine, sine, reach, info)
        )
        near_core.append(partner(near[o], "c", 1))

    gate_turned, up_turned = shared_gate.T, shared_up.T
    early, near_core[0] = lax.optimization_barrier(((gate_turned, expert_out[0]), near_core[0]))
    early = [partner(weight, "c", 1) for weight in early]
    middle, near_core = lax.optimization_barrier(
        ((up_turned, shared_down), near_core)
    )
    middle = [partner(weight, "c", 1) for weight in middle]
    near_core, early = lax.optimization_barrier((near_core, early))

    terms = [None] * side
    fresh = [None] * side
    follow = None
    late = expert_in[0]
    for o in reversed(range(side)):
        if follow is not None:
            near_core[o], follow = lax.optimization_barrier((near_core[o], follow))
        own_part, other_part, fresh_own, fresh_other = attend(
            info[o],
            near[o],
            near_core[o],
            attn_gain[None],
            w_qkv,
            cosine,
            sine,
            reach,
            cache[:, 0],
            w_out,
        )
        fresh[o] = jnp.stack([fresh_own, fresh_other])
        other = partner(other_part, "c", 1)
        if o == side - 1:
            other, middle, late = lax.optimization_barrier((other, middle, late))
            late = partner(late, "c", 1)
        if o:
            follow = (own_part + other.astype(jnp.float32)).astype(jnp.bfloat16)
            crossed = partner(follow, "x", o).astype(jnp.float32)
            terms[o] = crossed if o == side - 1 else crossed + terms[o + 1]
    own_term = own_part + terms[1] if side > 1 else own_part
    own_term, late = lax.optimization_barrier((own_term, late))
    others = [other]
    resid, normed, payload = finish(own_rows, own_term, others, ffn_gain[None], routes[0])
    inner = [expert_in[0], late]
    outer = [expert_out[0], early[1]]
    shared_weights = [gate_turned, up_turned, shared_down, early[0], *middle]
    order = me ^ jnp.arange(group_count, dtype=jnp.int32)
    kept = accepted[order][:, :, None] == jnp.arange(tree, dtype=jnp.int32)
    accepted_kv = jnp.einsum(
        "ran,rnd->rad",
        kept.astype(jnp.bfloat16),
        jnp.concatenate(fresh, axis=0),
        preferred_element_type=jnp.float32,
    ).astype(jnp.bfloat16)[order][:, None]

    expert_count = router.shape[1]
    top_count = routes.shape[2]
    capacity = 4 * tree * top_count // (3 * expert_count)
    plane = lax.axis_size(PLANE)
    line = lax.axis_size("z")
    near_experts = lax.axis_index("z") * plane + (
        lax.axis_index(PLANE) ^ jnp.arange(plane, dtype=jnp.int32)
    )
    line_rows = [payload] + [partner(payload, "z", k) for k in range(1, line)]
    beside = [partner(normed, "x", o) for o in range(1, side)]

    shared, beside = shared_terms(normed, beside, shared_weights)
    line_rows[1], beside = lax.optimization_barrier((line_rows[1], beside))

    sent = []
    spread = {}
    for ks in GROUPS:
        pieces, spreads = select(
            near_experts, router, [line_rows[k] for k in ks], plane, capacity, top_count
        )
        spread.update(zip(ks, spreads))
        sent.append([partner(pieces[o], PLANE, o) for o in range(plane)])
    parts = [partner(beside[o - 1], "x", o) for o in range(1, side)]
    made = None
    results = {}
    for ks, pieces in zip(GROUPS, sent):
        if made is not None:
            pieces, made, parts = lax.optimization_barrier((pieces, made, parts))
        made = experts(pieces, len(ks), inner, outer)
        results.update(zip(ks, made))
    totals = {}
    landed = {}
    for k, after, arrived in BACK:
        pieces = results[k]
        if after is not None:
            pieces, totals[after] = lax.optimization_barrier((pieces, totals[after]))
        if arrived is not None:
            pieces, landed[arrived] = lax.optimization_barrier((pieces, landed[arrived]))
        back = [partner(pieces[o], PLANE, o) for o in range(plane)]
        totals[k] = combine(spread[k], back, jnp.bfloat16 if k else jnp.float32)
        if k:
            landed[k] = partner(totals[k], "z", k)
    parts += list(landed.values())
    routed = totals[0]
    hidden_out = final(live[0][:, None], resid, shared, routed, parts)
    return (hidden_out[None], accepted_kv)


def solution(mesh):
    line = 4
    shape = (line, mesh.shape["req"] // line, mesh.shape["head"] // 2, 2)
    grid = Mesh(mesh.devices.reshape(shape), ALL)
    req = ("z", "y")
    in_specs = (
        P(ALL, None, None),
        P(ALL, None),
        P(req, None),
        P(req),
        P(req, None),
        P(ALL, None, None),
        P(req, HEAD, None, None),
        P(),
        P(None, HEAD),
        P(HEAD, None),
        P(),
        P(None, HEAD),
        P(None, HEAD),
        P(HEAD, None),
        P(),
        P(ALL, None, None),
        P(ALL, None, None),
    )
    out_specs = (P(ALL, None, None), P(req, HEAD, None, None))
    return jax.shard_map(body, mesh=grid, in_specs=in_specs, out_specs=out_specs, check_vma=False)
```

```python
import functools
import math

import jax
import jax.numpy as jnp
import numpy as np
from jax import lax
from jax.experimental import pallas as pl
from jax.experimental.pallas import tpu as pltpu
from jax.sharding import Mesh
from jax.sharding import PartitionSpec as P

EPSILON = 1e-06
ROPE_BASE = 10000.0
GROUPS = ((0, 3), (2, 1))
BACK = ((3, None, None), (2, None, None), (1, 3, None), (0, 2, 3))
CHUNK = 512
EXTRA = 128
SMALL = pl.CostEstimate(flops=1024, bytes_accessed=1024, transcendentals=0)
ALL = ("z", "y", "x", "c")
PLANE = ("y", "x")
HEAD = ("x", "c")


def partner(value, axes, offset):
    if offset == 0:
        return value
    size = lax.axis_size(axes)
    return lax.ppermute(value, axes, [(i, i ^ offset) for i in range(size)])


def dot(left, right):
    return jnp.dot(left, right, preferred_element_type=jnp.float32)


def prepare_kernel(lengths, parents, frequency, reach, cosine, sine):
    requests, tree = parents.shape
    row = lax.broadcasted_iota(jnp.int32, (tree, tree), 0)
    column = lax.broadcasted_iota(jnp.int32, (tree, tree), 1)
    places = column.astype(jnp.float32)
    known = parents[...].astype(jnp.float32)
    near = []
    for r in range(requests):
        spread = jnp.where(row == column, known[r : r + 1], 0.0)
        parent = jnp.sum(spread, axis=-1, keepdims=True)
        near.append(jnp.where((parent == places) | (row == column), 1.0, 0.0))
    for turn in range((tree - 1).bit_length()):
        for r in range(requests):
            step = near[r].astype(jnp.bfloat16)
            near[r] = jnp.minimum(dot(step, step), 1.0)
    half = cosine.shape[2] // 2
    lane = lax.broadcasted_iota(jnp.int32, cosine.shape[1:], 1)
    for r in range(requests):
        reach[r] = near[r]
        depth = jnp.sum(near[r], axis=-1, keepdims=True) - 1.0
        angle = (lengths[r].astype(jnp.float32) + depth) * frequency[...]
        cosine[r] = jnp.cos(angle)
        sines = jnp.sin(angle)
        sine[r] = jnp.where(lane < half, -sines, sines)


def prepare(lengths, parents, head_dim):
    requests, tree = parents.shape
    half = head_dim // 2
    frequency = ROPE_BASE ** (-np.arange(half, dtype=np.float64) / half)
    frequency = np.concatenate([frequency, frequency])[None].astype(np.float32)
    table = jax.ShapeDtypeStruct((requests, tree, head_dim), jnp.float32)
    return pl.pallas_call(
        prepare_kernel,
        in_specs=[in_smem(), in_vmem(), in_vmem()],
        out_specs=[in_vmem()] * 3,
        out_shape=[jax.ShapeDtypeStruct((requests, tree, tree), jnp.float32), table, table],
        compiler_params=pltpu.CompilerParams(vmem_limit_bytes=16 * 2**20),
        cost_estimate=SMALL,
        name="prepare",
    )(lengths, parents, frequency)


def attend_kernel(
    place, lengths, first, second, gain, weight, cosine, sine, reach, cache, outward, *rest, offset
):
    term, term_other = rest[0:2]
    fresh = rest[2:4]
    weight_here, cache_here, gain_here, outward_here, sems = rest[4:]
    tree = first.shape[0]
    width, columns = weight.shape
    head_dim = cosine.shape[2]
    group = columns // head_dim - 2
    deep = width // 2

    gain_copy = pltpu.make_async_copy(gain, gain_here, sems.at[0])
    weight_copies = [
        pltpu.make_async_copy(
            weight.at[pl.ds(i * deep, deep)], weight_here.at[pl.ds(i * deep, deep)], sems.at[1 + i]
        )
        for i in range(2)
    ]
    cache_copies = [
        pltpu.make_async_copy(
            cache.at[place[0] ^ (offset + i)], cache_here.at[i], sems.at[3 + i]
        )
        for i in range(2)
    ]
    outward_copy = pltpu.make_async_copy(outward, outward_here, sems.at[5])
    for copy in [gain_copy, *weight_copies]:
        copy.start()

    wide = jnp.concatenate([first[...], second[...]], axis=0).astype(jnp.float32)
    power = jnp.mean(wide * wide, axis=-1, keepdims=True)
    gain_copy.wait()
    normed = (wide * lax.rsqrt(power + EPSILON) * gain_here[...]).astype(jnp.bfloat16)
    weight_copies[0].wait()
    cache_copies[0].start()
    projected = dot(normed[:, :deep], weight_here[:deep])
    weight_copies[1].wait()
    cache_copies[1].start()
    projected = projected + dot(normed[:, deep:], weight_here[deep:])
    scale = 1.0 / math.sqrt(head_dim)
    results = []

    for i in range(2):
        own = projected[i * tree : (i + 1) * tree]
        request = place[0] ^ (offset + i)
        length = lengths[request]

        def rope(values):
            return values * cosine[request] + pltpu.roll(values, head_dim // 2, 1) * sine[request]

        def column(c):
            return own[:, c * head_dim : (c + 1) * head_dim]

        query = jnp.concatenate(
            [rope(column(h)).astype(jnp.bfloat16) for h in range(group)], axis=0
        )
        key_new = rope(column(group)).astype(jnp.bfloat16)
        value_new = column(group + 1).astype(jnp.bfloat16)
        fresh[i][:, :head_dim] = key_new
        fresh[i][:, head_dim:] = value_new

        def against(keys):
            return (
                lax.dot_general(
                    query, keys, (((1,), (1,)), ((), ())), preferred_element_type=jnp.float32
                )
                * scale
            )

        allowed = jnp.concatenate([reach[request]] * group, axis=0) > 0.5
        scores = jnp.where(allowed, against(key_new), -1e30)
        peak = jnp.max(scores, axis=-1, keepdims=True)
        weights = jnp.exp(scores - peak)
        total = jnp.sum(weights, axis=-1, keepdims=True)
        summed = dot(weights.astype(jnp.bfloat16), value_new)
        cache_copies[i].wait()
        if i == 0:
            outward_copy.start()

        def chunk(j, carry):
            peak, total, summed = carry
            block = pl.ds(pl.multiple_of(j * CHUNK, CHUNK), CHUNK)
            scores = against(cache_here[i, block, :head_dim])
            place = j * CHUNK + lax.broadcasted_iota(jnp.int32, scores.shape, 1)
            scores = jnp.where(place < length, scores, -1e30)
            higher = jnp.maximum(peak, jnp.max(scores, axis=-1, keepdims=True))
            fade = jnp.exp(peak - higher)
            weights = jnp.exp(scores - higher)
            total = total * fade + jnp.sum(weights, axis=-1, keepdims=True)
            values = cache_here[i, block, head_dim:]
            summed = summed * fade + dot(weights.astype(jnp.bfloat16), values)
            return (higher, total, summed)

        peak, total, summed = lax.fori_loop(
            0, lax.div(length + CHUNK - 1, CHUNK), chunk, (peak, total, summed)
        )
        result = (summed / total).astype(jnp.bfloat16)
        result = jnp.concatenate(
            [result[h * tree : (h + 1) * tree] for h in range(group)], axis=1
        )
        results.append(result)
    outward_copy.wait()
    terms = dot(jnp.concatenate(results, axis=0), outward_here[...])
    term[...] = terms[:tree]
    term_other[...] = terms[tree:].astype(jnp.bfloat16)


def in_vmem():
    return pl.BlockSpec(memory_space=pltpu.VMEM)


def in_smem():
    return pl.BlockSpec(memory_space=pltpu.SMEM)


def in_hbm():
    return pl.BlockSpec(memory_space=pltpu.HBM)


def attend(offset, place, lengths, first, second, gain, weight, cosine, sine, reach, cache, outward):
    tree, width = first.shape
    slots, pair = cache.shape[1:]
    head_dim = pair // 2
    columns = weight.shape[1]
    group_columns = columns - pair
    return pl.pallas_call(
        functools.partial(attend_kernel, offset=offset),
        in_specs=[
            in_smem(),
            in_smem(),
            in_vmem(),
            in_vmem(),
            in_hbm(),
            in_hbm(),
            in_vmem(),
            in_vmem(),
            in_vmem(),
            in_hbm(),
            in_hbm(),
        ],
        out_specs=[in_vmem()] * 4,
        out_shape=[
            jax.ShapeDtypeStruct((tree, width), jnp.float32),
            jax.ShapeDtypeStruct((tree, width), jnp.bfloat16),
        ]
        + [jax.ShapeDtypeStruct((tree, pair), jnp.bfloat16)] * 2,
        scratch_shapes=[
            pltpu.VMEM((width, columns), jnp.bfloat16),
            pltpu.VMEM((2, slots, pair), jnp.bfloat16),
            pltpu.VMEM((1, width), jnp.float32),
            pltpu.VMEM((group_columns, width), jnp.bfloat16),
            pltpu.SemaphoreType.DMA((6,)),
        ],
        compiler_params=pltpu.CompilerParams(vmem_limit_bytes=60 * 2**20),
        cost_estimate=SMALL,
        name="attend",
    )(place, lengths, first, second, gain, weight, cosine, sine, reach, cache, outward)


def silu(values):
    return values / (1.0 + jnp.exp(-values))


def expert_kernel(*refs, plane, count, deep):
    pieces = refs[:plane]
    weights = refs[plane : plane + 4]
    outs = refs[plane + 4 : plane + 4 + count * plane]
    rows, inner_a, outer_a, inner_b, outer_b, sems = refs[plane + 4 + count * plane :]
    each = pieces[0].shape[0]
    width = rows.shape[1]
    parts = width // deep
    copies = []
    for n, (inner, outer, inner_here, outer_here) in enumerate(
        ((weights[0], weights[1], inner_a, outer_a), (weights[2], weights[3], inner_b, outer_b))
    ):
        base = n * (parts + 1)
        for p in range(parts):
            block = pl.ds(p * deep, deep)
            copies.append(
                pltpu.make_async_copy(inner.at[block], inner_here.at[block], sems.at[base + p])
            )
        copies.append(pltpu.make_async_copy(outer, outer_here, sems.at[base + parts]))
    for copy in copies[:2]:
        copy.start()

    def take(number):
        copies[number].wait()
        if number + 2 < len(copies):
            copies[number + 2].start()

    for i in range(plane):
        rows[i * each : (i + 1) * each] = pieces[i][...]
    result = None
    for n, (inner_here, outer_here) in enumerate(((inner_a, outer_a), (inner_b, outer_b))):
        base = n * (parts + 1)
        both = None
        for p in range(parts):
            take(base + p)
            term = dot(rows[:, p * deep : (p + 1) * deep], inner_here[p * deep : (p + 1) * deep])
            both = term if both is None else both + term
        half = both.shape[1] // 2
        hidden = (silu(both[:, :half]) * both[:, half:]).astype(jnp.bfloat16)
        take(base + parts)
        term = dot(hidden, outer_here[...]).astype(jnp.bfloat16).astype(jnp.float32)
        result = term if result is None else result + term
    step = each // count
    for n in range(count * plane):
        base = (n % plane) * each + (n // plane) * step
        outs[n][...] = result[base : base + step].astype(jnp.bfloat16)


def experts(pieces, count, inner, outer):
    plane = len(pieces)
    each, width = pieces[0].shape
    hidden = inner[0].shape[1]
    deep = width // 2
    kernel = functools.partial(expert_kernel, plane=plane, count=count, deep=deep)
    weight_scratch = [
        pltpu.VMEM((width, hidden), jnp.bfloat16),
        pltpu.VMEM((hidden // 2, width), jnp.bfloat16),
    ]
    made = pl.pallas_call(
        kernel,
        in_specs=[in_vmem()] * plane + [in_hbm()] * 4,
        out_specs=[in_vmem()] * (count * plane),
        out_shape=[jax.ShapeDtypeStruct((each // count, width), jnp.bfloat16)] * (count * plane),
        scratch_shapes=[pltpu.VMEM((plane * each, width), jnp.bfloat16)]
        + weight_scratch * 2
        + [pltpu.SemaphoreType.DMA((2 * (width // deep + 1),))],
        compiler_params=pltpu.CompilerParams(vmem_limit_bytes=40 * 2**20),
        cost_estimate=SMALL,
        name="expert",
    )(*pieces, inner[0], outer[0], inner[1], outer[1])
    return [list(made[i * plane : (i + 1) * plane]) for i in range(count)]


def shared_kernel(*refs, side):
    blocks = refs[:side]
    weights = refs[side : side + 6]
    outs = refs[side + 6 : 2 * side + 6]
    here, sems = refs[2 * side + 6 :]
    copies = [pltpu.make_async_copy(weights[i], here.at[i], sems.at[i]) for i in range(6)]
    for copy in copies[:2]:
        copy.start()

    def take(number):
        copies[number].wait()
        if number + 2 < len(copies):
            copies[number + 2].start()

    tree = blocks[0].shape[0]
    rows = jnp.concatenate([block[...] for block in blocks], axis=0).T

    def turned(i):
        take(i)
        return dot(here[i], rows)

    result = None
    for n in range(2):
        hidden = silu(turned(3 * n))
        hidden = (hidden * turned(3 * n + 1)).astype(jnp.bfloat16)
        take(3 * n + 2)
        term = lax.dot_general(
            hidden, here[3 * n + 2], (((0,), (0,)), ((), ())), preferred_element_type=jnp.float32
        )
        result = term if result is None else result + term
    for i in range(side):
        outs[i][...] = result[i * tree : (i + 1) * tree].astype(outs[i].dtype)


def shared_terms(own, beside, weights):
    tree, width = own.shape
    units = weights[0].shape[0]
    side = 1 + len(beside)
    outs = pl.pallas_call(
        functools.partial(shared_kernel, side=side),
        in_specs=[in_vmem()] * side + [in_hbm()] * 6,
        out_specs=[in_vmem()] * side,
        out_shape=[jax.ShapeDtypeStruct((tree, width), jnp.float32)]
        + [jax.ShapeDtypeStruct((tree, width), jnp.bfloat16)] * (side - 1),
        scratch_shapes=[
            pltpu.VMEM((6, units, width), jnp.bfloat16),
            pltpu.SemaphoreType.DMA((6,)),
        ],
        compiler_params=pltpu.CompilerParams(vmem_limit_bytes=60 * 2**20),
        cost_estimate=SMALL,
        name="shared",
    )(own, *beside, *weights)
    return outs[0], list(outs[1:])


def finish_kernel(tokens, term, gain, routes, *refs):
    others = refs[:-3]
    resid, normed, payload = refs[-3:]
    width = tokens.shape[1]
    attn = term[...]
    for other in others:
        attn = attn + other[...].astype(jnp.float32)
    rounded = (tokens[...].astype(jnp.float32) + attn).astype(jnp.bfloat16)
    resid[...] = rounded
    wide = rounded.astype(jnp.float32)
    power = jnp.mean(wide * wide, axis=-1, keepdims=True)
    rows = (wide * lax.rsqrt(power + EPSILON) * gain[...]).astype(jnp.bfloat16)
    normed[...] = rows
    payload[:, :width] = rows
    extra = payload.shape[1] - width
    lane = lax.broadcasted_iota(jnp.int32, (tokens.shape[0], extra), 1)
    numbers = jnp.zeros(lane.shape, jnp.float32)
    for t in range(routes.shape[1]):
        numbers = jnp.where(lane == t, routes[:, t : t + 1].astype(jnp.float32), numbers)
    payload[:, width:] = numbers.astype(jnp.bfloat16)


def finish(tokens, term, others, gain, routes):
    tree, width = tokens.shape
    return pl.pallas_call(
        finish_kernel,
        in_specs=[in_vmem()] * (4 + len(others)),
        out_specs=[in_vmem()] * 3,
        out_shape=[
            jax.ShapeDtypeStruct((tree, width), jnp.bfloat16),
            jax.ShapeDtypeStruct((tree, width), jnp.bfloat16),
            jax.ShapeDtypeStruct((tree, width + EXTRA), jnp.bfloat16),
        ],
        compiler_params=pltpu.CompilerParams(vmem_limit_bytes=16 * 2**20),
        cost_estimate=SMALL,
        name="finish",
    )(tokens, term, gain, routes, *others)


def select_kernel(*refs, count, plane, capacity, top_count):
    near = refs[0]
    router = refs[1]
    sources = refs[2 : 2 + count]
    outs = refs[2 + count : 2 + count + plane]
    spreads = refs[2 + count + plane :]
    width, expert_count = router.shape
    tree = sources[0].shape[0]
    lane = lax.broadcasted_iota(jnp.int32, (tree, plane * capacity), 1)
    place = lax.rem(lane, capacity).astype(jnp.float32)
    owner = lax.div(lane, capacity)
    expert = lax.broadcasted_iota(jnp.int32, (tree, expert_count), 1)
    row = lax.broadcasted_iota(jnp.int32, (tree, tree), 0)
    column = lax.broadcasted_iota(jnp.int32, (tree, tree), 1)
    before = jnp.where(column < row, 1.0, 0.0).astype(jnp.bfloat16)
    for i in range(count):
        rows = sources[i][:, :width]
        routes = sources[i][:, width:].astype(jnp.float32)
        member = jnp.zeros((tree, expert_count), jnp.float32)
        for t in range(top_count):
            named = routes[:, t : t + 1] == expert.astype(jnp.float32)
            member = jnp.where(named, 1.0, member)
        ranks = dot(before, member.astype(jnp.bfloat16))
        slots = jnp.where(member > 0.5, ranks, -1.0)
        logits = dot(rows, router[...])
        picked = member / (1.0 + jnp.exp(-logits))
        gates = picked / jnp.sum(picked, axis=-1, keepdims=True)
        slot = jnp.zeros(lane.shape, jnp.float32)
        gate = jnp.zeros(lane.shape, jnp.float32)
        for o in range(plane):
            mine = expert == near[o]
            slot_o = jnp.sum(jnp.where(mine, slots, 0.0), axis=-1, keepdims=True)
            gate_o = jnp.sum(jnp.where(mine, gates, 0.0), axis=-1, keepdims=True)
            slot = jnp.where(owner == o, slot_o, slot)
            gate = jnp.where(owner == o, gate_o, gate)
        pick = slot == place
        spreads[i][...] = jnp.where(pick, gate, 0.0).astype(jnp.bfloat16)
        chosen = lax.dot_general(
            jnp.where(pick, 1.0, 0.0).astype(jnp.bfloat16),
            rows,
            (((0,), (0,)), ((), ())),
            preferred_element_type=jnp.float32,
        ).astype(jnp.bfloat16)
        for o in range(plane):
            outs[o][i * capacity : (i + 1) * capacity] = chosen[o * capacity : (o + 1) * capacity]


def select(near, router, sources, plane, capacity, top_count):
    tree = sources[0].shape[0]
    width = router.shape[0]
    count = len(sources)
    made = pl.pallas_call(
        functools.partial(
            select_kernel, count=count, plane=plane, capacity=capacity, top_count=top_count
        ),
        in_specs=[in_smem()] + [in_vmem()] * (1 + count),
        out_specs=[in_vmem()] * (plane + count),
        out_shape=[jax.ShapeDtypeStruct((count * capacity, width), jnp.bfloat16)] * plane
        + [jax.ShapeDtypeStruct((tree, plane * capacity), jnp.bfloat16)] * count,
        compiler_params=pltpu.CompilerParams(vmem_limit_bytes=16 * 2**20),
        cost_estimate=SMALL,
        name="select",
    )(near, router, *sources)
    return list(made[:plane]), list(made[plane:])


def combine_kernel(spread, *refs):
    out = refs[-1]
    back = jnp.concatenate([piece[...] for piece in refs[:-1]], axis=0)
    out[...] = dot(spread[...], back).astype(out.dtype)


def combine(spread, pieces, dtype):
    tree = spread.shape[0]
    width = pieces[0].shape[1]
    return pl.pallas_call(
        combine_kernel,
        in_specs=[in_vmem()] * (1 + len(pieces)),
        out_specs=in_vmem(),
        out_shape=jax.ShapeDtypeStruct((tree, width), dtype),
        compiler_params=pltpu.CompilerParams(vmem_limit_bytes=16 * 2**20),
        cost_estimate=SMALL,
        name="combine",
    )(spread, *pieces)


def final_kernel(live, resid, shared, routed, *refs):
    total = resid[...].astype(jnp.float32) + shared[...] + routed[...]
    for part in refs[:-1]:
        total = total + part[...].astype(jnp.float32)
    refs[-1][...] = jnp.where(live[...] == 1, total, 0.0).astype(jnp.bfloat16)


def final(live, resid, shared, routed, parts):
    return pl.pallas_call(
        final_kernel,
        in_specs=[in_vmem()] * (4 + len(parts)),
        out_specs=in_vmem(),
        out_shape=jax.ShapeDtypeStruct(resid.shape, jnp.bfloat16),
        compiler_params=pltpu.CompilerParams(vmem_limit_bytes=16 * 2**20),
        cost_estimate=SMALL,
        name="final",
    )(live, resid, shared, routed, *parts)


def body(
    tokens,
    live,
    parents,
    lengths,
    accepted,
    routes,
    cache,
    attn_gain,
    w_qkv,
    w_out,
    ffn_gain,
    shared_gate,
    shared_up,
    shared_down,
    router,
    expert_in,
    expert_out,
):
    tree = tokens.shape[1]
    width = tokens.shape[2]
    own_rows = tokens[0]
    group_count = lax.axis_size(HEAD)
    head_dim = cache.shape[3] // 2
    me = lax.axis_index(HEAD)

    side = lax.axis_size("x")
    near = [own_rows] + [partner(own_rows, "x", o) for o in range(1, side)]
    near_core = [partner(own_rows, "c", 1)]

    reach, cosine, sine = prepare(lengths, parents, head_dim)
    place = me.astype(jnp.int32)[None]
    for o in range(1, side):
        near[o], cosine, sine, reach, place = lax.optimization_barrier(
            (near[o], cosine, sine, reach, place)
        )
        near_core.append(partner(near[o], "c", 1))

    gate_turned, up_turned = shared_gate.T, shared_up.T
    early, near_core[0] = lax.optimization_barrier(((gate_turned, expert_out[0]), near_core[0]))
    early = [partner(weight, "c", 1) for weight in early]
    middle, near_core = lax.optimization_barrier(
        ((up_turned, shared_down), near_core)
    )
    middle = [partner(weight, "c", 1) for weight in middle]
    near_core, early = lax.optimization_barrier((near_core, early))

    terms = [None] * side
    fresh = [None] * side
    follow = None
    late = expert_in[0]
    for o in reversed(range(side)):
        if follow is not None:
            near_core[o], follow = lax.optimization_barrier((near_core[o], follow))
        own_part, other_part, fresh_own, fresh_other = attend(
            2 * o,
            place,
            lengths,
            near[o],
            near_core[o],
            attn_gain[None],
            w_qkv,
            cosine,
            sine,
            reach,
            cache[:, 0],
            w_out,
        )
        fresh[o] = jnp.stack([fresh_own, fresh_other])
        other = partner(other_part, "c", 1)
        if o == side - 1:
            other, middle, late = lax.optimization_barrier((other, middle, late))
            late = partner(late, "c", 1)
        if o:
            follow = (own_part + other.astype(jnp.float32)).astype(jnp.bfloat16)
            crossed = partner(follow, "x", o).astype(jnp.float32)
            terms[o] = crossed if o == side - 1 else crossed + terms[o + 1]
    own_term = own_part + terms[1] if side > 1 else own_part
    own_term, late = lax.optimization_barrier((own_term, late))
    others = [other]
    resid, normed, payload = finish(own_rows, own_term, others, ffn_gain[None], routes[0])
    inner = [expert_in[0], late]
    outer = [expert_out[0], early[1]]
    shared_weights = [gate_turned, up_turned, shared_down, early[0], *middle]
    order = me ^ jnp.arange(group_count, dtype=jnp.int32)
    kept = accepted[order][:, :, None] == jnp.arange(tree, dtype=jnp.int32)
    accepted_kv = jnp.einsum(
        "ran,rnd->rad",
        kept.astype(jnp.bfloat16),
        jnp.concatenate(fresh, axis=0),
        preferred_element_type=jnp.float32,
    ).astype(jnp.bfloat16)[order][:, None]

    expert_count = router.shape[1]
    top_count = routes.shape[2]
    capacity = 4 * tree * top_count // (3 * expert_count)
    plane = lax.axis_size(PLANE)
    line = lax.axis_size("z")
    near_experts = lax.axis_index("z") * plane + (
        lax.axis_index(PLANE) ^ jnp.arange(plane, dtype=jnp.int32)
    )
    line_rows = [payload] + [partner(payload, "z", k) for k in range(1, line)]
    beside = [partner(normed, "x", o) for o in range(1, side)]

    shared, beside = shared_terms(normed, beside, shared_weights)
    line_rows[3], beside = lax.optimization_barrier((line_rows[3], beside))

    sent = []
    spread = {}
    for ks in GROUPS:
        pieces, spreads = select(
            near_experts, router, [line_rows[k] for k in ks], plane, capacity, top_count
        )
        spread.update(zip(ks, spreads))
        sent.append([partner(pieces[o], PLANE, o) for o in range(plane)])
    parts = [partner(beside[o - 1], "x", o) for o in range(1, side)]
    made = None
    results = {}
    for ks, pieces in zip(GROUPS, sent):
        if made is not None:
            pieces, made, parts = lax.optimization_barrier((pieces, made, parts))
        made = experts(pieces, len(ks), inner, outer)
        results.update(zip(ks, made))
    totals = {}
    landed = {}
    for k, after, arrived in BACK:
        pieces = results[k]
        if after is not None:
            pieces, totals[after] = lax.optimization_barrier((pieces, totals[after]))
        if arrived is not None:
            pieces, landed[arrived] = lax.optimization_barrier((pieces, landed[arrived]))
        back = [partner(pieces[o], PLANE, o) for o in range(plane)]
        totals[k] = combine(spread[k], back, jnp.bfloat16 if k else jnp.float32)
        if k:
            landed[k] = partner(totals[k], "z", k)
    parts += list(landed.values())
    routed = totals[0]
    hidden_out = final(live[0][:, None], resid, shared, routed, parts)
    return (hidden_out[None], accepted_kv)


def solution(mesh):
    line = 4
    shape = (line, mesh.shape["req"] // line, mesh.shape["head"] // 2, 2)
    grid = Mesh(mesh.devices.reshape(shape), ALL)
    req = ("z", "y")
    in_specs = (
        P(ALL, None, None),
        P(ALL, None),
        P(req, None),
        P(req),
        P(req, None),
        P(ALL, None, None),
        P(req, HEAD, None, None),
        P(),
        P(None, HEAD),
        P(HEAD, None),
        P(),
        P(None, HEAD),
        P(None, HEAD),
        P(HEAD, None),
        P(),
        P(ALL, None, None),
        P(ALL, None, None),
    )
    out_specs = (P(ALL, None, None), P(req, HEAD, None, None))
    return jax.shard_map(body, mesh=grid, in_specs=in_specs, out_specs=out_specs, check_vma=False)
```

```python
import functools
import math

import jax
import jax.numpy as jnp
import numpy as np
from jax import lax
from jax.experimental import pallas as pl
from jax.experimental.pallas import tpu as pltpu
from jax.sharding import Mesh
from jax.sharding import PartitionSpec as P

EPSILON = 1e-06
ROPE_BASE = 10000.0
GROUPS = ((0, 3), (2, 1))
BACK = ((3, None, None), (2, None, None), (1, 3, None), (0, 2, 3))
CHUNK = 512
EXTRA = 128
SMALL = pl.CostEstimate(flops=1024, bytes_accessed=1024, transcendentals=0)
ALL = ("z", "y", "x", "c")
PLANE = ("y", "x")
HEAD = ("x", "c")


def partner(value, axes, offset):
    if offset == 0:
        return value
    size = lax.axis_size(axes)
    return lax.ppermute(value, axes, [(i, i ^ offset) for i in range(size)])


def dot(left, right):
    return jnp.dot(left, right, preferred_element_type=jnp.float32)


def prepare_kernel(lengths, parents, frequency, reach, cosine, sine):
    requests, tree = parents.shape
    row = lax.broadcasted_iota(jnp.int32, (tree, tree), 0)
    column = lax.broadcasted_iota(jnp.int32, (tree, tree), 1)
    places = column.astype(jnp.float32)
    known = parents[...].astype(jnp.float32)
    near = []
    for r in range(requests):
        spread = jnp.where(row == column, known[r : r + 1], 0.0)
        parent = jnp.sum(spread, axis=-1, keepdims=True)
        near.append(jnp.where((parent == places) | (row == column), 1.0, 0.0))
    for turn in range((tree - 1).bit_length()):
        for r in range(requests):
            step = near[r].astype(jnp.bfloat16)
            near[r] = jnp.minimum(dot(step, step), 1.0)
    half = cosine.shape[2] // 2
    lane = lax.broadcasted_iota(jnp.int32, cosine.shape[1:], 1)
    for r in range(requests):
        reach[r] = near[r]
        depth = jnp.sum(near[r], axis=-1, keepdims=True) - 1.0
        angle = (lengths[r].astype(jnp.float32) + depth) * frequency[...]
        cosine[r] = jnp.cos(angle)
        sines = jnp.sin(angle)
        sine[r] = jnp.where(lane < half, -sines, sines)


def prepare(lengths, parents, head_dim):
    requests, tree = parents.shape
    half = head_dim // 2
    frequency = ROPE_BASE ** (-np.arange(half, dtype=np.float64) / half)
    frequency = np.concatenate([frequency, frequency])[None].astype(np.float32)
    table = jax.ShapeDtypeStruct((requests, tree, head_dim), jnp.float32)
    return pl.pallas_call(
        prepare_kernel,
        in_specs=[in_smem(), in_vmem(), in_vmem()],
        out_specs=[in_vmem()] * 3,
        out_shape=[jax.ShapeDtypeStruct((requests, tree, tree), jnp.float32), table, table],
        compiler_params=pltpu.CompilerParams(vmem_limit_bytes=16 * 2**20),
        cost_estimate=SMALL,
        name="prepare",
    )(lengths, parents, frequency)


def attend_kernel(
    place, lengths, first, second, gain, weight, cosine, sine, reach, cache, outward, *rest, offset
):
    term, term_other = rest[0:2]
    fresh = rest[2:4]
    weight_here, cache_here, gain_here, outward_here, sems = rest[4:]
    tree = first.shape[0]
    width, columns = weight.shape
    head_dim = cosine.shape[2]
    group = columns // head_dim - 2
    deep = width // 2

    gain_copy = pltpu.make_async_copy(gain, gain_here, sems.at[0])
    weight_copies = [
        pltpu.make_async_copy(
            weight.at[pl.ds(i * deep, deep)], weight_here.at[pl.ds(i * deep, deep)], sems.at[1 + i]
        )
        for i in range(2)
    ]
    cache_copies = [
        pltpu.make_async_copy(
            cache.at[place[0] ^ (offset + i)], cache_here.at[i], sems.at[3 + i]
        )
        for i in range(2)
    ]
    outward_copy = pltpu.make_async_copy(outward, outward_here, sems.at[5])
    for copy in [gain_copy, *weight_copies]:
        copy.start()

    wide = jnp.concatenate([first[...], second[...]], axis=0).astype(jnp.float32)
    power = jnp.mean(wide * wide, axis=-1, keepdims=True)
    gain_copy.wait()
    normed = (wide * lax.rsqrt(power + EPSILON) * gain_here[...]).astype(jnp.bfloat16)
    weight_copies[0].wait()
    cache_copies[0].start()
    projected = dot(normed[:, :deep], weight_here[:deep])
    weight_copies[1].wait()
    cache_copies[1].start()
    projected = projected + dot(normed[:, deep:], weight_here[deep:])
    scale = 1.0 / math.sqrt(head_dim)
    results = []

    for i in range(2):
        own = projected[i * tree : (i + 1) * tree]
        request = place[0] ^ (offset + i)
        length = lengths[request]

        def rope(values):
            return values * cosine[request] + pltpu.roll(values, head_dim // 2, 1) * sine[request]

        def column(c):
            return own[:, c * head_dim : (c + 1) * head_dim]

        query = jnp.concatenate(
            [rope(column(h)).astype(jnp.bfloat16) for h in range(group)], axis=0
        )
        key_new = rope(column(group)).astype(jnp.bfloat16)
        value_new = column(group + 1).astype(jnp.bfloat16)
        fresh[i][:, :head_dim] = key_new
        fresh[i][:, head_dim:] = value_new

        def against(keys):
            return (
                lax.dot_general(
                    query, keys, (((1,), (1,)), ((), ())), preferred_element_type=jnp.float32
                )
                * scale
            )

        allowed = jnp.concatenate([reach[request]] * group, axis=0) > 0.5
        scores = jnp.where(allowed, against(key_new), -1e30)
        peak = jnp.max(scores, axis=-1, keepdims=True)
        weights = jnp.exp(scores - peak)
        total = jnp.sum(weights, axis=-1, keepdims=True)
        summed = dot(weights.astype(jnp.bfloat16), value_new)
        cache_copies[i].wait()
        if i == 0:
            outward_copy.start()

        def chunk(j, carry):
            peak, total, summed = carry
            block = pl.ds(pl.multiple_of(j * CHUNK, CHUNK), CHUNK)
            scores = against(cache_here[i, block, :head_dim])
            place = j * CHUNK + lax.broadcasted_iota(jnp.int32, scores.shape, 1)
            scores = jnp.where(place < length, scores, -1e30)
            higher = jnp.maximum(peak, jnp.max(scores, axis=-1, keepdims=True))
            fade = jnp.exp(peak - higher)
            weights = jnp.exp(scores - higher)
            total = total * fade + jnp.sum(weights, axis=-1, keepdims=True)
            values = cache_here[i, block, head_dim:]
            summed = summed * fade + dot(weights.astype(jnp.bfloat16), values)
            return (higher, total, summed)

        peak, total, summed = lax.fori_loop(
            0, lax.div(length + CHUNK - 1, CHUNK), chunk, (peak, total, summed)
        )
        result = (summed / total).astype(jnp.bfloat16)
        result = jnp.concatenate(
            [result[h * tree : (h + 1) * tree] for h in range(group)], axis=1
        )
        results.append(result)
    outward_copy.wait()
    terms = dot(jnp.concatenate(results, axis=0), outward_here[...])
    term[...] = terms[:tree]
    term_other[...] = terms[tree:].astype(jnp.bfloat16)


def in_vmem():
    return pl.BlockSpec(memory_space=pltpu.VMEM)


def in_smem():
    return pl.BlockSpec(memory_space=pltpu.SMEM)


def in_hbm():
    return pl.BlockSpec(memory_space=pltpu.HBM)


def attend(offset, place, lengths, first, second, gain, weight, cosine, sine, reach, cache, outward):
    tree, width = first.shape
    slots, pair = cache.shape[1:]
    head_dim = pair // 2
    columns = weight.shape[1]
    group_columns = columns - pair
    return pl.pallas_call(
        functools.partial(attend_kernel, offset=offset),
        in_specs=[
            in_smem(),
            in_smem(),
            in_vmem(),
            in_vmem(),
            in_hbm(),
            in_hbm(),
            in_vmem(),
            in_vmem(),
            in_vmem(),
            in_hbm(),
            in_hbm(),
        ],
        out_specs=[in_vmem()] * 4,
        out_shape=[
            jax.ShapeDtypeStruct((tree, width), jnp.float32),
            jax.ShapeDtypeStruct((tree, width), jnp.bfloat16),
        ]
        + [jax.ShapeDtypeStruct((tree, pair), jnp.bfloat16)] * 2,
        scratch_shapes=[
            pltpu.VMEM((width, columns), jnp.bfloat16),
            pltpu.VMEM((2, slots, pair), jnp.bfloat16),
            pltpu.VMEM((1, width), jnp.float32),
            pltpu.VMEM((group_columns, width), jnp.bfloat16),
            pltpu.SemaphoreType.DMA((6,)),
        ],
        compiler_params=pltpu.CompilerParams(vmem_limit_bytes=60 * 2**20),
        cost_estimate=SMALL,
        name="attend",
    )(place, lengths, first, second, gain, weight, cosine, sine, reach, cache, outward)


def add_kernel(left, right, out):
    total = left[...].astype(jnp.float32) + right[...].astype(jnp.float32)
    out[...] = total.astype(out.dtype)


def add(left, right, dtype):
    return pl.pallas_call(
        add_kernel,
        in_specs=[in_vmem()] * 2,
        out_specs=in_vmem(),
        out_shape=jax.ShapeDtypeStruct(left.shape, dtype),
        compiler_params=pltpu.CompilerParams(vmem_limit_bytes=16 * 2**20),
        cost_estimate=SMALL,
        name="add",
    )(left, right)


def silu(values):
    return values / (1.0 + jnp.exp(-values))


def expert_kernel(*refs, plane, count, deep):
    pieces = refs[:plane]
    weights = refs[plane : plane + 4]
    outs = refs[plane + 4 : plane + 4 + count * plane]
    rows, inner_a, outer_a, inner_b, outer_b, sems = refs[plane + 4 + count * plane :]
    each = pieces[0].shape[0]
    width = rows.shape[1]
    parts = width // deep
    copies = []
    for n, (inner, outer, inner_here, outer_here) in enumerate(
        ((weights[0], weights[1], inner_a, outer_a), (weights[2], weights[3], inner_b, outer_b))
    ):
        base = n * (parts + 1)
        for p in range(parts):
            block = pl.ds(p * deep, deep)
            copies.append(
                pltpu.make_async_copy(inner.at[block], inner_here.at[block], sems.at[base + p])
            )
        copies.append(pltpu.make_async_copy(outer, outer_here, sems.at[base + parts]))
    for copy in copies[:2]:
        copy.start()

    def take(number):
        copies[number].wait()
        if number + 2 < len(copies):
            copies[number + 2].start()

    for i in range(plane):
        rows[i * each : (i + 1) * each] = pieces[i][...]
    result = None
    for n, (inner_here, outer_here) in enumerate(((inner_a, outer_a), (inner_b, outer_b))):
        base = n * (parts + 1)
        both = None
        for p in range(parts):
            take(base + p)
            term = dot(rows[:, p * deep : (p + 1) * deep], inner_here[p * deep : (p + 1) * deep])
            both = term if both is None else both + term
        half = both.shape[1] // 2
        hidden = (silu(both[:, :half]) * both[:, half:]).astype(jnp.bfloat16)
        take(base + parts)
        term = dot(hidden, outer_here[...]).astype(jnp.bfloat16).astype(jnp.float32)
        result = term if result is None else result + term
    step = each // count
    for n in range(count * plane):
        base = (n % plane) * each + (n // plane) * step
        outs[n][...] = result[base : base + step].astype(jnp.bfloat16)


def experts(pieces, count, inner, outer):
    plane = len(pieces)
    each, width = pieces[0].shape
    hidden = inner[0].shape[1]
    deep = width // 2
    kernel = functools.partial(expert_kernel, plane=plane, count=count, deep=deep)
    weight_scratch = [
        pltpu.VMEM((width, hidden), jnp.bfloat16),
        pltpu.VMEM((hidden // 2, width), jnp.bfloat16),
    ]
    made = pl.pallas_call(
        kernel,
        in_specs=[in_vmem()] * plane + [in_hbm()] * 4,
        out_specs=[in_vmem()] * (count * plane),
        out_shape=[jax.ShapeDtypeStruct((each // count, width), jnp.bfloat16)] * (count * plane),
        scratch_shapes=[pltpu.VMEM((plane * each, width), jnp.bfloat16)]
        + weight_scratch * 2
        + [pltpu.SemaphoreType.DMA((2 * (width // deep + 1),))],
        compiler_params=pltpu.CompilerParams(vmem_limit_bytes=40 * 2**20),
        cost_estimate=SMALL,
        name="expert",
    )(*pieces, inner[0], outer[0], inner[1], outer[1])
    return [list(made[i * plane : (i + 1) * plane]) for i in range(count)]


def hold_kernel(*refs):
    refs[-1][...] = refs[0][...]


def hold(token, weights):
    return pl.pallas_call(
        hold_kernel,
        in_specs=[in_vmem()] + [in_hbm()] * len(weights),
        out_specs=in_vmem(),
        out_shape=jax.ShapeDtypeStruct(token.shape, token.dtype),
        compiler_params=pltpu.CompilerParams(vmem_limit_bytes=16 * 2**20),
        cost_estimate=SMALL,
        name="hold",
    )(token, *weights)


def shared_kernel(*refs, side):
    blocks = refs[:side]
    weights = refs[side : side + 6]
    outs = refs[side + 6 : 2 * side + 6]
    here, sems = refs[2 * side + 6 :]
    copies = [pltpu.make_async_copy(weights[i], here.at[i], sems.at[i]) for i in range(6)]
    for copy in copies[:2]:
        copy.start()

    def take(number):
        copies[number].wait()
        if number + 2 < len(copies):
            copies[number + 2].start()

    tree = blocks[0].shape[0]
    rows = jnp.concatenate([block[...] for block in blocks], axis=0).T

    def turned(i):
        take(i)
        return dot(here[i], rows)

    result = None
    for n in range(2):
        hidden = silu(turned(3 * n))
        hidden = (hidden * turned(3 * n + 1)).astype(jnp.bfloat16)
        take(3 * n + 2)
        term = lax.dot_general(
            hidden, here[3 * n + 2], (((0,), (0,)), ((), ())), preferred_element_type=jnp.float32
        )
        result = term if result is None else result + term
    for i in range(side):
        outs[i][...] = result[i * tree : (i + 1) * tree].astype(outs[i].dtype)


def shared_terms(own, beside, weights):
    tree, width = own.shape
    units = weights[0].shape[0]
    side = 1 + len(beside)
    outs = pl.pallas_call(
        functools.partial(shared_kernel, side=side),
        in_specs=[in_vmem()] * side + [in_hbm()] * 6,
        out_specs=[in_vmem()] * side,
        out_shape=[jax.ShapeDtypeStruct((tree, width), jnp.float32)]
        + [jax.ShapeDtypeStruct((tree, width), jnp.bfloat16)] * (side - 1),
        scratch_shapes=[
            pltpu.VMEM((6, units, width), jnp.bfloat16),
            pltpu.SemaphoreType.DMA((6,)),
        ],
        compiler_params=pltpu.CompilerParams(vmem_limit_bytes=60 * 2**20),
        cost_estimate=SMALL,
        name="shared",
    )(own, *beside, *weights)
    return outs[0], list(outs[1:])


def finish_kernel(tokens, term, gain, routes, *refs):
    others = refs[:-3]
    resid, normed, payload = refs[-3:]
    width = tokens.shape[1]
    attn = term[...]
    for other in others:
        attn = attn + other[...].astype(jnp.float32)
    rounded = (tokens[...].astype(jnp.float32) + attn).astype(jnp.bfloat16)
    resid[...] = rounded
    wide = rounded.astype(jnp.float32)
    power = jnp.mean(wide * wide, axis=-1, keepdims=True)
    rows = (wide * lax.rsqrt(power + EPSILON) * gain[...]).astype(jnp.bfloat16)
    normed[...] = rows
    payload[:, :width] = rows
    extra = payload.shape[1] - width
    lane = lax.broadcasted_iota(jnp.int32, (tokens.shape[0], extra), 1)
    numbers = jnp.zeros(lane.shape, jnp.float32)
    for t in range(routes.shape[1]):
        numbers = jnp.where(lane == t, routes[:, t : t + 1].astype(jnp.float32), numbers)
    payload[:, width:] = numbers.astype(jnp.bfloat16)


def finish(tokens, term, others, gain, routes):
    tree, width = tokens.shape
    return pl.pallas_call(
        finish_kernel,
        in_specs=[in_vmem()] * (4 + len(others)),
        out_specs=[in_vmem()] * 3,
        out_shape=[
            jax.ShapeDtypeStruct((tree, width), jnp.bfloat16),
            jax.ShapeDtypeStruct((tree, width), jnp.bfloat16),
            jax.ShapeDtypeStruct((tree, width + EXTRA), jnp.bfloat16),
        ],
        compiler_params=pltpu.CompilerParams(vmem_limit_bytes=16 * 2**20),
        cost_estimate=SMALL,
        name="finish",
    )(tokens, term, gain, routes, *others)


def select_kernel(*refs, count, plane, capacity, top_count):
    near = refs[0]
    router = refs[1]
    sources = refs[2 : 2 + count]
    outs = refs[2 + count : 2 + count + plane]
    spreads = refs[2 + count + plane :]
    width, expert_count = router.shape
    tree = sources[0].shape[0]
    lane = lax.broadcasted_iota(jnp.int32, (tree, plane * capacity), 1)
    place = lax.rem(lane, capacity).astype(jnp.float32)
    owner = lax.div(lane, capacity)
    expert = lax.broadcasted_iota(jnp.int32, (tree, expert_count), 1)
    row = lax.broadcasted_iota(jnp.int32, (tree, tree), 0)
    column = lax.broadcasted_iota(jnp.int32, (tree, tree), 1)
    before = jnp.where(column < row, 1.0, 0.0).astype(jnp.bfloat16)
    for i in range(count):
        rows = sources[i][:, :width]
        routes = sources[i][:, width:].astype(jnp.float32)
        member = jnp.zeros((tree, expert_count), jnp.float32)
        for t in range(top_count):
            named = routes[:, t : t + 1] == expert.astype(jnp.float32)
            member = jnp.where(named, 1.0, member)
        ranks = dot(before, member.astype(jnp.bfloat16))
        slots = jnp.where(member > 0.5, ranks, -1.0)
        logits = dot(rows, router[...])
        picked = member / (1.0 + jnp.exp(-logits))
        gates = picked / jnp.sum(picked, axis=-1, keepdims=True)
        slot = jnp.zeros(lane.shape, jnp.float32)
        gate = jnp.zeros(lane.shape, jnp.float32)
        for o in range(plane):
            mine = expert == near[o]
            slot_o = jnp.sum(jnp.where(mine, slots, 0.0), axis=-1, keepdims=True)
            gate_o = jnp.sum(jnp.where(mine, gates, 0.0), axis=-1, keepdims=True)
            slot = jnp.where(owner == o, slot_o, slot)
            gate = jnp.where(owner == o, gate_o, gate)
        pick = slot == place
        spreads[i][...] = jnp.where(pick, gate, 0.0).astype(jnp.bfloat16)
        chosen = lax.dot_general(
            jnp.where(pick, 1.0, 0.0).astype(jnp.bfloat16),
            rows,
            (((0,), (0,)), ((), ())),
            preferred_element_type=jnp.float32,
        ).astype(jnp.bfloat16)
        for o in range(plane):
            outs[o][i * capacity : (i + 1) * capacity] = chosen[o * capacity : (o + 1) * capacity]


def select(near, router, sources, plane, capacity, top_count):
    tree = sources[0].shape[0]
    width = router.shape[0]
    count = len(sources)
    made = pl.pallas_call(
        functools.partial(
            select_kernel, count=count, plane=plane, capacity=capacity, top_count=top_count
        ),
        in_specs=[in_smem()] + [in_vmem()] * (1 + count),
        out_specs=[in_vmem()] * (plane + count),
        out_shape=[jax.ShapeDtypeStruct((count * capacity, width), jnp.bfloat16)] * plane
        + [jax.ShapeDtypeStruct((tree, plane * capacity), jnp.bfloat16)] * count,
        compiler_params=pltpu.CompilerParams(vmem_limit_bytes=16 * 2**20),
        cost_estimate=SMALL,
        name="select",
    )(near, router, *sources)
    return list(made[:plane]), list(made[plane:])


def combine_kernel(spread, *refs):
    out = refs[-1]
    back = jnp.concatenate([piece[...] for piece in refs[:-1]], axis=0)
    out[...] = dot(spread[...], back).astype(out.dtype)


def combine(spread, pieces, dtype):
    tree = spread.shape[0]
    width = pieces[0].shape[1]
    return pl.pallas_call(
        combine_kernel,
        in_specs=[in_vmem()] * (1 + len(pieces)),
        out_specs=in_vmem(),
        out_shape=jax.ShapeDtypeStruct((tree, width), dtype),
        compiler_params=pltpu.CompilerParams(vmem_limit_bytes=16 * 2**20),
        cost_estimate=SMALL,
        name="combine",
    )(spread, *pieces)


def final_kernel(live, resid, shared, routed, *refs):
    total = resid[...].astype(jnp.float32) + shared[...] + routed[...]
    for part in refs[:-1]:
        total = total + part[...].astype(jnp.float32)
    refs[-1][...] = jnp.where(live[...] == 1, total, 0.0).astype(jnp.bfloat16)


def final(live, resid, shared, routed, parts):
    return pl.pallas_call(
        final_kernel,
        in_specs=[in_vmem()] * (4 + len(parts)),
        out_specs=in_vmem(),
        out_shape=jax.ShapeDtypeStruct(resid.shape, jnp.bfloat16),
        compiler_params=pltpu.CompilerParams(vmem_limit_bytes=16 * 2**20),
        cost_estimate=SMALL,
        name="final",
    )(live, resid, shared, routed, *parts)


def body(
    tokens,
    live,
    parents,
    lengths,
    accepted,
    routes,
    cache,
    attn_gain,
    w_qkv,
    w_out,
    ffn_gain,
    shared_gate,
    shared_up,
    shared_down,
    router,
    expert_in,
    expert_out,
):
    tree = tokens.shape[1]
    width = tokens.shape[2]
    own_rows = tokens[0]
    group_count = lax.axis_size(HEAD)
    head_dim = cache.shape[3] // 2
    me = lax.axis_index(HEAD)

    side = lax.axis_size("x")
    near = [own_rows] + [partner(own_rows, "x", o) for o in range(1, side)]
    near_core = [partner(own_rows, "c", 1)]

    reach, cosine, sine = prepare(lengths, parents, head_dim)
    place = me.astype(jnp.int32)[None]
    for o in range(1, side):
        near[o], cosine, sine, reach, place = lax.optimization_barrier(
            (near[o], cosine, sine, reach, place)
        )
        near_core.append(partner(near[o], "c", 1))

    gate_turned, up_turned = shared_gate.T, shared_up.T
    early, near_core[0] = lax.optimization_barrier(((gate_turned, expert_out[0]), near_core[0]))
    early = [partner(weight, "c", 1) for weight in early]
    middle, near_core = lax.optimization_barrier(
        ((up_turned, shared_down), near_core)
    )
    middle = [partner(weight, "c", 1) for weight in middle]
    near_core, early = lax.optimization_barrier((near_core, early))

    terms = [None] * side
    fresh = [None] * side
    follow = None
    late = expert_in[0]
    for o in reversed(range(side)):
        if follow is not None:
            near_core[o], follow = lax.optimization_barrier((near_core[o], follow))
        own_part, other_part, fresh_own, fresh_other = attend(
            2 * o,
            place,
            lengths,
            near[o],
            near_core[o],
            attn_gain[None],
            w_qkv,
            cosine,
            sine,
            reach,
            cache[:, 0],
            w_out,
        )
        fresh[o] = jnp.stack([fresh_own, fresh_other])
        other = partner(other_part, "c", 1)
        if o == side - 1:
            other, middle, late = lax.optimization_barrier((other, middle, late))
            late = partner(late, "c", 1)
        if o:
            follow = add(own_part, other, jnp.bfloat16)
            terms[o] = partner(follow, "x", o)
    own_term = own_part
    for o in range(1, side):
        own_term = add(own_term, terms[o], jnp.float32)
    own_term, late = lax.optimization_barrier((own_term, late))
    others = [other]
    resid, normed, payload = finish(own_rows, own_term, others, ffn_gain[None], routes[0])
    inner = [expert_in[0], late]
    outer = [expert_out[0], early[1]]
    shared_weights = [gate_turned, up_turned, shared_down, early[0], *middle]
    order = me ^ jnp.arange(group_count, dtype=jnp.int32)
    kept = accepted[order][:, :, None] == jnp.arange(tree, dtype=jnp.int32)
    accepted_kv = jnp.einsum(
        "ran,rnd->rad",
        kept.astype(jnp.bfloat16),
        jnp.concatenate(fresh, axis=0),
        preferred_element_type=jnp.float32,
    ).astype(jnp.bfloat16)[order][:, None]

    expert_count = router.shape[1]
    top_count = routes.shape[2]
    capacity = 4 * tree * top_count // (3 * expert_count)
    plane = lax.axis_size(PLANE)
    line = lax.axis_size("z")
    near_experts = lax.axis_index("z") * plane + (
        lax.axis_index(PLANE) ^ jnp.arange(plane, dtype=jnp.int32)
    )
    line_rows = [payload] + [partner(payload, "z", k) for k in range(1, line)]
    beside = [partner(normed, "x", o) for o in range(1, side)]

    shared, beside = shared_terms(normed, beside, shared_weights)
    line_rows[3], beside = lax.optimization_barrier((line_rows[3], beside))

    sent = []
    spread = {}
    for ks in GROUPS:
        pieces, spreads = select(
            near_experts, router, [line_rows[k] for k in ks], plane, capacity, top_count
        )
        spread.update(zip(ks, spreads))
        if len(sent) == 1:
            token = hold(spreads[0], [inner[0], outer[0], inner[1], outer[1]])
            sent[0], spread[ks[0]] = lax.optimization_barrier((sent[0], token))
        sent.append([partner(pieces[o], PLANE, o) for o in range(plane)])
    parts = [partner(beside[o - 1], "x", o) for o in range(1, side)]
    made = None
    results = {}
    for ks, pieces in zip(GROUPS, sent):
        if made is not None:
            pieces, made, parts = lax.optimization_barrier((pieces, made, parts))
        made = experts(pieces, len(ks), inner, outer)
        results.update(zip(ks, made))
    totals = {}
    landed = {}
    for k, after, arrived in BACK:
        pieces = results[k]
        if after is not None:
            pieces, totals[after] = lax.optimization_barrier((pieces, totals[after]))
        if arrived is not None:
            pieces, landed[arrived] = lax.optimization_barrier((pieces, landed[arrived]))
        back = [partner(pieces[o], PLANE, o) for o in range(plane)]
        totals[k] = combine(spread[k], back, jnp.bfloat16 if k else jnp.float32)
        if k:
            landed[k] = partner(totals[k], "z", k)
    parts += list(landed.values())
    routed = totals[0]
    hidden_out = final(live[0][:, None], resid, shared, routed, parts)
    return (hidden_out[None], accepted_kv)


def solution(mesh):
    line = 4
    shape = (line, mesh.shape["req"] // line, mesh.shape["head"] // 2, 2)
    grid = Mesh(mesh.devices.reshape(shape), ALL)
    req = ("z", "y")
    in_specs = (
        P(ALL, None, None),
        P(ALL, None),
        P(req, None),
        P(req),
        P(req, None),
        P(ALL, None, None),
        P(req, HEAD, None, None),
        P(),
        P(None, HEAD),
        P(HEAD, None),
        P(),
        P(None, HEAD),
        P(None, HEAD),
        P(HEAD, None),
        P(),
        P(ALL, None, None),
        P(ALL, None, None),
    )
    out_specs = (P(ALL, None, None), P(req, HEAD, None, None))
    return jax.shard_map(body, mesh=grid, in_specs=in_specs, out_specs=out_specs, check_vma=False)
```

```python
import functools
import math

import jax
import jax.numpy as jnp
import numpy as np
from jax import lax
from jax.experimental import pallas as pl
from jax.experimental.pallas import tpu as pltpu
from jax.sharding import Mesh
from jax.sharding import PartitionSpec as P

EPSILON = 1e-06
ROPE_BASE = 10000.0
GROUPS = ((0, 3), (2, 1))
BACK = ((3, None, None), (2, None, None), (1, 3, None), (0, 2, 3))
CHUNK = 512
EXTRA = 128
SMALL = pl.CostEstimate(flops=1024, bytes_accessed=1024, transcendentals=0)
ALL = ("z", "y", "x", "c")
PLANE = ("y", "x")
HEAD = ("x", "c")


def partner(value, axes, offset):
    if offset == 0:
        return value
    size = lax.axis_size(axes)
    return lax.ppermute(value, axes, [(i, i ^ offset) for i in range(size)])


def dot(left, right):
    return jnp.dot(left, right, preferred_element_type=jnp.float32)


def prepare_kernel(lengths, parents, frequency, reach, cosine, sine):
    requests, tree = parents.shape
    row = lax.broadcasted_iota(jnp.int32, (tree, tree), 0)
    column = lax.broadcasted_iota(jnp.int32, (tree, tree), 1)
    places = column.astype(jnp.float32)
    known = parents[...].astype(jnp.float32)
    near = []
    for r in range(requests):
        spread = jnp.where(row == column, known[r : r + 1], 0.0)
        parent = jnp.sum(spread, axis=-1, keepdims=True)
        near.append(jnp.where((parent == places) | (row == column), 1.0, 0.0))
    for turn in range((tree - 1).bit_length()):
        for r in range(requests):
            step = near[r].astype(jnp.bfloat16)
            near[r] = jnp.minimum(dot(step, step), 1.0)
    half = cosine.shape[2] // 2
    lane = lax.broadcasted_iota(jnp.int32, cosine.shape[1:], 1)
    for r in range(requests):
        reach[r] = near[r]
        depth = jnp.sum(near[r], axis=-1, keepdims=True) - 1.0
        angle = (lengths[r].astype(jnp.float32) + depth) * frequency[...]
        cosine[r] = jnp.cos(angle)
        sines = jnp.sin(angle)
        sine[r] = jnp.where(lane < half, -sines, sines)


def prepare(lengths, parents, head_dim):
    requests, tree = parents.shape
    half = head_dim // 2
    frequency = ROPE_BASE ** (-np.arange(half, dtype=np.float64) / half)
    frequency = np.concatenate([frequency, frequency])[None].astype(np.float32)
    table = jax.ShapeDtypeStruct((requests, tree, head_dim), jnp.float32)
    return pl.pallas_call(
        prepare_kernel,
        in_specs=[in_smem(), in_vmem(), in_vmem()],
        out_specs=[in_vmem()] * 3,
        out_shape=[jax.ShapeDtypeStruct((requests, tree, tree), jnp.float32), table, table],
        compiler_params=pltpu.CompilerParams(vmem_limit_bytes=16 * 2**20),
        cost_estimate=SMALL,
        name="prepare",
    )(lengths, parents, frequency)


def attend_kernel(
    place, lengths, first, second, gain, weight, cosine, sine, reach, cache, outward, *rest, offset
):
    term, term_other = rest[0:2]
    fresh = rest[2:4]
    weight_here, cache_here, gain_here, outward_here, sems = rest[4:]
    tree = first.shape[0]
    width, columns = weight.shape
    head_dim = cosine.shape[2]
    group = columns // head_dim - 2
    deep = width // 2

    gain_copy = pltpu.make_async_copy(gain, gain_here, sems.at[0])
    weight_copies = [
        pltpu.make_async_copy(
            weight.at[pl.ds(i * deep, deep)], weight_here.at[pl.ds(i * deep, deep)], sems.at[1 + i]
        )
        for i in range(2)
    ]
    cache_copies = [
        pltpu.make_async_copy(
            cache.at[place[0] ^ (offset + i)], cache_here.at[i], sems.at[3 + i]
        )
        for i in range(2)
    ]
    outward_copy = pltpu.make_async_copy(outward, outward_here, sems.at[5])
    for copy in [gain_copy, *weight_copies]:
        copy.start()

    wide = jnp.concatenate([first[...], second[...]], axis=0).astype(jnp.float32)
    power = jnp.mean(wide * wide, axis=-1, keepdims=True)
    gain_copy.wait()
    normed = (wide * lax.rsqrt(power + EPSILON) * gain_here[...]).astype(jnp.bfloat16)
    weight_copies[0].wait()
    cache_copies[0].start()
    projected = dot(normed[:, :deep], weight_here[:deep])
    weight_copies[1].wait()
    cache_copies[1].start()
    projected = projected + dot(normed[:, deep:], weight_here[deep:])
    scale = 1.0 / math.sqrt(head_dim)
    results = []

    for i in range(2):
        own = projected[i * tree : (i + 1) * tree]
        request = place[0] ^ (offset + i)
        length = lengths[request]

        def rope(values):
            return values * cosine[request] + pltpu.roll(values, head_dim // 2, 1) * sine[request]

        def column(c):
            return own[:, c * head_dim : (c + 1) * head_dim]

        query = jnp.concatenate(
            [rope(column(h)).astype(jnp.bfloat16) for h in range(group)], axis=0
        )
        key_new = rope(column(group)).astype(jnp.bfloat16)
        value_new = column(group + 1).astype(jnp.bfloat16)
        fresh[i][:, :head_dim] = key_new
        fresh[i][:, head_dim:] = value_new

        def against(keys):
            return (
                lax.dot_general(
                    query, keys, (((1,), (1,)), ((), ())), preferred_element_type=jnp.float32
                )
                * scale
            )

        allowed = jnp.concatenate([reach[request]] * group, axis=0) > 0.5
        scores = jnp.where(allowed, against(key_new), -1e30)
        peak = jnp.max(scores, axis=-1, keepdims=True)
        weights = jnp.exp(scores - peak)
        total = jnp.sum(weights, axis=-1, keepdims=True)
        summed = dot(weights.astype(jnp.bfloat16), value_new)
        cache_copies[i].wait()
        if i == 0:
            outward_copy.start()

        def chunk(j, carry):
            peak, total, summed = carry
            block = pl.ds(pl.multiple_of(j * CHUNK, CHUNK), CHUNK)
            scores = against(cache_here[i, block, :head_dim])
            place = j * CHUNK + lax.broadcasted_iota(jnp.int32, scores.shape, 1)
            scores = jnp.where(place < length, scores, -1e30)
            higher = jnp.maximum(peak, jnp.max(scores, axis=-1, keepdims=True))
            fade = jnp.exp(peak - higher)
            weights = jnp.exp(scores - higher)
            total = total * fade + jnp.sum(weights, axis=-1, keepdims=True)
            values = cache_here[i, block, head_dim:]
            summed = summed * fade + dot(weights.astype(jnp.bfloat16), values)
            return (higher, total, summed)

        peak, total, summed = lax.fori_loop(
            0, lax.div(length + CHUNK - 1, CHUNK), chunk, (peak, total, summed)
        )
        result = (summed / total).astype(jnp.bfloat16)
        result = jnp.concatenate(
            [result[h * tree : (h + 1) * tree] for h in range(group)], axis=1
        )
        results.append(result)
    outward_copy.wait()
    terms = dot(jnp.concatenate(results, axis=0), outward_here[...])
    term[...] = terms[:tree]
    term_other[...] = terms[tree:].astype(jnp.bfloat16)


def in_vmem():
    return pl.BlockSpec(memory_space=pltpu.VMEM)


def in_smem():
    return pl.BlockSpec(memory_space=pltpu.SMEM)


def in_hbm():
    return pl.BlockSpec(memory_space=pltpu.HBM)


def attend(offset, place, lengths, first, second, gain, weight, cosine, sine, reach, cache, outward):
    tree, width = first.shape
    slots, pair = cache.shape[1:]
    head_dim = pair // 2
    columns = weight.shape[1]
    group_columns = columns - pair
    return pl.pallas_call(
        functools.partial(attend_kernel, offset=offset),
        in_specs=[
            in_smem(),
            in_smem(),
            in_vmem(),
            in_vmem(),
            in_hbm(),
            in_hbm(),
            in_vmem(),
            in_vmem(),
            in_vmem(),
            in_hbm(),
            in_hbm(),
        ],
        out_specs=[in_vmem()] * 4,
        out_shape=[
            jax.ShapeDtypeStruct((tree, width), jnp.float32),
            jax.ShapeDtypeStruct((tree, width), jnp.bfloat16),
        ]
        + [jax.ShapeDtypeStruct((tree, pair), jnp.bfloat16)] * 2,
        scratch_shapes=[
            pltpu.VMEM((width, columns), jnp.bfloat16),
            pltpu.VMEM((2, slots, pair), jnp.bfloat16),
            pltpu.VMEM((1, width), jnp.float32),
            pltpu.VMEM((group_columns, width), jnp.bfloat16),
            pltpu.SemaphoreType.DMA((6,)),
        ],
        compiler_params=pltpu.CompilerParams(vmem_limit_bytes=60 * 2**20),
        cost_estimate=SMALL,
        name="attend",
    )(place, lengths, first, second, gain, weight, cosine, sine, reach, cache, outward)


def add_kernel(left, right, out):
    total = left[...].astype(jnp.float32) + right[...].astype(jnp.float32)
    out[...] = total.astype(out.dtype)


def add(left, right, dtype):
    return pl.pallas_call(
        add_kernel,
        in_specs=[in_vmem()] * 2,
        out_specs=in_vmem(),
        out_shape=jax.ShapeDtypeStruct(left.shape, dtype),
        compiler_params=pltpu.CompilerParams(vmem_limit_bytes=16 * 2**20),
        cost_estimate=SMALL,
        name="add",
    )(left, right)


def silu(values):
    return values / (1.0 + jnp.exp(-values))


def expert_kernel(*refs, plane, count, tiles):
    pieces = refs[:plane]
    weights = refs[plane : plane + 4]
    outs = refs[plane + 4 : plane + 4 + count * plane]
    rows, inner_a, outer_a, inner_b, outer_b, both, hidden, first, sems = refs[
        plane + 4 + count * plane :
    ]
    each = pieces[0].shape[0]
    parts = len(tiles)
    copies = []
    for inner, outer, inner_here, outer_here in (
        (weights[0], weights[1], inner_a, outer_a),
        (weights[2], weights[3], inner_b, outer_b),
    ):
        for start, size in tiles:
            block = pl.ds(start, size)
            number = len(copies)
            copies.append(
                pltpu.make_async_copy(inner.at[block], inner_here.at[block], sems.at[number])
            )
        copies.append(pltpu.make_async_copy(outer, outer_here, sems.at[len(copies)]))
    for copy in copies[:2]:
        copy.start()

    def take(number):
        copies[number].wait()
        if number + 2 < len(copies):
            copies[number + 2].start()

    for i in range(plane):
        rows[i * each : (i + 1) * each] = pieces[i][...]
    for n, (inner_here, outer_here) in enumerate(((inner_a, outer_a), (inner_b, outer_b))):
        base = n * (parts + 1)
        for p, (start, size) in enumerate(tiles):
            take(base + p)
            term = dot(rows[:, start : start + size], inner_here[start : start + size])
            both[...] = term if p == 0 else both[...] + term
        half = both.shape[1] // 2
        hidden[...] = (silu(both[:, :half]) * both[:, half:]).astype(jnp.bfloat16)
        take(base + parts)
        term = dot(hidden[...], outer_here[...]).astype(jnp.bfloat16)
        if n == 0:
            first[...] = term
    result = (first[...].astype(jnp.float32) + term.astype(jnp.float32)).astype(jnp.bfloat16)
    step = each // count
    for n in range(count * plane):
        base = (n % plane) * each + (n // plane) * step
        outs[n][...] = result[base : base + step]


def experts(pieces, count, inner, outer):
    plane = len(pieces)
    each, width = pieces[0].shape
    hidden = inner[0].shape[1]
    tiles = ((0, width // 2), (width // 2, width - width // 2))
    rows = plane * each
    weight_scratch = [
        pltpu.VMEM((width, hidden), jnp.bfloat16),
        pltpu.VMEM((hidden // 2, width), jnp.bfloat16),
    ]
    made = pl.pallas_call(
        functools.partial(expert_kernel, plane=plane, count=count, tiles=tiles),
        in_specs=[in_vmem()] * plane + [in_hbm()] * 4,
        out_specs=[in_vmem()] * (count * plane),
        out_shape=[jax.ShapeDtypeStruct((each // count, width), jnp.bfloat16)] * (count * plane),
        scratch_shapes=[pltpu.VMEM((rows, width), jnp.bfloat16)]
        + weight_scratch * 2
        + [
            pltpu.VMEM((rows, hidden), jnp.float32),
            pltpu.VMEM((rows, hidden // 2), jnp.bfloat16),
            pltpu.VMEM((rows, width), jnp.bfloat16),
            pltpu.SemaphoreType.DMA((2 * (len(tiles) + 1),)),
        ],
        compiler_params=pltpu.CompilerParams(vmem_limit_bytes=60 * 2**20),
        cost_estimate=SMALL,
        name="expert",
    )(*pieces, inner[0], outer[0], inner[1], outer[1])
    return [list(made[i * plane : (i + 1) * plane]) for i in range(count)]


def shared_kernel(*refs, side):
    blocks = refs[:side]
    weights = refs[side : side + 6]
    outs = refs[side + 6 : 2 * side + 6]
    here, sems = refs[2 * side + 6 :]
    copies = [pltpu.make_async_copy(weights[i], here.at[i], sems.at[i]) for i in range(6)]
    for copy in copies[:2]:
        copy.start()

    def take(number):
        copies[number].wait()
        if number + 2 < len(copies):
            copies[number + 2].start()

    tree = blocks[0].shape[0]
    rows = jnp.concatenate([block[...] for block in blocks], axis=0).T

    def turned(i):
        take(i)
        return dot(here[i], rows)

    result = None
    for n in range(2):
        hidden = silu(turned(3 * n))
        hidden = (hidden * turned(3 * n + 1)).astype(jnp.bfloat16)
        take(3 * n + 2)
        term = lax.dot_general(
            hidden, here[3 * n + 2], (((0,), (0,)), ((), ())), preferred_element_type=jnp.float32
        )
        result = term if result is None else result + term
    for i in range(side):
        outs[i][...] = result[i * tree : (i + 1) * tree].astype(outs[i].dtype)


def shared_terms(own, beside, weights):
    tree, width = own.shape
    units = weights[0].shape[0]
    side = 1 + len(beside)
    outs = pl.pallas_call(
        functools.partial(shared_kernel, side=side),
        in_specs=[in_vmem()] * side + [in_hbm()] * 6,
        out_specs=[in_vmem()] * side,
        out_shape=[jax.ShapeDtypeStruct((tree, width), jnp.float32)]
        + [jax.ShapeDtypeStruct((tree, width), jnp.bfloat16)] * (side - 1),
        scratch_shapes=[
            pltpu.VMEM((6, units, width), jnp.bfloat16),
            pltpu.SemaphoreType.DMA((6,)),
        ],
        compiler_params=pltpu.CompilerParams(vmem_limit_bytes=60 * 2**20),
        cost_estimate=SMALL,
        name="shared",
    )(own, *beside, *weights)
    return outs[0], list(outs[1:])


def finish_kernel(tokens, term, gain, routes, *refs):
    others = refs[:-3]
    resid, normed, payload = refs[-3:]
    width = tokens.shape[1]
    attn = term[...]
    for other in others:
        attn = attn + other[...].astype(jnp.float32)
    rounded = (tokens[...].astype(jnp.float32) + attn).astype(jnp.bfloat16)
    resid[...] = rounded
    wide = rounded.astype(jnp.float32)
    power = jnp.mean(wide * wide, axis=-1, keepdims=True)
    rows = (wide * lax.rsqrt(power + EPSILON) * gain[...]).astype(jnp.bfloat16)
    normed[...] = rows
    payload[:, :width] = rows
    extra = payload.shape[1] - width
    lane = lax.broadcasted_iota(jnp.int32, (tokens.shape[0], extra), 1)
    numbers = jnp.zeros(lane.shape, jnp.float32)
    for t in range(routes.shape[1]):
        numbers = jnp.where(lane == t, routes[:, t : t + 1].astype(jnp.float32), numbers)
    payload[:, width:] = numbers.astype(jnp.bfloat16)


def finish(tokens, term, others, gain, routes):
    tree, width = tokens.shape
    return pl.pallas_call(
        finish_kernel,
        in_specs=[in_vmem()] * (4 + len(others)),
        out_specs=[in_vmem()] * 3,
        out_shape=[
            jax.ShapeDtypeStruct((tree, width), jnp.bfloat16),
            jax.ShapeDtypeStruct((tree, width), jnp.bfloat16),
            jax.ShapeDtypeStruct((tree, width + EXTRA), jnp.bfloat16),
        ],
        compiler_params=pltpu.CompilerParams(vmem_limit_bytes=16 * 2**20),
        cost_estimate=SMALL,
        name="finish",
    )(tokens, term, gain, routes, *others)


def select_kernel(*refs, count, plane, capacity, top_count):
    near = refs[0]
    router = refs[1]
    sources = refs[2 : 2 + count]
    outs = refs[2 + count : 2 + count + plane]
    spreads = refs[2 + count + plane :]
    width, expert_count = router.shape
    tree = sources[0].shape[0]
    lane = lax.broadcasted_iota(jnp.int32, (tree, plane * capacity), 1)
    place = lax.rem(lane, capacity).astype(jnp.float32)
    owner = lax.div(lane, capacity)
    expert = lax.broadcasted_iota(jnp.int32, (tree, expert_count), 1)
    row = lax.broadcasted_iota(jnp.int32, (tree, tree), 0)
    column = lax.broadcasted_iota(jnp.int32, (tree, tree), 1)
    before = jnp.where(column < row, 1.0, 0.0).astype(jnp.bfloat16)
    for i in range(count):
        rows = sources[i][:, :width]
        routes = sources[i][:, width:].astype(jnp.float32)
        member = jnp.zeros((tree, expert_count), jnp.float32)
        for t in range(top_count):
            named = routes[:, t : t + 1] == expert.astype(jnp.float32)
            member = jnp.where(named, 1.0, member)
        ranks = dot(before, member.astype(jnp.bfloat16))
        slots = jnp.where(member > 0.5, ranks, -1.0)
        logits = dot(rows, router[...])
        picked = member / (1.0 + jnp.exp(-logits))
        gates = picked / jnp.sum(picked, axis=-1, keepdims=True)
        slot = jnp.zeros(lane.shape, jnp.float32)
        gate = jnp.zeros(lane.shape, jnp.float32)
        for o in range(plane):
            mine = expert == near[o]
            slot_o = jnp.sum(jnp.where(mine, slots, 0.0), axis=-1, keepdims=True)
            gate_o = jnp.sum(jnp.where(mine, gates, 0.0), axis=-1, keepdims=True)
            slot = jnp.where(owner == o, slot_o, slot)
            gate = jnp.where(owner == o, gate_o, gate)
        pick = slot == place
        spreads[i][...] = jnp.where(pick, gate, 0.0).astype(jnp.bfloat16)
        chosen = lax.dot_general(
            jnp.where(pick, 1.0, 0.0).astype(jnp.bfloat16),
            rows,
            (((0,), (0,)), ((), ())),
            preferred_element_type=jnp.float32,
        ).astype(jnp.bfloat16)
        for o in range(plane):
            outs[o][i * capacity : (i + 1) * capacity] = chosen[o * capacity : (o + 1) * capacity]


def select(near, router, sources, plane, capacity, top_count):
    tree = sources[0].shape[0]
    width = router.shape[0]
    count = len(sources)
    made = pl.pallas_call(
        functools.partial(
            select_kernel, count=count, plane=plane, capacity=capacity, top_count=top_count
        ),
        in_specs=[in_smem()] + [in_vmem()] * (1 + count),
        out_specs=[in_vmem()] * (plane + count),
        out_shape=[jax.ShapeDtypeStruct((count * capacity, width), jnp.bfloat16)] * plane
        + [jax.ShapeDtypeStruct((tree, plane * capacity), jnp.bfloat16)] * count,
        compiler_params=pltpu.CompilerParams(vmem_limit_bytes=16 * 2**20),
        cost_estimate=SMALL,
        name="select",
    )(near, router, *sources)
    return list(made[:plane]), list(made[plane:])


def combine_kernel(spread, *refs):
    out = refs[-1]
    back = jnp.concatenate([piece[...] for piece in refs[:-1]], axis=0)
    out[...] = dot(spread[...], back).astype(out.dtype)


def combine(spread, pieces, dtype):
    tree = spread.shape[0]
    width = pieces[0].shape[1]
    return pl.pallas_call(
        combine_kernel,
        in_specs=[in_vmem()] * (1 + len(pieces)),
        out_specs=in_vmem(),
        out_shape=jax.ShapeDtypeStruct((tree, width), dtype),
        compiler_params=pltpu.CompilerParams(vmem_limit_bytes=16 * 2**20),
        cost_estimate=SMALL,
        name="combine",
    )(spread, *pieces)


def final_kernel(live, resid, shared, routed, *refs):
    total = resid[...].astype(jnp.float32) + shared[...] + routed[...]
    for part in refs[:-1]:
        total = total + part[...].astype(jnp.float32)
    refs[-1][...] = jnp.where(live[...] == 1, total, 0.0).astype(jnp.bfloat16)


def final(live, resid, shared, routed, parts):
    return pl.pallas_call(
        final_kernel,
        in_specs=[in_vmem()] * (4 + len(parts)),
        out_specs=in_vmem(),
        out_shape=jax.ShapeDtypeStruct(resid.shape, jnp.bfloat16),
        compiler_params=pltpu.CompilerParams(vmem_limit_bytes=16 * 2**20),
        cost_estimate=SMALL,
        name="final",
    )(live, resid, shared, routed, *parts)


def body(
    tokens,
    live,
    parents,
    lengths,
    accepted,
    routes,
    cache,
    attn_gain,
    w_qkv,
    w_out,
    ffn_gain,
    shared_gate,
    shared_up,
    shared_down,
    router,
    expert_in,
    expert_out,
):
    tree = tokens.shape[1]
    width = tokens.shape[2]
    own_rows = tokens[0]
    group_count = lax.axis_size(HEAD)
    head_dim = cache.shape[3] // 2
    me = lax.axis_index(HEAD)

    side = lax.axis_size("x")
    near = [own_rows] + [partner(own_rows, "x", o) for o in range(1, side)]
    near_core = [partner(own_rows, "c", 1)]

    reach, cosine, sine = prepare(lengths, parents, head_dim)
    place = me.astype(jnp.int32)[None]
    for o in range(1, side):
        near[o], cosine, sine, reach, place = lax.optimization_barrier(
            (near[o], cosine, sine, reach, place)
        )
        near_core.append(partner(near[o], "c", 1))

    gate_turned, up_turned = shared_gate.T, shared_up.T
    early, near_core[0] = lax.optimization_barrier(((gate_turned, expert_out[0]), near_core[0]))
    early = [partner(weight, "c", 1) for weight in early]
    middle, near_core = lax.optimization_barrier(
        ((up_turned, shared_down), near_core)
    )
    middle = [partner(weight, "c", 1) for weight in middle]
    near_core, early = lax.optimization_barrier((near_core, early))

    terms = [None] * side
    fresh = [None] * side
    follow = None
    late = expert_in[0]
    for o in reversed(range(side)):
        if follow is not None:
            near_core[o], follow = lax.optimization_barrier((near_core[o], follow))
        own_part, other_part, fresh_own, fresh_other = attend(
            2 * o,
            place,
            lengths,
            near[o],
            near_core[o],
            attn_gain[None],
            w_qkv,
            cosine,
            sine,
            reach,
            cache[:, 0],
            w_out,
        )
        fresh[o] = jnp.stack([fresh_own, fresh_other])
        other = partner(other_part, "c", 1)
        if o == side - 1:
            other, middle, late = lax.optimization_barrier((other, middle, late))
            late = partner(late, "c", 1)
        if o:
            follow = add(own_part, other, jnp.bfloat16)
            terms[o] = partner(follow, "x", o)
    own_term = own_part
    for o in range(1, side):
        own_term = add(own_term, terms[o], jnp.float32)
    own_term, late = lax.optimization_barrier((own_term, late))
    others = [other]
    resid, normed, payload = finish(own_rows, own_term, others, ffn_gain[None], routes[0])
    inner = [expert_in[0], late]
    outer = [expert_out[0], early[1]]
    shared_weights = [gate_turned, up_turned, shared_down, early[0], *middle]
    order = me ^ jnp.arange(group_count, dtype=jnp.int32)
    kept = accepted[order][:, :, None] == jnp.arange(tree, dtype=jnp.int32)
    accepted_kv = jnp.einsum(
        "ran,rnd->rad",
        kept.astype(jnp.bfloat16),
        jnp.concatenate(fresh, axis=0),
        preferred_element_type=jnp.float32,
    ).astype(jnp.bfloat16)[order][:, None]

    expert_count = router.shape[1]
    top_count = routes.shape[2]
    capacity = 4 * tree * top_count // (3 * expert_count)
    plane = lax.axis_size(PLANE)
    line = lax.axis_size("z")
    near_experts = lax.axis_index("z") * plane + (
        lax.axis_index(PLANE) ^ jnp.arange(plane, dtype=jnp.int32)
    )
    beside = [partner(normed, "x", o) for o in range(1, side)]
    calm, beside = lax.optimization_barrier((payload, beside))
    line_rows = [payload] + [
        partner(payload if k in GROUPS[0] else calm, "z", k) for k in range(1, line)
    ]

    sent = []
    spread = {}
    for ks in GROUPS:
        pieces, spreads = select(
            near_experts, router, [line_rows[k] for k in ks], plane, capacity, top_count
        )
        spread.update(zip(ks, spreads))
        sent.append([partner(pieces[o], PLANE, o) for o in range(plane)])
        if len(sent) == 1:
            normed, spread[ks[0]] = lax.optimization_barrier((normed, spread[ks[0]]))
            shared, beside = shared_terms(
                normed, beside, [gate_turned, up_turned, shared_down, early[0], *middle]
            )
    parts = [partner(beside[o - 1], "x", o) for o in range(1, side)]
    made = None
    results = {}
    for ks, pieces in zip(GROUPS, sent):
        if made is not None:
            pieces, made, parts = lax.optimization_barrier((pieces, made, parts))
        made = experts(pieces, len(ks), inner, outer)
        results.update(zip(ks, made))
    totals = {}
    landed = {}
    for k, after, arrived in BACK:
        pieces = results[k]
        if after is not None:
            pieces, totals[after] = lax.optimization_barrier((pieces, totals[after]))
        if arrived is not None:
            pieces, landed[arrived] = lax.optimization_barrier((pieces, landed[arrived]))
        back = [partner(pieces[o], PLANE, o) for o in range(plane)]
        totals[k] = combine(spread[k], back, jnp.bfloat16 if k else jnp.float32)
        if k:
            landed[k] = partner(totals[k], "z", k)
    parts += list(landed.values())
    routed = totals[0]
    hidden_out = final(live[0][:, None], resid, shared, routed, parts)
    return (hidden_out[None], accepted_kv)


def solution(mesh):
    line = 4
    shape = (line, mesh.shape["req"] // line, mesh.shape["head"] // 2, 2)
    grid = Mesh(mesh.devices.reshape(shape), ALL)
    req = ("z", "y")
    in_specs = (
        P(ALL, None, None),
        P(ALL, None),
        P(req, None),
        P(req),
        P(req, None),
        P(ALL, None, None),
        P(req, HEAD, None, None),
        P(),
        P(None, HEAD),
        P(HEAD, None),
        P(),
        P(None, HEAD),
        P(None, HEAD),
        P(HEAD, None),
        P(),
        P(ALL, None, None),
        P(ALL, None, None),
    )
    out_specs = (P(ALL, None, None), P(req, HEAD, None, None))
    return jax.shard_map(body, mesh=grid, in_specs=in_specs, out_specs=out_specs, check_vma=False)
```

```python
import functools
import math

import jax
import jax.numpy as jnp
import numpy as np
from jax import lax
from jax.experimental import pallas as pl
from jax.experimental.pallas import tpu as pltpu
from jax.sharding import Mesh
from jax.sharding import PartitionSpec as P

EPSILON = 1e-06
ROPE_BASE = 10000.0
GROUPS = ((3,), (2, 1))
BACK = ((3, None, None), (2, None, None), (1, 3, None), (0, 2, 3))
CHUNK = 512
EXTRA = 128
SMALL = pl.CostEstimate(flops=1024, bytes_accessed=1024, transcendentals=0)
ALL = ("z", "y", "x", "c")
PLANE = ("y", "x")
HEAD = ("x", "c")


def partner(value, axes, offset):
    if offset == 0:
        return value
    size = lax.axis_size(axes)
    return lax.ppermute(value, axes, [(i, i ^ offset) for i in range(size)])


def dot(left, right):
    return jnp.dot(left, right, preferred_element_type=jnp.float32)


def prepare_kernel(lengths, parents, frequency, reach, cosine, sine):
    requests, tree = parents.shape
    row = lax.broadcasted_iota(jnp.int32, (tree, tree), 0)
    column = lax.broadcasted_iota(jnp.int32, (tree, tree), 1)
    places = column.astype(jnp.float32)
    known = parents[...].astype(jnp.float32)
    near = []
    for r in range(requests):
        spread = jnp.where(row == column, known[r : r + 1], 0.0)
        parent = jnp.sum(spread, axis=-1, keepdims=True)
        near.append(jnp.where((parent == places) | (row == column), 1.0, 0.0))
    for turn in range((tree - 1).bit_length()):
        for r in range(requests):
            step = near[r].astype(jnp.bfloat16)
            near[r] = jnp.minimum(dot(step, step), 1.0)
    half = cosine.shape[2] // 2
    lane = lax.broadcasted_iota(jnp.int32, cosine.shape[1:], 1)
    for r in range(requests):
        reach[r] = near[r]
        depth = jnp.sum(near[r], axis=-1, keepdims=True) - 1.0
        angle = (lengths[r].astype(jnp.float32) + depth) * frequency[...]
        cosine[r] = jnp.cos(angle)
        sines = jnp.sin(angle)
        sine[r] = jnp.where(lane < half, -sines, sines)


def prepare(lengths, parents, head_dim):
    requests, tree = parents.shape
    half = head_dim // 2
    frequency = ROPE_BASE ** (-np.arange(half, dtype=np.float64) / half)
    frequency = np.concatenate([frequency, frequency])[None].astype(np.float32)
    table = jax.ShapeDtypeStruct((requests, tree, head_dim), jnp.float32)
    return pl.pallas_call(
        prepare_kernel,
        in_specs=[in_smem(), in_vmem(), in_vmem()],
        out_specs=[in_vmem()] * 3,
        out_shape=[jax.ShapeDtypeStruct((requests, tree, tree), jnp.float32), table, table],
        compiler_params=pltpu.CompilerParams(vmem_limit_bytes=16 * 2**20),
        cost_estimate=SMALL,
        name="prepare",
    )(lengths, parents, frequency)


def attend_kernel(
    place, lengths, first, second, gain, weight, cosine, sine, reach, cache, outward, *rest, offset
):
    term, term_other = rest[0:2]
    fresh = rest[2:4]
    weight_here, cache_here, gain_here, outward_here, sems = rest[4:]
    tree = first.shape[0]
    width, columns = weight.shape
    head_dim = cosine.shape[2]
    group = columns // head_dim - 2
    deep = width // 2

    gain_copy = pltpu.make_async_copy(gain, gain_here, sems.at[0])
    weight_copies = [
        pltpu.make_async_copy(
            weight.at[pl.ds(i * deep, deep)], weight_here.at[pl.ds(i * deep, deep)], sems.at[1 + i]
        )
        for i in range(2)
    ]
    cache_copies = [
        pltpu.make_async_copy(
            cache.at[place[0] ^ (offset + i)], cache_here.at[i], sems.at[3 + i]
        )
        for i in range(2)
    ]
    outward_copy = pltpu.make_async_copy(outward, outward_here, sems.at[5])
    for copy in [gain_copy, *weight_copies]:
        copy.start()

    wide = jnp.concatenate([first[...], second[...]], axis=0).astype(jnp.float32)
    power = jnp.mean(wide * wide, axis=-1, keepdims=True)
    gain_copy.wait()
    normed = (wide * lax.rsqrt(power + EPSILON) * gain_here[...]).astype(jnp.bfloat16)
    weight_copies[0].wait()
    cache_copies[0].start()
    projected = dot(normed[:, :deep], weight_here[:deep])
    weight_copies[1].wait()
    cache_copies[1].start()
    projected = projected + dot(normed[:, deep:], weight_here[deep:])
    scale = 1.0 / math.sqrt(head_dim)
    results = []

    for i in range(2):
        own = projected[i * tree : (i + 1) * tree]
        request = place[0] ^ (offset + i)
        length = lengths[request]

        def rope(values):
            return values * cosine[request] + pltpu.roll(values, head_dim // 2, 1) * sine[request]

        def column(c):
            return own[:, c * head_dim : (c + 1) * head_dim]

        query = jnp.concatenate(
            [rope(column(h)).astype(jnp.bfloat16) for h in range(group)], axis=0
        )
        key_new = rope(column(group)).astype(jnp.bfloat16)
        value_new = column(group + 1).astype(jnp.bfloat16)
        fresh[i][:, :head_dim] = key_new
        fresh[i][:, head_dim:] = value_new

        def against(keys):
            return (
                lax.dot_general(
                    query, keys, (((1,), (1,)), ((), ())), preferred_element_type=jnp.float32
                )
                * scale
            )

        allowed = jnp.concatenate([reach[request]] * group, axis=0) > 0.5
        scores = jnp.where(allowed, against(key_new), -1e30)
        peak = jnp.max(scores, axis=-1, keepdims=True)
        weights = jnp.exp(scores - peak)
        total = jnp.sum(weights, axis=-1, keepdims=True)
        summed = dot(weights.astype(jnp.bfloat16), value_new)
        cache_copies[i].wait()
        if i == 0:
            outward_copy.start()

        def chunk(j, carry):
            peak, total, summed = carry
            block = pl.ds(pl.multiple_of(j * CHUNK, CHUNK), CHUNK)
            scores = against(cache_here[i, block, :head_dim])
            place = j * CHUNK + lax.broadcasted_iota(jnp.int32, scores.shape, 1)
            scores = jnp.where(place < length, scores, -1e30)
            higher = jnp.maximum(peak, jnp.max(scores, axis=-1, keepdims=True))
            fade = jnp.exp(peak - higher)
            weights = jnp.exp(scores - higher)
            total = total * fade + jnp.sum(weights, axis=-1, keepdims=True)
            values = cache_here[i, block, head_dim:]
            summed = summed * fade + dot(weights.astype(jnp.bfloat16), values)
            return (higher, total, summed)

        peak, total, summed = lax.fori_loop(
            0, lax.div(length + CHUNK - 1, CHUNK), chunk, (peak, total, summed)
        )
        result = (summed / total).astype(jnp.bfloat16)
        result = jnp.concatenate(
            [result[h * tree : (h + 1) * tree] for h in range(group)], axis=1
        )
        results.append(result)
    outward_copy.wait()
    terms = dot(jnp.concatenate(results, axis=0), outward_here[...])
    term[...] = terms[:tree]
    term_other[...] = terms[tree:].astype(jnp.bfloat16)


def in_vmem():
    return pl.BlockSpec(memory_space=pltpu.VMEM)


def in_smem():
    return pl.BlockSpec(memory_space=pltpu.SMEM)


def in_hbm():
    return pl.BlockSpec(memory_space=pltpu.HBM)


def attend(offset, place, lengths, first, second, gain, weight, cosine, sine, reach, cache, outward):
    tree, width = first.shape
    slots, pair = cache.shape[1:]
    head_dim = pair // 2
    columns = weight.shape[1]
    group_columns = columns - pair
    return pl.pallas_call(
        functools.partial(attend_kernel, offset=offset),
        in_specs=[
            in_smem(),
            in_smem(),
            in_vmem(),
            in_vmem(),
            in_hbm(),
            in_hbm(),
            in_vmem(),
            in_vmem(),
            in_vmem(),
            in_hbm(),
            in_hbm(),
        ],
        out_specs=[in_vmem()] * 4,
        out_shape=[
            jax.ShapeDtypeStruct((tree, width), jnp.float32),
            jax.ShapeDtypeStruct((tree, width), jnp.bfloat16),
        ]
        + [jax.ShapeDtypeStruct((tree, pair), jnp.bfloat16)] * 2,
        scratch_shapes=[
            pltpu.VMEM((width, columns), jnp.bfloat16),
            pltpu.VMEM((2, slots, pair), jnp.bfloat16),
            pltpu.VMEM((1, width), jnp.float32),
            pltpu.VMEM((group_columns, width), jnp.bfloat16),
            pltpu.SemaphoreType.DMA((6,)),
        ],
        compiler_params=pltpu.CompilerParams(vmem_limit_bytes=60 * 2**20),
        cost_estimate=SMALL,
        name="attend",
    )(place, lengths, first, second, gain, weight, cosine, sine, reach, cache, outward)


def add_kernel(left, right, out):
    total = left[...].astype(jnp.float32) + right[...].astype(jnp.float32)
    out[...] = total.astype(out.dtype)


def add(left, right, dtype):
    return pl.pallas_call(
        add_kernel,
        in_specs=[in_vmem()] * 2,
        out_specs=in_vmem(),
        out_shape=jax.ShapeDtypeStruct(left.shape, dtype),
        compiler_params=pltpu.CompilerParams(vmem_limit_bytes=16 * 2**20),
        cost_estimate=SMALL,
        name="add",
    )(left, right)


def silu(values):
    return values / (1.0 + jnp.exp(-values))


def expert_kernel(*refs, layout, count, deep):
    pieces = refs[:count]
    weights = refs[count : count + 4]
    outs = refs[count + 4 : count + 4 + len(layout)]
    rows, inner_a, outer_a, inner_b, outer_b, sems = refs[count + 4 + len(layout) :]
    width = rows.shape[1]
    parts = width // deep
    copies = []
    for n, (inner, outer, inner_here, outer_here) in enumerate(
        ((weights[0], weights[1], inner_a, outer_a), (weights[2], weights[3], inner_b, outer_b))
    ):
        base = n * (parts + 1)
        for p in range(parts):
            block = pl.ds(p * deep, deep)
            copies.append(
                pltpu.make_async_copy(inner.at[block], inner_here.at[block], sems.at[base + p])
            )
        copies.append(pltpu.make_async_copy(outer, outer_here, sems.at[base + parts]))
    for copy in copies[:2]:
        copy.start()

    def take(number):
        copies[number].wait()
        if number + 2 < len(copies):
            copies[number + 2].start()

    base = 0
    for piece in pieces:
        rows[base : base + piece.shape[0]] = piece[...]
        base += piece.shape[0]
    result = None
    for n, (inner_here, outer_here) in enumerate(((inner_a, outer_a), (inner_b, outer_b))):
        base = n * (parts + 1)
        both = None
        for p in range(parts):
            take(base + p)
            term = dot(rows[:, p * deep : (p + 1) * deep], inner_here[p * deep : (p + 1) * deep])
            both = term if both is None else both + term
        half = both.shape[1] // 2
        hidden = (silu(both[:, :half]) * both[:, half:]).astype(jnp.bfloat16)
        take(base + parts)
        term = dot(hidden, outer_here[...]).astype(jnp.bfloat16).astype(jnp.float32)
        result = term if result is None else result + term
    step = rows.shape[0] // len(layout)
    for n, place in enumerate(layout):
        outs[place][...] = result[n * step : (n + 1) * step].astype(jnp.bfloat16)


def experts(pieces, layout, plane, inner, outer):
    count = len(pieces)
    rows = sum(piece.shape[0] for piece in pieces)
    width = pieces[0].shape[1]
    hidden = inner[0].shape[1]
    deep = width // 2
    step = rows // len(layout)
    weight_scratch = [
        pltpu.VMEM((width, hidden), jnp.bfloat16),
        pltpu.VMEM((hidden // 2, width), jnp.bfloat16),
    ]
    made = pl.pallas_call(
        functools.partial(expert_kernel, layout=layout, count=count, deep=deep),
        in_specs=[in_vmem()] * count + [in_hbm()] * 4,
        out_specs=[in_vmem()] * len(layout),
        out_shape=[jax.ShapeDtypeStruct((step, width), jnp.bfloat16)] * len(layout),
        scratch_shapes=[pltpu.VMEM((rows, width), jnp.bfloat16)]
        + weight_scratch * 2
        + [pltpu.SemaphoreType.DMA((2 * (width // deep + 1),))],
        compiler_params=pltpu.CompilerParams(vmem_limit_bytes=40 * 2**20),
        cost_estimate=SMALL,
        name="expert",
    )(*pieces, inner[0], outer[0], inner[1], outer[1])
    return [list(made[i : i + plane]) for i in range(0, len(layout), plane)]


def shared_kernel(*refs, side):
    blocks = refs[:side]
    weights = refs[side : side + 6]
    outs = refs[side + 6 : 2 * side + 6]
    here, sems = refs[2 * side + 6 :]
    copies = [pltpu.make_async_copy(weights[i], here.at[i], sems.at[i]) for i in range(6)]
    for copy in copies[:2]:
        copy.start()

    def take(number):
        copies[number].wait()
        if number + 2 < len(copies):
            copies[number + 2].start()

    tree = blocks[0].shape[0]
    width = here.shape[2]
    rows = jnp.concatenate([block[:, :width] for block in blocks], axis=0).T

    def turned(i):
        take(i)
        return dot(here[i], rows)

    result = None
    for n in range(2):
        hidden = silu(turned(3 * n))
        hidden = (hidden * turned(3 * n + 1)).astype(jnp.bfloat16)
        take(3 * n + 2)
        term = lax.dot_general(
            hidden, here[3 * n + 2], (((0,), (0,)), ((), ())), preferred_element_type=jnp.float32
        )
        result = term if result is None else result + term
    for i in range(side):
        outs[i][...] = result[i * tree : (i + 1) * tree].astype(outs[i].dtype)


def shared_terms(own, beside, weights):
    tree = own.shape[0]
    units, width = weights[0].shape
    side = 1 + len(beside)
    outs = pl.pallas_call(
        functools.partial(shared_kernel, side=side),
        in_specs=[in_vmem()] * side + [in_hbm()] * 6,
        out_specs=[in_vmem()] * side,
        out_shape=[jax.ShapeDtypeStruct((tree, width), jnp.float32)]
        + [jax.ShapeDtypeStruct((tree, width), jnp.bfloat16)] * (side - 1),
        scratch_shapes=[
            pltpu.VMEM((6, units, width), jnp.bfloat16),
            pltpu.SemaphoreType.DMA((6,)),
        ],
        compiler_params=pltpu.CompilerParams(vmem_limit_bytes=60 * 2**20),
        cost_estimate=SMALL,
        name="shared",
    )(own, *beside, *weights)
    return outs[0], list(outs[1:])


def finish_kernel(tokens, term, gain, routes, *refs):
    others = refs[:-3]
    resid, normed, payload = refs[-3:]
    width = tokens.shape[1]
    attn = term[...]
    for other in others:
        attn = attn + other[...].astype(jnp.float32)
    rounded = (tokens[...].astype(jnp.float32) + attn).astype(jnp.bfloat16)
    resid[...] = rounded
    wide = rounded.astype(jnp.float32)
    power = jnp.mean(wide * wide, axis=-1, keepdims=True)
    rows = (wide * lax.rsqrt(power + EPSILON) * gain[...]).astype(jnp.bfloat16)
    normed[...] = rows
    payload[:, :width] = rows
    extra = payload.shape[1] - width
    lane = lax.broadcasted_iota(jnp.int32, (tokens.shape[0], extra), 1)
    numbers = jnp.zeros(lane.shape, jnp.float32)
    for t in range(routes.shape[1]):
        numbers = jnp.where(lane == t, routes[:, t : t + 1].astype(jnp.float32), numbers)
    payload[:, width:] = numbers.astype(jnp.bfloat16)


def finish(tokens, term, others, gain, routes):
    tree, width = tokens.shape
    return pl.pallas_call(
        finish_kernel,
        in_specs=[in_vmem()] * (4 + len(others)),
        out_specs=[in_vmem()] * 3,
        out_shape=[
            jax.ShapeDtypeStruct((tree, width), jnp.bfloat16),
            jax.ShapeDtypeStruct((tree, width), jnp.bfloat16),
            jax.ShapeDtypeStruct((tree, width + EXTRA), jnp.bfloat16),
        ],
        compiler_params=pltpu.CompilerParams(vmem_limit_bytes=16 * 2**20),
        cost_estimate=SMALL,
        name="finish",
    )(tokens, term, gain, routes, *others)


def select_kernel(*refs, count, plane, capacity, top_count):
    near = refs[0]
    router = refs[1]
    sources = refs[2 : 2 + count]
    outs = refs[2 + count : 2 + count + plane]
    spreads = refs[2 + count + plane :]
    width, expert_count = router.shape
    tree = sources[0].shape[0]
    lane = lax.broadcasted_iota(jnp.int32, (tree, plane * capacity), 1)
    place = lax.rem(lane, capacity).astype(jnp.float32)
    owner = lax.div(lane, capacity)
    expert = lax.broadcasted_iota(jnp.int32, (tree, expert_count), 1)
    row = lax.broadcasted_iota(jnp.int32, (tree, tree), 0)
    column = lax.broadcasted_iota(jnp.int32, (tree, tree), 1)
    before = jnp.where(column < row, 1.0, 0.0).astype(jnp.bfloat16)
    for i in range(count):
        rows = sources[i][:, :width]
        routes = sources[i][:, width:].astype(jnp.float32)
        member = jnp.zeros((tree, expert_count), jnp.float32)
        for t in range(top_count):
            named = routes[:, t : t + 1] == expert.astype(jnp.float32)
            member = jnp.where(named, 1.0, member)
        ranks = dot(before, member.astype(jnp.bfloat16))
        slots = jnp.where(member > 0.5, ranks, -1.0)
        logits = dot(rows, router[...])
        picked = member / (1.0 + jnp.exp(-logits))
        gates = picked / jnp.sum(picked, axis=-1, keepdims=True)
        slot = jnp.zeros(lane.shape, jnp.float32)
        gate = jnp.zeros(lane.shape, jnp.float32)
        for o in range(plane):
            mine = expert == near[o]
            slot_o = jnp.sum(jnp.where(mine, slots, 0.0), axis=-1, keepdims=True)
            gate_o = jnp.sum(jnp.where(mine, gates, 0.0), axis=-1, keepdims=True)
            slot = jnp.where(owner == o, slot_o, slot)
            gate = jnp.where(owner == o, gate_o, gate)
        pick = slot == place
        spreads[i][...] = jnp.where(pick, gate, 0.0).astype(jnp.bfloat16)
        chosen = lax.dot_general(
            jnp.where(pick, 1.0, 0.0).astype(jnp.bfloat16),
            rows,
            (((0,), (0,)), ((), ())),
            preferred_element_type=jnp.float32,
        ).astype(jnp.bfloat16)
        for o in range(plane):
            outs[o][i * capacity : (i + 1) * capacity] = chosen[o * capacity : (o + 1) * capacity]


def select(near, router, sources, plane, capacity, top_count):
    tree = sources[0].shape[0]
    width = router.shape[0]
    count = len(sources)
    made = pl.pallas_call(
        functools.partial(
            select_kernel, count=count, plane=plane, capacity=capacity, top_count=top_count
        ),
        in_specs=[in_smem()] + [in_vmem()] * (1 + count),
        out_specs=[in_vmem()] * (plane + count),
        out_shape=[jax.ShapeDtypeStruct((count * capacity, width), jnp.bfloat16)] * plane
        + [jax.ShapeDtypeStruct((tree, plane * capacity), jnp.bfloat16)] * count,
        compiler_params=pltpu.CompilerParams(vmem_limit_bytes=16 * 2**20),
        cost_estimate=SMALL,
        name="select",
    )(near, router, *sources)
    return list(made[:plane]), list(made[plane:])


def combine_kernel(spread, *refs):
    out = refs[-1]
    back = jnp.concatenate([piece[...] for piece in refs[:-1]], axis=0)
    out[...] = dot(spread[...], back).astype(out.dtype)


def combine(spread, pieces, dtype):
    tree = spread.shape[0]
    width = pieces[0].shape[1]
    return pl.pallas_call(
        combine_kernel,
        in_specs=[in_vmem()] * (1 + len(pieces)),
        out_specs=in_vmem(),
        out_shape=jax.ShapeDtypeStruct((tree, width), dtype),
        compiler_params=pltpu.CompilerParams(vmem_limit_bytes=16 * 2**20),
        cost_estimate=SMALL,
        name="combine",
    )(spread, *pieces)


def final_kernel(live, resid, shared, routed, *refs):
    total = resid[...].astype(jnp.float32) + shared[...] + routed[...]
    for part in refs[:-1]:
        total = total + part[...].astype(jnp.float32)
    refs[-1][...] = jnp.where(live[...] == 1, total, 0.0).astype(jnp.bfloat16)


def final(live, resid, shared, routed, parts):
    return pl.pallas_call(
        final_kernel,
        in_specs=[in_vmem()] * (4 + len(parts)),
        out_specs=in_vmem(),
        out_shape=jax.ShapeDtypeStruct(resid.shape, jnp.bfloat16),
        compiler_params=pltpu.CompilerParams(vmem_limit_bytes=16 * 2**20),
        cost_estimate=SMALL,
        name="final",
    )(live, resid, shared, routed, *parts)


def body(
    tokens,
    live,
    parents,
    lengths,
    accepted,
    routes,
    cache,
    attn_gain,
    w_qkv,
    w_out,
    ffn_gain,
    shared_gate,
    shared_up,
    shared_down,
    router,
    expert_in,
    expert_out,
):
    tree = tokens.shape[1]
    width = tokens.shape[2]
    own_rows = tokens[0]
    group_count = lax.axis_size(HEAD)
    head_dim = cache.shape[3] // 2
    me = lax.axis_index(HEAD)

    side = lax.axis_size("x")
    near = [own_rows] + [partner(own_rows, "x", o) for o in range(1, side)]
    near_core = [partner(own_rows, "c", 1)]

    reach, cosine, sine = prepare(lengths, parents, head_dim)
    place = me.astype(jnp.int32)[None]
    for o in range(1, side):
        near[o], cosine, sine, reach, place = lax.optimization_barrier(
            (near[o], cosine, sine, reach, place)
        )
        near_core.append(partner(near[o], "c", 1))

    gate_turned, up_turned = shared_gate.T, shared_up.T
    early, near_core[0] = lax.optimization_barrier(((gate_turned, expert_out[0]), near_core[0]))
    early = [partner(weight, "c", 1) for weight in early]
    middle, near_core = lax.optimization_barrier(
        ((up_turned, shared_down), near_core)
    )
    middle = [partner(weight, "c", 1) for weight in middle]
    near_core, early = lax.optimization_barrier((near_core, early))

    terms = [None] * side
    fresh = [None] * side
    follow = None
    late = expert_in[0]
    for o in reversed(range(side)):
        if follow is not None:
            near_core[o], follow = lax.optimization_barrier((near_core[o], follow))
        own_part, other_part, fresh_own, fresh_other = attend(
            2 * o,
            place,
            lengths,
            near[o],
            near_core[o],
            attn_gain[None],
            w_qkv,
            cosine,
            sine,
            reach,
            cache[:, 0],
            w_out,
        )
        fresh[o] = jnp.stack([fresh_own, fresh_other])
        other = partner(other_part, "c", 1)
        if o == side - 1:
            other, middle, late = lax.optimization_barrier((other, middle, late))
            late = partner(late, "c", 1)
        if o:
            follow = add(own_part, other, jnp.bfloat16)
            terms[o] = partner(follow, "x", o)
    own_term = own_part
    for o in range(1, side):
        own_term = add(own_term, terms[o], jnp.float32)
    own_term, late = lax.optimization_barrier((own_term, late))
    others = [other]
    resid, normed, payload = finish(own_rows, own_term, others, ffn_gain[None], routes[0])
    inner = [expert_in[0], late]
    outer = [expert_out[0], early[1]]
    shared_weights = [gate_turned, up_turned, shared_down, early[0], *middle]
    order = me ^ jnp.arange(group_count, dtype=jnp.int32)
    kept = accepted[order][:, :, None] == jnp.arange(tree, dtype=jnp.int32)
    accepted_kv = jnp.einsum(
        "ran,rnd->rad",
        kept.astype(jnp.bfloat16),
        jnp.concatenate(fresh, axis=0),
        preferred_element_type=jnp.float32,
    ).astype(jnp.bfloat16)[order][:, None]

    expert_count = router.shape[1]
    top_count = routes.shape[2]
    capacity = 4 * tree * top_count // (3 * expert_count)
    plane = lax.axis_size(PLANE)
    line = lax.axis_size("z")
    near_experts = lax.axis_index("z") * plane + (
        lax.axis_index(PLANE) ^ jnp.arange(plane, dtype=jnp.int32)
    )
    line_rows = [payload] + [partner(payload, "z", k) for k in range(1, line)]
    beside = [partner(payload, "x", o) for o in range(1, side)]

    spread = {}

    def choose(ks, sources, experts_near, count):
        return select(experts_near, router, sources, count, capacity, top_count)

    first_pieces, spreads = choose((0,), [payload], near_experts, plane)
    spread[0] = spreads[0]
    first_pieces, beside = lax.optimization_barrier((first_pieces, beside))
    local, unused = choose((0,), [payload, *beside], near_experts[:1], 1)
    first = local + [partner(first_pieces[o], PLANE, o) for o in range(side, plane)]

    shared, beside = shared_terms(
        normed, beside, [gate_turned, up_turned, shared_down, early[0], *middle]
    )
    line_rows[3], beside, first = lax.optimization_barrier((line_rows[3], beside, first))

    sent = []
    layouts = []
    for ks in GROUPS:
        pieces, spreads = choose(ks, [line_rows[k] for k in ks], near_experts, plane)
        spread.update(zip(ks, spreads))
        if sent:
            pieces[-1], sent[0][-plane + 1] = lax.optimization_barrier(
                (pieces[-1], sent[0][-plane + 1])
            )
        moved = [partner(pieces[o], PLANE, o) for o in range(plane)]
        layout = [i * plane + o for o in range(plane) for i in range(len(ks))]
        if not sent:
            moved = first + moved
            layout = list(range(plane)) + [plane + place for place in layout]
        sent.append(moved)
        layouts.append(layout)

    beside, sent[0] = lax.optimization_barrier((beside, sent[0]))
    parts = [partner(beside[o - 1], "x", o) for o in range(1, side)]
    made = None
    results = {}
    for ks, pieces, layout in zip(GROUPS, sent, layouts):
        if made is not None:
            pieces, made, parts = lax.optimization_barrier((pieces, made, parts))
        made = experts(pieces, layout, plane, inner, outer)
        results.update(zip(ks if results else (0, *ks), made))
    totals = {}
    landed = {}
    for k, after, arrived in BACK:
        pieces = results[k]
        if after is not None:
            pieces, totals[after] = lax.optimization_barrier((pieces, totals[after]))
        if arrived is not None:
            pieces, landed[arrived] = lax.optimization_barrier((pieces, landed[arrived]))
        back = [partner(pieces[o], PLANE, o) for o in range(plane)]
        totals[k] = combine(spread[k], back, jnp.bfloat16 if k else jnp.float32)
        if k:
            landed[k] = partner(totals[k], "z", k)
    parts += list(landed.values())
    routed = totals[0]
    hidden_out = final(live[0][:, None], resid, shared, routed, parts)
    return (hidden_out[None], accepted_kv)


def solution(mesh):
    line = 4
    shape = (line, mesh.shape["req"] // line, mesh.shape["head"] // 2, 2)
    grid = Mesh(mesh.devices.reshape(shape), ALL)
    req = ("z", "y")
    in_specs = (
        P(ALL, None, None),
        P(ALL, None),
        P(req, None),
        P(req),
        P(req, None),
        P(ALL, None, None),
        P(req, HEAD, None, None),
        P(),
        P(None, HEAD),
        P(HEAD, None),
        P(),
        P(None, HEAD),
        P(None, HEAD),
        P(HEAD, None),
        P(),
        P(ALL, None, None),
        P(ALL, None, None),
    )
    out_specs = (P(ALL, None, None), P(req, HEAD, None, None))
    return jax.shard_map(body, mesh=grid, in_specs=in_specs, out_specs=out_specs, check_vma=False)
```

```python
import functools
import math

import jax
import jax.numpy as jnp
import numpy as np
from jax import lax
from jax.experimental import pallas as pl
from jax.experimental.pallas import tpu as pltpu
from jax.sharding import Mesh
from jax.sharding import PartitionSpec as P

EPSILON = 1e-06
ROPE_BASE = 10000.0
GROUPS = ((0, 3), (2, 1))
BACK = ((3, None, None), (2, None, None), (1, 3, None), (0, 2, 3))
CHUNK = 512
EXTRA = 128
SMALL = pl.CostEstimate(flops=1024, bytes_accessed=1024, transcendentals=0)
ALL = ("z", "y", "x", "c")
PLANE = ("y", "x")
HEAD = ("x", "c")


def partner(value, axes, offset):
    if offset == 0:
        return value
    size = lax.axis_size(axes)
    return lax.ppermute(value, axes, [(i, i ^ offset) for i in range(size)])


def dot(left, right):
    return jnp.dot(left, right, preferred_element_type=jnp.float32)


def prepare_kernel(lengths, parents, frequency, reach, cosine, sine):
    requests, tree = parents.shape
    row = lax.broadcasted_iota(jnp.int32, (tree, tree), 0)
    column = lax.broadcasted_iota(jnp.int32, (tree, tree), 1)
    places = column.astype(jnp.float32)
    known = parents[...].astype(jnp.float32)
    near = []
    for r in range(requests):
        spread = jnp.where(row == column, known[r : r + 1], 0.0)
        parent = jnp.sum(spread, axis=-1, keepdims=True)
        near.append(jnp.where((parent == places) | (row == column), 1.0, 0.0))
    for turn in range((tree - 1).bit_length()):
        for r in range(requests):
            step = near[r].astype(jnp.bfloat16)
            near[r] = jnp.minimum(dot(step, step), 1.0)
    half = cosine.shape[2] // 2
    lane = lax.broadcasted_iota(jnp.int32, cosine.shape[1:], 1)
    for r in range(requests):
        reach[r] = near[r]
        depth = jnp.sum(near[r], axis=-1, keepdims=True) - 1.0
        angle = (lengths[r].astype(jnp.float32) + depth) * frequency[...]
        cosine[r] = jnp.cos(angle)
        sines = jnp.sin(angle)
        sine[r] = jnp.where(lane < half, -sines, sines)


def prepare(lengths, parents, head_dim):
    requests, tree = parents.shape
    half = head_dim // 2
    frequency = ROPE_BASE ** (-np.arange(half, dtype=np.float64) / half)
    frequency = np.concatenate([frequency, frequency])[None].astype(np.float32)
    table = jax.ShapeDtypeStruct((requests, tree, head_dim), jnp.float32)
    return pl.pallas_call(
        prepare_kernel,
        in_specs=[in_smem(), in_vmem(), in_vmem()],
        out_specs=[in_vmem()] * 3,
        out_shape=[jax.ShapeDtypeStruct((requests, tree, tree), jnp.float32), table, table],
        compiler_params=pltpu.CompilerParams(vmem_limit_bytes=16 * 2**20),
        cost_estimate=SMALL,
        name="prepare",
    )(lengths, parents, frequency)


def attend_kernel(
    place, lengths, first, second, gain, weight, cosine, sine, reach, cache, outward, *rest, offset
):
    term, term_other = rest[0:2]
    fresh = rest[2:4]
    weight_here, cache_here, gain_here, outward_here, sems = rest[4:]
    tree = first.shape[0]
    width, columns = weight.shape
    head_dim = cosine.shape[2]
    group = columns // head_dim - 2
    deep = width // 2

    gain_copy = pltpu.make_async_copy(gain, gain_here, sems.at[0])
    weight_copies = [
        pltpu.make_async_copy(
            weight.at[pl.ds(i * deep, deep)], weight_here.at[pl.ds(i * deep, deep)], sems.at[1 + i]
        )
        for i in range(2)
    ]
    cache_copies = [
        pltpu.make_async_copy(
            cache.at[place[0] ^ (offset + i)], cache_here.at[i], sems.at[3 + i]
        )
        for i in range(2)
    ]
    outward_copy = pltpu.make_async_copy(outward, outward_here, sems.at[5])
    for copy in [gain_copy, *weight_copies]:
        copy.start()

    wide = jnp.concatenate([first[...], second[...]], axis=0).astype(jnp.float32)
    power = jnp.mean(wide * wide, axis=-1, keepdims=True)
    gain_copy.wait()
    normed = (wide * lax.rsqrt(power + EPSILON) * gain_here[...]).astype(jnp.bfloat16)
    weight_copies[0].wait()
    cache_copies[0].start()
    projected = dot(normed[:, :deep], weight_here[:deep])
    weight_copies[1].wait()
    cache_copies[1].start()
    projected = projected + dot(normed[:, deep:], weight_here[deep:])
    scale = 1.0 / math.sqrt(head_dim)
    outward_copy.start()

    def rope(values, request):
        return values * cosine[request] + pltpu.roll(values, head_dim // 2, 1) * sine[request]

    def against(query, keys):
        return (
            lax.dot_general(
                query, keys, (((1,), (1,)), ((), ())), preferred_element_type=jnp.float32
            )
            * scale
        )

    requests = [place[0] ^ (offset + i) for i in range(2)]
    bounds = [lengths[request] for request in requests]
    queries = []
    states = []
    for i, request in enumerate(requests):
        own = projected[i * tree : (i + 1) * tree]
        columns_of = [own[:, c * head_dim : (c + 1) * head_dim] for c in range(group + 2)]
        query = jnp.concatenate(
            [rope(columns_of[h], request).astype(jnp.bfloat16) for h in range(group)], axis=0
        )
        key_new = rope(columns_of[group], request).astype(jnp.bfloat16)
        value_new = columns_of[group + 1].astype(jnp.bfloat16)
        fresh[i][:, :head_dim] = key_new
        fresh[i][:, head_dim:] = value_new
        allowed = jnp.concatenate([reach[request]] * group, axis=0) > 0.5
        scores = jnp.where(allowed, against(query, key_new), -1e30)
        peak = jnp.max(scores, axis=-1, keepdims=True)
        weights = jnp.exp(scores - peak)
        total = jnp.sum(weights, axis=-1, keepdims=True)
        summed = dot(weights.astype(jnp.bfloat16), value_new)
        queries.append(query)
        states.append((peak, total, summed))
    for copy in cache_copies:
        copy.wait()

    def chunk(j, states):
        block = pl.ds(pl.multiple_of(j * CHUNK, CHUNK), CHUNK)
        later = []
        for i, (peak, total, summed) in enumerate(states):
            scores = against(queries[i], cache_here[i, block, :head_dim])
            slot = j * CHUNK + lax.broadcasted_iota(jnp.int32, scores.shape, 1)
            scores = jnp.where(slot < bounds[i], scores, -1e30)
            higher = jnp.maximum(peak, jnp.max(scores, axis=-1, keepdims=True))
            fade = jnp.exp(peak - higher)
            weights = jnp.exp(scores - higher)
            total = total * fade + jnp.sum(weights, axis=-1, keepdims=True)
            values = cache_here[i, block, head_dim:]
            summed = summed * fade + dot(weights.astype(jnp.bfloat16), values)
            later.append((higher, total, summed))
        return tuple(later)

    longest = jnp.maximum(bounds[0], bounds[1])
    states = lax.fori_loop(0, lax.div(longest + CHUNK - 1, CHUNK), chunk, tuple(states))
    results = []
    for peak, total, summed in states:
        result = (summed / total).astype(jnp.bfloat16)
        results.append(
            jnp.concatenate([result[h * tree : (h + 1) * tree] for h in range(group)], axis=1)
        )
    outward_copy.wait()
    terms = dot(jnp.concatenate(results, axis=0), outward_here[...])
    term[...] = terms[:tree]
    term_other[...] = terms[tree:].astype(jnp.bfloat16)


def in_vmem():
    return pl.BlockSpec(memory_space=pltpu.VMEM)


def in_smem():
    return pl.BlockSpec(memory_space=pltpu.SMEM)


def in_hbm():
    return pl.BlockSpec(memory_space=pltpu.HBM)


def attend(offset, place, lengths, first, second, gain, weight, cosine, sine, reach, cache, outward):
    tree, width = first.shape
    slots, pair = cache.shape[1:]
    head_dim = pair // 2
    columns = weight.shape[1]
    group_columns = columns - pair
    return pl.pallas_call(
        functools.partial(attend_kernel, offset=offset),
        in_specs=[
            in_smem(),
            in_smem(),
            in_vmem(),
            in_vmem(),
            in_hbm(),
            in_hbm(),
            in_vmem(),
            in_vmem(),
            in_vmem(),
            in_hbm(),
            in_hbm(),
        ],
        out_specs=[in_vmem()] * 4,
        out_shape=[
            jax.ShapeDtypeStruct((tree, width), jnp.float32),
            jax.ShapeDtypeStruct((tree, width), jnp.bfloat16),
        ]
        + [jax.ShapeDtypeStruct((tree, pair), jnp.bfloat16)] * 2,
        scratch_shapes=[
            pltpu.VMEM((width, columns), jnp.bfloat16),
            pltpu.VMEM((2, slots, pair), jnp.bfloat16),
            pltpu.VMEM((1, width), jnp.float32),
            pltpu.VMEM((group_columns, width), jnp.bfloat16),
            pltpu.SemaphoreType.DMA((6,)),
        ],
        compiler_params=pltpu.CompilerParams(vmem_limit_bytes=60 * 2**20),
        cost_estimate=SMALL,
        name="attend",
    )(place, lengths, first, second, gain, weight, cosine, sine, reach, cache, outward)


def silu(values):
    return values / (1.0 + jnp.exp(-values))


def expert_kernel(*refs, plane, count, tiles):
    pieces = refs[:plane]
    weights = refs[plane : plane + 4]
    outs = refs[plane + 4 : plane + 4 + count * plane]
    rows, inner_a, outer_a, inner_b, outer_b, both, hidden, first, sems = refs[
        plane + 4 + count * plane :
    ]
    each = pieces[0].shape[0]
    parts = len(tiles)
    copies = []
    for inner, outer, inner_here, outer_here in (
        (weights[0], weights[1], inner_a, outer_a),
        (weights[2], weights[3], inner_b, outer_b),
    ):
        for start, size in tiles:
            block = pl.ds(start, size)
            number = len(copies)
            copies.append(
                pltpu.make_async_copy(inner.at[block], inner_here.at[block], sems.at[number])
            )
        copies.append(pltpu.make_async_copy(outer, outer_here, sems.at[len(copies)]))
    for copy in copies[:2]:
        copy.start()

    def take(number):
        copies[number].wait()
        if number + 2 < len(copies):
            copies[number + 2].start()

    for i in range(plane):
        rows[i * each : (i + 1) * each] = pieces[i][...]
    for n, (inner_here, outer_here) in enumerate(((inner_a, outer_a), (inner_b, outer_b))):
        base = n * (parts + 1)
        for p, (start, size) in enumerate(tiles):
            take(base + p)
            term = dot(rows[:, start : start + size], inner_here[start : start + size])
            both[...] = term if p == 0 else both[...] + term
        half = both.shape[1] // 2
        hidden[...] = (silu(both[:, :half]) * both[:, half:]).astype(jnp.bfloat16)
        take(base + parts)
        term = dot(hidden[...], outer_here[...]).astype(jnp.bfloat16)
        if n == 0:
            first[...] = term
    result = (first[...].astype(jnp.float32) + term.astype(jnp.float32)).astype(jnp.bfloat16)
    step = each // count
    for n in range(count * plane):
        base = (n % plane) * each + (n // plane) * step
        outs[n][...] = result[base : base + step]


def experts(pieces, count, inner, outer, room):
    plane = len(pieces)
    each, width = pieces[0].shape
    hidden = inner[0].shape[1]
    tiles = ((0, width // 2), (width // 2, width - width // 2))
    rows = plane * each
    weight_scratch = [
        pltpu.VMEM((width, hidden), jnp.bfloat16),
        pltpu.VMEM((hidden // 2, width), jnp.bfloat16),
    ]
    made = pl.pallas_call(
        functools.partial(expert_kernel, plane=plane, count=count, tiles=tiles),
        in_specs=[in_vmem()] * plane + [in_hbm()] * 4,
        out_specs=[in_vmem()] * (count * plane),
        out_shape=[jax.ShapeDtypeStruct((each // count, width), jnp.bfloat16)] * (count * plane),
        scratch_shapes=[pltpu.VMEM((rows, width), jnp.bfloat16)]
        + weight_scratch * 2
        + [
            pltpu.VMEM((rows, hidden), jnp.float32),
            pltpu.VMEM((rows, hidden // 2), jnp.bfloat16),
            pltpu.VMEM((rows, width), jnp.bfloat16),
            pltpu.SemaphoreType.DMA((2 * (len(tiles) + 1),)),
        ],
        compiler_params=pltpu.CompilerParams(vmem_limit_bytes=room * 2**20),
        cost_estimate=SMALL,
        name="expert",
    )(*pieces, inner[0], outer[0], inner[1], outer[1])
    return [list(made[i * plane : (i + 1) * plane]) for i in range(count)]


def shared_kernel(*refs, side):
    blocks = refs[:side]
    weights = refs[side : side + 6]
    outs = refs[side + 6 : 2 * side + 6]
    here, sems = refs[2 * side + 6 :]
    copies = [pltpu.make_async_copy(weights[i], here.at[i], sems.at[i]) for i in range(6)]
    for copy in copies[:2]:
        copy.start()

    def take(number):
        copies[number].wait()
        if number + 2 < len(copies):
            copies[number + 2].start()

    tree = blocks[0].shape[0]
    rows = jnp.concatenate([block[...] for block in blocks], axis=0).T

    def turned(i):
        take(i)
        return dot(here[i], rows)

    result = None
    for n in range(2):
        hidden = silu(turned(3 * n))
        hidden = (hidden * turned(3 * n + 1)).astype(jnp.bfloat16)
        take(3 * n + 2)
        term = lax.dot_general(
            hidden, here[3 * n + 2], (((0,), (0,)), ((), ())), preferred_element_type=jnp.float32
        )
        result = term if result is None else result + term
    for i in range(side):
        outs[i][...] = result[i * tree : (i + 1) * tree].astype(outs[i].dtype)


def shared_terms(own, beside, weights):
    tree, width = own.shape
    units = weights[0].shape[0]
    side = 1 + len(beside)
    outs = pl.pallas_call(
        functools.partial(shared_kernel, side=side),
        in_specs=[in_vmem()] * side + [in_hbm()] * 6,
        out_specs=[in_vmem()] * side,
        out_shape=[jax.ShapeDtypeStruct((tree, width), jnp.float32)]
        + [jax.ShapeDtypeStruct((tree, width), jnp.bfloat16)] * (side - 1),
        scratch_shapes=[
            pltpu.VMEM((6, units, width), jnp.bfloat16),
            pltpu.SemaphoreType.DMA((6,)),
        ],
        compiler_params=pltpu.CompilerParams(vmem_limit_bytes=60 * 2**20),
        cost_estimate=SMALL,
        name="shared",
    )(own, *beside, *weights)
    return outs[0], list(outs[1:])


def finish_kernel(tokens, term, gain, routes, *refs):
    others = refs[:-3]
    resid, normed, payload = refs[-3:]
    width = tokens.shape[1]
    attn = term[...]
    for other in others:
        attn = attn + other[...].astype(jnp.float32)
    rounded = (tokens[...].astype(jnp.float32) + attn).astype(jnp.bfloat16)
    resid[...] = rounded
    wide = rounded.astype(jnp.float32)
    power = jnp.mean(wide * wide, axis=-1, keepdims=True)
    rows = (wide * lax.rsqrt(power + EPSILON) * gain[...]).astype(jnp.bfloat16)
    normed[...] = rows
    payload[:, :width] = rows
    extra = payload.shape[1] - width
    lane = lax.broadcasted_iota(jnp.int32, (tokens.shape[0], extra), 1)
    numbers = jnp.zeros(lane.shape, jnp.float32)
    for t in range(routes.shape[1]):
        numbers = jnp.where(lane == t, routes[:, t : t + 1].astype(jnp.float32), numbers)
    payload[:, width:] = numbers.astype(jnp.bfloat16)


def finish(tokens, term, others, gain, routes):
    tree, width = tokens.shape
    return pl.pallas_call(
        finish_kernel,
        in_specs=[in_vmem()] * (4 + len(others)),
        out_specs=[in_vmem()] * 3,
        out_shape=[
            jax.ShapeDtypeStruct((tree, width), jnp.bfloat16),
            jax.ShapeDtypeStruct((tree, width), jnp.bfloat16),
            jax.ShapeDtypeStruct((tree, width + EXTRA), jnp.bfloat16),
        ],
        compiler_params=pltpu.CompilerParams(vmem_limit_bytes=16 * 2**20),
        cost_estimate=SMALL,
        name="finish",
    )(tokens, term, gain, routes, *others)


def select_kernel(*refs, count, plane, capacity, top_count):
    near = refs[0]
    router = refs[1]
    sources = refs[2 : 2 + count]
    outs = refs[2 + count : 2 + count + plane]
    spreads = refs[2 + count + plane :]
    width, expert_count = router.shape
    tree = sources[0].shape[0]
    lane = lax.broadcasted_iota(jnp.int32, (tree, plane * capacity), 1)
    place = lax.rem(lane, capacity).astype(jnp.float32)
    owner = lax.div(lane, capacity)
    expert = lax.broadcasted_iota(jnp.int32, (tree, expert_count), 1)
    row = lax.broadcasted_iota(jnp.int32, (tree, tree), 0)
    column = lax.broadcasted_iota(jnp.int32, (tree, tree), 1)
    before = jnp.where(column < row, 1.0, 0.0).astype(jnp.bfloat16)
    for i in range(count):
        rows = sources[i][:, :width]
        routes = sources[i][:, width:].astype(jnp.float32)
        member = jnp.zeros((tree, expert_count), jnp.float32)
        for t in range(top_count):
            named = routes[:, t : t + 1] == expert.astype(jnp.float32)
            member = jnp.where(named, 1.0, member)
        ranks = dot(before, member.astype(jnp.bfloat16))
        slots = jnp.where(member > 0.5, ranks, -1.0)
        logits = dot(rows, router[...])
        picked = member / (1.0 + jnp.exp(-logits))
        gates = picked / jnp.sum(picked, axis=-1, keepdims=True)
        slot = jnp.zeros(lane.shape, jnp.float32)
        gate = jnp.zeros(lane.shape, jnp.float32)
        for o in range(plane):
            mine = expert == near[o]
            slot_o = jnp.sum(jnp.where(mine, slots, 0.0), axis=-1, keepdims=True)
            gate_o = jnp.sum(jnp.where(mine, gates, 0.0), axis=-1, keepdims=True)
            slot = jnp.where(owner == o, slot_o, slot)
            gate = jnp.where(owner == o, gate_o, gate)
        pick = slot == place
        spreads[i][...] = jnp.where(pick, gate, 0.0).astype(jnp.bfloat16)
        chosen = lax.dot_general(
            jnp.where(pick, 1.0, 0.0).astype(jnp.bfloat16),
            rows,
            (((0,), (0,)), ((), ())),
            preferred_element_type=jnp.float32,
        ).astype(jnp.bfloat16)
        for o in range(plane):
            outs[o][i * capacity : (i + 1) * capacity] = chosen[o * capacity : (o + 1) * capacity]


def select(near, router, sources, plane, capacity, top_count):
    tree = sources[0].shape[0]
    width = router.shape[0]
    count = len(sources)
    made = pl.pallas_call(
        functools.partial(
            select_kernel, count=count, plane=plane, capacity=capacity, top_count=top_count
        ),
        in_specs=[in_smem()] + [in_vmem()] * (1 + count),
        out_specs=[in_vmem()] * (plane + count),
        out_shape=[jax.ShapeDtypeStruct((count * capacity, width), jnp.bfloat16)] * plane
        + [jax.ShapeDtypeStruct((tree, plane * capacity), jnp.bfloat16)] * count,
        compiler_params=pltpu.CompilerParams(vmem_limit_bytes=16 * 2**20),
        cost_estimate=SMALL,
        name="select",
    )(near, router, *sources)
    return list(made[:plane]), list(made[plane:])


def combine_kernel(spread, *refs):
    out = refs[-1]
    back = jnp.concatenate([piece[...] for piece in refs[:-1]], axis=0)
    out[...] = dot(spread[...], back).astype(out.dtype)


def combine(spread, pieces, dtype):
    tree = spread.shape[0]
    width = pieces[0].shape[1]
    return pl.pallas_call(
        combine_kernel,
        in_specs=[in_vmem()] * (1 + len(pieces)),
        out_specs=in_vmem(),
        out_shape=jax.ShapeDtypeStruct((tree, width), dtype),
        compiler_params=pltpu.CompilerParams(vmem_limit_bytes=16 * 2**20),
        cost_estimate=SMALL,
        name="combine",
    )(spread, *pieces)


def final_kernel(live, resid, shared, routed, *refs):
    total = resid[...].astype(jnp.float32) + shared[...] + routed[...]
    for part in refs[:-1]:
        total = total + part[...].astype(jnp.float32)
    refs[-1][...] = jnp.where(live[...] == 1, total, 0.0).astype(jnp.bfloat16)


def final(live, resid, shared, routed, parts):
    return pl.pallas_call(
        final_kernel,
        in_specs=[in_vmem()] * (4 + len(parts)),
        out_specs=in_vmem(),
        out_shape=jax.ShapeDtypeStruct(resid.shape, jnp.bfloat16),
        compiler_params=pltpu.CompilerParams(vmem_limit_bytes=16 * 2**20),
        cost_estimate=SMALL,
        name="final",
    )(live, resid, shared, routed, *parts)


def body(
    tokens,
    live,
    parents,
    lengths,
    accepted,
    routes,
    cache,
    attn_gain,
    w_qkv,
    w_out,
    ffn_gain,
    shared_gate,
    shared_up,
    shared_down,
    router,
    expert_in,
    expert_out,
):
    tree = tokens.shape[1]
    width = tokens.shape[2]
    own_rows = tokens[0]
    group_count = lax.axis_size(HEAD)
    head_dim = cache.shape[3] // 2
    me = lax.axis_index(HEAD)

    side = lax.axis_size("x")
    near = [own_rows] + [partner(own_rows, "x", o) for o in range(1, side)]
    near_core = [partner(own_rows, "c", 1)]

    reach, cosine, sine = prepare(lengths, parents, head_dim)
    place = me.astype(jnp.int32)[None]
    for o in range(1, side):
        near[o], cosine, sine, reach, place = lax.optimization_barrier(
            (near[o], cosine, sine, reach, place)
        )
        near_core.append(partner(near[o], "c", 1))

    gate_turned, up_turned = shared_gate.T, shared_up.T
    early, near_core[0] = lax.optimization_barrier(((gate_turned, expert_out[0]), near_core[0]))
    early = [partner(weight, "c", 1) for weight in early]
    middle, near_core = lax.optimization_barrier(
        ((up_turned, shared_down), near_core)
    )
    middle = [partner(weight, "c", 1) for weight in middle]
    near_core, early = lax.optimization_barrier((near_core, early))

    terms = [None] * side
    fresh = [None] * side
    follow = None
    late = expert_in[0]
    for o in reversed(range(side)):
        if follow is not None:
            near_core[o], follow = lax.optimization_barrier((near_core[o], follow))
        own_part, other_part, fresh_own, fresh_other = attend(
            2 * o,
            place,
            lengths,
            near[o],
            near_core[o],
            attn_gain[None],
            w_qkv,
            cosine,
            sine,
            reach,
            cache[:, 0],
            w_out,
        )
        fresh[o] = jnp.stack([fresh_own, fresh_other])
        other = partner(other_part, "c", 1)
        if o == side - 1:
            other, middle, late = lax.optimization_barrier((other, middle, late))
            late = partner(late, "c", 1)
        if o:
            follow = (own_part + other.astype(jnp.float32)).astype(jnp.bfloat16)
            crossed = partner(follow, "x", o).astype(jnp.float32)
            terms[o] = crossed if o == side - 1 else crossed + terms[o + 1]
    own_term = own_part + terms[1] if side > 1 else own_part
    own_term, late = lax.optimization_barrier((own_term, late))
    others = [other]
    resid, normed, payload = finish(own_rows, own_term, others, ffn_gain[None], routes[0])
    inner = [expert_in[0], late]
    outer = [expert_out[0], early[1]]
    shared_weights = [gate_turned, up_turned, shared_down, early[0], *middle]
    order = me ^ jnp.arange(group_count, dtype=jnp.int32)
    kept = accepted[order][:, :, None] == jnp.arange(tree, dtype=jnp.int32)
    accepted_kv = jnp.einsum(
        "ran,rnd->rad",
        kept.astype(jnp.bfloat16),
        jnp.concatenate(fresh, axis=0),
        preferred_element_type=jnp.float32,
    ).astype(jnp.bfloat16)[order][:, None]

    expert_count = router.shape[1]
    top_count = routes.shape[2]
    capacity = 4 * tree * top_count // (3 * expert_count)
    plane = lax.axis_size(PLANE)
    line = lax.axis_size("z")
    near_experts = lax.axis_index("z") * plane + (
        lax.axis_index(PLANE) ^ jnp.arange(plane, dtype=jnp.int32)
    )
    line_rows = [payload] + [partner(payload, "z", k) for k in range(1, line)]
    beside = [partner(normed, "x", o) for o in range(1, side)]

    shared, beside = shared_terms(normed, beside, shared_weights)
    line_rows[3], beside = lax.optimization_barrier((line_rows[3], beside))

    sent = []
    spread = {}
    for ks in GROUPS:
        pieces, spreads = select(
            near_experts, router, [line_rows[k] for k in ks], plane, capacity, top_count
        )
        spread.update(zip(ks, spreads))
        sent.append([partner(pieces[o], PLANE, o) for o in range(plane)])
    parts = [partner(beside[o - 1], "x", o) for o in range(1, side)]
    made = None
    results = {}
    for ks, pieces in zip(GROUPS, sent):
        if made is not None:
            pieces, made, parts = lax.optimization_barrier((pieces, made, parts))
        made = experts(pieces, len(ks), inner, outer, 40 if results else 60)
        results.update(zip(ks, made))
    totals = {}
    landed = {}
    for k, after, arrived in BACK:
        pieces = results[k]
        if after is not None:
            pieces, totals[after] = lax.optimization_barrier((pieces, totals[after]))
        if arrived is not None:
            pieces, landed[arrived] = lax.optimization_barrier((pieces, landed[arrived]))
        back = [partner(pieces[o], PLANE, o) for o in range(plane)]
        totals[k] = combine(spread[k], back, jnp.bfloat16 if k else jnp.float32)
        if k:
            landed[k] = partner(totals[k], "z", k)
    parts += list(landed.values())
    routed = totals[0]
    hidden_out = final(live[0][:, None], resid, shared, routed, parts)
    return (hidden_out[None], accepted_kv)


def solution(mesh):
    line = 4
    shape = (line, mesh.shape["req"] // line, mesh.shape["head"] // 2, 2)
    grid = Mesh(mesh.devices.reshape(shape), ALL)
    req = ("z", "y")
    in_specs = (
        P(ALL, None, None),
        P(ALL, None),
        P(req, None),
        P(req),
        P(req, None),
        P(ALL, None, None),
        P(req, HEAD, None, None),
        P(),
        P(None, HEAD),
        P(HEAD, None),
        P(),
        P(None, HEAD),
        P(None, HEAD),
        P(HEAD, None),
        P(),
        P(ALL, None, None),
        P(ALL, None, None),
    )
    out_specs = (P(ALL, None, None), P(req, HEAD, None, None))
    return jax.shard_map(body, mesh=grid, in_specs=in_specs, out_specs=out_specs, check_vma=False)
```

```python
import functools
import math

import jax
import jax.numpy as jnp
import numpy as np
from jax import lax
from jax.experimental import pallas as pl
from jax.experimental.pallas import tpu as pltpu
from jax.sharding import Mesh
from jax.sharding import PartitionSpec as P

EPSILON = 1e-06
ROPE_BASE = 10000.0
GROUPS = ((0, 3), (2, 1))
BACK = ((3, None, None), (2, None, None), (1, 3, None), (0, 2, 3))
CHUNK = 512
EXTRA = 128
SMALL = pl.CostEstimate(flops=1024, bytes_accessed=1024, transcendentals=0)
ALL = ("z", "y", "x", "c")
PLANE = ("y", "x")
HEAD = ("x", "c")


def partner(value, axes, offset):
    if offset == 0:
        return value
    size = lax.axis_size(axes)
    return lax.ppermute(value, axes, [(i, i ^ offset) for i in range(size)])


def dot(left, right):
    return jnp.dot(left, right, preferred_element_type=jnp.float32)


def prepare_kernel(lengths, parents, frequency, reach, cosine, sine):
    requests, tree = parents.shape
    row = lax.broadcasted_iota(jnp.int32, (tree, tree), 0)
    column = lax.broadcasted_iota(jnp.int32, (tree, tree), 1)
    places = column.astype(jnp.float32)
    known = parents[...].astype(jnp.float32)
    near = []
    for r in range(requests):
        spread = jnp.where(row == column, known[r : r + 1], 0.0)
        parent = jnp.sum(spread, axis=-1, keepdims=True)
        near.append(jnp.where((parent == places) | (row == column), 1.0, 0.0))
    for turn in range((tree - 1).bit_length()):
        for r in range(requests):
            step = near[r].astype(jnp.bfloat16)
            near[r] = jnp.minimum(dot(step, step), 1.0)
    half = cosine.shape[2] // 2
    lane = lax.broadcasted_iota(jnp.int32, cosine.shape[1:], 1)
    for r in range(requests):
        reach[r] = near[r]
        depth = jnp.sum(near[r], axis=-1, keepdims=True) - 1.0
        angle = (lengths[r].astype(jnp.float32) + depth) * frequency[...]
        cosine[r] = jnp.cos(angle)
        sines = jnp.sin(angle)
        sine[r] = jnp.where(lane < half, -sines, sines)


def prepare(lengths, parents, head_dim):
    requests, tree = parents.shape
    half = head_dim // 2
    frequency = ROPE_BASE ** (-np.arange(half, dtype=np.float64) / half)
    frequency = np.concatenate([frequency, frequency])[None].astype(np.float32)
    table = jax.ShapeDtypeStruct((requests, tree, head_dim), jnp.float32)
    return pl.pallas_call(
        prepare_kernel,
        in_specs=[in_smem(), in_vmem(), in_vmem()],
        out_specs=[in_vmem()] * 3,
        out_shape=[jax.ShapeDtypeStruct((requests, tree, tree), jnp.float32), table, table],
        compiler_params=pltpu.CompilerParams(vmem_limit_bytes=16 * 2**20),
        cost_estimate=SMALL,
        name="prepare",
    )(lengths, parents, frequency)


def attend_kernel(
    place, lengths, first, second, gain, weight, cosine, sine, reach, cache, outward, *rest, offset
):
    term, term_other = rest[0:2]
    fresh = rest[2:4]
    weight_here, cache_here, gain_here, outward_here, sems = rest[4:]
    tree = first.shape[0]
    width, columns = weight.shape
    head_dim = cosine.shape[2]
    group = columns // head_dim - 2
    deep = width // 2

    gain_copy = pltpu.make_async_copy(gain, gain_here, sems.at[0])
    weight_copies = [
        pltpu.make_async_copy(
            weight.at[pl.ds(i * deep, deep)], weight_here.at[pl.ds(i * deep, deep)], sems.at[1 + i]
        )
        for i in range(2)
    ]
    cache_copies = [
        pltpu.make_async_copy(
            cache.at[place[0] ^ (offset + i)], cache_here.at[i], sems.at[3 + i]
        )
        for i in range(2)
    ]
    outward_copy = pltpu.make_async_copy(outward, outward_here, sems.at[5])
    for copy in [gain_copy, *weight_copies]:
        copy.start()

    wide = jnp.concatenate([first[...], second[...]], axis=0).astype(jnp.float32)
    power = jnp.mean(wide * wide, axis=-1, keepdims=True)
    gain_copy.wait()
    normed = (wide * lax.rsqrt(power + EPSILON) * gain_here[...]).astype(jnp.bfloat16)
    weight_copies[0].wait()
    cache_copies[0].start()
    projected = dot(normed[:, :deep], weight_here[:deep])
    weight_copies[1].wait()
    cache_copies[1].start()
    projected = projected + dot(normed[:, deep:], weight_here[deep:])
    scale = 1.0 / math.sqrt(head_dim)
    results = []

    for i in range(2):
        own = projected[i * tree : (i + 1) * tree]
        request = place[0] ^ (offset + i)
        length = lengths[request]

        def rope(values):
            return values * cosine[request] + pltpu.roll(values, head_dim // 2, 1) * sine[request]

        def column(c):
            return own[:, c * head_dim : (c + 1) * head_dim]

        query = jnp.concatenate(
            [rope(column(h)).astype(jnp.bfloat16) for h in range(group)], axis=0
        )
        key_new = rope(column(group)).astype(jnp.bfloat16)
        value_new = column(group + 1).astype(jnp.bfloat16)
        fresh[i][:, :head_dim] = key_new
        fresh[i][:, head_dim:] = value_new

        def against(keys):
            return (
                lax.dot_general(
                    query, keys, (((1,), (1,)), ((), ())), preferred_element_type=jnp.float32
                )
                * scale
            )

        allowed = jnp.concatenate([reach[request]] * group, axis=0) > 0.5
        scores = jnp.where(allowed, against(key_new), -1e30)
        peak = jnp.max(scores, axis=-1, keepdims=True)
        weights = jnp.exp(scores - peak)
        total = jnp.sum(weights, axis=-1, keepdims=True)
        summed = dot(weights.astype(jnp.bfloat16), value_new)
        cache_copies[i].wait()
        if i == 0:
            outward_copy.start()

        def chunk(j, carry):
            peak, total, summed = carry
            block = pl.ds(pl.multiple_of(j * CHUNK, CHUNK), CHUNK)
            scores = against(cache_here[i, block, :head_dim])
            place = j * CHUNK + lax.broadcasted_iota(jnp.int32, scores.shape, 1)
            scores = jnp.where(place < length, scores, -1e30)
            higher = jnp.maximum(peak, jnp.max(scores, axis=-1, keepdims=True))
            fade = jnp.exp(peak - higher)
            weights = jnp.exp(scores - higher)
            total = total * fade + jnp.sum(weights, axis=-1, keepdims=True)
            values = cache_here[i, block, head_dim:]
            summed = summed * fade + dot(weights.astype(jnp.bfloat16), values)
            return (higher, total, summed)

        peak, total, summed = lax.fori_loop(
            0, lax.div(length + CHUNK - 1, CHUNK), chunk, (peak, total, summed)
        )
        result = (summed / total).astype(jnp.bfloat16)
        result = jnp.concatenate(
            [result[h * tree : (h + 1) * tree] for h in range(group)], axis=1
        )
        results.append(result)
    outward_copy.wait()
    terms = dot(jnp.concatenate(results, axis=0), outward_here[...])
    term[...] = terms[:tree]
    term_other[...] = terms[tree:].astype(jnp.bfloat16)


def in_vmem():
    return pl.BlockSpec(memory_space=pltpu.VMEM)


def in_smem():
    return pl.BlockSpec(memory_space=pltpu.SMEM)


def in_hbm():
    return pl.BlockSpec(memory_space=pltpu.HBM)


def attend(offset, place, lengths, first, second, gain, weight, cosine, sine, reach, cache, outward):
    tree, width = first.shape
    slots, pair = cache.shape[1:]
    head_dim = pair // 2
    columns = weight.shape[1]
    group_columns = columns - pair
    return pl.pallas_call(
        functools.partial(attend_kernel, offset=offset),
        in_specs=[
            in_smem(),
            in_smem(),
            in_vmem(),
            in_vmem(),
            in_hbm(),
            in_hbm(),
            in_vmem(),
            in_vmem(),
            in_vmem(),
            in_hbm(),
            in_hbm(),
        ],
        out_specs=[in_vmem()] * 4,
        out_shape=[
            jax.ShapeDtypeStruct((tree, width), jnp.float32),
            jax.ShapeDtypeStruct((tree, width), jnp.bfloat16),
        ]
        + [jax.ShapeDtypeStruct((tree, pair), jnp.bfloat16)] * 2,
        scratch_shapes=[
            pltpu.VMEM((width, columns), jnp.bfloat16),
            pltpu.VMEM((2, slots, pair), jnp.bfloat16),
            pltpu.VMEM((1, width), jnp.float32),
            pltpu.VMEM((group_columns, width), jnp.bfloat16),
            pltpu.SemaphoreType.DMA((6,)),
        ],
        compiler_params=pltpu.CompilerParams(vmem_limit_bytes=60 * 2**20),
        cost_estimate=SMALL,
        name="attend",
    )(place, lengths, first, second, gain, weight, cosine, sine, reach, cache, outward)


def silu(values):
    return values / (1.0 + jnp.exp(-values))


def expert_kernel(*refs, plane, count, tiles):
    pieces = refs[:plane]
    weights = refs[plane : plane + 4]
    outs = refs[plane + 4 : plane + 4 + count * plane]
    rows, inner_a, outer_a, inner_b, outer_b, both, hidden, first, sems = refs[
        plane + 4 + count * plane :
    ]
    each = pieces[0].shape[0]
    parts = len(tiles)
    copies = []
    for inner, outer, inner_here, outer_here in (
        (weights[0], weights[1], inner_a, outer_a),
        (weights[2], weights[3], inner_b, outer_b),
    ):
        for start, size in tiles:
            block = pl.ds(start, size)
            number = len(copies)
            copies.append(
                pltpu.make_async_copy(inner.at[block], inner_here.at[block], sems.at[number])
            )
        copies.append(pltpu.make_async_copy(outer, outer_here, sems.at[len(copies)]))
    for copy in copies[:2]:
        copy.start()

    def take(number):
        copies[number].wait()
        if number + 2 < len(copies):
            copies[number + 2].start()

    for i in range(plane):
        rows[i * each : (i + 1) * each] = pieces[i][...]
    for n, (inner_here, outer_here) in enumerate(((inner_a, outer_a), (inner_b, outer_b))):
        base = n * (parts + 1)
        for p, (start, size) in enumerate(tiles):
            take(base + p)
            term = dot(rows[:, start : start + size], inner_here[start : start + size])
            both[...] = term if p == 0 else both[...] + term
        half = both.shape[1] // 2
        hidden[...] = (silu(both[:, :half]) * both[:, half:]).astype(jnp.bfloat16)
        take(base + parts)
        term = dot(hidden[...], outer_here[...]).astype(jnp.bfloat16)
        if n == 0:
            first[...] = term
    result = (first[...].astype(jnp.float32) + term.astype(jnp.float32)).astype(jnp.bfloat16)
    step = each // count
    for n in range(count * plane):
        base = (n % plane) * each + (n // plane) * step
        outs[n][...] = result[base : base + step]


def experts(pieces, count, inner, outer):
    plane = len(pieces)
    each, width = pieces[0].shape
    hidden = inner[0].shape[1]
    tiles = ((0, width // 2), (width // 2, width - width // 2))
    rows = plane * each
    weight_scratch = [
        pltpu.VMEM((width, hidden), jnp.bfloat16),
        pltpu.VMEM((hidden // 2, width), jnp.bfloat16),
    ]
    made = pl.pallas_call(
        functools.partial(expert_kernel, plane=plane, count=count, tiles=tiles),
        in_specs=[in_vmem()] * plane + [in_hbm()] * 4,
        out_specs=[in_vmem()] * (count * plane),
        out_shape=[jax.ShapeDtypeStruct((each // count, width), jnp.bfloat16)] * (count * plane),
        scratch_shapes=[pltpu.VMEM((rows, width), jnp.bfloat16)]
        + weight_scratch * 2
        + [
            pltpu.VMEM((rows, hidden), jnp.float32),
            pltpu.VMEM((rows, hidden // 2), jnp.bfloat16),
            pltpu.VMEM((rows, width), jnp.bfloat16),
            pltpu.SemaphoreType.DMA((2 * (len(tiles) + 1),)),
        ],
        compiler_params=pltpu.CompilerParams(vmem_limit_bytes=40 * 2**20),
        cost_estimate=SMALL,
        name="expert",
    )(*pieces, inner[0], outer[0], inner[1], outer[1])
    return [list(made[i * plane : (i + 1) * plane]) for i in range(count)]


def shared_kernel(*refs, side):
    blocks = refs[:side]
    weights = refs[side : side + 6]
    outs = refs[side + 6 : 2 * side + 6]
    here, sems = refs[2 * side + 6 :]
    copies = [pltpu.make_async_copy(weights[i], here.at[i], sems.at[i]) for i in range(6)]
    for copy in copies[:2]:
        copy.start()

    def take(number):
        copies[number].wait()
        if number + 2 < len(copies):
            copies[number + 2].start()

    tree = blocks[0].shape[0]
    rows = jnp.concatenate([block[...] for block in blocks], axis=0).T

    def turned(i):
        take(i)
        return dot(here[i], rows)

    result = None
    for n in range(2):
        hidden = silu(turned(3 * n))
        hidden = (hidden * turned(3 * n + 1)).astype(jnp.bfloat16)
        take(3 * n + 2)
        term = lax.dot_general(
            hidden, here[3 * n + 2], (((0,), (0,)), ((), ())), preferred_element_type=jnp.float32
        )
        result = term if result is None else result + term
    for i in range(side):
        outs[i][...] = result[i * tree : (i + 1) * tree].astype(outs[i].dtype)


def shared_terms(own, beside, weights):
    tree, width = own.shape
    units = weights[0].shape[0]
    side = 1 + len(beside)
    outs = pl.pallas_call(
        functools.partial(shared_kernel, side=side),
        in_specs=[in_vmem()] * side + [in_hbm()] * 6,
        out_specs=[in_vmem()] * side,
        out_shape=[jax.ShapeDtypeStruct((tree, width), jnp.float32)]
        + [jax.ShapeDtypeStruct((tree, width), jnp.bfloat16)] * (side - 1),
        scratch_shapes=[
            pltpu.VMEM((6, units, width), jnp.bfloat16),
            pltpu.SemaphoreType.DMA((6,)),
        ],
        compiler_params=pltpu.CompilerParams(vmem_limit_bytes=60 * 2**20),
        cost_estimate=SMALL,
        name="shared",
    )(own, *beside, *weights)
    return outs[0], list(outs[1:])


def finish_kernel(tokens, term, gain, routes, *refs):
    others = refs[:-3]
    resid, normed, payload = refs[-3:]
    width = tokens.shape[1]
    attn = term[...]
    for other in others:
        attn = attn + other[...].astype(jnp.float32)
    rounded = (tokens[...].astype(jnp.float32) + attn).astype(jnp.bfloat16)
    resid[...] = rounded
    wide = rounded.astype(jnp.float32)
    power = jnp.mean(wide * wide, axis=-1, keepdims=True)
    rows = (wide * lax.rsqrt(power + EPSILON) * gain[...]).astype(jnp.bfloat16)
    normed[...] = rows
    payload[:, :width] = rows
    extra = payload.shape[1] - width
    lane = lax.broadcasted_iota(jnp.int32, (tokens.shape[0], extra), 1)
    numbers = jnp.zeros(lane.shape, jnp.float32)
    for t in range(routes.shape[1]):
        numbers = jnp.where(lane == t, routes[:, t : t + 1].astype(jnp.float32), numbers)
    payload[:, width:] = numbers.astype(jnp.bfloat16)


def finish(tokens, term, others, gain, routes):
    tree, width = tokens.shape
    return pl.pallas_call(
        finish_kernel,
        in_specs=[in_vmem()] * (4 + len(others)),
        out_specs=[in_vmem()] * 3,
        out_shape=[
            jax.ShapeDtypeStruct((tree, width), jnp.bfloat16),
            jax.ShapeDtypeStruct((tree, width), jnp.bfloat16),
            jax.ShapeDtypeStruct((tree, width + EXTRA), jnp.bfloat16),
        ],
        compiler_params=pltpu.CompilerParams(vmem_limit_bytes=16 * 2**20),
        cost_estimate=SMALL,
        name="finish",
    )(tokens, term, gain, routes, *others)


def select_kernel(*refs, count, plane, capacity, top_count):
    near = refs[0]
    router = refs[1]
    sources = refs[2 : 2 + count]
    outs = refs[2 + count : 2 + count + plane]
    spreads = refs[2 + count + plane :]
    width, expert_count = router.shape
    tree = sources[0].shape[0]
    lane = lax.broadcasted_iota(jnp.int32, (tree, plane * capacity), 1)
    place = lax.rem(lane, capacity).astype(jnp.float32)
    owner = lax.div(lane, capacity)
    expert = lax.broadcasted_iota(jnp.int32, (tree, expert_count), 1)
    row = lax.broadcasted_iota(jnp.int32, (tree, tree), 0)
    column = lax.broadcasted_iota(jnp.int32, (tree, tree), 1)
    before = jnp.where(column < row, 1.0, 0.0).astype(jnp.bfloat16)
    for i in range(count):
        rows = sources[i][:, :width]
        routes = sources[i][:, width:].astype(jnp.float32)
        member = jnp.zeros((tree, expert_count), jnp.float32)
        for t in range(top_count):
            named = routes[:, t : t + 1] == expert.astype(jnp.float32)
            member = jnp.where(named, 1.0, member)
        ranks = dot(before, member.astype(jnp.bfloat16))
        slots = jnp.where(member > 0.5, ranks, -1.0)
        logits = dot(rows, router[...])
        picked = member / (1.0 + jnp.exp(-logits))
        gates = picked / jnp.sum(picked, axis=-1, keepdims=True)
        slot = jnp.zeros(lane.shape, jnp.float32)
        gate = jnp.zeros(lane.shape, jnp.float32)
        for o in range(plane):
            mine = expert == near[o]
            slot_o = jnp.sum(jnp.where(mine, slots, 0.0), axis=-1, keepdims=True)
            gate_o = jnp.sum(jnp.where(mine, gates, 0.0), axis=-1, keepdims=True)
            slot = jnp.where(owner == o, slot_o, slot)
            gate = jnp.where(owner == o, gate_o, gate)
        pick = slot == place
        spreads[i][...] = jnp.where(pick, gate, 0.0).astype(jnp.bfloat16)
        chosen = lax.dot_general(
            jnp.where(pick, 1.0, 0.0).astype(jnp.bfloat16),
            rows,
            (((0,), (0,)), ((), ())),
            preferred_element_type=jnp.float32,
        ).astype(jnp.bfloat16)
        for o in range(plane):
            outs[o][i * capacity : (i + 1) * capacity] = chosen[o * capacity : (o + 1) * capacity]


def select(near, router, sources, plane, capacity, top_count):
    tree = sources[0].shape[0]
    width = router.shape[0]
    count = len(sources)
    made = pl.pallas_call(
        functools.partial(
            select_kernel, count=count, plane=plane, capacity=capacity, top_count=top_count
        ),
        in_specs=[in_smem()] + [in_vmem()] * (1 + count),
        out_specs=[in_vmem()] * (plane + count),
        out_shape=[jax.ShapeDtypeStruct((count * capacity, width), jnp.bfloat16)] * plane
        + [jax.ShapeDtypeStruct((tree, plane * capacity), jnp.bfloat16)] * count,
        compiler_params=pltpu.CompilerParams(vmem_limit_bytes=16 * 2**20),
        cost_estimate=SMALL,
        name="select",
    )(near, router, *sources)
    return list(made[:plane]), list(made[plane:])


def combine_kernel(spread, *refs):
    out = refs[-1]
    back = jnp.concatenate([piece[...] for piece in refs[:-1]], axis=0)
    out[...] = dot(spread[...], back).astype(out.dtype)


def combine(spread, pieces, dtype):
    tree = spread.shape[0]
    width = pieces[0].shape[1]
    return pl.pallas_call(
        combine_kernel,
        in_specs=[in_vmem()] * (1 + len(pieces)),
        out_specs=in_vmem(),
        out_shape=jax.ShapeDtypeStruct((tree, width), dtype),
        compiler_params=pltpu.CompilerParams(vmem_limit_bytes=16 * 2**20),
        cost_estimate=SMALL,
        name="combine",
    )(spread, *pieces)


def final_kernel(live, resid, shared, routed, *refs):
    total = resid[...].astype(jnp.float32) + shared[...] + routed[...]
    for part in refs[:-1]:
        total = total + part[...].astype(jnp.float32)
    refs[-1][...] = jnp.where(live[...] == 1, total, 0.0).astype(jnp.bfloat16)


def final(live, resid, shared, routed, parts):
    return pl.pallas_call(
        final_kernel,
        in_specs=[in_vmem()] * (4 + len(parts)),
        out_specs=in_vmem(),
        out_shape=jax.ShapeDtypeStruct(resid.shape, jnp.bfloat16),
        compiler_params=pltpu.CompilerParams(vmem_limit_bytes=16 * 2**20),
        cost_estimate=SMALL,
        name="final",
    )(live, resid, shared, routed, *parts)


def body(
    tokens,
    live,
    parents,
    lengths,
    accepted,
    routes,
    cache,
    attn_gain,
    w_qkv,
    w_out,
    ffn_gain,
    shared_gate,
    shared_up,
    shared_down,
    router,
    expert_in,
    expert_out,
):
    tree = tokens.shape[1]
    width = tokens.shape[2]
    own_rows = tokens[0]
    group_count = lax.axis_size(HEAD)
    head_dim = cache.shape[3] // 2
    me = lax.axis_index(HEAD)

    side = lax.axis_size("x")
    near = [own_rows] + [partner(own_rows, "x", o) for o in range(1, side)]
    near_core = [partner(own_rows, "c", 1)]

    reach, cosine, sine = prepare(lengths, parents, head_dim)
    place = me.astype(jnp.int32)[None]
    for o in range(1, side):
        near[o], cosine, sine, reach, place = lax.optimization_barrier(
            (near[o], cosine, sine, reach, place)
        )
        near_core.append(partner(near[o], "c", 1))

    gate_turned, up_turned = shared_gate.T, shared_up.T
    early, near_core[0] = lax.optimization_barrier(((gate_turned, expert_out[0]), near_core[0]))
    early = [partner(weight, "c", 1) for weight in early]
    middle, near_core = lax.optimization_barrier(
        ((up_turned, shared_down), near_core)
    )
    middle = [partner(weight, "c", 1) for weight in middle]
    near_core, early = lax.optimization_barrier((near_core, early))

    terms = [None] * side
    fresh = [None] * side
    follow = None
    late = expert_in[0]
    for o in reversed(range(side)):
        if follow is not None:
            near_core[o], follow = lax.optimization_barrier((near_core[o], follow))
        own_part, other_part, fresh_own, fresh_other = attend(
            2 * o,
            place,
            lengths,
            near[o],
            near_core[o],
            attn_gain[None],
            w_qkv,
            cosine,
            sine,
            reach,
            cache[:, 0],
            w_out,
        )
        fresh[o] = jnp.stack([fresh_own, fresh_other])
        other = partner(other_part, "c", 1)
        if o == side - 1:
            other, middle, late = lax.optimization_barrier((other, middle, late))
            late = partner(late, "c", 1)
        if o:
            follow = (own_part + other.astype(jnp.float32)).astype(jnp.bfloat16)
            crossed = partner(follow, "x", o).astype(jnp.float32)
            terms[o] = crossed if o == side - 1 else crossed + terms[o + 1]
    own_term = own_part + terms[1] if side > 1 else own_part
    own_term, late = lax.optimization_barrier((own_term, late))
    others = [other]
    resid, normed, payload = finish(own_rows, own_term, others, ffn_gain[None], routes[0])
    inner = [expert_in[0], late]
    outer = [expert_out[0], early[1]]
    shared_weights = [gate_turned, up_turned, shared_down, early[0], *middle]
    order = me ^ jnp.arange(group_count, dtype=jnp.int32)
    kept = accepted[order][:, :, None] == jnp.arange(tree, dtype=jnp.int32)
    accepted_kv = jnp.einsum(
        "ran,rnd->rad",
        kept.astype(jnp.bfloat16),
        jnp.concatenate(fresh, axis=0),
        preferred_element_type=jnp.float32,
    ).astype(jnp.bfloat16)[order][:, None]

    expert_count = router.shape[1]
    top_count = routes.shape[2]
    capacity = 4 * tree * top_count // (3 * expert_count)
    plane = lax.axis_size(PLANE)
    line = lax.axis_size("z")
    near_experts = lax.axis_index("z") * plane + (
        lax.axis_index(PLANE) ^ jnp.arange(plane, dtype=jnp.int32)
    )
    line_rows = [payload] + [partner(payload, "z", k) for k in range(1, line)]
    beside = [partner(normed, "x", o) for o in range(1, side)]

    shared, beside = shared_terms(normed, beside, shared_weights)
    line_rows[3], beside = lax.optimization_barrier((line_rows[3], beside))

    sent = []
    spread = {}
    for ks in GROUPS:
        pieces, spreads = select(
            near_experts, router, [line_rows[k] for k in ks], plane, capacity, top_count
        )
        spread.update(zip(ks, spreads))
        sent.append([partner(pieces[o], PLANE, o) for o in range(plane)])
    parts = [partner(beside[o - 1], "x", o) for o in range(1, side)]
    made = None
    results = {}
    for ks, pieces in zip(GROUPS, sent):
        if made is not None:
            pieces, made, parts = lax.optimization_barrier((pieces, made, parts))
        made = experts(pieces, len(ks), inner, outer)
        results.update(zip(ks, made))
    totals = {}
    landed = {}
    for k, after, arrived in BACK:
        pieces = results[k]
        if after is not None:
            pieces, totals[after] = lax.optimization_barrier((pieces, totals[after]))
        if arrived is not None:
            pieces, landed[arrived] = lax.optimization_barrier((pieces, landed[arrived]))
        back = [partner(pieces[o], PLANE, o) for o in range(plane)]
        totals[k] = combine(spread[k], back, jnp.bfloat16 if k else jnp.float32)
        if k:
            landed[k] = partner(totals[k], "z", k)
    parts += list(landed.values())
    routed = totals[0]
    hidden_out = final(live[0][:, None], resid, shared, routed, parts)
    return (hidden_out[None], accepted_kv)


def solution(mesh):
    line = 4
    shape = (line, mesh.shape["req"] // line, mesh.shape["head"] // 2, 2)
    grid = Mesh(mesh.devices.reshape(shape), ALL)
    req = ("z", "y")
    in_specs = (
        P(ALL, None, None),
        P(ALL, None),
        P(req, None),
        P(req),
        P(req, None),
        P(ALL, None, None),
        P(req, HEAD, None, None),
        P(),
        P(None, HEAD),
        P(HEAD, None),
        P(),
        P(None, HEAD),
        P(None, HEAD),
        P(HEAD, None),
        P(),
        P(ALL, None, None),
        P(ALL, None, None),
    )
    out_specs = (P(ALL, None, None), P(req, HEAD, None, None))
    return jax.shard_map(body, mesh=grid, in_specs=in_specs, out_specs=out_specs, check_vma=False)
```

```python
import functools
import math

import jax
import jax.numpy as jnp
import numpy as np
from jax import lax
from jax.experimental import pallas as pl
from jax.experimental.pallas import tpu as pltpu
from jax.sharding import Mesh
from jax.sharding import PartitionSpec as P

EPSILON = 1e-06
ROPE_BASE = 10000.0
GROUPS = ((0, 3), (2, 1))
BACK = ((3, None, None), (2, None, None), (1, 3, None), (0, 2, 3))
CHUNK = 512
EXTRA = 128
LARGE = pl.CostEstimate(flops=23000000000, bytes_accessed=72000000, transcendentals=0)
SMALL = pl.CostEstimate(flops=1024, bytes_accessed=1024, transcendentals=0)
ALL = ("z", "y", "x", "c")
PLANE = ("y", "x")
HEAD = ("x", "c")


def partner(value, axes, offset):
    if offset == 0:
        return value
    size = lax.axis_size(axes)
    return lax.ppermute(value, axes, [(i, i ^ offset) for i in range(size)])


def dot(left, right):
    return jnp.dot(left, right, preferred_element_type=jnp.float32)


def prepare_kernel(lengths, parents, frequency, reach, cosine, sine):
    requests, tree = parents.shape
    row = lax.broadcasted_iota(jnp.int32, (tree, tree), 0)
    column = lax.broadcasted_iota(jnp.int32, (tree, tree), 1)
    places = column.astype(jnp.float32)
    known = parents[...].astype(jnp.float32)
    near = []
    for r in range(requests):
        spread = jnp.where(row == column, known[r : r + 1], 0.0)
        parent = jnp.sum(spread, axis=-1, keepdims=True)
        near.append(jnp.where((parent == places) | (row == column), 1.0, 0.0))
    for turn in range((tree - 1).bit_length()):
        for r in range(requests):
            step = near[r].astype(jnp.bfloat16)
            near[r] = jnp.minimum(dot(step, step), 1.0)
    half = cosine.shape[2] // 2
    lane = lax.broadcasted_iota(jnp.int32, cosine.shape[1:], 1)
    for r in range(requests):
        reach[r] = near[r]
        depth = jnp.sum(near[r], axis=-1, keepdims=True) - 1.0
        angle = (lengths[r].astype(jnp.float32) + depth) * frequency[...]
        cosine[r] = jnp.cos(angle)
        sines = jnp.sin(angle)
        sine[r] = jnp.where(lane < half, -sines, sines)


def prepare(lengths, parents, head_dim):
    requests, tree = parents.shape
    half = head_dim // 2
    frequency = ROPE_BASE ** (-np.arange(half, dtype=np.float64) / half)
    frequency = np.concatenate([frequency, frequency])[None].astype(np.float32)
    table = jax.ShapeDtypeStruct((requests, tree, head_dim), jnp.float32)
    return pl.pallas_call(
        prepare_kernel,
        in_specs=[in_smem(), in_vmem(), in_vmem()],
        out_specs=[in_vmem()] * 3,
        out_shape=[jax.ShapeDtypeStruct((requests, tree, tree), jnp.float32), table, table],
        compiler_params=pltpu.CompilerParams(vmem_limit_bytes=16 * 2**20),
        cost_estimate=SMALL,
        name="prepare",
    )(lengths, parents, frequency)


def attend_kernel(
    place, lengths, first, second, gain, weight, cosine, sine, reach, cache, outward, *rest, offset
):
    term, term_other = rest[0:2]
    fresh = rest[2:4]
    weight_here, cache_here, gain_here, outward_here, sems = rest[4:]
    tree = first.shape[0]
    width, columns = weight.shape
    head_dim = cosine.shape[2]
    group = columns // head_dim - 2
    deep = width // 2

    gain_copy = pltpu.make_async_copy(gain, gain_here, sems.at[0])
    weight_copies = [
        pltpu.make_async_copy(
            weight.at[pl.ds(i * deep, deep)], weight_here.at[pl.ds(i * deep, deep)], sems.at[1 + i]
        )
        for i in range(2)
    ]
    cache_copies = [
        pltpu.make_async_copy(
            cache.at[place[0] ^ (offset + i)], cache_here.at[i], sems.at[3 + i]
        )
        for i in range(2)
    ]
    outward_copy = pltpu.make_async_copy(outward, outward_here, sems.at[5])
    for copy in [gain_copy, *weight_copies]:
        copy.start()

    wide = jnp.concatenate([first[...], second[...]], axis=0).astype(jnp.float32)
    power = jnp.mean(wide * wide, axis=-1, keepdims=True)
    gain_copy.wait()
    normed = (wide * lax.rsqrt(power + EPSILON) * gain_here[...]).astype(jnp.bfloat16)
    weight_copies[0].wait()
    cache_copies[0].start()
    projected = dot(normed[:, :deep], weight_here[:deep])
    weight_copies[1].wait()
    cache_copies[1].start()
    projected = projected + dot(normed[:, deep:], weight_here[deep:])
    scale = 1.0 / math.sqrt(head_dim)
    results = []

    for i in range(2):
        own = projected[i * tree : (i + 1) * tree]
        request = place[0] ^ (offset + i)
        length = lengths[request]

        def rope(values):
            return values * cosine[request] + pltpu.roll(values, head_dim // 2, 1) * sine[request]

        def column(c):
            return own[:, c * head_dim : (c + 1) * head_dim]

        query = jnp.concatenate(
            [rope(column(h)).astype(jnp.bfloat16) for h in range(group)], axis=0
        )
        key_new = rope(column(group)).astype(jnp.bfloat16)
        value_new = column(group + 1).astype(jnp.bfloat16)
        fresh[i][:, :head_dim] = key_new
        fresh[i][:, head_dim:] = value_new

        def against(keys):
            return (
                lax.dot_general(
                    query, keys, (((1,), (1,)), ((), ())), preferred_element_type=jnp.float32
                )
                * scale
            )

        allowed = jnp.concatenate([reach[request]] * group, axis=0) > 0.5
        scores = jnp.where(allowed, against(key_new), -1e30)
        peak = jnp.max(scores, axis=-1, keepdims=True)
        weights = jnp.exp(scores - peak)
        total = jnp.sum(weights, axis=-1, keepdims=True)
        summed = dot(weights.astype(jnp.bfloat16), value_new)
        cache_copies[i].wait()
        if i == 0:
            outward_copy.start()

        def chunk(j, carry):
            peak, total, summed = carry
            block = pl.ds(pl.multiple_of(j * CHUNK, CHUNK), CHUNK)
            scores = against(cache_here[i, block, :head_dim])
            place = j * CHUNK + lax.broadcasted_iota(jnp.int32, scores.shape, 1)
            scores = jnp.where(place < length, scores, -1e30)
            higher = jnp.maximum(peak, jnp.max(scores, axis=-1, keepdims=True))
            fade = jnp.exp(peak - higher)
            weights = jnp.exp(scores - higher)
            total = total * fade + jnp.sum(weights, axis=-1, keepdims=True)
            values = cache_here[i, block, head_dim:]
            summed = summed * fade + dot(weights.astype(jnp.bfloat16), values)
            return (higher, total, summed)

        peak, total, summed = lax.fori_loop(
            0, lax.div(length + CHUNK - 1, CHUNK), chunk, (peak, total, summed)
        )
        result = (summed / total).astype(jnp.bfloat16)
        result = jnp.concatenate(
            [result[h * tree : (h + 1) * tree] for h in range(group)], axis=1
        )
        results.append(result)
    outward_copy.wait()
    terms = dot(jnp.concatenate(results, axis=0), outward_here[...])
    term[...] = terms[:tree]
    term_other[...] = terms[tree:].astype(jnp.bfloat16)


def in_vmem():
    return pl.BlockSpec(memory_space=pltpu.VMEM)


def in_smem():
    return pl.BlockSpec(memory_space=pltpu.SMEM)


def in_hbm():
    return pl.BlockSpec(memory_space=pltpu.HBM)


def attend(offset, place, lengths, first, second, gain, weight, cosine, sine, reach, cache, outward):
    tree, width = first.shape
    slots, pair = cache.shape[1:]
    head_dim = pair // 2
    columns = weight.shape[1]
    group_columns = columns - pair
    return pl.pallas_call(
        functools.partial(attend_kernel, offset=offset),
        in_specs=[
            in_smem(),
            in_smem(),
            in_vmem(),
            in_vmem(),
            in_hbm(),
            in_hbm(),
            in_vmem(),
            in_vmem(),
            in_vmem(),
            in_hbm(),
            in_hbm(),
        ],
        out_specs=[in_vmem()] * 4,
        out_shape=[
            jax.ShapeDtypeStruct((tree, width), jnp.float32),
            jax.ShapeDtypeStruct((tree, width), jnp.bfloat16),
        ]
        + [jax.ShapeDtypeStruct((tree, pair), jnp.bfloat16)] * 2,
        scratch_shapes=[
            pltpu.VMEM((width, columns), jnp.bfloat16),
            pltpu.VMEM((2, slots, pair), jnp.bfloat16),
            pltpu.VMEM((1, width), jnp.float32),
            pltpu.VMEM((group_columns, width), jnp.bfloat16),
            pltpu.SemaphoreType.DMA((6,)),
        ],
        compiler_params=pltpu.CompilerParams(vmem_limit_bytes=60 * 2**20),
        cost_estimate=SMALL,
        name="attend",
    )(place, lengths, first, second, gain, weight, cosine, sine, reach, cache, outward)


def silu(values):
    return values / (1.0 + jnp.exp(-values))


def expert_kernel(*refs, plane, count, tiles):
    pieces = refs[:plane]
    weights = refs[plane : plane + 4]
    outs = refs[plane + 4 : plane + 4 + count * plane]
    rows, inner_a, outer_a, inner_b, outer_b, both, hidden, first, sems = refs[
        plane + 4 + count * plane :
    ]
    each = pieces[0].shape[0]
    parts = len(tiles)
    copies = []
    for inner, outer, inner_here, outer_here in (
        (weights[0], weights[1], inner_a, outer_a),
        (weights[2], weights[3], inner_b, outer_b),
    ):
        for start, size in tiles:
            block = pl.ds(start, size)
            number = len(copies)
            copies.append(
                pltpu.make_async_copy(inner.at[block], inner_here.at[block], sems.at[number])
            )
        copies.append(pltpu.make_async_copy(outer, outer_here, sems.at[len(copies)]))
    for copy in copies[:2]:
        copy.start()

    def take(number):
        copies[number].wait()
        if number + 2 < len(copies):
            copies[number + 2].start()

    for i in range(plane):
        rows[i * each : (i + 1) * each] = pieces[i][...]
    for n, (inner_here, outer_here) in enumerate(((inner_a, outer_a), (inner_b, outer_b))):
        base = n * (parts + 1)
        for p, (start, size) in enumerate(tiles):
            take(base + p)
            term = dot(rows[:, start : start + size], inner_here[start : start + size])
            both[...] = term if p == 0 else both[...] + term
        half = both.shape[1] // 2
        hidden[...] = (silu(both[:, :half]) * both[:, half:]).astype(jnp.bfloat16)
        take(base + parts)
        term = dot(hidden[...], outer_here[...]).astype(jnp.bfloat16)
        if n == 0:
            first[...] = term
    result = (first[...].astype(jnp.float32) + term.astype(jnp.float32)).astype(jnp.bfloat16)
    step = each // count
    for n in range(count * plane):
        base = (n % plane) * each + (n // plane) * step
        outs[n][...] = result[base : base + step]


def experts(pieces, count, inner, outer):
    plane = len(pieces)
    each, width = pieces[0].shape
    hidden = inner[0].shape[1]
    tiles = ((0, width // 2), (width // 2, width - width // 2))
    rows = plane * each
    weight_scratch = [
        pltpu.VMEM((width, hidden), jnp.bfloat16),
        pltpu.VMEM((hidden // 2, width), jnp.bfloat16),
    ]
    made = pl.pallas_call(
        functools.partial(expert_kernel, plane=plane, count=count, tiles=tiles),
        in_specs=[in_vmem()] * plane + [in_hbm()] * 4,
        out_specs=[in_vmem()] * (count * plane),
        out_shape=[jax.ShapeDtypeStruct((each // count, width), jnp.bfloat16)] * (count * plane),
        scratch_shapes=[pltpu.VMEM((rows, width), jnp.bfloat16)]
        + weight_scratch * 2
        + [
            pltpu.VMEM((rows, hidden), jnp.float32),
            pltpu.VMEM((rows, hidden // 2), jnp.bfloat16),
            pltpu.VMEM((rows, width), jnp.bfloat16),
            pltpu.SemaphoreType.DMA((2 * (len(tiles) + 1),)),
        ],
        compiler_params=pltpu.CompilerParams(vmem_limit_bytes=40 * 2**20),
        cost_estimate=SMALL,
        name="expert",
    )(*pieces, inner[0], outer[0], inner[1], outer[1])
    return [list(made[i * plane : (i + 1) * plane]) for i in range(count)]


def shared_kernel(*refs, side):
    blocks = refs[:side]
    weights = refs[side : side + 6]
    outs = refs[side + 6 : 2 * side + 6]
    here, sems = refs[2 * side + 6 :]
    copies = [pltpu.make_async_copy(weights[i], here.at[i], sems.at[i]) for i in range(6)]
    for copy in copies[:2]:
        copy.start()

    def take(number):
        copies[number].wait()
        if number + 2 < len(copies):
            copies[number + 2].start()

    tree = blocks[0].shape[0]
    rows = jnp.concatenate([block[...] for block in blocks], axis=0).T

    def turned(i):
        take(i)
        return dot(here[i], rows)

    result = None
    for n in range(2):
        hidden = silu(turned(3 * n))
        hidden = (hidden * turned(3 * n + 1)).astype(jnp.bfloat16)
        take(3 * n + 2)
        term = lax.dot_general(
            hidden, here[3 * n + 2], (((0,), (0,)), ((), ())), preferred_element_type=jnp.float32
        )
        result = term if result is None else result + term
    for i in range(side):
        outs[i][...] = result[i * tree : (i + 1) * tree].astype(outs[i].dtype)


def shared_terms(own, beside, weights):
    tree, width = own.shape
    units = weights[0].shape[0]
    side = 1 + len(beside)
    outs = pl.pallas_call(
        functools.partial(shared_kernel, side=side),
        in_specs=[in_vmem()] * side + [in_hbm()] * 6,
        out_specs=[in_vmem()] * side,
        out_shape=[jax.ShapeDtypeStruct((tree, width), jnp.float32)]
        + [jax.ShapeDtypeStruct((tree, width), jnp.bfloat16)] * (side - 1),
        scratch_shapes=[
            pltpu.VMEM((6, units, width), jnp.bfloat16),
            pltpu.SemaphoreType.DMA((6,)),
        ],
        compiler_params=pltpu.CompilerParams(vmem_limit_bytes=60 * 2**20),
        cost_estimate=SMALL,
        name="shared",
    )(own, *beside, *weights)
    return outs[0], list(outs[1:])


def finish_kernel(tokens, term, gain, routes, *refs):
    others = refs[:-3]
    resid, normed, payload = refs[-3:]
    width = tokens.shape[1]
    attn = term[...]
    for other in others:
        attn = attn + other[...].astype(jnp.float32)
    rounded = (tokens[...].astype(jnp.float32) + attn).astype(jnp.bfloat16)
    resid[...] = rounded
    wide = rounded.astype(jnp.float32)
    power = jnp.mean(wide * wide, axis=-1, keepdims=True)
    rows = (wide * lax.rsqrt(power + EPSILON) * gain[...]).astype(jnp.bfloat16)
    normed[...] = rows
    payload[:, :width] = rows
    extra = payload.shape[1] - width
    lane = lax.broadcasted_iota(jnp.int32, (tokens.shape[0], extra), 1)
    numbers = jnp.zeros(lane.shape, jnp.float32)
    for t in range(routes.shape[1]):
        numbers = jnp.where(lane == t, routes[:, t : t + 1].astype(jnp.float32), numbers)
    payload[:, width:] = numbers.astype(jnp.bfloat16)


def finish(tokens, term, others, gain, routes):
    tree, width = tokens.shape
    return pl.pallas_call(
        finish_kernel,
        in_specs=[in_vmem()] * (4 + len(others)),
        out_specs=[in_vmem()] * 3,
        out_shape=[
            jax.ShapeDtypeStruct((tree, width), jnp.bfloat16),
            jax.ShapeDtypeStruct((tree, width), jnp.bfloat16),
            jax.ShapeDtypeStruct((tree, width + EXTRA), jnp.bfloat16),
        ],
        compiler_params=pltpu.CompilerParams(vmem_limit_bytes=16 * 2**20),
        cost_estimate=SMALL,
        name="finish",
    )(tokens, term, gain, routes, *others)


def select_kernel(*refs, count, plane, capacity, top_count):
    near = refs[0]
    router = refs[1]
    sources = refs[2 : 2 + count]
    outs = refs[2 + count : 2 + count + plane]
    spreads = refs[2 + count + plane :]
    width, expert_count = router.shape
    tree = sources[0].shape[0]
    lane = lax.broadcasted_iota(jnp.int32, (tree, plane * capacity), 1)
    place = lax.rem(lane, capacity).astype(jnp.float32)
    owner = lax.div(lane, capacity)
    expert = lax.broadcasted_iota(jnp.int32, (tree, expert_count), 1)
    row = lax.broadcasted_iota(jnp.int32, (tree, tree), 0)
    column = lax.broadcasted_iota(jnp.int32, (tree, tree), 1)
    before = jnp.where(column < row, 1.0, 0.0).astype(jnp.bfloat16)
    for i in range(count):
        rows = sources[i][:, :width]
        routes = sources[i][:, width:].astype(jnp.float32)
        member = jnp.zeros((tree, expert_count), jnp.float32)
        for t in range(top_count):
            named = routes[:, t : t + 1] == expert.astype(jnp.float32)
            member = jnp.where(named, 1.0, member)
        ranks = dot(before, member.astype(jnp.bfloat16))
        slots = jnp.where(member > 0.5, ranks, -1.0)
        logits = dot(rows, router[...])
        picked = member / (1.0 + jnp.exp(-logits))
        gates = picked / jnp.sum(picked, axis=-1, keepdims=True)
        slot = jnp.zeros(lane.shape, jnp.float32)
        gate = jnp.zeros(lane.shape, jnp.float32)
        for o in range(plane):
            mine = expert == near[o]
            slot_o = jnp.sum(jnp.where(mine, slots, 0.0), axis=-1, keepdims=True)
            gate_o = jnp.sum(jnp.where(mine, gates, 0.0), axis=-1, keepdims=True)
            slot = jnp.where(owner == o, slot_o, slot)
            gate = jnp.where(owner == o, gate_o, gate)
        pick = slot == place
        spreads[i][...] = jnp.where(pick, gate, 0.0).astype(jnp.bfloat16)
        chosen = lax.dot_general(
            jnp.where(pick, 1.0, 0.0).astype(jnp.bfloat16),
            rows,
            (((0,), (0,)), ((), ())),
            preferred_element_type=jnp.float32,
        ).astype(jnp.bfloat16)
        for o in range(plane):
            outs[o][i * capacity : (i + 1) * capacity] = chosen[o * capacity : (o + 1) * capacity]


def select(near, router, sources, plane, capacity, top_count, cost):
    tree = sources[0].shape[0]
    width = router.shape[0]
    count = len(sources)
    made = pl.pallas_call(
        functools.partial(
            select_kernel, count=count, plane=plane, capacity=capacity, top_count=top_count
        ),
        in_specs=[in_smem()] + [in_vmem()] * (1 + count),
        out_specs=[in_vmem()] * (plane + count),
        out_shape=[jax.ShapeDtypeStruct((count * capacity, width), jnp.bfloat16)] * plane
        + [jax.ShapeDtypeStruct((tree, plane * capacity), jnp.bfloat16)] * count,
        compiler_params=pltpu.CompilerParams(vmem_limit_bytes=16 * 2**20),
        cost_estimate=cost,
        name="select",
    )(near, router, *sources)
    return list(made[:plane]), list(made[plane:])


def combine_kernel(spread, *refs):
    out = refs[-1]
    back = jnp.concatenate([piece[...] for piece in refs[:-1]], axis=0)
    out[...] = dot(spread[...], back).astype(out.dtype)


def combine(spread, pieces, dtype):
    tree = spread.shape[0]
    width = pieces[0].shape[1]
    return pl.pallas_call(
        combine_kernel,
        in_specs=[in_vmem()] * (1 + len(pieces)),
        out_specs=in_vmem(),
        out_shape=jax.ShapeDtypeStruct((tree, width), dtype),
        compiler_params=pltpu.CompilerParams(vmem_limit_bytes=16 * 2**20),
        cost_estimate=SMALL,
        name="combine",
    )(spread, *pieces)


def final_kernel(live, resid, shared, routed, *refs):
    total = resid[...].astype(jnp.float32) + shared[...] + routed[...]
    for part in refs[:-1]:
        total = total + part[...].astype(jnp.float32)
    refs[-1][...] = jnp.where(live[...] == 1, total, 0.0).astype(jnp.bfloat16)


def final(live, resid, shared, routed, parts):
    return pl.pallas_call(
        final_kernel,
        in_specs=[in_vmem()] * (4 + len(parts)),
        out_specs=in_vmem(),
        out_shape=jax.ShapeDtypeStruct(resid.shape, jnp.bfloat16),
        compiler_params=pltpu.CompilerParams(vmem_limit_bytes=16 * 2**20),
        cost_estimate=SMALL,
        name="final",
    )(live, resid, shared, routed, *parts)


def body(
    tokens,
    live,
    parents,
    lengths,
    accepted,
    routes,
    cache,
    attn_gain,
    w_qkv,
    w_out,
    ffn_gain,
    shared_gate,
    shared_up,
    shared_down,
    router,
    expert_in,
    expert_out,
):
    tree = tokens.shape[1]
    width = tokens.shape[2]
    own_rows = tokens[0]
    group_count = lax.axis_size(HEAD)
    head_dim = cache.shape[3] // 2
    me = lax.axis_index(HEAD)

    side = lax.axis_size("x")
    near = [own_rows] + [partner(own_rows, "x", o) for o in range(1, side)]
    near_core = [partner(own_rows, "c", 1)]

    reach, cosine, sine = prepare(lengths, parents, head_dim)
    place = me.astype(jnp.int32)[None]
    for o in range(1, side):
        near[o], cosine, sine, reach, place = lax.optimization_barrier(
            (near[o], cosine, sine, reach, place)
        )
        near_core.append(partner(near[o], "c", 1))

    gate_turned, up_turned = shared_gate.T, shared_up.T
    early, near_core[0] = lax.optimization_barrier(((gate_turned, expert_out[0]), near_core[0]))
    early = [partner(weight, "c", 1) for weight in early]
    middle, near_core = lax.optimization_barrier(
        ((up_turned, shared_down), near_core)
    )
    middle = [partner(weight, "c", 1) for weight in middle]
    near_core, early = lax.optimization_barrier((near_core, early))

    terms = [None] * side
    fresh = [None] * side
    follow = None
    late = expert_in[0]
    for o in reversed(range(side)):
        if follow is not None:
            near_core[o], follow = lax.optimization_barrier((near_core[o], follow))
        own_part, other_part, fresh_own, fresh_other = attend(
            2 * o,
            place,
            lengths,
            near[o],
            near_core[o],
            attn_gain[None],
            w_qkv,
            cosine,
            sine,
            reach,
            cache[:, 0],
            w_out,
        )
        fresh[o] = jnp.stack([fresh_own, fresh_other])
        other = partner(other_part, "c", 1)
        if o == side - 1:
            other, middle, late = lax.optimization_barrier((other, middle, late))
            late = partner(late, "c", 1)
        if o:
            follow = (own_part + other.astype(jnp.float32)).astype(jnp.bfloat16)
            crossed = partner(follow, "x", o).astype(jnp.float32)
            terms[o] = crossed if o == side - 1 else crossed + terms[o + 1]
    own_term = own_part + terms[1] if side > 1 else own_part
    own_term, late = lax.optimization_barrier((own_term, late))
    others = [other]
    resid, normed, payload = finish(own_rows, own_term, others, ffn_gain[None], routes[0])
    inner = [expert_in[0], late]
    outer = [expert_out[0], early[1]]
    shared_weights = [gate_turned, up_turned, shared_down, early[0], *middle]
    order = me ^ jnp.arange(group_count, dtype=jnp.int32)
    kept = accepted[order][:, :, None] == jnp.arange(tree, dtype=jnp.int32)
    accepted_kv = jnp.einsum(
        "ran,rnd->rad",
        kept.astype(jnp.bfloat16),
        jnp.concatenate(fresh, axis=0),
        preferred_element_type=jnp.float32,
    ).astype(jnp.bfloat16)[order][:, None]

    expert_count = router.shape[1]
    top_count = routes.shape[2]
    capacity = 4 * tree * top_count // (3 * expert_count)
    plane = lax.axis_size(PLANE)
    line = lax.axis_size("z")
    near_experts = lax.axis_index("z") * plane + (
        lax.axis_index(PLANE) ^ jnp.arange(plane, dtype=jnp.int32)
    )
    line_rows = [payload] + [partner(payload, "z", k) for k in range(1, line)]
    beside = [partner(normed, "x", o) for o in range(1, side)]

    shared, beside = shared_terms(normed, beside, shared_weights)
    line_rows[3], beside = lax.optimization_barrier((line_rows[3], beside))

    sent = []
    spread = {}
    for ks in GROUPS:
        pieces, spreads = select(
            near_experts,
            router,
            [line_rows[k] for k in ks],
            plane,
            capacity,
            top_count,
            LARGE if sent else SMALL,
        )
        spread.update(zip(ks, spreads))
        sent.append([partner(pieces[o], PLANE, o) for o in range(plane)])
    parts = [partner(beside[o - 1], "x", o) for o in range(1, side)]
    made = None
    results = {}
    for ks, pieces in zip(GROUPS, sent):
        if made is not None:
            pieces, made, parts = lax.optimization_barrier((pieces, made, parts))
        made = experts(pieces, len(ks), inner, outer)
        results.update(zip(ks, made))
    totals = {}
    landed = {}
    for k, after, arrived in BACK:
        pieces = results[k]
        if after is not None:
            pieces, totals[after] = lax.optimization_barrier((pieces, totals[after]))
        if arrived is not None:
            pieces, landed[arrived] = lax.optimization_barrier((pieces, landed[arrived]))
        back = [partner(pieces[o], PLANE, o) for o in range(plane)]
        totals[k] = combine(spread[k], back, jnp.bfloat16 if k else jnp.float32)
        if k:
            landed[k] = partner(totals[k], "z", k)
    parts += list(landed.values())
    routed = totals[0]
    hidden_out = final(live[0][:, None], resid, shared, routed, parts)
    return (hidden_out[None], accepted_kv)


def solution(mesh):
    line = 4
    shape = (line, mesh.shape["req"] // line, mesh.shape["head"] // 2, 2)
    grid = Mesh(mesh.devices.reshape(shape), ALL)
    req = ("z", "y")
    in_specs = (
        P(ALL, None, None),
        P(ALL, None),
        P(req, None),
        P(req),
        P(req, None),
        P(ALL, None, None),
        P(req, HEAD, None, None),
        P(),
        P(None, HEAD),
        P(HEAD, None),
        P(),
        P(None, HEAD),
        P(None, HEAD),
        P(HEAD, None),
        P(),
        P(ALL, None, None),
        P(ALL, None, None),
    )
    out_specs = (P(ALL, None, None), P(req, HEAD, None, None))
    return jax.shard_map(body, mesh=grid, in_specs=in_specs, out_specs=out_specs, check_vma=False)
```

```python
import functools
import math

import jax
import jax.numpy as jnp
import numpy as np
from jax import lax
from jax.experimental import pallas as pl
from jax.experimental.pallas import tpu as pltpu
from jax.sharding import Mesh
from jax.sharding import PartitionSpec as P

EPSILON = 1e-06
ROPE_BASE = 10000.0
GROUPS = ((0, 3), (2, 1))
BACK = ((3, None, None), (2, None, None), (1, 3, None), (0, 2, 3))
CHUNK = 512
EXTRA = 128
LARGE = pl.CostEstimate(flops=23000000000, bytes_accessed=72000000, transcendentals=0)
SMALL = pl.CostEstimate(flops=1024, bytes_accessed=1024, transcendentals=0)
ALL = ("z", "y", "x", "c")
PLANE = ("y", "x")
HEAD = ("x", "c")


def partner(value, axes, offset):
    if offset == 0:
        return value
    size = lax.axis_size(axes)
    return lax.ppermute(value, axes, [(i, i ^ offset) for i in range(size)])


def dot(left, right):
    return jnp.dot(left, right, preferred_element_type=jnp.float32)


def prepare_kernel(lengths, parents, frequency, reach, cosine, sine):
    requests, tree = parents.shape
    row = lax.broadcasted_iota(jnp.int32, (tree, tree), 0)
    column = lax.broadcasted_iota(jnp.int32, (tree, tree), 1)
    places = column.astype(jnp.float32)
    known = parents[...].astype(jnp.float32)
    near = []
    for r in range(requests):
        spread = jnp.where(row == column, known[r : r + 1], 0.0)
        parent = jnp.sum(spread, axis=-1, keepdims=True)
        near.append(jnp.where((parent == places) | (row == column), 1.0, 0.0))
    for turn in range((tree - 1).bit_length()):
        for r in range(requests):
            step = near[r].astype(jnp.bfloat16)
            near[r] = jnp.minimum(dot(step, step), 1.0)
    half = cosine.shape[2] // 2
    lane = lax.broadcasted_iota(jnp.int32, cosine.shape[1:], 1)
    for r in range(requests):
        reach[r] = near[r]
        depth = jnp.sum(near[r], axis=-1, keepdims=True) - 1.0
        angle = (lengths[r].astype(jnp.float32) + depth) * frequency[...]
        cosine[r] = jnp.cos(angle)
        sines = jnp.sin(angle)
        sine[r] = jnp.where(lane < half, -sines, sines)


def prepare(lengths, parents, head_dim):
    requests, tree = parents.shape
    half = head_dim // 2
    frequency = ROPE_BASE ** (-np.arange(half, dtype=np.float64) / half)
    frequency = np.concatenate([frequency, frequency])[None].astype(np.float32)
    table = jax.ShapeDtypeStruct((requests, tree, head_dim), jnp.float32)
    return pl.pallas_call(
        prepare_kernel,
        in_specs=[in_smem(), in_vmem(), in_vmem()],
        out_specs=[in_vmem()] * 3,
        out_shape=[jax.ShapeDtypeStruct((requests, tree, tree), jnp.float32), table, table],
        compiler_params=pltpu.CompilerParams(vmem_limit_bytes=16 * 2**20),
        cost_estimate=SMALL,
        name="prepare",
    )(lengths, parents, frequency)


def attend_kernel(
    place, lengths, first, second, gain, weight, cosine, sine, reach, cache, outward, *rest, offset
):
    term, term_other = rest[0:2]
    fresh = rest[2:4]
    weight_here, cache_here, gain_here, outward_here, sems = rest[4:]
    tree = first.shape[0]
    width, columns = weight.shape
    head_dim = cosine.shape[2]
    group = columns // head_dim - 2
    deep = width // 2

    gain_copy = pltpu.make_async_copy(gain, gain_here, sems.at[0])
    weight_copies = [
        pltpu.make_async_copy(
            weight.at[pl.ds(i * deep, deep)], weight_here.at[pl.ds(i * deep, deep)], sems.at[1 + i]
        )
        for i in range(2)
    ]
    cache_copies = [
        pltpu.make_async_copy(
            cache.at[place[0] ^ (offset + i)], cache_here.at[i], sems.at[3 + i]
        )
        for i in range(2)
    ]
    outward_copy = pltpu.make_async_copy(outward, outward_here, sems.at[5])
    for copy in [gain_copy, *weight_copies]:
        copy.start()

    wide = jnp.concatenate([first[...], second[...]], axis=0).astype(jnp.float32)
    power = jnp.mean(wide * wide, axis=-1, keepdims=True)
    gain_copy.wait()
    normed = (wide * lax.rsqrt(power + EPSILON) * gain_here[...]).astype(jnp.bfloat16)
    weight_copies[0].wait()
    cache_copies[0].start()
    projected = dot(normed[:, :deep], weight_here[:deep])
    weight_copies[1].wait()
    cache_copies[1].start()
    projected = projected + dot(normed[:, deep:], weight_here[deep:])
    scale = 1.0 / math.sqrt(head_dim)
    results = []

    for i in range(2):
        own = projected[i * tree : (i + 1) * tree]
        request = place[0] ^ (offset + i)
        length = lengths[request]

        def rope(values):
            return values * cosine[request] + pltpu.roll(values, head_dim // 2, 1) * sine[request]

        def column(c):
            return own[:, c * head_dim : (c + 1) * head_dim]

        query = jnp.concatenate(
            [rope(column(h)).astype(jnp.bfloat16) for h in range(group)], axis=0
        )
        key_new = rope(column(group)).astype(jnp.bfloat16)
        value_new = column(group + 1).astype(jnp.bfloat16)
        fresh[i][:, :head_dim] = key_new
        fresh[i][:, head_dim:] = value_new

        def against(keys):
            return (
                lax.dot_general(
                    query, keys, (((1,), (1,)), ((), ())), preferred_element_type=jnp.float32
                )
                * scale
            )

        allowed = jnp.concatenate([reach[request]] * group, axis=0) > 0.5
        scores = jnp.where(allowed, against(key_new), -1e30)
        peak = jnp.max(scores, axis=-1, keepdims=True)
        weights = jnp.exp(scores - peak)
        total = jnp.sum(weights, axis=-1, keepdims=True)
        summed = dot(weights.astype(jnp.bfloat16), value_new)
        cache_copies[i].wait()
        if i == 0:
            outward_copy.start()

        def chunk(j, carry):
            peak, total, summed = carry
            block = pl.ds(pl.multiple_of(j * CHUNK, CHUNK), CHUNK)
            scores = against(cache_here[i, block, :head_dim])
            place = j * CHUNK + lax.broadcasted_iota(jnp.int32, scores.shape, 1)
            scores = jnp.where(place < length, scores, -1e30)
            higher = jnp.maximum(peak, jnp.max(scores, axis=-1, keepdims=True))
            fade = jnp.exp(peak - higher)
            weights = jnp.exp(scores - higher)
            total = total * fade + jnp.sum(weights, axis=-1, keepdims=True)
            values = cache_here[i, block, head_dim:]
            summed = summed * fade + dot(weights.astype(jnp.bfloat16), values)
            return (higher, total, summed)

        peak, total, summed = lax.fori_loop(
            0, lax.div(length + CHUNK - 1, CHUNK), chunk, (peak, total, summed)
        )
        result = (summed / total).astype(jnp.bfloat16)
        result = jnp.concatenate(
            [result[h * tree : (h + 1) * tree] for h in range(group)], axis=1
        )
        results.append(result)
    outward_copy.wait()
    terms = dot(jnp.concatenate(results, axis=0), outward_here[...])
    term[...] = terms[:tree]
    term_other[...] = terms[tree:].astype(jnp.bfloat16)


def in_vmem():
    return pl.BlockSpec(memory_space=pltpu.VMEM)


def in_smem():
    return pl.BlockSpec(memory_space=pltpu.SMEM)


def in_hbm():
    return pl.BlockSpec(memory_space=pltpu.HBM)


def attend(offset, place, lengths, first, second, gain, weight, cosine, sine, reach, cache, outward):
    tree, width = first.shape
    slots, pair = cache.shape[1:]
    head_dim = pair // 2
    columns = weight.shape[1]
    group_columns = columns - pair
    return pl.pallas_call(
        functools.partial(attend_kernel, offset=offset),
        in_specs=[
            in_smem(),
            in_smem(),
            in_vmem(),
            in_vmem(),
            in_hbm(),
            in_hbm(),
            in_vmem(),
            in_vmem(),
            in_vmem(),
            in_hbm(),
            in_hbm(),
        ],
        out_specs=[in_vmem()] * 4,
        out_shape=[
            jax.ShapeDtypeStruct((tree, width), jnp.float32),
            jax.ShapeDtypeStruct((tree, width), jnp.bfloat16),
        ]
        + [jax.ShapeDtypeStruct((tree, pair), jnp.bfloat16)] * 2,
        scratch_shapes=[
            pltpu.VMEM((width, columns), jnp.bfloat16),
            pltpu.VMEM((2, slots, pair), jnp.bfloat16),
            pltpu.VMEM((1, width), jnp.float32),
            pltpu.VMEM((group_columns, width), jnp.bfloat16),
            pltpu.SemaphoreType.DMA((6,)),
        ],
        compiler_params=pltpu.CompilerParams(vmem_limit_bytes=60 * 2**20),
        cost_estimate=SMALL,
        name="attend",
    )(place, lengths, first, second, gain, weight, cosine, sine, reach, cache, outward)


def silu(values):
    return values / (1.0 + jnp.exp(-values))


def expert_kernel(*refs, plane, count, tiles):
    pieces = refs[:plane]
    weights = refs[plane : plane + 4]
    outs = refs[plane + 4 : plane + 4 + count * plane]
    rows, inner_a, outer_a, inner_b, outer_b, both, hidden, first, sems = refs[
        plane + 4 + count * plane :
    ]
    each = pieces[0].shape[0]
    parts = len(tiles)
    copies = []
    for inner, outer, inner_here, outer_here in (
        (weights[0], weights[1], inner_a, outer_a),
        (weights[2], weights[3], inner_b, outer_b),
    ):
        for start, size in tiles:
            block = pl.ds(start, size)
            number = len(copies)
            copies.append(
                pltpu.make_async_copy(inner.at[block], inner_here.at[block], sems.at[number])
            )
        copies.append(pltpu.make_async_copy(outer, outer_here, sems.at[len(copies)]))
    for copy in copies[:2]:
        copy.start()

    def take(number):
        copies[number].wait()
        if number + 2 < len(copies):
            copies[number + 2].start()

    for i in range(plane):
        rows[i * each : (i + 1) * each] = pieces[i][...]
    for n, (inner_here, outer_here) in enumerate(((inner_a, outer_a), (inner_b, outer_b))):
        base = n * (parts + 1)
        for p, (start, size) in enumerate(tiles):
            take(base + p)
            term = dot(rows[:, start : start + size], inner_here[start : start + size])
            both[...] = term if p == 0 else both[...] + term
        half = both.shape[1] // 2
        hidden[...] = (silu(both[:, :half]) * both[:, half:]).astype(jnp.bfloat16)
        take(base + parts)
        term = dot(hidden[...], outer_here[...]).astype(jnp.bfloat16)
        if n == 0:
            first[...] = term
    result = (first[...].astype(jnp.float32) + term.astype(jnp.float32)).astype(jnp.bfloat16)
    step = each // count
    for n in range(count * plane):
        base = (n % plane) * each + (n // plane) * step
        outs[n][...] = result[base : base + step]


def experts(pieces, count, inner, outer):
    plane = len(pieces)
    each, width = pieces[0].shape
    hidden = inner[0].shape[1]
    tiles = ((0, width // 2), (width // 2, width - width // 2))
    rows = plane * each
    weight_scratch = [
        pltpu.VMEM((width, hidden), jnp.bfloat16),
        pltpu.VMEM((hidden // 2, width), jnp.bfloat16),
    ]
    made = pl.pallas_call(
        functools.partial(expert_kernel, plane=plane, count=count, tiles=tiles),
        in_specs=[in_vmem()] * plane + [in_hbm()] * 4,
        out_specs=[in_vmem()] * (count * plane),
        out_shape=[jax.ShapeDtypeStruct((each // count, width), jnp.bfloat16)] * (count * plane),
        scratch_shapes=[pltpu.VMEM((rows, width), jnp.bfloat16)]
        + weight_scratch * 2
        + [
            pltpu.VMEM((rows, hidden), jnp.float32),
            pltpu.VMEM((rows, hidden // 2), jnp.bfloat16),
            pltpu.VMEM((rows, width), jnp.bfloat16),
            pltpu.SemaphoreType.DMA((2 * (len(tiles) + 1),)),
        ],
        compiler_params=pltpu.CompilerParams(vmem_limit_bytes=40 * 2**20),
        cost_estimate=SMALL,
        name="expert",
    )(*pieces, inner[0], outer[0], inner[1], outer[1])
    return [list(made[i * plane : (i + 1) * plane]) for i in range(count)]


def shared_kernel(*refs, side):
    blocks = refs[:side]
    weights = refs[side : side + 6]
    outs = refs[side + 6 : 2 * side + 6]
    here, sems = refs[2 * side + 6 :]
    copies = [pltpu.make_async_copy(weights[i], here.at[i], sems.at[i]) for i in range(6)]
    for copy in copies[:2]:
        copy.start()

    def take(number):
        copies[number].wait()
        if number + 2 < len(copies):
            copies[number + 2].start()

    tree = blocks[0].shape[0]
    rows = jnp.concatenate([block[...] for block in blocks], axis=0).T

    def turned(i):
        take(i)
        return dot(here[i], rows)

    result = None
    for n in range(2):
        hidden = silu(turned(3 * n))
        hidden = (hidden * turned(3 * n + 1)).astype(jnp.bfloat16)
        take(3 * n + 2)
        term = lax.dot_general(
            hidden, here[3 * n + 2], (((0,), (0,)), ((), ())), preferred_element_type=jnp.float32
        )
        result = term if result is None else result + term
    for i in range(side):
        outs[i][...] = result[i * tree : (i + 1) * tree].astype(outs[i].dtype)


def shared_terms(own, beside, weights):
    tree, width = own.shape
    units = weights[0].shape[0]
    side = 1 + len(beside)
    outs = pl.pallas_call(
        functools.partial(shared_kernel, side=side),
        in_specs=[in_vmem()] * side + [in_hbm()] * 6,
        out_specs=[in_vmem()] * side,
        out_shape=[jax.ShapeDtypeStruct((tree, width), jnp.float32)]
        + [jax.ShapeDtypeStruct((tree, width), jnp.bfloat16)] * (side - 1),
        scratch_shapes=[
            pltpu.VMEM((6, units, width), jnp.bfloat16),
            pltpu.SemaphoreType.DMA((6,)),
        ],
        compiler_params=pltpu.CompilerParams(vmem_limit_bytes=60 * 2**20),
        cost_estimate=SMALL,
        name="shared",
    )(own, *beside, *weights)
    return outs[0], list(outs[1:])


def finish_kernel(tokens, term, gain, routes, *refs):
    others = refs[:-3]
    resid, normed, payload = refs[-3:]
    width = tokens.shape[1]
    attn = term[...]
    for other in others:
        attn = attn + other[...].astype(jnp.float32)
    rounded = (tokens[...].astype(jnp.float32) + attn).astype(jnp.bfloat16)
    resid[...] = rounded
    wide = rounded.astype(jnp.float32)
    power = jnp.mean(wide * wide, axis=-1, keepdims=True)
    rows = (wide * lax.rsqrt(power + EPSILON) * gain[...]).astype(jnp.bfloat16)
    normed[...] = rows
    payload[:, :width] = rows
    extra = payload.shape[1] - width
    lane = lax.broadcasted_iota(jnp.int32, (tokens.shape[0], extra), 1)
    numbers = jnp.zeros(lane.shape, jnp.float32)
    for t in range(routes.shape[1]):
        numbers = jnp.where(lane == t, routes[:, t : t + 1].astype(jnp.float32), numbers)
    payload[:, width:] = numbers.astype(jnp.bfloat16)


def finish(tokens, term, others, gain, routes):
    tree, width = tokens.shape
    return pl.pallas_call(
        finish_kernel,
        in_specs=[in_vmem()] * (4 + len(others)),
        out_specs=[in_vmem()] * 3,
        out_shape=[
            jax.ShapeDtypeStruct((tree, width), jnp.bfloat16),
            jax.ShapeDtypeStruct((tree, width), jnp.bfloat16),
            jax.ShapeDtypeStruct((tree, width + EXTRA), jnp.bfloat16),
        ],
        compiler_params=pltpu.CompilerParams(vmem_limit_bytes=16 * 2**20),
        cost_estimate=SMALL,
        name="finish",
    )(tokens, term, gain, routes, *others)


def select_kernel(*refs, count, plane, capacity, top_count):
    near = refs[0]
    router = refs[1]
    sources = refs[2 : 2 + count]
    outs = refs[2 + count : 2 + count + plane]
    spreads = refs[2 + count + plane :]
    width, expert_count = router.shape
    tree = sources[0].shape[0]
    lane = lax.broadcasted_iota(jnp.int32, (tree, plane * capacity), 1)
    place = lax.rem(lane, capacity).astype(jnp.float32)
    owner = lax.div(lane, capacity)
    expert = lax.broadcasted_iota(jnp.int32, (tree, expert_count), 1)
    row = lax.broadcasted_iota(jnp.int32, (tree, tree), 0)
    column = lax.broadcasted_iota(jnp.int32, (tree, tree), 1)
    before = jnp.where(column < row, 1.0, 0.0).astype(jnp.bfloat16)
    for i in range(count):
        rows = sources[i][:, :width]
        routes = sources[i][:, width:].astype(jnp.float32)
        member = jnp.zeros((tree, expert_count), jnp.float32)
        for t in range(top_count):
            named = routes[:, t : t + 1] == expert.astype(jnp.float32)
            member = jnp.where(named, 1.0, member)
        ranks = dot(before, member.astype(jnp.bfloat16))
        slots = jnp.where(member > 0.5, ranks, -1.0)
        logits = dot(rows, router[...])
        picked = member / (1.0 + jnp.exp(-logits))
        gates = picked / jnp.sum(picked, axis=-1, keepdims=True)
        slot = jnp.zeros(lane.shape, jnp.float32)
        gate = jnp.zeros(lane.shape, jnp.float32)
        for o in range(plane):
            mine = expert == near[o]
            slot_o = jnp.sum(jnp.where(mine, slots, 0.0), axis=-1, keepdims=True)
            gate_o = jnp.sum(jnp.where(mine, gates, 0.0), axis=-1, keepdims=True)
            slot = jnp.where(owner == o, slot_o, slot)
            gate = jnp.where(owner == o, gate_o, gate)
        pick = slot == place
        spreads[i][...] = jnp.where(pick, gate, 0.0).astype(jnp.bfloat16)
        chosen = lax.dot_general(
            jnp.where(pick, 1.0, 0.0).astype(jnp.bfloat16),
            rows,
            (((0,), (0,)), ((), ())),
            preferred_element_type=jnp.float32,
        ).astype(jnp.bfloat16)
        for o in range(plane):
            outs[o][i * capacity : (i + 1) * capacity] = chosen[o * capacity : (o + 1) * capacity]


def select(near, router, sources, plane, capacity, top_count, cost):
    tree = sources[0].shape[0]
    width = router.shape[0]
    count = len(sources)
    made = pl.pallas_call(
        functools.partial(
            select_kernel, count=count, plane=plane, capacity=capacity, top_count=top_count
        ),
        in_specs=[in_smem()] + [in_vmem()] * (1 + count),
        out_specs=[in_vmem()] * (plane + count),
        out_shape=[jax.ShapeDtypeStruct((count * capacity, width), jnp.bfloat16)] * plane
        + [jax.ShapeDtypeStruct((tree, plane * capacity), jnp.bfloat16)] * count,
        compiler_params=pltpu.CompilerParams(vmem_limit_bytes=16 * 2**20),
        cost_estimate=cost,
        name="select",
    )(near, router, *sources)
    return list(made[:plane]), list(made[plane:])


def combine_kernel(spread, *refs):
    out = refs[-1]
    back = jnp.concatenate([piece[...] for piece in refs[:-1]], axis=0)
    out[...] = dot(spread[...], back).astype(out.dtype)


def combine(spread, pieces, dtype):
    tree = spread.shape[0]
    width = pieces[0].shape[1]
    return pl.pallas_call(
        combine_kernel,
        in_specs=[in_vmem()] * (1 + len(pieces)),
        out_specs=in_vmem(),
        out_shape=jax.ShapeDtypeStruct((tree, width), dtype),
        compiler_params=pltpu.CompilerParams(vmem_limit_bytes=16 * 2**20),
        cost_estimate=SMALL,
        name="combine",
    )(spread, *pieces)


def final_kernel(live, resid, shared, routed, *refs):
    total = resid[...].astype(jnp.float32) + shared[...] + routed[...]
    for part in refs[:-1]:
        total = total + part[...].astype(jnp.float32)
    refs[-1][...] = jnp.where(live[...] == 1, total, 0.0).astype(jnp.bfloat16)


def final(live, resid, shared, routed, parts):
    return pl.pallas_call(
        final_kernel,
        in_specs=[in_vmem()] * (4 + len(parts)),
        out_specs=in_vmem(),
        out_shape=jax.ShapeDtypeStruct(resid.shape, jnp.bfloat16),
        compiler_params=pltpu.CompilerParams(vmem_limit_bytes=16 * 2**20),
        cost_estimate=SMALL,
        name="final",
    )(live, resid, shared, routed, *parts)


def body(
    tokens,
    live,
    parents,
    lengths,
    accepted,
    routes,
    cache,
    attn_gain,
    w_qkv,
    w_out,
    ffn_gain,
    shared_gate,
    shared_up,
    shared_down,
    router,
    expert_in,
    expert_out,
):
    tree = tokens.shape[1]
    width = tokens.shape[2]
    own_rows = tokens[0]
    group_count = lax.axis_size(HEAD)
    head_dim = cache.shape[3] // 2
    me = lax.axis_index(HEAD)

    side = lax.axis_size("x")
    near = [own_rows] + [partner(own_rows, "x", o) for o in range(1, side)]
    near_core = [partner(own_rows, "c", 1)]

    reach, cosine, sine = prepare(lengths, parents, head_dim)
    place = me.astype(jnp.int32)[None]
    for o in range(1, side):
        near[o], cosine, sine, reach, place = lax.optimization_barrier(
            (near[o], cosine, sine, reach, place)
        )
        near_core.append(partner(near[o], "c", 1))

    gate_turned, up_turned = shared_gate.T, shared_up.T
    early, near_core[0] = lax.optimization_barrier(((gate_turned, expert_out[0]), near_core[0]))
    early = [partner(weight, "c", 1) for weight in early]
    middle, near_core = lax.optimization_barrier(
        ((up_turned, shared_down), near_core)
    )
    middle = [partner(weight, "c", 1) for weight in middle]
    near_core, early = lax.optimization_barrier((near_core, early))

    terms = [None] * side
    fresh = [None] * side
    follow = None
    late = expert_in[0]
    for o in reversed(range(side)):
        if follow is not None:
            near_core[o], follow = lax.optimization_barrier((near_core[o], follow))
        own_part, other_part, fresh_own, fresh_other = attend(
            2 * o,
            place,
            lengths,
            near[o],
            near_core[o],
            attn_gain[None],
            w_qkv,
            cosine,
            sine,
            reach,
            cache[:, 0],
            w_out,
        )
        fresh[o] = jnp.stack([fresh_own, fresh_other])
        other = partner(other_part, "c", 1)
        if o == side - 1:
            other, middle, late = lax.optimization_barrier((other, middle, late))
            late = partner(late, "c", 1)
        if o:
            follow = (own_part + other.astype(jnp.float32)).astype(jnp.bfloat16)
            crossed = partner(follow, "x", o).astype(jnp.float32)
            terms[o] = crossed if o == side - 1 else crossed + terms[o + 1]
    own_term = own_part + terms[1] if side > 1 else own_part
    own_term, late = lax.optimization_barrier((own_term, late))
    others = [other]
    resid, normed, payload = finish(own_rows, own_term, others, ffn_gain[None], routes[0])
    inner = [expert_in[0], late]
    outer = [expert_out[0], early[1]]
    shared_weights = [gate_turned, up_turned, shared_down, early[0], *middle]
    order = me ^ jnp.arange(group_count, dtype=jnp.int32)
    kept = accepted[order][:, :, None] == jnp.arange(tree, dtype=jnp.int32)
    accepted_kv = jnp.einsum(
        "ran,rnd->rad",
        kept.astype(jnp.bfloat16),
        jnp.concatenate(fresh, axis=0),
        preferred_element_type=jnp.float32,
    ).astype(jnp.bfloat16)[order][:, None]

    expert_count = router.shape[1]
    top_count = routes.shape[2]
    capacity = 4 * tree * top_count // (3 * expert_count)
    plane = lax.axis_size(PLANE)
    line = lax.axis_size("z")
    near_experts = lax.axis_index("z") * plane + (
        lax.axis_index(PLANE) ^ jnp.arange(plane, dtype=jnp.int32)
    )
    line_rows = [payload] + [partner(payload, "z", k) for k in range(1, line)]
    beside = [partner(normed, "x", o) for o in range(1, side)]

    shared, beside = shared_terms(normed, beside, shared_weights)
    line_rows[3], beside = lax.optimization_barrier((line_rows[3], beside))

    sent = []
    spread = {}
    for ks in GROUPS:
        pieces, spreads = select(
            near_experts,
            router,
            [line_rows[k] for k in ks],
            plane,
            capacity,
            top_count,
            LARGE if sent else SMALL,
        )
        spread.update(zip(ks, spreads))
        sent.append([partner(pieces[o], PLANE, o) for o in range(plane)])
    parts = [partner(beside[o - 1], "x", o) for o in range(1, side)]
    made = None
    results = {}
    for ks, pieces in zip(GROUPS, sent):
        if made is not None:
            pieces, made = lax.optimization_barrier((pieces, made))
        made = experts(pieces, len(ks), inner, outer)
        results.update(zip(ks, made))
    totals = {}
    landed = {}
    for k, after, arrived in BACK:
        pieces = results[k]
        if k == BACK[1][0]:
            pieces, parts = lax.optimization_barrier((pieces, parts))
        if after is not None:
            pieces, totals[after] = lax.optimization_barrier((pieces, totals[after]))
        if arrived is not None:
            pieces, landed[arrived] = lax.optimization_barrier((pieces, landed[arrived]))
        back = [partner(pieces[o], PLANE, o) for o in range(plane)]
        totals[k] = combine(spread[k], back, jnp.bfloat16 if k else jnp.float32)
        if k:
            landed[k] = partner(totals[k], "z", k)
    parts += list(landed.values())
    routed = totals[0]
    hidden_out = final(live[0][:, None], resid, shared, routed, parts)
    return (hidden_out[None], accepted_kv)


def solution(mesh):
    line = 4
    shape = (line, mesh.shape["req"] // line, mesh.shape["head"] // 2, 2)
    grid = Mesh(mesh.devices.reshape(shape), ALL)
    req = ("z", "y")
    in_specs = (
        P(ALL, None, None),
        P(ALL, None),
        P(req, None),
        P(req),
        P(req, None),
        P(ALL, None, None),
        P(req, HEAD, None, None),
        P(),
        P(None, HEAD),
        P(HEAD, None),
        P(),
        P(None, HEAD),
        P(None, HEAD),
        P(HEAD, None),
        P(),
        P(ALL, None, None),
        P(ALL, None, None),
    )
    out_specs = (P(ALL, None, None), P(req, HEAD, None, None))
    return jax.shard_map(body, mesh=grid, in_specs=in_specs, out_specs=out_specs, check_vma=False)
```

```python
import functools
import math

import jax
import jax.numpy as jnp
import numpy as np
from jax import lax
from jax.experimental import pallas as pl
from jax.experimental.pallas import tpu as pltpu
from jax.sharding import Mesh
from jax.sharding import PartitionSpec as P

EPSILON = 1e-06
ROPE_BASE = 10000.0
GROUPS = ((0, 3), (2, 1))
BACK = ((3, None, None), (2, None, None), (1, 3, None), (0, 2, 3))
CHUNK = 512
EXTRA = 128
LARGE = pl.CostEstimate(flops=23000000000, bytes_accessed=72000000, transcendentals=0)
SMALL = pl.CostEstimate(flops=1024, bytes_accessed=1024, transcendentals=0)
ALL = ("z", "y", "x", "c")
PLANE = ("y", "x")
HEAD = ("x", "c")


def partner(value, axes, offset):
    if offset == 0:
        return value
    size = lax.axis_size(axes)
    return lax.ppermute(value, axes, [(i, i ^ offset) for i in range(size)])


def dot(left, right):
    return jnp.dot(left, right, preferred_element_type=jnp.float32)


def prepare_kernel(lengths, parents, frequency, reach, cosine, sine):
    requests, tree = parents.shape
    row = lax.broadcasted_iota(jnp.int32, (tree, tree), 0)
    column = lax.broadcasted_iota(jnp.int32, (tree, tree), 1)
    places = column.astype(jnp.float32)
    known = parents[...].astype(jnp.float32)
    near = []
    for r in range(requests):
        spread = jnp.where(row == column, known[r : r + 1], 0.0)
        parent = jnp.sum(spread, axis=-1, keepdims=True)
        near.append(jnp.where((parent == places) | (row == column), 1.0, 0.0))
    for turn in range((tree - 1).bit_length()):
        for r in range(requests):
            step = near[r].astype(jnp.bfloat16)
            near[r] = jnp.minimum(dot(step, step), 1.0)
    half = cosine.shape[2] // 2
    lane = lax.broadcasted_iota(jnp.int32, cosine.shape[1:], 1)
    for r in range(requests):
        reach[r] = near[r]
        depth = jnp.sum(near[r], axis=-1, keepdims=True) - 1.0
        angle = (lengths[r].astype(jnp.float32) + depth) * frequency[...]
        cosine[r] = jnp.cos(angle)
        sines = jnp.sin(angle)
        sine[r] = jnp.where(lane < half, -sines, sines)


def prepare(lengths, parents, head_dim):
    requests, tree = parents.shape
    half = head_dim // 2
    frequency = ROPE_BASE ** (-np.arange(half, dtype=np.float64) / half)
    frequency = np.concatenate([frequency, frequency])[None].astype(np.float32)
    table = jax.ShapeDtypeStruct((requests, tree, head_dim), jnp.float32)
    return pl.pallas_call(
        prepare_kernel,
        in_specs=[in_smem(), in_vmem(), in_vmem()],
        out_specs=[in_vmem()] * 3,
        out_shape=[jax.ShapeDtypeStruct((requests, tree, tree), jnp.float32), table, table],
        compiler_params=pltpu.CompilerParams(vmem_limit_bytes=16 * 2**20),
        cost_estimate=SMALL,
        name="prepare",
    )(lengths, parents, frequency)


def attend_kernel(
    place, lengths, first, second, gain, weight, cosine, sine, reach, cache, outward, *rest, offset
):
    term, term_other = rest[0:2]
    fresh = rest[2:4]
    weight_here, cache_here, gain_here, outward_here, sems = rest[4:]
    tree = first.shape[0]
    width, columns = weight.shape
    head_dim = cosine.shape[2]
    group = columns // head_dim - 2
    deep = width // 2

    gain_copy = pltpu.make_async_copy(gain, gain_here, sems.at[0])
    weight_copies = [
        pltpu.make_async_copy(
            weight.at[pl.ds(i * deep, deep)], weight_here.at[pl.ds(i * deep, deep)], sems.at[1 + i]
        )
        for i in range(2)
    ]
    cache_copies = [
        pltpu.make_async_copy(
            cache.at[place[0] ^ (offset + i)], cache_here.at[i], sems.at[3 + i]
        )
        for i in range(2)
    ]
    outward_copy = pltpu.make_async_copy(outward, outward_here, sems.at[5])
    for copy in [gain_copy, *weight_copies]:
        copy.start()

    wide = jnp.concatenate([first[...], second[...]], axis=0).astype(jnp.float32)
    power = jnp.mean(wide * wide, axis=-1, keepdims=True)
    gain_copy.wait()
    normed = (wide * lax.rsqrt(power + EPSILON) * gain_here[...]).astype(jnp.bfloat16)
    weight_copies[0].wait()
    cache_copies[0].start()
    projected = dot(normed[:, :deep], weight_here[:deep])
    weight_copies[1].wait()
    cache_copies[1].start()
    projected = projected + dot(normed[:, deep:], weight_here[deep:])
    scale = 1.0 / math.sqrt(head_dim)
    results = []

    for i in range(2):
        own = projected[i * tree : (i + 1) * tree]
        request = place[0] ^ (offset + i)
        length = lengths[request]

        def rope(values):
            return values * cosine[request] + pltpu.roll(values, head_dim // 2, 1) * sine[request]

        def column(c):
            return own[:, c * head_dim : (c + 1) * head_dim]

        query = jnp.concatenate(
            [rope(column(h)).astype(jnp.bfloat16) for h in range(group)], axis=0
        )
        key_new = rope(column(group)).astype(jnp.bfloat16)
        value_new = column(group + 1).astype(jnp.bfloat16)
        fresh[i][:, :head_dim] = key_new
        fresh[i][:, head_dim:] = value_new

        def against(keys):
            return (
                lax.dot_general(
                    query, keys, (((1,), (1,)), ((), ())), preferred_element_type=jnp.float32
                )
                * scale
            )

        allowed = jnp.concatenate([reach[request]] * group, axis=0) > 0.5
        scores = jnp.where(allowed, against(key_new), -1e30)
        peak = jnp.max(scores, axis=-1, keepdims=True)
        weights = jnp.exp(scores - peak)
        total = jnp.sum(weights, axis=-1, keepdims=True)
        summed = dot(weights.astype(jnp.bfloat16), value_new)
        cache_copies[i].wait()
        if i == 0:
            outward_copy.start()

        def chunk(j, carry):
            peak, total, summed = carry
            block = pl.ds(pl.multiple_of(j * CHUNK, CHUNK), CHUNK)
            scores = against(cache_here[i, block, :head_dim])
            place = j * CHUNK + lax.broadcasted_iota(jnp.int32, scores.shape, 1)
            scores = jnp.where(place < length, scores, -1e30)
            higher = jnp.maximum(peak, jnp.max(scores, axis=-1, keepdims=True))
            fade = jnp.exp(peak - higher)
            weights = jnp.exp(scores - higher)
            total = total * fade + jnp.sum(weights, axis=-1, keepdims=True)
            values = cache_here[i, block, head_dim:]
            summed = summed * fade + dot(weights.astype(jnp.bfloat16), values)
            return (higher, total, summed)

        peak, total, summed = lax.fori_loop(
            0, lax.div(length + CHUNK - 1, CHUNK), chunk, (peak, total, summed)
        )
        result = (summed / total).astype(jnp.bfloat16)
        result = jnp.concatenate(
            [result[h * tree : (h + 1) * tree] for h in range(group)], axis=1
        )
        results.append(result)
    outward_copy.wait()
    terms = dot(jnp.concatenate(results, axis=0), outward_here[...])
    term[...] = terms[:tree]
    term_other[...] = terms[tree:].astype(jnp.bfloat16)


def in_vmem():
    return pl.BlockSpec(memory_space=pltpu.VMEM)


def in_smem():
    return pl.BlockSpec(memory_space=pltpu.SMEM)


def in_hbm():
    return pl.BlockSpec(memory_space=pltpu.HBM)


def attend(offset, place, lengths, first, second, gain, weight, cosine, sine, reach, cache, outward):
    tree, width = first.shape
    slots, pair = cache.shape[1:]
    head_dim = pair // 2
    columns = weight.shape[1]
    group_columns = columns - pair
    return pl.pallas_call(
        functools.partial(attend_kernel, offset=offset),
        in_specs=[
            in_smem(),
            in_smem(),
            in_vmem(),
            in_vmem(),
            in_hbm(),
            in_hbm(),
            in_vmem(),
            in_vmem(),
            in_vmem(),
            in_hbm(),
            in_hbm(),
        ],
        out_specs=[in_vmem()] * 4,
        out_shape=[
            jax.ShapeDtypeStruct((tree, width), jnp.float32),
            jax.ShapeDtypeStruct((tree, width), jnp.bfloat16),
        ]
        + [jax.ShapeDtypeStruct((tree, pair), jnp.bfloat16)] * 2,
        scratch_shapes=[
            pltpu.VMEM((width, columns), jnp.bfloat16),
            pltpu.VMEM((2, slots, pair), jnp.bfloat16),
            pltpu.VMEM((1, width), jnp.float32),
            pltpu.VMEM((group_columns, width), jnp.bfloat16),
            pltpu.SemaphoreType.DMA((6,)),
        ],
        compiler_params=pltpu.CompilerParams(vmem_limit_bytes=58 * 2**20),
        cost_estimate=SMALL,
        name="attend",
    )(place, lengths, first, second, gain, weight, cosine, sine, reach, cache, outward)


def silu(values):
    return values / (1.0 + jnp.exp(-values))


def expert_kernel(*refs, plane, count, tiles):
    pieces = refs[:plane]
    weights = refs[plane : plane + 4]
    outs = refs[plane + 4 : plane + 4 + count * plane]
    rows, inner_a, outer_a, inner_b, outer_b, both, hidden, first, sems = refs[
        plane + 4 + count * plane :
    ]
    each = pieces[0].shape[0]
    parts = len(tiles)
    copies = []
    for inner, outer, inner_here, outer_here in (
        (weights[0], weights[1], inner_a, outer_a),
        (weights[2], weights[3], inner_b, outer_b),
    ):
        for start, size in tiles:
            block = pl.ds(start, size)
            number = len(copies)
            copies.append(
                pltpu.make_async_copy(inner.at[block], inner_here.at[block], sems.at[number])
            )
        copies.append(pltpu.make_async_copy(outer, outer_here, sems.at[len(copies)]))
    for copy in copies[:2]:
        copy.start()

    def take(number):
        copies[number].wait()
        if number + 2 < len(copies):
            copies[number + 2].start()

    for i in range(plane):
        rows[i * each : (i + 1) * each] = pieces[i][...]
    for n, (inner_here, outer_here) in enumerate(((inner_a, outer_a), (inner_b, outer_b))):
        base = n * (parts + 1)
        for p, (start, size) in enumerate(tiles):
            take(base + p)
            term = dot(rows[:, start : start + size], inner_here[start : start + size])
            both[...] = term if p == 0 else both[...] + term
        half = both.shape[1] // 2
        hidden[...] = (silu(both[:, :half]) * both[:, half:]).astype(jnp.bfloat16)
        take(base + parts)
        term = dot(hidden[...], outer_here[...]).astype(jnp.bfloat16)
        if n == 0:
            first[...] = term
    result = (first[...].astype(jnp.float32) + term.astype(jnp.float32)).astype(jnp.bfloat16)
    step = each // count
    for n in range(count * plane):
        base = (n % plane) * each + (n // plane) * step
        outs[n][...] = result[base : base + step]


def experts(pieces, count, inner, outer):
    plane = len(pieces)
    each, width = pieces[0].shape
    hidden = inner[0].shape[1]
    tiles = ((0, width // 2), (width // 2, width - width // 2))
    rows = plane * each
    weight_scratch = [
        pltpu.VMEM((width, hidden), jnp.bfloat16),
        pltpu.VMEM((hidden // 2, width), jnp.bfloat16),
    ]
    made = pl.pallas_call(
        functools.partial(expert_kernel, plane=plane, count=count, tiles=tiles),
        in_specs=[in_vmem()] * plane + [in_hbm()] * 4,
        out_specs=[in_vmem()] * (count * plane),
        out_shape=[jax.ShapeDtypeStruct((each // count, width), jnp.bfloat16)] * (count * plane),
        scratch_shapes=[pltpu.VMEM((rows, width), jnp.bfloat16)]
        + weight_scratch * 2
        + [
            pltpu.VMEM((rows, hidden), jnp.float32),
            pltpu.VMEM((rows, hidden // 2), jnp.bfloat16),
            pltpu.VMEM((rows, width), jnp.bfloat16),
            pltpu.SemaphoreType.DMA((2 * (len(tiles) + 1),)),
        ],
        compiler_params=pltpu.CompilerParams(vmem_limit_bytes=40 * 2**20),
        cost_estimate=SMALL,
        name="expert",
    )(*pieces, inner[0], outer[0], inner[1], outer[1])
    return [list(made[i * plane : (i + 1) * plane]) for i in range(count)]


def shared_kernel(*refs, side):
    blocks = refs[:side]
    weights = refs[side : side + 6]
    outs = refs[side + 6 : 2 * side + 6]
    here, sems = refs[2 * side + 6 :]
    copies = [pltpu.make_async_copy(weights[i], here.at[i], sems.at[i]) for i in range(6)]
    for copy in copies[:2]:
        copy.start()

    def take(number):
        copies[number].wait()
        if number + 2 < len(copies):
            copies[number + 2].start()

    tree = blocks[0].shape[0]
    rows = jnp.concatenate([block[...] for block in blocks], axis=0).T

    def turned(i):
        take(i)
        return dot(here[i], rows)

    result = None
    for n in range(2):
        hidden = silu(turned(3 * n))
        hidden = (hidden * turned(3 * n + 1)).astype(jnp.bfloat16)
        take(3 * n + 2)
        term = lax.dot_general(
            hidden, here[3 * n + 2], (((0,), (0,)), ((), ())), preferred_element_type=jnp.float32
        )
        result = term if result is None else result + term
    for i in range(side):
        outs[i][...] = result[i * tree : (i + 1) * tree].astype(outs[i].dtype)


def shared_terms(own, beside, weights):
    tree, width = own.shape
    units = weights[0].shape[0]
    side = 1 + len(beside)
    outs = pl.pallas_call(
        functools.partial(shared_kernel, side=side),
        in_specs=[in_vmem()] * side + [in_hbm()] * 6,
        out_specs=[in_vmem()] * side,
        out_shape=[jax.ShapeDtypeStruct((tree, width), jnp.float32)]
        + [jax.ShapeDtypeStruct((tree, width), jnp.bfloat16)] * (side - 1),
        scratch_shapes=[
            pltpu.VMEM((6, units, width), jnp.bfloat16),
            pltpu.SemaphoreType.DMA((6,)),
        ],
        compiler_params=pltpu.CompilerParams(vmem_limit_bytes=60 * 2**20),
        cost_estimate=SMALL,
        name="shared",
    )(own, *beside, *weights)
    return outs[0], list(outs[1:])


def finish_kernel(tokens, term, gain, routes, *refs):
    others = refs[:-3]
    resid, normed, payload = refs[-3:]
    width = tokens.shape[1]
    attn = term[...]
    for other in others:
        attn = attn + other[...].astype(jnp.float32)
    rounded = (tokens[...].astype(jnp.float32) + attn).astype(jnp.bfloat16)
    resid[...] = rounded
    wide = rounded.astype(jnp.float32)
    power = jnp.mean(wide * wide, axis=-1, keepdims=True)
    rows = (wide * lax.rsqrt(power + EPSILON) * gain[...]).astype(jnp.bfloat16)
    normed[...] = rows
    payload[:, :width] = rows
    extra = payload.shape[1] - width
    lane = lax.broadcasted_iota(jnp.int32, (tokens.shape[0], extra), 1)
    numbers = jnp.zeros(lane.shape, jnp.float32)
    for t in range(routes.shape[1]):
        numbers = jnp.where(lane == t, routes[:, t : t + 1].astype(jnp.float32), numbers)
    payload[:, width:] = numbers.astype(jnp.bfloat16)


def finish(tokens, term, others, gain, routes):
    tree, width = tokens.shape
    return pl.pallas_call(
        finish_kernel,
        in_specs=[in_vmem()] * (4 + len(others)),
        out_specs=[in_vmem()] * 3,
        out_shape=[
            jax.ShapeDtypeStruct((tree, width), jnp.bfloat16),
            jax.ShapeDtypeStruct((tree, width), jnp.bfloat16),
            jax.ShapeDtypeStruct((tree, width + EXTRA), jnp.bfloat16),
        ],
        compiler_params=pltpu.CompilerParams(vmem_limit_bytes=16 * 2**20),
        cost_estimate=SMALL,
        name="finish",
    )(tokens, term, gain, routes, *others)


def select_kernel(*refs, count, plane, capacity, top_count):
    near = refs[0]
    router = refs[1]
    sources = refs[2 : 2 + count]
    outs = refs[2 + count : 2 + count + plane]
    spreads = refs[2 + count + plane :]
    width, expert_count = router.shape
    tree = sources[0].shape[0]
    lane = lax.broadcasted_iota(jnp.int32, (tree, plane * capacity), 1)
    place = lax.rem(lane, capacity).astype(jnp.float32)
    owner = lax.div(lane, capacity)
    expert = lax.broadcasted_iota(jnp.int32, (tree, expert_count), 1)
    row = lax.broadcasted_iota(jnp.int32, (tree, tree), 0)
    column = lax.broadcasted_iota(jnp.int32, (tree, tree), 1)
    before = jnp.where(column < row, 1.0, 0.0).astype(jnp.bfloat16)
    for i in range(count):
        rows = sources[i][:, :width]
        routes = sources[i][:, width:].astype(jnp.float32)
        member = jnp.zeros((tree, expert_count), jnp.float32)
        for t in range(top_count):
            named = routes[:, t : t + 1] == expert.astype(jnp.float32)
            member = jnp.where(named, 1.0, member)
        ranks = dot(before, member.astype(jnp.bfloat16))
        slots = jnp.where(member > 0.5, ranks, -1.0)
        logits = dot(rows, router[...])
        picked = member / (1.0 + jnp.exp(-logits))
        gates = picked / jnp.sum(picked, axis=-1, keepdims=True)
        slot = jnp.zeros(lane.shape, jnp.float32)
        gate = jnp.zeros(lane.shape, jnp.float32)
        for o in range(plane):
            mine = expert == near[o]
            slot_o = jnp.sum(jnp.where(mine, slots, 0.0), axis=-1, keepdims=True)
            gate_o = jnp.sum(jnp.where(mine, gates, 0.0), axis=-1, keepdims=True)
            slot = jnp.where(owner == o, slot_o, slot)
            gate = jnp.where(owner == o, gate_o, gate)
        pick = slot == place
        spreads[i][...] = jnp.where(pick, gate, 0.0).astype(jnp.bfloat16)
        chosen = lax.dot_general(
            jnp.where(pick, 1.0, 0.0).astype(jnp.bfloat16),
            rows,
            (((0,), (0,)), ((), ())),
            preferred_element_type=jnp.float32,
        ).astype(jnp.bfloat16)
        for o in range(plane):
            outs[o][i * capacity : (i + 1) * capacity] = chosen[o * capacity : (o + 1) * capacity]


def select(near, router, sources, plane, capacity, top_count, cost):
    tree = sources[0].shape[0]
    width = router.shape[0]
    count = len(sources)
    made = pl.pallas_call(
        functools.partial(
            select_kernel, count=count, plane=plane, capacity=capacity, top_count=top_count
        ),
        in_specs=[in_smem()] + [in_vmem()] * (1 + count),
        out_specs=[in_vmem()] * (plane + count),
        out_shape=[jax.ShapeDtypeStruct((count * capacity, width), jnp.bfloat16)] * plane
        + [jax.ShapeDtypeStruct((tree, plane * capacity), jnp.bfloat16)] * count,
        compiler_params=pltpu.CompilerParams(vmem_limit_bytes=16 * 2**20),
        cost_estimate=cost,
        name="select",
    )(near, router, *sources)
    return list(made[:plane]), list(made[plane:])


def combine_kernel(spread, *refs):
    out = refs[-1]
    back = jnp.concatenate([piece[...] for piece in refs[:-1]], axis=0)
    out[...] = dot(spread[...], back).astype(out.dtype)


def combine(spread, pieces, dtype):
    tree = spread.shape[0]
    width = pieces[0].shape[1]
    return pl.pallas_call(
        combine_kernel,
        in_specs=[in_vmem()] * (1 + len(pieces)),
        out_specs=in_vmem(),
        out_shape=jax.ShapeDtypeStruct((tree, width), dtype),
        compiler_params=pltpu.CompilerParams(vmem_limit_bytes=16 * 2**20),
        cost_estimate=SMALL,
        name="combine",
    )(spread, *pieces)


def final_kernel(live, resid, shared, routed, *refs):
    total = resid[...].astype(jnp.float32) + shared[...] + routed[...]
    for part in refs[:-1]:
        total = total + part[...].astype(jnp.float32)
    refs[-1][...] = jnp.where(live[...] == 1, total, 0.0).astype(jnp.bfloat16)


def final(live, resid, shared, routed, parts):
    return pl.pallas_call(
        final_kernel,
        in_specs=[in_vmem()] * (4 + len(parts)),
        out_specs=in_vmem(),
        out_shape=jax.ShapeDtypeStruct(resid.shape, jnp.bfloat16),
        compiler_params=pltpu.CompilerParams(vmem_limit_bytes=16 * 2**20),
        cost_estimate=SMALL,
        name="final",
    )(live, resid, shared, routed, *parts)


def body(
    tokens,
    live,
    parents,
    lengths,
    accepted,
    routes,
    cache,
    attn_gain,
    w_qkv,
    w_out,
    ffn_gain,
    shared_gate,
    shared_up,
    shared_down,
    router,
    expert_in,
    expert_out,
):
    tree = tokens.shape[1]
    width = tokens.shape[2]
    own_rows = tokens[0]
    group_count = lax.axis_size(HEAD)
    head_dim = cache.shape[3] // 2
    me = lax.axis_index(HEAD)

    side = lax.axis_size("x")
    near = [own_rows] + [partner(own_rows, "x", o) for o in range(1, side)]
    near_core = [partner(own_rows, "c", 1)]

    reach, cosine, sine = prepare(lengths, parents, head_dim)
    place = me.astype(jnp.int32)[None]
    for o in range(1, side):
        near[o], cosine, sine, reach, place = lax.optimization_barrier(
            (near[o], cosine, sine, reach, place)
        )
        near_core.append(partner(near[o], "c", 1))

    gate_turned, up_turned = shared_gate.T, shared_up.T
    early, near_core[0] = lax.optimization_barrier(((gate_turned, expert_out[0]), near_core[0]))
    early = [partner(weight, "c", 1) for weight in early]
    middle, near_core = lax.optimization_barrier(
        ((up_turned, shared_down), near_core)
    )
    middle = [partner(weight, "c", 1) for weight in middle]
    near_core, early = lax.optimization_barrier((near_core, early))

    terms = [None] * side
    fresh = [None] * side
    follow = None
    late = expert_in[0]
    for o in reversed(range(side)):
        if follow is not None:
            near_core[o], follow = lax.optimization_barrier((near_core[o], follow))
        own_part, other_part, fresh_own, fresh_other = attend(
            2 * o,
            place,
            lengths,
            near[o],
            near_core[o],
            attn_gain[None],
            w_qkv,
            cosine,
            sine,
            reach,
            cache[:, 0],
            w_out,
        )
        fresh[o] = jnp.stack([fresh_own, fresh_other])
        other = partner(other_part, "c", 1)
        if o == side - 1:
            other, middle, late = lax.optimization_barrier((other, middle, late))
            late = partner(late, "c", 1)
        if o:
            follow = (own_part + other.astype(jnp.float32)).astype(jnp.bfloat16)
            crossed = partner(follow, "x", o).astype(jnp.float32)
            terms[o] = crossed if o == side - 1 else crossed + terms[o + 1]
    own_term = own_part + terms[1] if side > 1 else own_part
    own_term, late = lax.optimization_barrier((own_term, late))
    others = [other]
    resid, normed, payload = finish(own_rows, own_term, others, ffn_gain[None], routes[0])
    inner = [expert_in[0], late]
    outer = [expert_out[0], early[1]]
    shared_weights = [gate_turned, up_turned, shared_down, early[0], *middle]
    order = me ^ jnp.arange(group_count, dtype=jnp.int32)
    kept = accepted[order][:, :, None] == jnp.arange(tree, dtype=jnp.int32)
    accepted_kv = jnp.einsum(
        "ran,rnd->rad",
        kept.astype(jnp.bfloat16),
        jnp.concatenate(fresh, axis=0),
        preferred_element_type=jnp.float32,
    ).astype(jnp.bfloat16)[order][:, None]

    expert_count = router.shape[1]
    top_count = routes.shape[2]
    capacity = 4 * tree * top_count // (3 * expert_count)
    plane = lax.axis_size(PLANE)
    line = lax.axis_size("z")
    near_experts = lax.axis_index("z") * plane + (
        lax.axis_index(PLANE) ^ jnp.arange(plane, dtype=jnp.int32)
    )
    line_rows = [payload] + [partner(payload, "z", k) for k in range(1, line)]
    beside = [partner(normed, "x", o) for o in range(1, side)]

    shared, beside = shared_terms(normed, beside, shared_weights)
    line_rows[3], beside = lax.optimization_barrier((line_rows[3], beside))

    sent = []
    spread = {}
    for ks in GROUPS:
        pieces, spreads = select(
            near_experts,
            router,
            [line_rows[k] for k in ks],
            plane,
            capacity,
            top_count,
            LARGE if sent else SMALL,
        )
        spread.update(zip(ks, spreads))
        sent.append([partner(pieces[o], PLANE, o) for o in range(plane)])
    parts = [partner(beside[o - 1], "x", o) for o in range(1, side)]
    made = None
    results = {}
    for ks, pieces in zip(GROUPS, sent):
        if made is not None:
            pieces, made = lax.optimization_barrier((pieces, made))
        made = experts(pieces, len(ks), inner, outer)
        results.update(zip(ks, made))
    totals = {}
    landed = {}
    for k, after, arrived in BACK:
        pieces = results[k]
        if k == BACK[1][0]:
            pieces, parts = lax.optimization_barrier((pieces, parts))
        if after is not None:
            pieces, totals[after] = lax.optimization_barrier((pieces, totals[after]))
        if arrived is not None:
            pieces, landed[arrived] = lax.optimization_barrier((pieces, landed[arrived]))
        back = [partner(pieces[o], PLANE, o) for o in range(plane)]
        totals[k] = combine(spread[k], back, jnp.bfloat16 if k else jnp.float32)
        if k:
            landed[k] = partner(totals[k], "z", k)
    parts += list(landed.values())
    routed = totals[0]
    hidden_out = final(live[0][:, None], resid, shared, routed, parts)
    return (hidden_out[None], accepted_kv)


def solution(mesh):
    line = 4
    shape = (line, mesh.shape["req"] // line, mesh.shape["head"] // 2, 2)
    grid = Mesh(mesh.devices.reshape(shape), ALL)
    req = ("z", "y")
    in_specs = (
        P(ALL, None, None),
        P(ALL, None),
        P(req, None),
        P(req),
        P(req, None),
        P(ALL, None, None),
        P(req, HEAD, None, None),
        P(),
        P(None, HEAD),
        P(HEAD, None),
        P(),
        P(None, HEAD),
        P(None, HEAD),
        P(HEAD, None),
        P(),
        P(ALL, None, None),
        P(ALL, None, None),
    )
    out_specs = (P(ALL, None, None), P(req, HEAD, None, None))
    return jax.shard_map(body, mesh=grid, in_specs=in_specs, out_specs=out_specs, check_vma=False)
```
